32 devices in a mesh: dp: 8 (over z, core), seq: 4 (over y, x).
Axes of the slice: x: 2, y: 2, z: 4, core: 2. Of those that a mesh axis runs over, the one named last changes fastest.
Arguments:
- inputs: bfloat16 [8, 2048, 1024], P('dp', 'seq'), may hold values from -6 to 6
- segments: int32 [8, 2048], P('dp'), may hold values from 0 to 34, as said below
- cotangent: bfloat16 [8, 2048, 1024], P('dp', 'seq'), may hold values from -6 to 6
- norm_gain_mix: float32 [1024], replicated, may hold values from 0.5 to 1.5
- w_query: float32 [1024, 1024], P('dp'), may hold values from -0.1875 to 0.1875
- w_key: float32 [1024, 1024], P('dp'), may hold values from -0.1875 to 0.1875
- w_value: float32 [1024, 2048], P('dp'), may hold values from -0.1875 to 0.1875
- w_outgate: float32 [1024, 2048], P('dp'), may hold values from -0.1875 to 0.1875
- w_gates: float32 [1024, 16], P('dp'), may hold values from -0.1875 to 0.1875
- conv_weight: float32 [4, 4096], replicated, may hold values from -3 to 3
- decay_log: float32 [8], replicated, may hold values from 0 to 2.77
- dt_bias: float32 [8], replicated, may hold values from -6.9 to -2.25
- out_norm_gain: float32 [256], replicated, may hold values from 0.5 to 1.5
- w_out: float32 [2048, 1024], P(None, 'dp'), may hold values from -0.25 to 0.25
- norm_gain_ffn: float32 [1024], replicated, may hold values from 0.5 to 1.5
- w_ffn_gate: float32 [1024, 2816], P('dp'), may hold values from -0.1875 to 0.1875
- w_ffn_up: float32 [1024, 2816], P('dp'), may hold values from -0.1875 to 0.1875
- w_ffn_down: float32 [2816, 1024], P(None, 'dp'), may hold values from -0.21875 to 0.21875
Outputs:
- output: bfloat16 [8, 2048, 1024], P('dp', 'seq')
- grad_inputs: float32 [8, 2048, 1024], P('dp', 'seq')
- grad_norm_gain_mix: float32 [1024], replicated
- grad_w_query: float32 [1024, 1024], P('dp')
- grad_w_key: float32 [1024, 1024], P('dp')
- grad_w_value: float32 [1024, 2048], P('dp')
- grad_w_outgate: float32 [1024, 2048], P('dp')
- grad_w_gates: float32 [1024, 16], P('dp')
- grad_conv_weight: float32 [4, 4096], replicated
- grad_decay_log: float32 [8], replicated
- grad_dt_bias: float32 [8], replicated
- grad_out_norm_gain: float32 [256], replicated
- grad_w_out: float32 [2048, 1024], P(None, 'dp')
- grad_norm_gain_ffn: float32 [1024], replicated
- grad_w_ffn_gate: float32 [1024, 2816], P('dp')
- grad_w_ffn_up: float32 [1024, 2816], P('dp')
- grad_w_ffn_down: float32 [2816, 1024], P(None, 'dp')
The draws below stay inside these ranges and needn't reach their ends.
Inputs may be any that keep to these rules, and one draw needn't show every extreme that they name: `segments`: per row, segment numbers start at 0, never fall, and rise by one at each document's first token; each row holds exactly 35 documents; one document of each row begins within the first 512 tokens and ends within the last 512.
All inputs are finite; a program needn't handle non-finite values.
Results may differ from the reference program's by a relative error of at most 0.019.
Values may be sent and summed in bfloat16 or wider, within the bound.
A program may use at most 448 MiB of HBM per device.

```python
import jax
import jax.numpy as jnp
from jax import lax

D = 1024
H = 8
DK = 128
DV = 256
FF = 2816
CONV = 4
STRETCH = 64
TOK_DEV = 512
HK = 1024
HV = 2048
CH = 4096
ROWS = 8
LEN = 2048


def draw_segments(key, part):
    key = jax.random.fold_in(key, 11)
    first_key, second_key, third_key = jax.random.split(key, 3)
    positions = jnp.arange(LEN)[None, :]
    opening = jax.random.randint(first_key, (ROWS, 1), TOK_DEV // 4, TOK_DEV // 2 + 1)
    closing = jax.random.randint(second_key, (ROWS, 1), LEN - TOK_DEV // 2, LEN - TOK_DEV // 4)
    row_keys = jax.random.split(third_key, ROWS)
    orders = jax.vmap(lambda one_key: jax.random.permutation(one_key, LEN))(row_keys).astype(jnp.int32)
    allowed = (positions > 0) & (positions < opening) | (positions > closing)
    scores = jnp.where(allowed, orders, -1)
    picked = lax.top_k(scores, TOK_DEV // 16)[1]
    extra = jnp.any(positions[:, :, None] == picked[:, None, :], axis=2)
    forced = (positions == opening) | (positions == closing)
    starts = forced | extra
    return jnp.cumsum(starts.astype(jnp.int32), axis=1).astype(jnp.int32)


def block_levels(stream_key, dims, shards, least, largest):
    factor_of = 1.0
    for position, blocks in shards:
        steps = jax.random.uniform(jax.random.fold_in(jax.random.fold_in(stream_key, 6), position), (blocks,), jnp.float32, least / len(shards), largest / len(shards))
        factor_of = factor_of * jnp.repeat(jnp.exp(steps), dims[position] // blocks).reshape((-1,) + (1,) * (len(dims) - 1 - position))
    return factor_of


def centred(key, dims, scale, most, shards=(), held_as=jnp.bfloat16):
    factor_of = block_levels(key, dims, shards, -0.22, 0.18) if shards else 1.0
    drawn = jax.random.normal(key, dims, jnp.float32) * scale * factor_of
    return jnp.minimum(jnp.maximum(drawn, -most), most).astype(held_as)


def setup_inputs(seed: int = 0) -> dict:
    seeds = jax.random.split(jax.random.key(seed), 19)
    inputs = centred(seeds[0], (ROWS, LEN, D), 1.0, 6.0, ((0, 8), (1, 4)))
    segments = draw_segments(jax.random.fold_in(seeds[18], 71), 0)
    cotangent = centred(seeds[2], (ROWS, LEN, D), 1.0, 6.0, ((0, 8), (1, 4)))
    norm_gain_mix = jnp.clip(1.0 + 0.1 * jax.random.normal(seeds[3], (D,), jnp.float32), 0.5, 1.5)
    w_query = centred(seeds[4], (D, HK), D ** -0.5, 0.1875, ((0, 8),), jnp.float32)
    w_key = centred(seeds[5], (D, HK), D ** -0.5, 0.1875, ((0, 8),), jnp.float32)
    w_value = centred(seeds[6], (D, HV), D ** -0.5, 0.1875, ((0, 8),), jnp.float32)
    w_outgate = centred(seeds[7], (D, HV), D ** -0.5, 0.1875, ((0, 8),), jnp.float32)
    w_gates = centred(seeds[8], (D, 2 * H), D ** -0.5, 0.1875, ((0, 8),), jnp.float32)
    conv_weight = centred(seeds[9], (CONV, CH), CONV ** -0.5, 3.0, (), jnp.float32)
    decay_log = jnp.clip(jax.random.uniform(seeds[10], (H,), jnp.float32, 0.0, 2.77), 0.0, 2.77)
    dt_bias = jnp.clip(jax.random.uniform(seeds[11], (H,), jnp.float32, -6.9, -2.25), -6.9, -2.25)
    out_norm_gain = jnp.clip(1.0 + 0.1 * jax.random.normal(seeds[12], (DV,), jnp.float32), 0.5, 1.5)
    w_out = centred(seeds[13], (HV, D), (HV // 4) ** -0.5, 0.25, ((1, 8),), jnp.float32)
    norm_gain_ffn = jnp.clip(1.0 + 0.1 * jax.random.normal(seeds[14], (D,), jnp.float32), 0.5, 1.5)
    w_ffn_gate = centred(seeds[15], (D, FF), D ** -0.5, 0.1875, ((0, 8),), jnp.float32)
    w_ffn_up = centred(seeds[16], (D, FF), D ** -0.5, 0.1875, ((0, 8),), jnp.float32)
    w_ffn_down = centred(seeds[17], (FF, D), (FF // 4) ** -0.5, 0.21875, ((1, 8),), jnp.float32)
    return {"inputs": inputs, "segments": segments, "cotangent": cotangent, "norm_gain_mix": norm_gain_mix, "w_query": w_query, "w_key": w_key, "w_value": w_value, "w_outgate": w_outgate, "w_gates": w_gates, "conv_weight": conv_weight, "decay_log": decay_log, "dt_bias": dt_bias, "out_norm_gain": out_norm_gain, "w_out": w_out, "norm_gain_ffn": norm_gain_ffn, "w_ffn_gate": w_ffn_gate, "w_ffn_up": w_ffn_up, "w_ffn_down": w_ffn_down}


@jax.custom_vjp
def low(v):
    return lax.optimization_barrier(v.astype(jnp.bfloat16)).astype(jnp.float32)

@jax.custom_vjp
def low_back(v):
    return v

def low_keep(v):
    return (low(v), None)

def low_pass(kept, grad):
    return (grad,)

def back_keep(v):
    return (v, None)

def back_low(kept, grad):
    return (low(grad),)
low.defvjp(low_keep, low_pass)
low_back.defvjp(back_keep, back_low)
precise = lax.Precision.HIGHEST

def product(left, right):
    return jnp.dot(left.astype(jnp.float32), right.astype(jnp.float32), precision=precise, preferred_element_type=jnp.float32)

def rms_scale(values, weights, epsilon):
    return values * lax.rsqrt(lax.optimization_barrier(jnp.mean(values * values, axis=-1, keepdims=True)) + epsilon) * weights

def unit_rows(values):
    return values * lax.rsqrt(lax.optimization_barrier(jnp.sum(values * values, axis=-1, keepdims=True)) + 1e-06)

def conv_mix(padded, seg_ext, conv_weight):
    length = padded.shape[0] - (CONV - 1)
    current = seg_ext[CONV - 1:]
    total = jnp.zeros((length, padded.shape[1]), jnp.float32)
    for offset in range(CONV):
        begin = CONV - 1 - offset
        same_doc = (seg_ext[begin:begin + length] == current).astype(jnp.float32)
        total = total + padded[begin:begin + length] * conv_weight[offset] * same_doc[:, None]
    return jax.nn.silu(total)

def prepare(padded, gate_logits, conv_weight, decay_log, dt_bias, seg_ext):
    mixed = conv_mix(padded, seg_ext, conv_weight)
    length = mixed.shape[0]
    query_rows = unit_rows(mixed[:, :H * DK].reshape(length, H, DK)) * DK ** (-0.5)
    key_rows = unit_rows(mixed[:, H * DK:2 * H * DK].reshape(length, H, DK))
    value_rows = mixed[:, 2 * H * DK:].reshape(length, H, DV)
    strength = jax.nn.sigmoid(gate_logits[:, H:])
    decay = -jnp.exp(decay_log) * jax.nn.softplus(gate_logits[:, :H] + dt_bias)
    return (query_rows, key_rows, value_rows, strength, decay)

def delta_stretch(state, block):
    query_rows, key_rows, value_rows, strength, decay, seg_block, seg_before = block
    length = query_rows.shape[0]
    cumulative = jnp.cumsum(decay, axis=0).T
    row_ids = jnp.arange(length)
    same_doc = seg_block[:, None] == seg_block[None, :]
    causal = (row_ids[:, None] >= row_ids[None, :]) & same_doc
    strict = causal & (row_ids[:, None] > row_ids[None, :])
    spread = jnp.where(causal[None], cumulative[:, :, None] - cumulative[:, None, :], 0.0)
    gamma = jnp.exp(spread) * causal[None]
    carry_scale = jnp.exp(cumulative) * (seg_block == seg_before)[None, :]
    queries = jnp.transpose(query_rows, (1, 0, 2))
    keys_t = jnp.transpose(key_rows, (1, 0, 2))
    values_t = jnp.transpose(value_rows, (1, 0, 2))
    beta_t = strength.T
    key_dots = jnp.einsum('hid,hjd->hij', keys_t, keys_t, precision=precise)
    system = jnp.eye(length, dtype=jnp.float32)[None] + beta_t[:, :, None] * gamma * key_dots * strict[None]
    target = beta_t[:, :, None] * (values_t - carry_scale[:, :, None] * jnp.einsum('hcd,hdw->hcw', keys_t, state, precision=precise))
    updates = jax.scipy.linalg.solve_triangular(system, target, lower=True, unit_diagonal=True)
    scores = jnp.einsum('hid,hjd->hij', queries, keys_t, precision=precise) * gamma
    readout = carry_scale[:, :, None] * jnp.einsum('hcd,hdw->hcw', queries, state, precision=precise)
    readout = readout + jnp.einsum('hij,hjw->hiw', scores, updates, precision=precise)
    new_state = carry_scale[:, -1][:, None, None] * state + jnp.einsum('hc,hcd,hcw->hdw', gamma[:, -1, :], keys_t, updates, precision=precise)
    return (new_state, jnp.transpose(readout, (1, 0, 2)))

def run_blocks(state, query_rows, key_rows, value_rows, strength, decay, seg_dev, seg_prev, stepper):
    length = query_rows.shape[0]
    count = length // STRETCH

    def blocked(values):
        return values.reshape((count, STRETCH) + values.shape[1:])
    starts = jnp.concatenate([seg_prev[None], seg_dev[STRETCH - 1:length - 1:STRETCH]])
    final, readout = lax.scan(stepper, state, (blocked(query_rows), blocked(key_rows), blocked(value_rows), blocked(strength), blocked(decay), blocked(seg_dev), starts))
    return (final, readout.reshape((length,) + readout.shape[2:]))

def gated_norm(attn, gate_pre, out_norm_gain):
    length = attn.shape[0]
    normed = rms_scale(attn, out_norm_gain, 1e-05)
    return (normed * jax.nn.silu(gate_pre.reshape(length, H, DV))).reshape(length, H * DV)

def forward_row(row_in, seg_row, norm_gain_mix, w_query, w_key, w_value, w_outgate, w_gates, conv_weight, decay_log, dt_bias, out_norm_gain, w_out, norm_gain_ffn, w_ffn_gate, w_ffn_up, w_ffn_down):
    hidden_in = low(rms_scale(row_in, norm_gain_mix, 1e-06))
    projected = low_back(low(jnp.concatenate([product(hidden_in, low(w_query)), product(hidden_in, low(w_key)), product(hidden_in, low(w_value))], axis=1)))
    gate_pre = low_back(product(hidden_in, low(w_outgate)))
    gate_logits = low_back(product(hidden_in, low(w_gates)))
    seg_ext = jnp.concatenate([jnp.full((CONV - 1,), -1, jnp.int32), seg_row.astype(jnp.int32)])
    padded = jnp.concatenate([jnp.zeros((CONV - 1, projected.shape[1]), jnp.float32), projected], axis=0)
    mixer_in = prepare(padded, gate_logits, conv_weight, decay_log, dt_bias, seg_ext)
    start_state = jnp.zeros((H, DK, DV), jnp.float32)
    final, attn = run_blocks(start_state, mixer_in[0], mixer_in[1], mixer_in[2], mixer_in[3], mixer_in[4], seg_ext[CONV - 1:], seg_ext[CONV - 2], jax.checkpoint(delta_stretch))
    gated = low(gated_norm(attn, gate_pre, out_norm_gain))
    resid = row_in + low_back(product(gated, low(w_out)))
    hidden_mid = low(rms_scale(resid, norm_gain_ffn, 1e-06))
    gate_val = low_back(product(hidden_mid, low(w_ffn_gate)))
    up_val = low_back(product(hidden_mid, low(w_ffn_up)))
    activ = low(jax.nn.silu(gate_val) * up_val)
    return resid + low_back(product(activ, low(w_ffn_down)))

def reference(inputs, segments, cotangent, norm_gain_mix, w_query, w_key, w_value, w_outgate, w_gates, conv_weight, decay_log, dt_bias, out_norm_gain, w_out, norm_gain_ffn, w_ffn_gate, w_ffn_up, w_ffn_down):
    params = (norm_gain_mix, w_query, w_key, w_value, w_outgate, w_gates, conv_weight, decay_log, dt_bias, out_norm_gain, w_out, norm_gain_ffn, w_ffn_gate, w_ffn_up, w_ffn_down)

    def one_row(totals, row):
        row_in, seg_row, cot_row = row

        def forward(row_values, *weights):
            return forward_row(row_values, seg_row, *weights)
        result, pullback = jax.vjp(forward, row_in.astype(jnp.float32), *params)
        grads = pullback(cot_row.astype(jnp.float32))
        totals = tuple((total_part + grad_part for total_part, grad_part in zip(totals, grads[1:])))
        return (totals, (result.astype(jnp.bfloat16), grads[0]))
    start_totals = tuple((jnp.zeros_like(weight_part) for weight_part in params))
    totals, rows_out = lax.scan(one_row, start_totals, (inputs, segments, cotangent))
    return (rows_out[0], rows_out[1], totals[0], totals[1], totals[2], totals[3], totals[4], totals[5], totals[6], totals[7], totals[8], totals[9], totals[10], totals[11], totals[12], totals[13], totals[14])
```

```python
import functools

import jax
import jax.numpy as jnp
from jax import lax
from jax.experimental import pallas as pl
from jax.experimental.pallas import tpu as pltpu
from jax.sharding import PartitionSpec as P

H = 8
DK = 128
DV = 256
CONV = 4
HALO = 16
CHUNK = 128
HC = 2 * DK + DV
LANES = 128
VMEM_LIMIT = 56 * 2**20

F32 = jnp.float32
BF16 = jnp.bfloat16
NN = ((1,), (0,))
NT = ((1,), (1,))
TN = ((0,), (0,))


def mm(left, right, dims=NN):
    return lax.dot_general(
        left.astype(BF16), right.astype(BF16), (dims, ((), ())), preferred_element_type=F32
    )


def mm_exact(left, right, dims=NN):
    return lax.dot_general(
        left, right, (dims, ((), ())), precision=lax.Precision.HIGHEST, preferred_element_type=F32
    )


def halves(value):
    high = value.astype(BF16)
    return high, (value - high.astype(F32)).astype(BF16)


def mm_three(left, right):
    left_high, left_low = halves(left)
    right_high, right_low = halves(right)
    return mm(left_high, right_high) + (mm(left_high, right_low) + mm(left_low, right_high))


def params(**more):
    return pltpu.CompilerParams(vmem_limit_bytes=VMEM_LIMIT, **more)


def cost(flops, nbytes):
    return pl.CostEstimate(flops=int(flops), bytes_accessed=int(nbytes), transcendentals=0)


def iota2(shape, axis):
    return lax.broadcasted_iota(jnp.int32, shape, axis)


def lane(value, index):
    picked = jnp.where(iota2(value.shape, 1) == index, value, 0.0)
    return jnp.sum(picked, axis=1, keepdims=True)


def to_row(column):
    size = column.shape[0]
    same = iota2((size, size), 0) == iota2((size, size), 1)
    return jnp.sum(jnp.where(same, column, 0.0), axis=0, keepdims=True)


def to_column(row):
    size = row.shape[1]
    same = iota2((size, size), 0) == iota2((size, size), 1)
    return jnp.sum(jnp.where(same, row, 0.0), axis=1, keepdims=True)


def project_kernel(x_ref, gain_ref, w_ref, wg_ref, p_ref, logit_ref, h_ref):
    @pl.when(pl.program_id(0) == 0)
    def _():
        value = x_ref[...].astype(F32)
        scale = lax.rsqrt(jnp.mean(value * value, axis=-1, keepdims=True) + 1e-06)
        h_ref[...] = (value * scale * gain_ref[...]).astype(BF16)
        logit_ref[...] = mm(h_ref[...], wg_ref[...])

    p_ref[...] = mm(h_ref[...], w_ref[...]).astype(BF16)


def project(x_ext, gain, w_qkv, w_gates):
    rows, width = x_ext.shape
    block = 512
    cols = w_qkv.shape[1]
    return pl.pallas_call(
        project_kernel,
        grid=(cols // block,),
        in_specs=[
            pl.BlockSpec((rows, width), lambda j: (0, 0)),
            pl.BlockSpec((1, width), lambda j: (0, 0)),
            pl.BlockSpec((width, block), lambda j: (0, j)),
            pl.BlockSpec((width, LANES), lambda j: (0, 0)),
        ],
        out_specs=[
            pl.BlockSpec((rows, block), lambda j: (0, j)),
            pl.BlockSpec((rows, LANES), lambda j: (0, 0)),
            pl.BlockSpec((rows, width), lambda j: (0, 0)),
        ],
        out_shape=[
            jax.ShapeDtypeStruct((rows, cols), BF16),
            jax.ShapeDtypeStruct((rows, LANES), F32),
            jax.ShapeDtypeStruct((rows, width), BF16),
        ],
        compiler_params=params(),
        cost_estimate=cost(2 * rows * width * cols, 2 * width * cols + 2 * rows * cols),
        name="project",
    )(x_ext, gain, w_qkv, w_gates)


def outgate_kernel(h_ref, w_ref, g_ref):
    g_ref[...] = mm(h_ref[HALO:, :], w_ref[...])


def outgate(hidden, w_og):
    rows, width = hidden.shape
    cols = w_og.shape[1]
    block = 512
    return pl.pallas_call(
        outgate_kernel,
        grid=(cols // block,),
        in_specs=[
            pl.BlockSpec((rows, width), lambda j: (0, 0)),
            pl.BlockSpec((width, block), lambda j: (0, j)),
        ],
        out_specs=pl.BlockSpec((rows - HALO, block), lambda j: (0, j)),
        out_shape=jax.ShapeDtypeStruct((rows - HALO, cols), F32),
        compiler_params=params(),
        cost_estimate=cost(2 * rows * width * cols, 2 * width * cols + 4 * rows * cols),
        name="outgate",
    )(hidden, w_og)


def outer_kernel(left_ref, right_ref, out_ref, *, skip_left, skip_right):
    out_ref[...] = mm(left_ref[skip_left:, :], right_ref[skip_right:, :], TN).astype(BF16)


def outer(left, right, block=512, skip_left=0, skip_right=0):
    rows, width = left.shape
    cols = right.shape[1]
    block = min(block, cols)
    return pl.pallas_call(
        functools.partial(outer_kernel, skip_left=skip_left, skip_right=skip_right),
        grid=(cols // block,),
        in_specs=[
            pl.BlockSpec((rows, width), lambda j: (0, 0)),
            pl.BlockSpec((right.shape[0], block), lambda j: (0, j)),
        ],
        out_specs=pl.BlockSpec((width, block), lambda j: (0, j)),
        out_shape=jax.ShapeDtypeStruct((width, cols), BF16),
        compiler_params=params(),
        cost_estimate=cost(2 * rows * width * cols, 2 * width * cols + 2 * rows * cols),
        name="outer",
    )(left, right)


def gate_tables(logit_ref, par_ref, beta_ref, decay_ref, cum_ref):
    logits = logit_ref[HALO:, :]
    beta_ref[...] = jax.nn.sigmoid(logits)
    shifted = logits + par_ref[1:2, :]
    soft = jnp.maximum(shifted, 0.0) + jnp.log1p(jnp.exp(-jnp.abs(shifted)))
    decay_ref[...] = -jnp.exp(par_ref[0:1, :]) * soft
    lower = (iota2((CHUNK, CHUNK), 0) >= iota2((CHUNK, CHUNK), 1)).astype(F32)
    for c in range(logits.shape[0] // CHUNK):
        part = decay_ref[c * CHUNK : (c + 1) * CHUNK, :]
        cum_ref[c * CHUNK : (c + 1) * CHUNK, :] = mm_exact(lower, part)


def mix_taps(p_ref, taps_ref, cols, pf_ref):
    tokens = cols.shape[0]
    pf_ref[...] = p_ref[...].astype(F32)
    total = pf_ref[HALO:, :] * taps_ref[0:1, :]
    for j in range(1, CONV):
        total += pf_ref[HALO - j : HALO - j + tokens, :] * taps_ref[j : j + 1, :] * cols[:, j : j + 1]
    return total


def chunk_tables(c, head, cols, segr_ref, cum_ref):
    rows = slice(c * CHUNK, (c + 1) * CHUNK)
    cum = lane(cum_ref[rows, :], head)
    cum_row = to_row(cum)
    same = cols[rows, 0:1] == segr_ref[0:1, rows]
    row_ids, col_ids = iota2((CHUNK, CHUNK), 0), iota2((CHUNK, CHUNK), 1)
    gamma = jnp.where((row_ids >= col_ids) & same, jnp.exp(jnp.minimum(cum - cum_row, 0.0)), 0.0)
    strict = jnp.where(row_ids > col_ids, gamma, 0.0)
    carry = jnp.exp(cum) * cols[rows, 4:5]
    last = jnp.exp(cum[CHUNK - 1 :, :] - cum) * cols[rows, 5:6]
    return gamma, strict, carry, last


def unit_lower_inverses(systems):
    size = systems[0].shape[0]
    row_ids, col_ids = iota2((size, size), 0), iota2((size, size), 1)
    eye = (row_ids == col_ids).astype(F32)
    found = [eye - jnp.where(row_ids // 2 == col_ids // 2, low, 0.0) for low in systems]
    width = 2
    while width < size:
        joined = (row_ids // (2 * width) == col_ids // (2 * width)) & (
            row_ids // width != col_ids // width
        )
        first = [mm_three(jnp.where(joined, low, 0.0), inv) for low, inv in zip(systems, found)]
        found = [inv - mm_three(inv, part) for inv, part in zip(found, first)]
        width *= 2
    return found


def forward_kernel(
    p_ref, taps_ref, logit_ref, par_ref, cols_ref, segr_ref,
    part_ref, resp_ref, map_ref, sum_ref, inv_ref, upd_ref, st_ref, stm_ref, amap_ref, rmap_ref,
    beta_ref, decay_ref, cum_ref, pf_ref, mix_ref,
):
    head = pl.program_id(0)

    @pl.when(head == 0)
    def _():
        gate_tables(logit_ref, par_ref, beta_ref, decay_ref, cum_ref)

    cols = cols_ref[...]
    tokens = cols.shape[0]
    total = mix_taps(p_ref, taps_ref, cols, pf_ref)
    mix_ref[...] = total * jax.nn.sigmoid(total)
    beta = lane(beta_ref[...], head + H)
    chunks = range(tokens // CHUNK)
    tables, lows, keys, queries = [], [], [], []
    for c in chunks:
        rows = slice(c * CHUNK, (c + 1) * CHUNK)
        query = mix_ref[rows, :DK]
        query = query * (lax.rsqrt(jnp.sum(query * query, axis=1, keepdims=True) + 1e-06) * DK**-0.5)
        key = mix_ref[rows, DK : 2 * DK]
        key = key * lax.rsqrt(jnp.sum(key * key, axis=1, keepdims=True) + 1e-06)
        gamma, strict, carry, last = chunk_tables(c, head, cols, segr_ref, cum_ref)
        dots = mm(jnp.concatenate([key, query], axis=0), key, NT)
        lows.append(beta[rows] * strict * dots[:CHUNK])
        tables.append((gamma * dots[CHUNK:], carry, last))
        keys.append(key)
        queries.append(query)
    inverses = unit_lower_inverses(lows)
    state = None
    for c in chunks:
        rows = slice(c * CHUNK, (c + 1) * CHUNK)
        scores, carry, last = tables[c]
        key, query = keys[c], queries[c]
        target = jnp.concatenate([mix_ref[rows, 2 * DK :], carry * key], axis=1) * beta[rows]
        updates = mm(inverses[c], target)
        inv_ref[0, c] = inverses[c].astype(BF16)
        upd_ref[0, rows, :] = updates
        weighted_t = jnp.transpose(last * key)
        both = mm(jnp.concatenate([weighted_t, scores], axis=0), updates)
        eye = (iota2((DK, DK), 0) == iota2((DK, DK), 1)).astype(F32)
        step_map = carry[CHUNK - 1 :, :] * eye - both[:DK, DV:]
        read_map = carry * query - both[DK:, DV:]
        amap_ref[0, c] = step_map.astype(BF16)
        rmap_ref[0, c] = read_map.astype(BF16)
        if c == 0:
            st_ref[0, c] = jnp.zeros((DK, DV), F32)
            stm_ref[0, c] = eye.astype(BF16)
            part_ref[rows, :] = both[DK:, :DV]
            resp_ref[rows, :] = read_map.astype(BF16)
            state = jnp.concatenate([both[:DK, :DV], step_map], axis=1)
        else:
            st_ref[0, c] = state[:, :DV]
            stm_ref[0, c] = state[:, DV:].astype(BF16)
            moved = mm(jnp.concatenate([step_map, read_map], axis=0), state)
            part_ref[rows, :] = both[DK:, :DV] + moved[DK:, :DV]
            resp_ref[rows, :] = moved[DK:, DV:].astype(BF16)
            state = moved[:DK] + jnp.concatenate(
                [both[:DK, :DV], jnp.zeros((DK, DK), F32)], axis=1
            )
    map_ref[0] = state[:, DV:].astype(BF16)
    sum_ref[0] = state[:, :DV].astype(BF16)


def delta_forward(proj, taps, logits, par, cols, segr):
    rows = proj.shape[0]
    tokens = rows - HALO
    chunks = tokens // CHUNK
    whole = lambda shape: pl.BlockSpec(shape, lambda h: (0,) * len(shape))
    by_head = lambda shape: pl.BlockSpec(shape, lambda h: (h,) + (0,) * (len(shape) - 1))
    return pl.pallas_call(
        forward_kernel,
        grid=(H,),
        in_specs=[
            pl.BlockSpec((rows, HC), lambda h: (0, h)),
            pl.BlockSpec((8, HC), lambda h: (0, h)),
            whole((rows, LANES)),
            whole((8, LANES)),
            whole((tokens, LANES)),
            whole((8, tokens)),
        ],
        out_specs=[
            pl.BlockSpec((tokens, DV), lambda h: (0, h)),
            pl.BlockSpec((tokens, DK), lambda h: (0, h)),
            by_head((1, DK, DK)),
            by_head((1, DK, DV)),
            by_head((1, chunks, CHUNK, CHUNK)),
            by_head((1, tokens, DV + DK)),
            by_head((1, chunks, DK, DV)),
            by_head((1, chunks, DK, DK)),
            by_head((1, chunks, DK, DK)),
            by_head((1, chunks, CHUNK, DK)),
        ],
        out_shape=[
            jax.ShapeDtypeStruct((tokens, H * DV), F32),
            jax.ShapeDtypeStruct((tokens, H * DK), BF16),
            jax.ShapeDtypeStruct((H, DK, DK), BF16),
            jax.ShapeDtypeStruct((H, DK, DV), BF16),
            jax.ShapeDtypeStruct((H, chunks, CHUNK, CHUNK), BF16),
            jax.ShapeDtypeStruct((H, tokens, DV + DK), F32),
            jax.ShapeDtypeStruct((H, chunks, DK, DV), F32),
            jax.ShapeDtypeStruct((H, chunks, DK, DK), BF16),
            jax.ShapeDtypeStruct((H, chunks, DK, DK), BF16),
            jax.ShapeDtypeStruct((H, chunks, CHUNK, DK), BF16),
        ],
        scratch_shapes=[
            pltpu.VMEM((tokens, LANES), F32),
            pltpu.VMEM((tokens, LANES), F32),
            pltpu.VMEM((tokens, LANES), F32),
            pltpu.VMEM((rows, HC), F32),
            pltpu.VMEM((tokens, HC), F32),
        ],
        compiler_params=params(),
        cost_estimate=cost(3e10, 3e7),
        name="delta_forward",
    )(proj, taps, logits, par, cols, segr)


def backward_kernel(
    place_ref, p_ref, taps_ref, logit_ref, par_ref, cols_ref, back_ref, segr_ref,
    dattn_ref, sin_ref, maps_ref, grads_ref,
    inv_ref, upd_ref, st_ref, stm_ref, amap_ref, rmap_ref,
    dp_ref, dlogit_ref, dtaps_ref, dpar_ref,
    beta_ref, decay_ref, cum_ref, pf_ref, pre_ref, dmix_ref,
):
    head = pl.program_id(0)
    place = place_ref[0]
    places = maps_ref.shape[0]

    @pl.when(head == 0)
    def _():
        gate_tables(logit_ref, par_ref, beta_ref, decay_ref, cum_ref)
        dlogit_ref[...] = jnp.zeros_like(dlogit_ref)
        dpar_ref[...] = jnp.zeros_like(dpar_ref)

    cols = cols_ref[...]
    tokens = cols.shape[0]
    chunks = range(tokens // CHUNK)
    pre = mix_taps(p_ref, taps_ref, cols, pf_ref)
    pre_ref[...] = pre
    beta = lane(beta_ref[...], head + H)

    def behind(lap, grad):
        source = places - 1 - lap
        return jnp.where(
            source > place,
            grads_ref[source, 0].astype(F32) + mm(maps_ref[source, 0], grad, TN),
            grad,
        )

    d_state = lax.fori_loop(0, places - 1, behind, jnp.zeros((DK, DV), F32))
    state_in = sin_ref[0]
    d_states = [None] * len(chunks)
    for c in reversed(chunks):
        rows = slice(c * CHUNK, (c + 1) * CHUNK)
        d_states[c] = d_state
        if c > 0:
            d_state = mm(amap_ref[0, c], d_state, TN) + mm(rmap_ref[0, c], dattn_ref[rows, :], TN)

    row_ids, col_ids = iota2((CHUNK, CHUNK), 0), iota2((CHUNK, CHUNK), 1)
    d_beta_all, d_decay_all = [], []
    for c in chunks:
        rows = slice(c * CHUNK, (c + 1) * CHUNK)
        mixed = pre_ref[rows, :]
        gate = jax.nn.sigmoid(mixed)
        slope = gate * (1.0 + mixed * (1.0 - gate))
        mixed = mixed * gate
        query_raw, key_raw, value = mixed[:, :DK], mixed[:, DK : 2 * DK], mixed[:, 2 * DK :]
        query_size = lax.rsqrt(jnp.sum(query_raw * query_raw, axis=1, keepdims=True) + 1e-06)
        key_size = lax.rsqrt(jnp.sum(key_raw * key_raw, axis=1, keepdims=True) + 1e-06)
        query_unit, key = query_raw * query_size, key_raw * key_size
        query = query_unit * DK**-0.5
        gamma, strict, carry, last = chunk_tables(c, head, cols, segr_ref, cum_ref)
        strength = beta[rows]
        dots = mm(jnp.concatenate([key, query], axis=0), key, NT)
        weights = strict * dots[:CHUNK]
        low = strength * weights
        scores = gamma * dots[CHUNK:]
        if c == 0:
            state = state_in
        else:
            state = st_ref[0, c] + mm(stm_ref[0, c], state_in)
        updates = upd_ref[0, rows, :DV] - mm(upd_ref[0, rows, DV:], state)
        d_attn = dattn_ref[rows, :]
        d_state = d_states[c]
        d_updates = mm(scores, d_attn, TN) + mm(last * key, d_state)
        solved = mm(inv_ref[0, c], d_updates, TN)
        both = jnp.concatenate([d_attn, solved.astype(BF16)], axis=0)
        by_updates = mm(both, updates, NT)
        by_state = mm(both, state, NT)
        d_scores = by_updates[:CHUNK]
        d_low = -by_updates[CHUNK:]
        d_query = carry * by_state[:CHUNK]
        key_state = jnp.sum(key * by_state[CHUNK:], axis=1, keepdims=True)
        d_carry = jnp.sum(query * by_state[:CHUNK], axis=1, keepdims=True) - strength * key_state
        d_beta = (
            jnp.sum(solved * value, axis=1, keepdims=True)
            - carry * key_state
            + jnp.sum(d_low * weights, axis=1, keepdims=True)
        )
        d_dots_q = d_scores * gamma
        d_dots_k = d_low * strength * strict
        by_key = mm(jnp.concatenate([d_dots_q, d_dots_k], axis=0), key)
        d_query += by_key[:CHUNK]
        from_state = mm(updates, d_state, NT)
        d_key = (
            by_key[CHUNK:]
            + mm(
                jnp.concatenate([d_dots_q, d_dots_k], axis=0),
                jnp.concatenate([query, key], axis=0),
                TN,
            )
            - strength * carry * by_state[CHUNK:]
            + last * from_state
        )
        d_last = jnp.sum(key * from_state, axis=1, keepdims=True) * last
        d_spread = d_scores * scores + d_low * low
        final = (iota2((CHUNK, 1), 0) == CHUNK - 1).astype(F32)
        d_carry += final * jnp.sum(d_state * state)
        d_cum = (
            jnp.sum(d_spread, axis=1, keepdims=True)
            - to_column(jnp.sum(d_spread, axis=0, keepdims=True))
            + final * jnp.sum(d_last)
            - d_last
            + d_carry * carry
        )
        d_decay = jnp.sum(
            jnp.where(row_ids <= col_ids, to_row(d_cum), 0.0), axis=1, keepdims=True
        )
        d_beta_all.append(d_beta)
        d_decay_all.append(d_decay)
        d_query = d_query * DK**-0.5
        d_query = query_size * (
            d_query - query_unit * jnp.sum(d_query * query_unit, axis=1, keepdims=True)
        )
        d_key = key_size * (d_key - key * jnp.sum(d_key * key, axis=1, keepdims=True))
        d_value = strength * solved
        dmix_ref[HALO + c * CHUNK : HALO + (c + 1) * CHUNK, :] = slope * jnp.concatenate(
            [d_query, d_key, d_value], axis=1
        )

    d_beta = jnp.concatenate(d_beta_all, axis=0)
    d_decay = jnp.concatenate(d_decay_all, axis=0)
    lanes = iota2((tokens, LANES), 1)
    slope = jax.nn.sigmoid(logit_ref[HALO:, :] + par_ref[1:2, :]) * -jnp.exp(par_ref[0:1, :])
    here = jnp.where(lanes == head, d_decay, 0.0)
    d_first = here * slope
    strengths = beta_ref[...]
    d_second = jnp.where(lanes == head + H, d_beta, 0.0) * strengths * (1.0 - strengths)
    dlogit_ref[...] += d_first + d_second
    dpar_ref[0:1, :] += jnp.sum(here * decay_ref[...], axis=0, keepdims=True)
    dpar_ref[1:2, :] += jnp.sum(d_first, axis=0, keepdims=True)

    dmix_ref[:HALO, :] = jnp.zeros((HALO, HC), F32)
    dmix_ref[HALO + tokens :, :] = jnp.zeros((8, HC), F32)
    d_mix = dmix_ref[HALO : HALO + tokens, :]
    dtaps_ref[...] = jnp.zeros_like(dtaps_ref)
    dtaps_ref[0:1, :] = jnp.sum(d_mix * pf_ref[HALO:, :], axis=0, keepdims=True)
    total = dmix_ref[: HALO + tokens, :] * taps_ref[0:1, :]
    for j in range(1, CONV):
        total += dmix_ref[j : j + HALO + tokens, :] * taps_ref[j : j + 1, :] * back_ref[:, j : j + 1]
        dtaps_ref[j : j + 1, :] = jnp.sum(
            d_mix * cols[:, j : j + 1] * pf_ref[HALO - j : HALO - j + tokens, :],
            axis=0,
            keepdims=True,
        )
    dp_ref[...] = total.astype(BF16)


def delta_backward(place, proj, taps, logits, par, cols, back, segr, d_attn, state_in, maps, grads, saved):
    rows = proj.shape[0]
    tokens = rows - HALO
    chunks = tokens // CHUNK
    places = maps.shape[0]
    whole = lambda shape: pl.BlockSpec(shape, lambda h: (0,) * len(shape))
    by_head = lambda shape: pl.BlockSpec(shape, lambda h: (h,) + (0,) * (len(shape) - 1))
    return pl.pallas_call(
        backward_kernel,
        grid=(H,),
        in_specs=[
            pl.BlockSpec(memory_space=pltpu.SMEM),
            pl.BlockSpec((rows, HC), lambda h: (0, h)),
            pl.BlockSpec((8, HC), lambda h: (0, h)),
            whole((rows, LANES)),
            whole((8, LANES)),
            whole((tokens, LANES)),
            whole((rows, LANES)),
            whole((8, tokens)),
            pl.BlockSpec((tokens, DV), lambda h: (0, h)),
            by_head((1, DK, DV)),
            pl.BlockSpec((places, 1, DK, DK), lambda h: (0, h, 0, 0)),
            pl.BlockSpec((places, 1, DK, DV), lambda h: (0, h, 0, 0)),
            by_head((1, chunks, CHUNK, CHUNK)),
            by_head((1, tokens, DV + DK)),
            by_head((1, chunks, DK, DV)),
            by_head((1, chunks, DK, DK)),
            by_head((1, chunks, DK, DK)),
            by_head((1, chunks, CHUNK, DK)),
        ],
        out_specs=[
            pl.BlockSpec((rows, HC), lambda h: (0, h)),
            whole((tokens, LANES)),
            pl.BlockSpec((8, HC), lambda h: (0, h)),
            whole((8, LANES)),
        ],
        out_shape=[
            jax.ShapeDtypeStruct((rows, H * HC), BF16),
            jax.ShapeDtypeStruct((tokens, LANES), F32),
            jax.ShapeDtypeStruct((8, H * HC), F32),
            jax.ShapeDtypeStruct((8, LANES), F32),
        ],
        scratch_shapes=[
            pltpu.VMEM((tokens, LANES), F32),
            pltpu.VMEM((tokens, LANES), F32),
            pltpu.VMEM((tokens, LANES), F32),
            pltpu.VMEM((rows, HC), F32),
            pltpu.VMEM((tokens, HC), F32),
            pltpu.VMEM((rows + 8, HC), F32),
        ],
        compiler_params=params(),
        cost_estimate=cost(4e10, 4e7),
        name="delta_backward",
    )(place, proj, taps, logits, par, cols, back, segr, d_attn, state_in, maps, grads, *saved)


def mixer_kernel(
    place_ref, part_ref, resp_ref, maps_ref, sums_ref, gpre_ref, gain_ref, w_ref, x_ref, gain2_ref,
    sin_ref, attn_ref, gated_ref, y_ref, h_ref,
):
    head = pl.program_id(0)
    place = place_ref[0]
    places = maps_ref.shape[0]

    def ahead(source, state):
        return jnp.where(
            source < place,
            sums_ref[source, 0].astype(F32) + mm(maps_ref[source, 0], state),
            state,
        )

    state = lax.fori_loop(0, places - 1, ahead, jnp.zeros((DK, DV), F32))
    sin_ref[0] = state
    attn = part_ref[...] + mm(resp_ref[...], state)
    attn_ref[...] = attn
    scale = lax.rsqrt(jnp.mean(attn * attn, axis=-1, keepdims=True) + 1e-05)
    gate = gpre_ref[...]
    gated = (attn * scale * gain_ref[...] * (gate * jax.nn.sigmoid(gate))).astype(BF16)
    gated_ref[...] = gated

    @pl.when(head == 0)
    def _():
        y_ref[...] = x_ref[...].astype(F32)

    y_ref[...] += mm(gated, w_ref[...])

    @pl.when(head == pl.num_programs(0) - 1)
    def _():
        value = y_ref[...]
        size = lax.rsqrt(jnp.mean(value * value, axis=-1, keepdims=True) + 1e-06)
        h_ref[...] = (value * size * gain2_ref[...]).astype(BF16)


def mixer_out(place, part, resp, maps, sums, gpre, gain, w_out, x, gain2):
    tokens, width = x.shape
    places = maps.shape[0]
    whole = lambda shape: pl.BlockSpec(shape, lambda h: (0,) * len(shape))
    return pl.pallas_call(
        mixer_kernel,
        grid=(H,),
        in_specs=[
            pl.BlockSpec(memory_space=pltpu.SMEM),
            pl.BlockSpec((tokens, DV), lambda h: (0, h)),
            pl.BlockSpec((tokens, DK), lambda h: (0, h)),
            pl.BlockSpec((places, 1, DK, DK), lambda h: (0, h, 0, 0)),
            pl.BlockSpec((places, 1, DK, DV), lambda h: (0, h, 0, 0)),
            pl.BlockSpec((tokens, DV), lambda h: (0, h)),
            whole((1, DV)),
            pl.BlockSpec((DV, width), lambda h: (h, 0)),
            whole((tokens, width)),
            whole((1, width)),
        ],
        out_specs=[
            pl.BlockSpec((1, DK, DV), lambda h: (h, 0, 0)),
            pl.BlockSpec((tokens, DV), lambda h: (0, h)),
            pl.BlockSpec((tokens, DV), lambda h: (0, h)),
            whole((tokens, width)),
            whole((tokens, width)),
        ],
        out_shape=[
            jax.ShapeDtypeStruct((H, DK, DV), F32),
            jax.ShapeDtypeStruct((tokens, H * DV), F32),
            jax.ShapeDtypeStruct((tokens, H * DV), BF16),
            jax.ShapeDtypeStruct((tokens, width), F32),
            jax.ShapeDtypeStruct((tokens, width), BF16),
        ],
        compiler_params=params(),
        cost_estimate=cost(2 * tokens * width * H * DV, 2e7),
        name="mixer_out",
    )(place, part, resp, maps, sums, gpre, gain, w_out, x, gain2)


def mixer_back_kernel(
    dmix_ref, w_ref, attn_ref, gpre_ref, gain_ref, resp_ref,
    dattn_ref, dgpre_ref, grad_ref, dgain_ref,
):
    @pl.when(pl.program_id(0) == 0)
    def _():
        dgain_ref[...] = jnp.zeros_like(dgain_ref)

    d_gated = mm(dmix_ref[...], w_ref[...], NT)
    attn = attn_ref[...]
    size = lax.rsqrt(jnp.mean(attn * attn, axis=-1, keepdims=True) + 1e-05)
    unit = attn * size
    gate = gpre_ref[...]
    slope = jax.nn.sigmoid(gate)
    swish = gate * slope
    gain = gain_ref[...]
    dgpre_ref[...] = (d_gated * (unit * gain) * (slope * (1.0 + gate * (1.0 - slope)))).astype(BF16)
    d_normed = d_gated * swish
    dgain_ref[0:1, :] += jnp.sum(d_normed * unit, axis=0, keepdims=True)
    d_unit = d_normed * gain
    d_attn = size * (d_unit - unit * jnp.mean(d_unit * unit, axis=-1, keepdims=True))
    d_attn = d_attn.astype(BF16)
    dattn_ref[...] = d_attn
    grad_ref[0] = mm(resp_ref[...], d_attn, TN).astype(BF16)


def mixer_back(d_mixer, w_out, attn, gpre, gain, resp):
    tokens, width = d_mixer.shape
    whole = lambda shape: pl.BlockSpec(shape, lambda h: (0,) * len(shape))
    return pl.pallas_call(
        mixer_back_kernel,
        grid=(H,),
        in_specs=[
            whole((tokens, width)),
            pl.BlockSpec((DV, width), lambda h: (h, 0)),
            pl.BlockSpec((tokens, DV), lambda h: (0, h)),
            pl.BlockSpec((tokens, DV), lambda h: (0, h)),
            whole((1, DV)),
            pl.BlockSpec((tokens, DK), lambda h: (0, h)),
        ],
        out_specs=[
            pl.BlockSpec((tokens, DV), lambda h: (0, h)),
            pl.BlockSpec((tokens, DV), lambda h: (0, h)),
            pl.BlockSpec((1, DK, DV), lambda h: (h, 0, 0)),
            whole((8, DV)),
        ],
        out_shape=[
            jax.ShapeDtypeStruct((tokens, H * DV), BF16),
            jax.ShapeDtypeStruct((tokens, H * DV), BF16),
            jax.ShapeDtypeStruct((H, DK, DV), BF16),
            jax.ShapeDtypeStruct((8, DV), F32),
        ],
        compiler_params=params(),
        cost_estimate=cost(2 * tokens * width * H * DV, 2e7),
        name="mixer_back",
    )(d_mixer, w_out, attn, gpre, gain, resp)


def ffn_kernel(
    h_ref, dout_ref, y_ref, gain_ref, wg_ref, wu_ref, wd_ref,
    out_ref, act_ref, dg_ref, du_ref, dy_ref, dmix_ref, dgain_ref, res_ref, dh_ref,
):
    step = pl.program_id(0)

    @pl.when(step == 0)
    def _():
        res_ref[...] = y_ref[...]
        dh_ref[...] = jnp.zeros_like(dh_ref)

    hidden = h_ref[...]
    gate = mm(hidden, wg_ref[...])
    up = mm(hidden, wu_ref[...])
    d_act = mm(dout_ref[...], wd_ref[...], NT)
    slope = jax.nn.sigmoid(gate)
    swish = gate * slope
    act = (swish * up).astype(BF16)
    act_ref[...] = act
    d_gate = (d_act * up * slope * (1.0 + gate * (1.0 - slope))).astype(BF16)
    d_up = (d_act * swish).astype(BF16)
    dg_ref[...] = d_gate
    du_ref[...] = d_up
    res_ref[...] += mm(act, wd_ref[...])
    dh_ref[...] += mm(d_gate, wg_ref[...], NT) + mm(d_up, wu_ref[...], NT)

    @pl.when(step == pl.num_programs(0) - 1)
    def _():
        out_ref[...] = res_ref[...].astype(BF16)
        value = y_ref[...]
        size = lax.rsqrt(jnp.mean(value * value, axis=-1, keepdims=True) + 1e-06)
        unit = value * size
        d_hidden = dh_ref[...]
        dgain_ref[...] = jnp.zeros_like(dgain_ref)
        dgain_ref[0:1, :] = jnp.sum(d_hidden * unit, axis=0, keepdims=True)
        d_unit = d_hidden * gain_ref[...]
        d_y = dout_ref[...].astype(F32) + size * (
            d_unit - unit * jnp.mean(d_unit * unit, axis=-1, keepdims=True)
        )
        dy_ref[...] = d_y
        dmix_ref[...] = d_y.astype(BF16)


def feed_forward(hidden, d_out, y1, gain, w_gate, w_up, w_down):
    tokens, width = hidden.shape
    inner = w_down.shape[0]
    block = 256
    whole = lambda shape: pl.BlockSpec(shape, lambda j: (0,) * len(shape))
    across = pl.BlockSpec((tokens, block), lambda j: (0, j))
    return pl.pallas_call(
        ffn_kernel,
        grid=(inner // block,),
        in_specs=[
            whole((tokens, width)),
            whole((tokens, width)),
            whole((tokens, width)),
            whole((1, width)),
            pl.BlockSpec((width, block), lambda j: (0, j)),
            pl.BlockSpec((width, block), lambda j: (0, j)),
            pl.BlockSpec((block, width), lambda j: (j, 0)),
        ],
        out_specs=[
            whole((tokens, width)), across, across, across,
            whole((tokens, width)), whole((tokens, width)), whole((8, width)),
        ],
        out_shape=[
            jax.ShapeDtypeStruct((tokens, width), BF16),
            jax.ShapeDtypeStruct((tokens, inner), BF16),
            jax.ShapeDtypeStruct((tokens, inner), BF16),
            jax.ShapeDtypeStruct((tokens, inner), BF16),
            jax.ShapeDtypeStruct((tokens, width), F32),
            jax.ShapeDtypeStruct((tokens, width), BF16),
            jax.ShapeDtypeStruct((8, width), F32),
        ],
        scratch_shapes=[pltpu.VMEM((tokens, width), F32), pltpu.VMEM((tokens, width), F32)],
        compiler_params=params(),
        cost_estimate=cost(12 * tokens * width * inner, 3e7),
        name="feed_forward",
    )(hidden, d_out, y1, gain, w_gate, w_up, w_down)


def input_grad_kernel(
    dp_ref, dg_ref, dl_ref, wq_ref, wo_ref, wl_ref, x_ref, gain_ref, dy_ref,
    out_ref, dgain_ref, acc_ref, *, first,
):
    step = pl.program_id(0)

    @pl.when(step == 0)
    def _():
        acc_ref[...] = mm(dl_ref[...], wl_ref[...], NT)

    @pl.when(step < first)
    def _():
        acc_ref[...] += mm(dp_ref[HALO:, :], wq_ref[...], NT)

    @pl.when(step >= first)
    def _():
        acc_ref[...] += mm(dg_ref[...], wo_ref[...], NT)

    @pl.when(step == pl.num_programs(0) - 1)
    def _():
        value = x_ref[...].astype(F32)
        size = lax.rsqrt(jnp.mean(value * value, axis=-1, keepdims=True) + 1e-06)
        unit = value * size
        d_hidden = acc_ref[...]
        dgain_ref[...] = jnp.zeros_like(dgain_ref)
        dgain_ref[0:1, :] = jnp.sum(d_hidden * unit, axis=0, keepdims=True)
        d_unit = d_hidden * gain_ref[...]
        out_ref[...] = dy_ref[...] + size * (
            d_unit - unit * jnp.mean(d_unit * unit, axis=-1, keepdims=True)
        )


def input_grad(d_proj, d_gpre, d_logit, w_qkv, w_og, w_gates, x, gain, d_y):
    tokens, width = x.shape
    rows = d_proj.shape[0]
    block = 512
    first, second = w_qkv.shape[1] // block, w_og.shape[1] // block
    whole = lambda shape: pl.BlockSpec(shape, lambda j: (0,) * len(shape))
    early = lambda j: (0, jnp.minimum(j, first - 1))
    late = lambda j: (0, jnp.maximum(j - first, 0))
    return pl.pallas_call(
        functools.partial(input_grad_kernel, first=first),
        grid=(first + second,),
        in_specs=[
            pl.BlockSpec((rows, block), early),
            pl.BlockSpec((tokens, block), late),
            whole((tokens, LANES)),
            pl.BlockSpec((width, block), early),
            pl.BlockSpec((width, block), late),
            whole((width, LANES)),
            whole((tokens, width)),
            whole((1, width)),
            whole((tokens, width)),
        ],
        out_specs=[whole((tokens, width)), whole((8, width))],
        out_shape=[
            jax.ShapeDtypeStruct((tokens, width), F32),
            jax.ShapeDtypeStruct((8, width), F32),
        ],
        scratch_shapes=[pltpu.VMEM((tokens, width), F32)],
        compiler_params=params(),
        cost_estimate=cost(2 * tokens * width * (first + second) * block, 3e7),
        name="input_grad",
    )(d_proj, d_gpre, d_logit, w_qkv, w_og, w_gates, x, gain, d_y)


def shifted(block, axis, distance):
    devices = range(lax.axis_size(axis))
    route = [(i - distance, i) for i in devices if i - distance in devices]
    return lax.ppermute(block, axis, route)


def by_heads(query, key, value):
    lead = query.shape[:-1]
    parts = [query.reshape(lead + (H, DK)), key.reshape(lead + (H, DK)), value.reshape(lead + (H, DV))]
    return jnp.concatenate(parts, axis=-1).reshape(lead + (H * HC,))


def from_heads(value):
    lead = value.shape[:-1]
    parts = value.reshape(lead + (H, HC))
    return (
        parts[..., :DK].reshape(lead + (H * DK,)),
        parts[..., DK : 2 * DK].reshape(lead + (H * DK,)),
        parts[..., 2 * DK :].reshape(lead + (H * DV,)),
    )


def token_tables(segments, place, tokens):
    seg_pad = jnp.concatenate([jnp.full((HALO,), -1, jnp.int32), segments, jnp.full((8,), -2, jnp.int32)])
    ext = lax.dynamic_slice_in_dim(seg_pad, place * tokens, tokens + HALO + 8)
    seg = ext[HALO : HALO + tokens]
    columns = [seg.astype(F32)]
    for j in range(1, CONV):
        columns.append((ext[HALO - j : HALO - j + tokens] == seg).astype(F32))
    blocks = seg.reshape(-1, CHUNK)
    before = ext[HALO - 1 : HALO - 1 + tokens : CHUNK]
    columns.append((blocks == before[:, None]).astype(F32).reshape(-1))
    columns.append((blocks == blocks[:, -1:]).astype(F32).reshape(-1))
    columns += [jnp.zeros_like(columns[0])] * (LANES - len(columns))
    cols = jnp.stack(columns, axis=1)
    rows = tokens + HALO
    back = [jnp.zeros((rows,), F32)]
    for j in range(1, CONV):
        back.append((ext[j : j + rows] == ext[:rows]).astype(F32))
    back += [jnp.zeros((rows,), F32)] * (LANES - len(back))
    segr = jnp.broadcast_to(seg.astype(F32)[None], (8, tokens))
    return cols, jnp.stack(back, axis=1), segr


def wide(value):
    return jnp.pad(value, ((0, 0), (0, LANES - value.shape[1])))


def local(
    inputs, segments, cotangent, norm_gain_mix, w_query, w_key, w_value, w_outgate, w_gates,
    conv_weight, decay_log, dt_bias, out_norm_gain, w_out, norm_gain_ffn, w_ffn_gate, w_ffn_up, w_ffn_down,
):
    x, d_out = inputs[0], cotangent[0]
    tokens = x.shape[0]
    place = lax.axis_index("seq")
    place_arr = place.reshape((1,)).astype(jnp.int32)
    low = lambda a: a.astype(BF16)
    gather = lambda a, axis: lax.all_gather(a, "dp", axis=axis, tiled=True)

    qkv_w = gather(
        jnp.concatenate([by_heads(low(w_query), low(w_key), low(w_value)), wide(low(w_gates))], axis=1), 0
    )
    gates_w = qkv_w[:, H * HC :]
    qkv_w = qkv_w[:, : H * HC]
    og_w = gather(low(w_outgate), 0)
    out_w = gather(low(w_out), 1)
    gate_w = gather(low(w_ffn_gate), 0)
    up_w = gather(low(w_ffn_up), 0)
    down_w = gather(low(w_ffn_down), 1)

    gain_mix, gain_ffn, gain_out = norm_gain_mix[None], norm_gain_ffn[None], out_norm_gain[None]
    taps_parts = by_heads(conv_weight[:, : H * DK], conv_weight[:, H * DK : 2 * H * DK], conv_weight[:, 2 * H * DK :])
    taps = jnp.pad(taps_parts, ((0, 8 - CONV), (0, 0)))
    par = jnp.pad(jnp.stack([decay_log, dt_bias]), ((0, 6), (0, LANES - H)))
    cols, back, segr = token_tables(segments[0], place, tokens)

    x_ext = jnp.concatenate([shifted(x[tokens - HALO :], "seq", 1), x], axis=0)
    proj, logits, hidden = project(x_ext, gain_mix, qkv_w, gates_w)
    gpre = outgate(hidden, og_w)
    part, resp, step_map, step_sum, *saved = delta_forward(proj, taps, logits, par, cols, segr)
    maps = lax.all_gather(step_map, "seq")
    sums = lax.all_gather(step_sum, "seq")
    state_in, attn, gated, y1, hidden_mid = mixer_out(
        place_arr, part, resp, maps, sums, gpre, gain_out, out_w, x, gain_ffn
    )
    result, act, d_gate, d_up, d_y, d_mixer, d_gain_ffn = feed_forward(
        hidden_mid, d_out, y1, gain_ffn, gate_w, up_w, down_w
    )
    d_attn, d_gpre, local_grad, d_gain_out = mixer_back(d_mixer, out_w, attn, gpre, gain_out, resp)
    grads = lax.all_gather(local_grad, "seq")

    def scattered(grad, axis):
        part_sum = lax.psum_scatter(grad, "dp", scatter_dimension=axis, tiled=True)
        return lax.psum(part_sum, "seq").astype(F32)

    g_down = scattered(outer(act, d_out), 1)
    g_gate = scattered(outer(hidden_mid, d_gate, 256), 0)
    g_up = scattered(outer(hidden_mid, d_up, 256), 0)
    g_out = scattered(outer(gated, d_mixer), 1)
    g_og = scattered(outer(hidden, d_gpre, 512, HALO, 0), 0)
    d_proj, d_logits, d_taps, d_par = delta_backward(
        place_arr, proj, taps, logits, par, cols, back, segr, d_attn, state_in, maps, grads, saved
    )
    sent_back = shifted(d_proj[:HALO], "seq", -1)
    d_proj = d_proj.at[tokens:].add(sent_back)
    d_logit = low(d_logits)
    g_qkv = scattered(outer(hidden, d_proj, 512, HALO, HALO), 0)
    g_gates = scattered(outer(hidden, d_logit, 128, HALO, 0), 0)
    d_inputs, d_gain_mix = input_grad(d_proj, d_gpre, d_logit, qkv_w, og_w, gates_w, x, gain_mix, d_y)

    g_query, g_key, g_value = from_heads(g_qkv)
    small = lax.psum(
        (
            d_gain_mix[0],
            jnp.concatenate(from_heads(d_taps[:CONV]), axis=1),
            d_par[0, :H],
            d_par[1, :H],
            d_gain_out[0],
            d_gain_ffn[0],
        ),
        ("dp", "seq"),
    )
    return (
        result[None], d_inputs[None], small[0], g_query, g_key, g_value, g_og, g_gates[:, : 2 * H],
        small[1], small[2], small[3], small[4], g_out, small[5], g_gate, g_up, g_down,
    )


def solution(mesh):
    rows, cols, copied = P("dp", None), P(None, "dp"), P()
    tokens = P("dp", "seq", None)
    in_specs = (
        tokens, rows, tokens, copied, rows, rows, rows, rows, rows,
        copied, copied, copied, copied, cols, copied, rows, rows, cols,
    )
    out_specs = (
        tokens, tokens, copied, rows, rows, rows, rows, rows,
        copied, copied, copied, copied, cols, copied, rows, rows, cols,
    )
    return jax.shard_map(local, mesh=mesh, in_specs=in_specs, out_specs=out_specs, check_vma=False)
```

```python
import functools

import jax
import jax.numpy as jnp
from jax import lax
from jax.experimental import pallas as pl
from jax.experimental.pallas import tpu as pltpu
from jax.sharding import PartitionSpec as P

H = 8
DK = 128
DV = 256
CONV = 4
HALO = 16
CHUNK = 128
HC = 2 * DK + DV
LANES = 128
PLANES, CORES, SPOTS = 4, 2, 4

AT_LOGIT = H * HC
AT_GATE = AT_LOGIT + 512
AT_OUT = AT_GATE + H * DV
AT_FFN = AT_OUT + H * DV
VMEM_LIMIT = 56 * 2**20

F32 = jnp.float32
BF16 = jnp.bfloat16
NN = ((1,), (0,))
NT = ((1,), (1,))
TN = ((0,), (0,))


def mm(left, right, dims=NN):
    return lax.dot_general(
        left.astype(BF16), right.astype(BF16), (dims, ((), ())), preferred_element_type=F32
    )


def mm_exact(left, right, dims=NN):
    return lax.dot_general(
        left, right, (dims, ((), ())), precision=lax.Precision.HIGHEST, preferred_element_type=F32
    )


def halves(value):
    high = value.astype(BF16)
    return high, (value - high.astype(F32)).astype(BF16)


def mm_three(left, right):
    left_high, left_low = halves(left)
    right_high, right_low = halves(right)
    return mm(left_high, right_high) + (mm(left_high, right_low) + mm(left_low, right_high))


def params(**more):
    return pltpu.CompilerParams(vmem_limit_bytes=VMEM_LIMIT, **more)


def cost(flops, nbytes):
    return pl.CostEstimate(flops=int(flops), bytes_accessed=int(nbytes), transcendentals=0)


def iota2(shape, axis):
    return lax.broadcasted_iota(jnp.int32, shape, axis)


def lane(value, index):
    picked = jnp.where(iota2(value.shape, 1) == index, value, 0.0)
    return jnp.sum(picked, axis=1, keepdims=True)


def to_row(column):
    size = column.shape[0]
    same = iota2((size, size), 0) == iota2((size, size), 1)
    return jnp.sum(jnp.where(same, column, 0.0), axis=0, keepdims=True)


def to_column(row):
    size = row.shape[1]
    same = iota2((size, size), 0) == iota2((size, size), 1)
    return jnp.sum(jnp.where(same, row, 0.0), axis=1, keepdims=True)


def outgate_kernel(h_ref, w_ref, g_ref):
    g_ref[...] = mm(h_ref[HALO:, :], w_ref[...])


def outgate(hidden, weights):
    rows, width = hidden.shape
    cols = H * DV
    block = 512
    return pl.pallas_call(
        outgate_kernel,
        grid=(cols // block,),
        in_specs=[
            pl.BlockSpec((rows, width), lambda j: (0, 0)),
            pl.BlockSpec((width, block), lambda j: (0, j + AT_GATE // block)),
        ],
        out_specs=pl.BlockSpec((rows - HALO, block), lambda j: (0, j)),
        out_shape=jax.ShapeDtypeStruct((rows - HALO, cols), F32),
        compiler_params=params(),
        cost_estimate=cost(2 * rows * width * cols, 2 * width * cols + 4 * rows * cols),
        name="outgate",
    )(hidden, weights)


def outer_kernel(*refs, skips, parts):
    pairs = len(skips)
    lefts, rights = refs[:pairs], refs[pairs : 2 * pairs]
    outs, turned = refs[2 * pairs : -pairs], refs[-pairs:]

    @pl.when(pl.program_id(0) == 0)
    def _():
        for left, scratch, (skip, _) in zip(lefts, turned, skips):
            scratch[...] = jnp.transpose(left[skip:, :])

    total = None
    for scratch, right, (_, skip) in zip(turned, rights, skips):
        term = mm(scratch[...], right[skip:, :])
        total = term if total is None else total + term
    total = total.astype(BF16)
    for out, blocks in zip(outs, parts):
        for slot, block in enumerate(blocks):
            out[slot * LANES : (slot + 1) * LANES, :] = total[block * LANES : (block + 1) * LANES]


def outer(lefts, rights, wide_rows, parts, skip_left=0, skip_right=0):
    cols = rights[0].shape[1]
    block = next(b for b in (512, 256, 128) if cols % b == 0)
    if cols == 1152:
        block = 384
    rows = [array.shape[0] for array, _ in lefts]
    kept = rows[0] - skip_left
    return pl.pallas_call(
        functools.partial(outer_kernel, skips=[(skip_left, skip_right)] * len(lefts), parts=parts),
        grid=(cols // block,),
        in_specs=[
            pl.BlockSpec((n, wide_rows), lambda j, at=at: (0, at)) for n, (_, at) in zip(rows, lefts)
        ]
        + [pl.BlockSpec((right.shape[0], block), lambda j: (0, j)) for right in rights],
        out_specs=[pl.BlockSpec((LANES * len(p), block), lambda j: (0, j)) for p in parts],
        out_shape=[jax.ShapeDtypeStruct((LANES * len(p), cols), BF16) for p in parts],
        scratch_shapes=[pltpu.VMEM((wide_rows, kept), BF16) for _ in lefts],
        compiler_params=params(),
        cost_estimate=cost(
            2 * len(lefts) * kept * wide_rows * cols, 2 * (wide_rows + sum(rows)) * cols
        ),
        name="outer",
    )(*[array for array, _ in lefts], *rights)


def gate_tables(logit_ref, par_ref, beta_ref, decay_ref, cum_ref):
    logits = logit_ref[HALO:, :]
    beta_ref[...] = jax.nn.sigmoid(logits)
    shifted = logits + par_ref[1:2, :]
    soft = jnp.maximum(shifted, 0.0) + jnp.log1p(jnp.exp(-jnp.abs(shifted)))
    decay_ref[...] = -jnp.exp(par_ref[0:1, :]) * soft
    lower = (iota2((CHUNK, CHUNK), 0) >= iota2((CHUNK, CHUNK), 1)).astype(F32)
    for c in range(logits.shape[0] // CHUNK):
        part = decay_ref[c * CHUNK : (c + 1) * CHUNK, :]
        cum_ref[c * CHUNK : (c + 1) * CHUNK, :] = mm_exact(lower, part)


def mix_taps(p_ref, taps_ref, cols, pf_ref):
    tokens = cols.shape[0]
    pf_ref[...] = p_ref[...].astype(F32)
    total = pf_ref[HALO:, :] * taps_ref[0:1, :]
    for j in range(1, CONV):
        total += pf_ref[HALO - j : HALO - j + tokens, :] * taps_ref[j : j + 1, :] * cols[:, j : j + 1]
    return total


def chunk_tables(c, head, cols, segr_ref, cum_ref):
    rows = slice(c * CHUNK, (c + 1) * CHUNK)
    cum = lane(cum_ref[rows, :], head)
    cum_row = to_row(cum)
    same = cols[rows, 0:1] == segr_ref[0:1, rows]
    row_ids, col_ids = iota2((CHUNK, CHUNK), 0), iota2((CHUNK, CHUNK), 1)
    gamma = jnp.where((row_ids >= col_ids) & same, jnp.exp(jnp.minimum(cum - cum_row, 0.0)), 0.0)
    strict = jnp.where(row_ids > col_ids, gamma, 0.0)
    carry = jnp.exp(cum) * cols[rows, 4:5]
    last = jnp.exp(cum[CHUNK - 1 :, :] - cum) * cols[rows, 5:6]
    return gamma, strict, carry, last


def unit_lower_inverses(systems):
    size = systems[0].shape[0]
    row_ids, col_ids = iota2((size, size), 0), iota2((size, size), 1)
    eye = (row_ids == col_ids).astype(F32)
    found = [eye - jnp.where(row_ids // 2 == col_ids // 2, low, 0.0) for low in systems]
    width = 2
    while width < size:
        joined = (row_ids // (2 * width) == col_ids // (2 * width)) & (
            row_ids // width != col_ids // width
        )
        first = [mm_three(jnp.where(joined, low, 0.0), inv) for low, inv in zip(systems, found)]
        found = [inv - mm_three(inv, part) for inv, part in zip(found, first)]
        width *= 2
    return found


def device(planes=0, core=0, spot=0):
    place, here = lax.axis_index("dp"), lax.axis_index("seq")
    z = lax.rem(place // CORES + planes, PLANES)
    flip = lambda value, bits: value + sum(
        bit * (1 - 2 * lax.rem(value // bit, 2)) for bit in (1, 2) if bits & bit
    )
    return {"dp": z * CORES + flip(lax.rem(place, CORES), core), "seq": flip(here, spot)}


def greet(partners):
    barrier = pltpu.get_barrier_semaphore()
    for partner in partners:
        pl.semaphore_signal(barrier, inc=1, device_id=device(**partner), device_id_type=pl.DeviceIdType.MESH)
    pl.semaphore_wait(barrier, len(partners))


def gather_spans(inner):
    spans = [((H - 1) * HC, HC + LANES), ((H - 2) * HC, HC)]
    spans += [(h * HC, 2 * HC) for h in (4, 2, 0)]
    for at, size in ((AT_GATE, H * DV), (AT_OUT, H * DV)) + tuple((AT_FFN + i * inner, inner) for i in range(3)):
        spans += [(at + low, min(1024, size - low)) for low in range(0, size, 1024)]
    return spans


class Gathering:
    STAGES = (0, 1, 2, 3, 5, 7, 8)
    FIRST = ((0, 1, 2, 3, 4, 5, 6), (0, 1, 2, 3, 4, 6, 7))

    def __init__(self, spans, shard_ref, full_ref, sems):
        self.spans, self.shard, self.full = spans, shard_ref, full_ref
        self.send_sem, self.recv_sem, self.local_sem = sems
        self.piece = shard_ref.shape[0] // SPOTS
        self.half = full_ref.shape[0] // CORES
        self.z = lax.axis_index("dp") // CORES

    def own(self):
        piece = self.piece
        return [
            pltpu.make_async_copy(
                self.shard.at[q * piece : (q + 1) * piece],
                self.full.at[q * PLANES * piece : (q * PLANES + 1) * piece],
                self.local_sem.at[q],
            )
            for q in range(SPOTS)
        ]

    def copy(self, group, kind):
        at, size = self.spans[group]
        cols = pl.ds(at, size)
        piece, full = self.piece, self.full
        block = PLANES * piece
        rows = lambda quarter: pl.ds(quarter * block + piece, block - piece)
        if kind < 6:
            read, step, written = ((0, 1, 1), (0, -1, 3), (1, 1, 2), (3, -1, 2), (2, 1, 3), (2, -1, 1))[kind]
            source = self.shard.at[0:piece, cols] if read == 0 else full.at[read * piece : (read + 1) * piece, cols]
            target = full.at[written * piece : (written + 1) * piece, cols]
            to, arrival = device(planes=step % PLANES), written - 1
        elif kind < 8:
            source = full.at[rows(0), cols]
            target = full.at[rows(kind - 5), cols]
            to, arrival = device(spot=kind - 5), kind - 3
        elif kind == 8:
            by = 1 + group % 2
            source = full.at[rows(by), cols]
            target = full.at[rows(3), cols]
            to, arrival = device(spot=3 - by), 5
        else:
            source = full.at[0 : self.half, cols]
            target = full.at[self.half : 2 * self.half, cols]
            to, arrival = device(core=1), 6
        return pltpu.make_async_remote_copy(
            src_ref=source,
            dst_ref=target,
            send_sem=self.send_sem.at[group, kind],
            recv_sem=self.recv_sem.at[group, arrival],
            device_id=to,
            device_id_type=pl.DeviceIdType.MESH,
        )

    def sends(self, kind):
        z = self.z
        return (z < 3, z > 0, (z > 0) & (z < 3), (z > 0) & (z < 3), z == 2, z == 1)[kind]

    def start(self, group, kind):
        @pl.when(self.sends(kind))
        def _():
            self.copy(group, kind).start()

    def arrive(self, group, kind, condition):
        @pl.when(condition)
        def _():
            self.copy(group, kind).wait_recv()

    def tick(self, at):
        z = self.z
        due = []
        for group in range(len(self.spans)):
            stages = (self.FIRST + (self.STAGES,) * len(self.spans))[group]
            due += [(stage, group) for stage in range(len(stages)) if group + stages[stage] == at]
        for stage, group in sorted(due, reverse=True):
            by = 1 + group % 2
            if stage == 0:
                self.start(group, 0)
                self.start(group, 1)
            elif stage == 1:
                self.arrive(group, 0, z > 0)
                self.start(group, 2)
                self.arrive(group, 1, z < 3)
                self.start(group, 3)
            elif stage == 2:
                self.copy(group, 2).wait_recv()
                self.start(group, 4)
                self.start(group, 5)
            elif stage == 3:
                self.arrive(group, 0, z == 0)
                self.arrive(group, 1, z == 3)
                self.copy(group, 5 + by).start()
                self.copy(group, 8 - by).start()
            elif stage == 4:
                self.copy(group, 5 + by).wait_recv()
                self.copy(group, 8).start()
            elif stage == 5:
                self.copy(group, 8 - by).wait_recv()
                self.copy(group, 8).wait_recv()
                if group == 0:
                    for local in self.own():
                        local.wait()
                self.copy(group, 9).start()
            else:
                self.copy(group, 9).wait_recv()

    def finish(self):
        for group in range(len(self.spans)):
            for kind in range(6):

                @pl.when(self.sends(kind))
                def _(group=group, kind=kind):
                    self.copy(group, kind).wait_send()

            for kind in range(6, 10):
                self.copy(group, kind).wait_send()


def forward_kernel(*refs, planned, spans):
    h_ref, shard_ref, taps_ref, par_ref, cols_ref, segr_ref = refs[:6]
    refs = refs[6:]
    full_ref = shard_ref
    if planned:
        full_ref, refs = refs[0], refs[1:]
    (
        p_ref, logit_ref, part_ref, resp_ref, exch_ref, inv_ref, upd_ref, st_ref, stm_ref, amap_ref, rmap_ref,
        beta_ref, decay_ref, cum_ref, pf_ref, mix_ref, w_ref, wl_ref, load_sem,
    ) = refs[:19]
    head = pl.program_id(0)

    def load(slot, at, size, to):
        return pltpu.make_async_copy(full_ref.at[:, pl.ds(at, size)], to, load_sem.at[slot])

    if planned:
        stage_ref, send_sem, recv_sem, local_sem, exch_send, exch_recv, exch_local = refs[19:]
        gathering = Gathering(spans, shard_ref, full_ref, (send_sem, recv_sem, local_sem))
        lead = gathering.FIRST[0][-1] + 1
        final_tick = len(spans) + gathering.STAGES[-1]

        @pl.when(head == 0)
        def _():
            greet([dict(planes=d) for d in (1, 2, 3)] + [dict(spot=s) for s in (1, 2, 3)] + [dict(core=1)])
            for local in gathering.own():
                local.start()
            for at in range(lead):
                gathering.tick(at)

        for h in range(1, H):

            @pl.when(head == h)
            def _(h=h):
                gathering.tick(lead + 2 * h - 1)

    mine = load(0, pl.multiple_of((H - 1 - head) * HC, HC), HC, w_ref)
    mine.start()

    @pl.when(head == 0)
    def _():
        gates = load(1, AT_LOGIT, LANES, wl_ref)
        gates.start()
        gates.wait()
        logit_ref[...] = mm(h_ref[...], wl_ref[...])
        gate_tables(logit_ref, par_ref, beta_ref, decay_ref, cum_ref)

    mine.wait()
    p_ref[...] = mm(h_ref[...], w_ref[...]).astype(BF16)
    cols = cols_ref[...]
    tokens = cols.shape[0]
    total = mix_taps(p_ref, taps_ref, cols, pf_ref)
    mix_ref[...] = total * jax.nn.sigmoid(total)
    if planned:
        for h in range(H):

            @pl.when(head == h)
            def _(h=h):
                gathering.tick(lead + 2 * h)

    beta = lane(beta_ref[...], head + H)
    chunks = range(tokens // CHUNK)
    tables, lows, keys, queries = [], [], [], []
    for c in chunks:
        rows = slice(c * CHUNK, (c + 1) * CHUNK)
        query = mix_ref[rows, :DK]
        query = query * (lax.rsqrt(jnp.sum(query * query, axis=1, keepdims=True) + 1e-06) * DK**-0.5)
        key = mix_ref[rows, DK : 2 * DK]
        key = key * lax.rsqrt(jnp.sum(key * key, axis=1, keepdims=True) + 1e-06)
        gamma, strict, carry, last = chunk_tables(c, head, cols, segr_ref, cum_ref)
        dots = mm(jnp.concatenate([key, query], axis=0), key, NT)
        lows.append(beta[rows] * strict * dots[:CHUNK])
        tables.append((gamma * dots[CHUNK:], carry, last))
        keys.append(key)
        queries.append(query)
    inverses = unit_lower_inverses(lows)
    state = None
    for c in chunks:
        rows = slice(c * CHUNK, (c + 1) * CHUNK)
        scores, carry, last = tables[c]
        key, query = keys[c], queries[c]
        target = jnp.concatenate([mix_ref[rows, 2 * DK :], carry * key], axis=1) * beta[rows]
        updates = mm(inverses[c], target)
        inv_ref[0, c] = inverses[c].astype(BF16)
        upd_ref[0, rows, :] = updates
        weighted_t = jnp.transpose(last * key)
        both = mm(jnp.concatenate([weighted_t, scores], axis=0), updates)
        eye = (iota2((DK, DK), 0) == iota2((DK, DK), 1)).astype(F32)
        step_map = carry[CHUNK - 1 :, :] * eye - both[:DK, DV:]
        read_map = carry * query - both[DK:, DV:]
        amap_ref[0, c] = step_map.astype(BF16)
        rmap_ref[0, c] = read_map.astype(BF16)
        if c == 0:
            st_ref[0, c] = jnp.zeros((DK, DV), F32)
            stm_ref[0, c] = eye.astype(BF16)
            part_ref[rows, :] = both[DK:, :DV]
            resp_ref[rows, :] = read_map.astype(BF16)
            state = jnp.concatenate([both[:DK, :DV], step_map], axis=1)
        else:
            st_ref[0, c] = state[:, :DV]
            stm_ref[0, c] = state[:, DV:].astype(BF16)
            moved = mm(jnp.concatenate([step_map, read_map], axis=0), state)
            part_ref[rows, :] = both[DK:, :DV] + moved[DK:, :DV]
            resp_ref[rows, :] = moved[DK:, DV:].astype(BF16)
            state = moved[:DK] + jnp.concatenate(
                [both[:DK, :DV], jnp.zeros((DK, DK), F32)], axis=1
            )
    if not planned:
        exch_ref[0, 0] = state.astype(BF16)
        return
    stage_ref[head] = state.astype(BF16)

    def keep(h):
        return pltpu.make_async_copy(stage_ref.at[h], exch_ref.at[0, h], exch_local.at[h])

    def give(h, spot):
        return pltpu.make_async_remote_copy(
            src_ref=stage_ref.at[h],
            dst_ref=exch_ref.at[spot, h],
            send_sem=exch_send.at[spot - 1, h],
            recv_sem=exch_recv.at[spot - 1, h],
            device_id=device(spot=spot),
            device_id_type=pl.DeviceIdType.MESH,
        )

    keep(head).start()
    for spot in range(1, SPOTS):
        give(head, spot).start()

    @pl.when(head == H - 1)
    def _():
        for at in range(lead + 2 * H - 1, final_tick):
            gathering.tick(at)
        gathering.finish()
        for h in range(H):
            keep(h).wait()
            for spot in range(1, SPOTS):
                give(h, spot).wait()


def delta_forward(hidden, weights, taps, par, cols, segr, planned, inner):
    rows, width = hidden.shape
    tokens = rows - HALO
    chunks = tokens // CHUNK
    whole = lambda shape: pl.BlockSpec(shape, lambda h: (0,) * len(shape))
    by_head = lambda shape: pl.BlockSpec(shape, lambda h: (h,) + (0,) * (len(shape) - 1))
    anywhere = pl.BlockSpec(memory_space=pl.ANY)
    spans = gather_spans(inner)
    out_specs = [
        pl.BlockSpec((rows, HC), lambda h: (0, h)),
        whole((rows, LANES)),
        pl.BlockSpec((tokens, DV), lambda h: (0, h)),
        pl.BlockSpec((tokens, DK), lambda h: (0, h)),
        anywhere if planned else pl.BlockSpec((1, 1, DK, DV + DK), lambda h: (0, h, 0, 0)),
        by_head((1, chunks, CHUNK, CHUNK)),
        by_head((1, tokens, DV + DK)),
        by_head((1, chunks, DK, DV)),
        by_head((1, chunks, DK, DK)),
        by_head((1, chunks, DK, DK)),
        by_head((1, chunks, CHUNK, DK)),
    ]
    out_shape = [
        jax.ShapeDtypeStruct((rows, H * HC), BF16),
        jax.ShapeDtypeStruct((rows, LANES), F32),
        jax.ShapeDtypeStruct((tokens, H * DV), F32),
        jax.ShapeDtypeStruct((tokens, H * DK), BF16),
        jax.ShapeDtypeStruct((SPOTS if planned else 1, H, DK, DV + DK), BF16),
        jax.ShapeDtypeStruct((H, chunks, CHUNK, CHUNK), BF16),
        jax.ShapeDtypeStruct((H, tokens, DV + DK), F32),
        jax.ShapeDtypeStruct((H, chunks, DK, DV), F32),
        jax.ShapeDtypeStruct((H, chunks, DK, DK), BF16),
        jax.ShapeDtypeStruct((H, chunks, DK, DK), BF16),
        jax.ShapeDtypeStruct((H, chunks, CHUNK, DK), BF16),
    ]
    scratch = [
        pltpu.VMEM((tokens, LANES), F32),
        pltpu.VMEM((tokens, LANES), F32),
        pltpu.VMEM((tokens, LANES), F32),
        pltpu.VMEM((rows, HC), F32),
        pltpu.VMEM((tokens, HC), F32),
        pltpu.VMEM((width, HC), BF16),
        pltpu.VMEM((width, LANES), BF16),
        pltpu.SemaphoreType.DMA((2,)),
    ]
    more = {}
    if planned:
        out_specs = [anywhere] + out_specs
        out_shape = [jax.ShapeDtypeStruct((width, weights.shape[1]), BF16)] + out_shape
        scratch += [
            pltpu.VMEM((H, DK, DV + DK), BF16),
            pltpu.SemaphoreType.DMA((len(spans), 10)),
            pltpu.SemaphoreType.DMA((len(spans), 7)),
            pltpu.SemaphoreType.DMA((SPOTS,)),
            pltpu.SemaphoreType.DMA((SPOTS - 1, H)),
            pltpu.SemaphoreType.DMA((SPOTS - 1, H)),
            pltpu.SemaphoreType.DMA((H,)),
        ]
        more = dict(collective_id=0, has_side_effects=True)
    return pl.pallas_call(
        functools.partial(forward_kernel, planned=planned, spans=spans),
        grid=(H,),
        in_specs=[
            whole((rows, width)),
            pl.BlockSpec(memory_space=pltpu.VMEM) if planned else anywhere,
            pl.BlockSpec((8, HC), lambda h: (0, h)),
            whole((8, LANES)),
            whole((tokens, LANES)),
            whole((8, tokens)),
        ],
        out_specs=out_specs,
        out_shape=out_shape,
        scratch_shapes=scratch,
        compiler_params=params(**more),
        cost_estimate=cost(6e9 * H, 5e6 * H),
        name="delta_forward",
    )(hidden, weights, taps, par, cols, segr)


def backward_kernel(
    place_ref, slot_ref, p_ref, taps_ref, logit_ref, par_ref, cols_ref, back_ref, segr_ref,
    dattn_ref, sin_ref, exch_ref, grads_ref,
    inv_ref, upd_ref, st_ref, stm_ref, amap_ref, rmap_ref,
    dp_ref, dlogit_ref, dtaps_ref, dpar_ref,
    beta_ref, decay_ref, cum_ref, pf_ref, pre_ref, dmix_ref, *, first
):
    head = pl.program_id(0) + first
    place = place_ref[0]
    places = exch_ref.shape[0]

    @pl.when(pl.program_id(0) == 0)
    def _():
        gate_tables(logit_ref, par_ref, beta_ref, decay_ref, cum_ref)
        dlogit_ref[...] = jnp.zeros_like(dlogit_ref)
        dpar_ref[...] = jnp.zeros_like(dpar_ref)

    cols = cols_ref[...]
    tokens = cols.shape[0]
    chunks = range(tokens // CHUNK)
    pre = mix_taps(p_ref, taps_ref, cols, pf_ref)
    pre_ref[...] = pre
    beta = lane(beta_ref[...], head + H)

    def behind(lap, grad):
        source = places - 1 - lap
        slot = slot_ref[source]
        return jnp.where(
            source > place,
            grads_ref[slot, 0].astype(F32) + mm(exch_ref[slot, 0], grad, TN),
            grad,
        )

    d_state = lax.fori_loop(0, places - 1, behind, jnp.zeros((DK, DV), F32))
    state_in = sin_ref[0]
    d_states = [None] * len(chunks)
    for c in reversed(chunks):
        rows = slice(c * CHUNK, (c + 1) * CHUNK)
        d_states[c] = d_state
        if c > 0:
            d_state = mm(amap_ref[0, c], d_state, TN) + mm(rmap_ref[0, c], dattn_ref[rows, :], TN)

    row_ids, col_ids = iota2((CHUNK, CHUNK), 0), iota2((CHUNK, CHUNK), 1)
    d_beta_all, d_decay_all = [], []
    for c in chunks:
        rows = slice(c * CHUNK, (c + 1) * CHUNK)
        mixed = pre_ref[rows, :]
        gate = jax.nn.sigmoid(mixed)
        slope = gate * (1.0 + mixed * (1.0 - gate))
        mixed = mixed * gate
        query_raw, key_raw, value = mixed[:, :DK], mixed[:, DK : 2 * DK], mixed[:, 2 * DK :]
        query_size = lax.rsqrt(jnp.sum(query_raw * query_raw, axis=1, keepdims=True) + 1e-06)
        key_size = lax.rsqrt(jnp.sum(key_raw * key_raw, axis=1, keepdims=True) + 1e-06)
        query_unit, key = query_raw * query_size, key_raw * key_size
        query = query_unit * DK**-0.5
        gamma, strict, carry, last = chunk_tables(c, head, cols, segr_ref, cum_ref)
        strength = beta[rows]
        dots = mm(jnp.concatenate([key, query], axis=0), key, NT)
        weights = strict * dots[:CHUNK]
        low = strength * weights
        scores = gamma * dots[CHUNK:]
        if c == 0:
            state = state_in
        else:
            state = st_ref[0, c] + mm(stm_ref[0, c], state_in)
        updates = upd_ref[0, rows, :DV] - mm(upd_ref[0, rows, DV:], state)
        d_attn = dattn_ref[rows, :]
        d_state = d_states[c]
        d_updates = mm(scores, d_attn, TN) + mm(last * key, d_state)
        solved = mm(inv_ref[0, c], d_updates, TN)
        both = jnp.concatenate([d_attn, solved.astype(BF16)], axis=0)
        by_updates = mm(both, updates, NT)
        by_state = mm(both, state, NT)
        d_scores = by_updates[:CHUNK]
        d_low = -by_updates[CHUNK:]
        d_query = carry * by_state[:CHUNK]
        key_state = jnp.sum(key * by_state[CHUNK:], axis=1, keepdims=True)
        d_carry = jnp.sum(query * by_state[:CHUNK], axis=1, keepdims=True) - strength * key_state
        d_beta = (
            jnp.sum(solved * value, axis=1, keepdims=True)
            - carry * key_state
            + jnp.sum(d_low * weights, axis=1, keepdims=True)
        )
        d_dots_q = d_scores * gamma
        d_dots_k = d_low * strength * strict
        by_key = mm(jnp.concatenate([d_dots_q, d_dots_k], axis=0), key)
        d_query += by_key[:CHUNK]
        from_state = mm(updates, d_state, NT)
        d_key = (
            by_key[CHUNK:]
            + mm(
                jnp.concatenate([d_dots_q, d_dots_k], axis=0),
                jnp.concatenate([query, key], axis=0),
                TN,
            )
            - strength * carry * by_state[CHUNK:]
            + last * from_state
        )
        d_last = jnp.sum(key * from_state, axis=1, keepdims=True) * last
        d_spread = d_scores * scores + d_low * low
        final = (iota2((CHUNK, 1), 0) == CHUNK - 1).astype(F32)
        d_carry += final * jnp.sum(d_state * state)
        d_cum = (
            jnp.sum(d_spread, axis=1, keepdims=True)
            - to_column(jnp.sum(d_spread, axis=0, keepdims=True))
            + final * jnp.sum(d_last)
            - d_last
            + d_carry * carry
        )
        d_decay = jnp.sum(
            jnp.where(row_ids <= col_ids, to_row(d_cum), 0.0), axis=1, keepdims=True
        )
        d_beta_all.append(d_beta)
        d_decay_all.append(d_decay)
        d_query = d_query * DK**-0.5
        d_query = query_size * (
            d_query - query_unit * jnp.sum(d_query * query_unit, axis=1, keepdims=True)
        )
        d_key = key_size * (d_key - key * jnp.sum(d_key * key, axis=1, keepdims=True))
        d_value = strength * solved
        dmix_ref[HALO + c * CHUNK : HALO + (c + 1) * CHUNK, :] = slope * jnp.concatenate(
            [d_query, d_key, d_value], axis=1
        )

    d_beta = jnp.concatenate(d_beta_all, axis=0)
    d_decay = jnp.concatenate(d_decay_all, axis=0)
    lanes = iota2((tokens, LANES), 1)
    slope = jax.nn.sigmoid(logit_ref[HALO:, :] + par_ref[1:2, :]) * -jnp.exp(par_ref[0:1, :])
    here = jnp.where(lanes == head, d_decay, 0.0)
    d_first = here * slope
    strengths = beta_ref[...]
    d_second = jnp.where(lanes == head + H, d_beta, 0.0) * strengths * (1.0 - strengths)
    dlogit_ref[...] += d_first + d_second
    dpar_ref[0:1, :] += jnp.sum(here * decay_ref[...], axis=0, keepdims=True)
    dpar_ref[1:2, :] += jnp.sum(d_first, axis=0, keepdims=True)

    dmix_ref[:HALO, :] = jnp.zeros((HALO, HC), F32)
    dmix_ref[HALO + tokens :, :] = jnp.zeros((8, HC), F32)
    d_mix = dmix_ref[HALO : HALO + tokens, :]
    dtaps_ref[...] = jnp.zeros_like(dtaps_ref)
    dtaps_ref[0:1, :] = jnp.sum(d_mix * pf_ref[HALO:, :], axis=0, keepdims=True)
    total = dmix_ref[: HALO + tokens, :] * taps_ref[0:1, :]
    for j in range(1, CONV):
        total += dmix_ref[j : j + HALO + tokens, :] * taps_ref[j : j + 1, :] * back_ref[:, j : j + 1]
        dtaps_ref[j : j + 1, :] = jnp.sum(
            d_mix * cols[:, j : j + 1] * pf_ref[HALO - j : HALO - j + tokens, :],
            axis=0,
            keepdims=True,
        )
    dp_ref[...] = total.astype(BF16)


def delta_backward(
    first, heads, place, slots, proj, taps, logits, par, cols, back, segr, d_attn, state_in, exch, grads, saved
):
    rows = proj.shape[0]
    tokens = rows - HALO
    chunks = tokens // CHUNK
    places = exch.shape[0]
    whole = lambda shape: pl.BlockSpec(shape, lambda h: (0,) * len(shape))
    by_head = lambda shape: pl.BlockSpec(shape, lambda h: (h + first,) + (0,) * (len(shape) - 1))
    return pl.pallas_call(
        functools.partial(backward_kernel, first=first),
        grid=(heads,),
        in_specs=[
            pl.BlockSpec(memory_space=pltpu.SMEM),
            pl.BlockSpec(memory_space=pltpu.SMEM),
            pl.BlockSpec((rows, HC), lambda h: (0, h + first)),
            pl.BlockSpec((8, HC), lambda h: (0, h + first)),
            whole((rows, LANES)),
            whole((8, LANES)),
            whole((tokens, LANES)),
            whole((rows, LANES)),
            whole((8, tokens)),
            pl.BlockSpec((tokens, DV), lambda h: (0, h + first)),
            by_head((1, DK, DV)),
            pl.BlockSpec((places, 1, DK, DK), lambda h: (0, h + first, 0, DV // DK)),
            pl.BlockSpec((places, 1, DK, DV), lambda h: (0, h + first, 0, 0)),
            by_head((1, chunks, CHUNK, CHUNK)),
            by_head((1, tokens, DV + DK)),
            by_head((1, chunks, DK, DV)),
            by_head((1, chunks, DK, DK)),
            by_head((1, chunks, DK, DK)),
            by_head((1, chunks, CHUNK, DK)),
        ],
        out_specs=[
            pl.BlockSpec((rows, HC), lambda h: (0, h)),
            whole((tokens, LANES)),
            pl.BlockSpec((8, HC), lambda h: (0, h)),
            whole((8, LANES)),
        ],
        out_shape=[
            jax.ShapeDtypeStruct((rows, heads * HC), BF16),
            jax.ShapeDtypeStruct((tokens, LANES), F32),
            jax.ShapeDtypeStruct((8, heads * HC), F32),
            jax.ShapeDtypeStruct((8, LANES), F32),
        ],
        scratch_shapes=[
            pltpu.VMEM((tokens, LANES), F32),
            pltpu.VMEM((tokens, LANES), F32),
            pltpu.VMEM((tokens, LANES), F32),
            pltpu.VMEM((rows, HC), F32),
            pltpu.VMEM((tokens, HC), F32),
            pltpu.VMEM((rows + 8, HC), F32),
        ],
        compiler_params=params(),
        cost_estimate=cost(8e9 * heads, 5e6 * heads),
        name="delta_backward",
    )(place, slots, proj, taps, logits, par, cols, back, segr, d_attn, state_in, exch, grads, *saved)


def mixer_kernel(
    place_ref, slot_ref, part_ref, resp_ref, exch_ref, gpre_ref, gain_ref, w_ref, x_ref, gain2_ref,
    sin_ref, attn_ref, gated_ref, y_ref, h_ref,
):
    head = pl.program_id(0)
    place = place_ref[0]
    places = exch_ref.shape[0]

    def ahead(source, state):
        slot = slot_ref[source]
        return jnp.where(
            source < place,
            exch_ref[slot, 0, :, :DV].astype(F32) + mm(exch_ref[slot, 0, :, DV:], state),
            state,
        )

    state = lax.fori_loop(0, places - 1, ahead, jnp.zeros((DK, DV), F32))
    sin_ref[0] = state
    attn = part_ref[...] + mm(resp_ref[...], state)
    attn_ref[...] = attn
    scale = lax.rsqrt(jnp.mean(attn * attn, axis=-1, keepdims=True) + 1e-05)
    gate = gpre_ref[...]
    gated = (attn * scale * gain_ref[...] * (gate * jax.nn.sigmoid(gate))).astype(BF16)
    gated_ref[...] = gated

    @pl.when(head == 0)
    def _():
        y_ref[...] = x_ref[...].astype(F32)

    y_ref[...] += mm(gated, w_ref[...], NT)

    @pl.when(head == pl.num_programs(0) - 1)
    def _():
        value = y_ref[...]
        size = lax.rsqrt(jnp.mean(value * value, axis=-1, keepdims=True) + 1e-06)
        h_ref[...] = (value * size * gain2_ref[...]).astype(BF16)


def mixer_out(place, slots, part, resp, exch, gpre, gain, weights, x, gain2):
    tokens, width = x.shape
    places = exch.shape[0]
    whole = lambda shape: pl.BlockSpec(shape, lambda h: (0,) * len(shape))
    return pl.pallas_call(
        mixer_kernel,
        grid=(H,),
        in_specs=[
            pl.BlockSpec(memory_space=pltpu.SMEM),
            pl.BlockSpec(memory_space=pltpu.SMEM),
            pl.BlockSpec((tokens, DV), lambda h: (0, h)),
            pl.BlockSpec((tokens, DK), lambda h: (0, h)),
            pl.BlockSpec((places, 1, DK, DV + DK), lambda h: (0, h, 0, 0)),
            pl.BlockSpec((tokens, DV), lambda h: (0, h)),
            whole((1, DV)),
            pl.BlockSpec((width, DV), lambda h: (0, h + AT_OUT // DV)),
            whole((tokens, width)),
            whole((1, width)),
        ],
        out_specs=[
            pl.BlockSpec((1, DK, DV), lambda h: (h, 0, 0)),
            pl.BlockSpec((tokens, DV), lambda h: (0, h)),
            pl.BlockSpec((tokens, DV), lambda h: (0, h)),
            whole((tokens, width)),
            whole((tokens, width)),
        ],
        out_shape=[
            jax.ShapeDtypeStruct((H, DK, DV), F32),
            jax.ShapeDtypeStruct((tokens, H * DV), F32),
            jax.ShapeDtypeStruct((tokens, H * DV), BF16),
            jax.ShapeDtypeStruct((tokens, width), F32),
            jax.ShapeDtypeStruct((tokens, width), BF16),
        ],
        compiler_params=params(),
        cost_estimate=cost(2 * tokens * width * H * DV, 2e7),
        name="mixer_out",
    )(place, slots, part, resp, exch, gpre, gain, weights, x, gain2)


def mixer_back_kernel(
    dmix_ref, w_ref, attn_ref, gpre_ref, gain_ref, resp_ref,
    dattn_ref, dgpre_ref, grad_ref, dgain_ref,
):
    @pl.when(pl.program_id(0) == 0)
    def _():
        dgain_ref[...] = jnp.zeros_like(dgain_ref)

    d_gated = mm(dmix_ref[...], w_ref[...])
    attn = attn_ref[...]
    size = lax.rsqrt(jnp.mean(attn * attn, axis=-1, keepdims=True) + 1e-05)
    unit = attn * size
    gate = gpre_ref[...]
    slope = jax.nn.sigmoid(gate)
    swish = gate * slope
    gain = gain_ref[...]
    dgpre_ref[...] = (d_gated * (unit * gain) * (slope * (1.0 + gate * (1.0 - slope)))).astype(BF16)
    d_normed = d_gated * swish
    dgain_ref[0:1, :] += jnp.sum(d_normed * unit, axis=0, keepdims=True)
    d_unit = d_normed * gain
    d_attn = size * (d_unit - unit * jnp.mean(d_unit * unit, axis=-1, keepdims=True))
    d_attn = d_attn.astype(BF16)
    dattn_ref[...] = d_attn
    grad_ref[0] = mm(resp_ref[...], d_attn, TN).astype(BF16)


def mixer_back(d_mixer, weights, attn, gpre, gain, resp):
    tokens, width = d_mixer.shape
    whole = lambda shape: pl.BlockSpec(shape, lambda h: (0,) * len(shape))
    return pl.pallas_call(
        mixer_back_kernel,
        grid=(H,),
        in_specs=[
            whole((tokens, width)),
            pl.BlockSpec((width, DV), lambda h: (0, h + AT_OUT // DV)),
            pl.BlockSpec((tokens, DV), lambda h: (0, h)),
            pl.BlockSpec((tokens, DV), lambda h: (0, h)),
            whole((1, DV)),
            pl.BlockSpec((tokens, DK), lambda h: (0, h)),
        ],
        out_specs=[
            pl.BlockSpec((tokens, DV), lambda h: (0, h)),
            pl.BlockSpec((tokens, DV), lambda h: (0, h)),
            pl.BlockSpec((1, DK, DV), lambda h: (h, 0, 0)),
            whole((8, DV)),
        ],
        out_shape=[
            jax.ShapeDtypeStruct((tokens, H * DV), BF16),
            jax.ShapeDtypeStruct((tokens, H * DV), BF16),
            jax.ShapeDtypeStruct((H, DK, DV), BF16),
            jax.ShapeDtypeStruct((8, DV), F32),
        ],
        compiler_params=params(),
        cost_estimate=cost(2 * tokens * width * H * DV, 2e7),
        name="mixer_back",
    )(d_mixer, weights, attn, gpre, gain, resp)


def ffn_kernel(
    h_ref, dout_ref, y_ref, gain_ref, wg_ref, wu_ref, wd_ref,
    out_ref, act_ref, dg_ref, du_ref, dy_ref, dmix_ref, dgain_ref, res_ref, dh_ref,
):
    step = pl.program_id(0)

    @pl.when(step == 0)
    def _():
        res_ref[...] = y_ref[...]
        dh_ref[...] = jnp.zeros_like(dh_ref)

    hidden = h_ref[...]
    w_gate, w_up, w_down = wg_ref[...], wu_ref[...], wd_ref[...]
    gate = mm(hidden, w_gate)
    up = mm(hidden, w_up)
    d_act = mm(dout_ref[...], w_down)
    slope = jax.nn.sigmoid(gate)
    swish = gate * slope
    act = (swish * up).astype(BF16)
    act_ref[...] = act
    d_gate = (d_act * up * slope * (1.0 + gate * (1.0 - slope))).astype(BF16)
    d_up = (d_act * swish).astype(BF16)
    dg_ref[...] = d_gate
    du_ref[...] = d_up
    res_ref[...] += mm(act, w_down, NT)
    dh_ref[...] += mm(d_gate, w_gate, NT) + mm(d_up, w_up, NT)

    @pl.when(step == pl.num_programs(0) - 1)
    def _():
        out_ref[...] = res_ref[...].astype(BF16)
        value = y_ref[...]
        size = lax.rsqrt(jnp.mean(value * value, axis=-1, keepdims=True) + 1e-06)
        unit = value * size
        d_hidden = dh_ref[...]
        dgain_ref[...] = jnp.zeros_like(dgain_ref)
        dgain_ref[0:1, :] = jnp.sum(d_hidden * unit, axis=0, keepdims=True)
        d_unit = d_hidden * gain_ref[...]
        d_y = dout_ref[...].astype(F32) + size * (
            d_unit - unit * jnp.mean(d_unit * unit, axis=-1, keepdims=True)
        )
        dy_ref[...] = d_y
        dmix_ref[...] = d_y.astype(BF16)


def feed_forward(hidden, d_out, y1, gain, weights, inner):
    tokens, width = hidden.shape
    block = 256
    weight = lambda at: pl.BlockSpec((width, block), lambda j: (0, j + at // block))
    whole = lambda shape: pl.BlockSpec(shape, lambda j: (0,) * len(shape))
    across = pl.BlockSpec((tokens, block), lambda j: (0, j))
    return pl.pallas_call(
        ffn_kernel,
        grid=(inner // block,),
        in_specs=[
            whole((tokens, width)),
            whole((tokens, width)),
            whole((tokens, width)),
            whole((1, width)),
        ]
        + [weight(AT_FFN + i * inner) for i in range(3)],
        out_specs=[
            whole((tokens, width)), across, across, across,
            whole((tokens, width)), whole((tokens, width)), whole((8, width)),
        ],
        out_shape=[
            jax.ShapeDtypeStruct((tokens, width), BF16),
            jax.ShapeDtypeStruct((tokens, inner), BF16),
            jax.ShapeDtypeStruct((tokens, inner), BF16),
            jax.ShapeDtypeStruct((tokens, inner), BF16),
            jax.ShapeDtypeStruct((tokens, width), F32),
            jax.ShapeDtypeStruct((tokens, width), BF16),
            jax.ShapeDtypeStruct((8, width), F32),
        ],
        scratch_shapes=[pltpu.VMEM((tokens, width), F32), pltpu.VMEM((tokens, width), F32)],
        compiler_params=params(),
        cost_estimate=cost(12 * tokens * width * inner, 3e7),
        name="feed_forward",
    )(hidden, d_out, y1, gain, weights, weights, weights)


def input_grad_kernel(*refs, groups, per_group):
    dps, refs = refs[:groups], refs[groups:]
    (dg_ref, dl_ref, w_ref, wl_ref, x_ref, gain_ref, dy_ref, turn_ref) = refs[:8]
    out_ref, dgain_ref, acc_ref = refs[8:]
    step = pl.program_id(0)

    @pl.when(step == 0)
    def _():
        acc_ref[...] = mm(dl_ref[...], wl_ref[...], NT)

    for g in range(groups):

        @pl.when(step // per_group == g)
        def _(g=g):
            acc_ref[...] += mm(dps[g][HALO:, :], w_ref[...], NT)

    @pl.when(step >= groups * per_group)
    def _():
        acc_ref[...] += mm(dg_ref[...], w_ref[...], NT)

    @pl.when(step == pl.num_programs(0) - 1)
    def _():
        value = x_ref[...].astype(F32)
        size = lax.rsqrt(jnp.mean(value * value, axis=-1, keepdims=True) + 1e-06)
        unit = value * size
        d_hidden = acc_ref[...]
        dgain_ref[...] = jnp.zeros_like(dgain_ref)
        dgain_ref[0:1, :] = jnp.sum(d_hidden * unit, axis=0, keepdims=True)
        d_unit = d_hidden * gain_ref[...]
        total = dy_ref[...] + size * (
            d_unit - unit * jnp.mean(d_unit * unit, axis=-1, keepdims=True)
        )
        high, low = halves(total)
        out_ref[...] = mm(high, turn_ref[...], NT) + mm(low, turn_ref[...], NT)


def input_grad(d_projs, d_gpre, d_logit, weights, x, gain, d_y, turn):
    tokens, width = x.shape
    rows = d_projs[0].shape[0]
    block = HC
    groups = len(d_projs)
    per_group, second = d_projs[0].shape[1] // block, d_gpre.shape[1] // block
    steps = H + second
    whole = lambda shape: pl.BlockSpec(shape, lambda j: (0,) * len(shape))
    at = lambda g: lambda j: (0, jnp.clip(j - g * per_group, 0, per_group - 1))
    late = lambda j: (0, jnp.maximum(j - H, 0))
    weight = lambda j: (0, jnp.where(j < H, H - 1 - j, j - H + AT_GATE // block))
    in_specs = [pl.BlockSpec((rows, block), at(g)) for g in range(groups)]
    in_specs += [
        pl.BlockSpec((tokens, block), late),
        whole((tokens, LANES)),
        pl.BlockSpec((width, block), weight),
        pl.BlockSpec((width, LANES), lambda j: (0, AT_LOGIT // LANES)),
        whole((tokens, width)),
        whole((1, width)),
        whole((tokens, width)),
        whole((width, width)),
    ]
    return pl.pallas_call(
        functools.partial(input_grad_kernel, groups=groups, per_group=per_group),
        grid=(steps,),
        in_specs=in_specs,
        out_specs=[whole((tokens, width)), whole((8, width))],
        out_shape=[
            jax.ShapeDtypeStruct((tokens, width), F32),
            jax.ShapeDtypeStruct((8, width), F32),
        ],
        scratch_shapes=[pltpu.VMEM((tokens, width), F32)],
        compiler_params=params(),
        cost_estimate=cost(2 * tokens * width * steps * block, 3e7),
        name="input_grad",
    )(*d_projs, d_gpre, d_logit, weights, weights, x, gain, d_y, turn)


def shifted(block, axis, distance):
    devices = range(lax.axis_size(axis))
    route = [(i - distance, i) for i in devices if i - distance in devices]
    return lax.ppermute(block, axis, route)


def send(value, planes=0, core=0, spot=0):
    route = []
    for z in range(PLANES):
        for c in range(CORES):
            for s in range(SPOTS):
                target = (((z + planes) % PLANES) * CORES + (c ^ core)) * SPOTS + (s ^ spot)
                route.append(((z * CORES + c) * SPOTS + s, target))
    return lax.ppermute(value, ("dp", "seq"), route)


def flipped(stack, spot):
    pairs = stack.reshape((2, 2) + stack.shape[1:])
    pairs = jnp.where(spot % 2 == 1, pairs[:, ::-1], pairs)
    pairs = jnp.where(spot // 2 == 1, pairs[::-1], pairs)
    return pairs.reshape(stack.shape)


class Torus:
    def __init__(self, spot, width):
        self.spot = spot
        place = lax.axis_index("dp")
        z, c = place // CORES, place % CORES
        piece = width // (PLANES * CORES * SPOTS)
        at = jnp.arange(width)
        core, rest = at // (width // 2), at % (width // 2)
        quarter, plane, low = rest // (PLANES * piece), rest // piece % PLANES, rest % piece
        self.order = (
            ((z - plane) % PLANES * CORES + (c ^ core)) * SPOTS + (spot ^ quarter)
        ) * piece + low
        self.turn = (jnp.arange(width)[:, None] == self.order[None, :]).astype(BF16)
        self.slots = jnp.arange(SPOTS, dtype=jnp.int32) ^ spot

    def mine(self, value):
        return lax.dot(value, self.turn, preferred_element_type=BF16)

    def natural(self, value):
        return lax.dot_general(value, self.turn, (NT, ((), ())), preferred_element_type=BF16)

    def vector(self, value):
        return jnp.take(value, self.order)

    def vector_back(self, value):
        return jnp.dot(value[None], self.turn.T.astype(F32), precision=lax.Precision.HIGHEST)[0]

    def share(self, shard):
        rows, cols = shard.shape
        return flipped(shard.reshape(SPOTS, rows // SPOTS, cols), self.spot).reshape(rows, cols)

    def others(self, value):
        return send(value, core=1)

    def left(self, value):
        half = value.shape[1] // 2
        return [(value, 0), (self.others(value[:, half:]), 0)]

    def right(self, value):
        return [value, self.others(value)]

    def reduce(self, left, right, turned, skip_left=0, skip_right=0):
        first, second = (1, 2) if turned else (2, 1)
        width = left[0][0].shape[1] // 2
        kept, sent = outer(left, right, width, [(0, second), (first, 3)], skip_left, skip_right)
        size = kept.shape[0] // 2
        total = kept.astype(F32) + send(sent, spot=first).astype(F32)
        near, far = total[:size].astype(BF16), total[size:].astype(BF16)
        total = near.astype(F32) + send(far, spot=second).astype(F32)
        piece = size // PLANES
        parts = [total[d * piece : (d + 1) * piece] for d in range(PLANES)]
        total = parts[0]
        for d in range(1, PLANES):
            total += send(parts[d].astype(BF16), planes=-d).astype(F32)
        total = total.astype(BF16)
        spread = [total] + [send(total, spot=s) for s in range(1, SPOTS)]
        stack = flipped(jnp.stack(spread), self.spot)
        return stack.reshape(SPOTS * piece, -1).astype(F32)

    def along(self, value):
        return jnp.stack([value] + [send(value, spot=s) for s in range(1, SPOTS)])

    def total(self, value):
        value = value + send(value, core=1)
        value = value + send(value, spot=1)
        value = value + send(value, spot=2)
        return value + (send(value, planes=1) + send(value, planes=2) + send(value, planes=3))


class Plain:
    def __init__(self, spot, width):
        self.turn = jnp.eye(width, dtype=BF16)
        self.slots = jnp.arange(lax.axis_size("seq"), dtype=jnp.int32)

    def mine(self, value):
        return value

    natural = vector = vector_back = mine

    def share(self, shard):
        return lax.all_gather(shard, "dp", axis=0, tiled=True)

    def left(self, value):
        return [(value, 0)]

    def right(self, value):
        return [value]

    def reduce(self, left, right, turned, skip_left=0, skip_right=0):
        width = left[0][0].shape[1]
        (full,) = outer(left, right, width, [tuple(range(width // LANES))], skip_left, skip_right)
        part = lax.psum_scatter(full, "dp", scatter_dimension=0, tiled=True)
        return lax.psum(part, "seq").astype(F32)

    def along(self, value):
        return lax.all_gather(value, "seq")

    def total(self, value):
        return lax.psum(value, ("dp", "seq"))


def by_heads(query, key, value):
    lead = query.shape[:-1]
    parts = [query.reshape(lead + (H, DK)), key.reshape(lead + (H, DK)), value.reshape(lead + (H, DV))]
    return jnp.concatenate(parts, axis=-1).reshape(lead + (H * HC,))


def from_heads(value):
    lead = value.shape[:-1]
    parts = value.reshape(lead + (H, HC))
    return (
        parts[..., :DK].reshape(lead + (H * DK,)),
        parts[..., DK : 2 * DK].reshape(lead + (H * DK,)),
        parts[..., 2 * DK :].reshape(lead + (H * DV,)),
    )


def token_tables(segments, place, tokens):
    seg_pad = jnp.concatenate([jnp.full((HALO,), -1, jnp.int32), segments, jnp.full((8,), -2, jnp.int32)])
    ext = lax.dynamic_slice_in_dim(seg_pad, place * tokens, tokens + HALO + 8)
    seg = ext[HALO : HALO + tokens]
    columns = [seg.astype(F32)]
    for j in range(1, CONV):
        columns.append((ext[HALO - j : HALO - j + tokens] == seg).astype(F32))
    blocks = seg.reshape(-1, CHUNK)
    before = ext[HALO - 1 : HALO - 1 + tokens : CHUNK]
    columns.append((blocks == before[:, None]).astype(F32).reshape(-1))
    columns.append((blocks == blocks[:, -1:]).astype(F32).reshape(-1))
    columns += [jnp.zeros_like(columns[0])] * (LANES - len(columns))
    cols = jnp.stack(columns, axis=1)
    rows = tokens + HALO
    back = [jnp.zeros((rows,), F32)]
    for j in range(1, CONV):
        back.append((ext[j : j + rows] == ext[:rows]).astype(F32))
    back += [jnp.zeros((rows,), F32)] * (LANES - len(back))
    segr = jnp.broadcast_to(seg.astype(F32)[None], (8, tokens))
    return cols, jnp.stack(back, axis=1), segr


def wide(value):
    return jnp.pad(value, ((0, 0), (0, LANES - value.shape[1])))


def local(
    inputs, segments, cotangent, norm_gain_mix, w_query, w_key, w_value, w_outgate, w_gates,
    conv_weight, decay_log, dt_bias, out_norm_gain, w_out, norm_gain_ffn, w_ffn_gate, w_ffn_up, w_ffn_down,
):
    tokens, width = inputs.shape[1:]
    place = lax.axis_index("seq")
    place_arr = place.reshape((1,)).astype(jnp.int32)
    planned = (lax.axis_size("dp"), lax.axis_size("seq")) == (PLANES * CORES, SPOTS)
    comm = (Torus if planned else Plain)(place, width)
    slots = comm.slots
    low = lambda a: a.astype(BF16)

    qkv = by_heads(low(w_query), low(w_key), low(w_value))
    qkv = jnp.concatenate([qkv[:, h * HC : (h + 1) * HC] for h in reversed(range(H))], axis=1)
    shard = jnp.concatenate(
        [
            qkv, jnp.pad(low(w_gates), ((0, 0), (0, AT_GATE - AT_LOGIT - 2 * H))), low(w_outgate), low(w_out).T,
            low(w_ffn_gate), low(w_ffn_up), low(w_ffn_down).T,
        ],
        axis=1,
    )
    inner = w_ffn_gate.shape[1]
    weights = comm.share(shard)

    gain_mix, gain_ffn = comm.vector(norm_gain_mix)[None], comm.vector(norm_gain_ffn)[None]
    gain_out = out_norm_gain[None]
    taps_parts = by_heads(conv_weight[:, : H * DK], conv_weight[:, H * DK : 2 * H * DK], conv_weight[:, 2 * H * DK :])
    taps = jnp.pad(taps_parts, ((0, 8 - CONV), (0, 0)))
    par = jnp.pad(jnp.stack([decay_log, dt_bias]), ((0, 6), (0, LANES - H)))
    cols, back, segr = token_tables(segments[0], place, tokens)

    halo = shifted(inputs[0, tokens - HALO :], "seq", 1)
    x_ext = comm.mine(jnp.concatenate([halo, inputs[0]], axis=0))
    x = x_ext[HALO:]
    d_out = comm.mine(cotangent[0])
    value = x_ext.astype(F32)
    size = lax.rsqrt(jnp.mean(value * value, axis=-1, keepdims=True) + 1e-06)
    hidden = low(value * size * gain_mix)

    outs = delta_forward(hidden, weights, taps, par, cols, segr, planned, inner)
    if planned:
        weights, outs = outs[0], outs[1:]
    proj, logits, part, resp, exch, *saved = outs
    if not planned:
        exch = comm.along(exch[0])
    gpre = outgate(hidden, weights)
    state_in, attn, gated, y1, hidden_mid = mixer_out(
        place_arr, slots, part, resp, exch, gpre, gain_out, weights, x, gain_ffn
    )
    result, act, d_gate, d_up, d_y, d_mixer, d_gain_ffn = feed_forward(
        hidden_mid, d_out, y1, gain_ffn, weights, inner
    )
    d_attn, d_gpre, local_grad, d_gain_out = mixer_back(d_mixer, weights, attn, gpre, gain_out, resp)
    grads = comm.along(local_grad)

    left_mid, left_out = comm.left(hidden_mid), comm.left(d_out)
    g_down = comm.reduce(left_out, comm.right(act), True)
    g_gate = comm.reduce(left_mid, comm.right(d_gate), False)
    g_up = comm.reduce(left_mid, comm.right(d_up), True)
    g_out = comm.reduce(comm.left(d_mixer), comm.right(gated), False)
    left_in = comm.left(hidden)
    g_og = comm.reduce(left_in, comm.right(d_gpre), True, HALO, 0)
    heads = 2
    groups = H // heads
    d_projs, d_taps, d_logits, d_par, g_heads = [], [], 0.0, 0.0, []
    for g in range(groups):
        d_proj, d_logit, d_tap, d_pars = delta_backward(
            g * heads, heads, place_arr, slots, proj, taps, logits, par, cols, back, segr,
            d_attn, state_in, exch, grads, saved,
        )
        sent_back = shifted(d_proj[:HALO], "seq", -1)
        d_proj = d_proj.at[tokens:].add(sent_back)
        d_projs.append(d_proj)
        d_taps.append(d_tap)
        d_logits, d_par = d_logits + d_logit, d_par + d_pars
        g_heads.append(comm.reduce(left_in, comm.right(d_proj), g % 2 == 0, HALO, HALO))
    d_logit = low(d_logits)
    g_gates = comm.reduce(left_in, comm.right(d_logit), False, HALO, 0)
    d_inputs, d_gain_mix = input_grad(
        d_projs, d_gpre, d_logit, weights, x, gain_mix, d_y, comm.turn
    )

    g_query, g_key, g_value = from_heads(jnp.concatenate(g_heads, axis=1))
    d_conv = jnp.concatenate(from_heads(jnp.concatenate(d_taps, axis=1)[:CONV]), axis=1)
    pieces = [
        comm.vector_back(d_gain_mix[0]), d_conv.reshape(-1), d_par[0, :H], d_par[1, :H],
        d_gain_out[0], comm.vector_back(d_gain_ffn[0]),
    ]
    flat = jnp.concatenate(pieces)
    flat = comm.total(jnp.pad(flat, (0, -flat.shape[0] % 1024)).reshape(-1, LANES)).reshape(-1)
    small, at = [], 0
    for one in pieces:
        small.append(flat[at : at + one.shape[0]])
        at += one.shape[0]
    return (
        comm.natural(result)[None], d_inputs[None], small[0], g_query, g_key, g_value, g_og,
        g_gates[:, : 2 * H], small[1].reshape(d_conv.shape), small[2], small[3], small[4], g_out.T,
        small[5], g_gate, g_up, g_down.T,
    )


def solution(mesh):
    rows, cols, copied = P("dp", None), P(None, "dp"), P()
    tokens = P("dp", "seq", None)
    in_specs = (
        tokens, rows, tokens, copied, rows, rows, rows, rows, rows,
        copied, copied, copied, copied, cols, copied, rows, rows, cols,
    )
    out_specs = (
        tokens, tokens, copied, rows, rows, rows, rows, rows,
        copied, copied, copied, copied, cols, copied, rows, rows, cols,
    )
    return jax.shard_map(local, mesh=mesh, in_specs=in_specs, out_specs=out_specs, check_vma=False)
```

```python
import functools

import jax
import jax.numpy as jnp
from jax import lax
from jax.experimental import pallas as pl
from jax.experimental.pallas import tpu as pltpu
from jax.sharding import PartitionSpec as P

H = 8
DK = 128
DV = 256
CONV = 4
HALO = 16
CHUNK = 128
HC = 2 * DK + DV
LANES = 128
PLANES, CORES, SPOTS = 4, 2, 4

AT_LOGIT = H * HC
AT_GATE = AT_LOGIT + 512
AT_OUT = AT_GATE + H * DV
AT_FFN = AT_OUT + H * DV
VMEM_LIMIT = 56 * 2**20

F32 = jnp.float32
BF16 = jnp.bfloat16
NN = ((1,), (0,))
NT = ((1,), (1,))
TN = ((0,), (0,))


def mm(left, right, dims=NN):
    return lax.dot_general(
        left.astype(BF16), right.astype(BF16), (dims, ((), ())), preferred_element_type=F32
    )


def mm_exact(left, right, dims=NN):
    return lax.dot_general(
        left, right, (dims, ((), ())), precision=lax.Precision.HIGHEST, preferred_element_type=F32
    )


def halves(value):
    high = value.astype(BF16)
    return high, (value - high.astype(F32)).astype(BF16)


def mm_three(left, right):
    left_high, left_low = halves(left)
    right_high, right_low = halves(right)
    return mm(left_high, right_high) + (mm(left_high, right_low) + mm(left_low, right_high))


def params(**more):
    return pltpu.CompilerParams(vmem_limit_bytes=VMEM_LIMIT, **more)


def cost(flops, nbytes):
    return pl.CostEstimate(flops=int(flops), bytes_accessed=int(nbytes), transcendentals=0)


def iota2(shape, axis):
    return lax.broadcasted_iota(jnp.int32, shape, axis)


def lane(value, index):
    picked = jnp.where(iota2(value.shape, 1) == index, value, 0.0)
    return jnp.sum(picked, axis=1, keepdims=True)


def to_row(column):
    size = column.shape[0]
    same = iota2((size, size), 0) == iota2((size, size), 1)
    return jnp.sum(jnp.where(same, column, 0.0), axis=0, keepdims=True)


def to_column(row):
    size = row.shape[1]
    same = iota2((size, size), 0) == iota2((size, size), 1)
    return jnp.sum(jnp.where(same, row, 0.0), axis=1, keepdims=True)


def outgate_kernel(h_ref, w_ref, g_ref):
    g_ref[...] = mm(h_ref[HALO:, :], w_ref[...])


def outgate(hidden, weights):
    rows, width = hidden.shape
    cols = H * DV
    block = 512
    return pl.pallas_call(
        outgate_kernel,
        grid=(cols // block,),
        in_specs=[
            pl.BlockSpec((rows, width), lambda j: (0, 0)),
            pl.BlockSpec((width, block), lambda j: (0, j + AT_GATE // block)),
        ],
        out_specs=pl.BlockSpec((rows - HALO, block), lambda j: (0, j)),
        out_shape=jax.ShapeDtypeStruct((rows - HALO, cols), F32),
        compiler_params=params(),
        cost_estimate=cost(2 * rows * width * cols, 2 * width * cols + 4 * rows * cols),
        name="outgate",
    )(hidden, weights)


def outer_kernel(left_ref, right_ref, out_ref, turn_ref, *, skip):
    @pl.when(pl.program_id(0) == 0)
    def _():
        turn_ref[...] = jnp.transpose(left_ref[skip:, :])

    out_ref[...] = mm(turn_ref[...], right_ref[...]).astype(BF16)


def outer(left, right, skip):
    rows, width = left.shape
    cols = right.shape[1]
    block = next(b for b in (512, 256, 128) if cols % b == 0)
    return pl.pallas_call(
        functools.partial(outer_kernel, skip=skip),
        grid=(cols // block,),
        in_specs=[
            pl.BlockSpec((rows, width), lambda j: (0, 0)),
            pl.BlockSpec((rows - skip, block), lambda j: (0, j)),
        ],
        out_specs=pl.BlockSpec((width, block), lambda j: (0, j)),
        out_shape=jax.ShapeDtypeStruct((width, cols), BF16),
        scratch_shapes=[pltpu.VMEM((width, rows - skip), BF16)],
        compiler_params=params(),
        cost_estimate=cost(2 * rows * width * cols, 2 * width * cols + 2 * rows * cols),
        name="outer",
    )(left, right)


def gate_tables(logit_ref, par_ref, beta_ref, decay_ref, cum_ref):
    logits = logit_ref[HALO:, :]
    beta_ref[...] = jax.nn.sigmoid(logits)
    shifted = logits + par_ref[1:2, :]
    soft = jnp.maximum(shifted, 0.0) + jnp.log1p(jnp.exp(-jnp.abs(shifted)))
    decay_ref[...] = -jnp.exp(par_ref[0:1, :]) * soft
    lower = (iota2((CHUNK, CHUNK), 0) >= iota2((CHUNK, CHUNK), 1)).astype(F32)
    for c in range(logits.shape[0] // CHUNK):
        part = decay_ref[c * CHUNK : (c + 1) * CHUNK, :]
        cum_ref[c * CHUNK : (c + 1) * CHUNK, :] = mm_exact(lower, part)


def mix_taps(p_ref, taps_ref, cols, pf_ref):
    tokens = cols.shape[0]
    pf_ref[...] = p_ref[...].astype(F32)
    total = pf_ref[HALO:, :] * taps_ref[0:1, :]
    for j in range(1, CONV):
        total += pf_ref[HALO - j : HALO - j + tokens, :] * taps_ref[j : j + 1, :] * cols[:, j : j + 1]
    return total


def chunk_tables(c, head, cols, segr_ref, cum_ref):
    rows = slice(c * CHUNK, (c + 1) * CHUNK)
    cum = lane(cum_ref[rows, :], head)
    cum_row = to_row(cum)
    same = cols[rows, 0:1] == segr_ref[0:1, rows]
    row_ids, col_ids = iota2((CHUNK, CHUNK), 0), iota2((CHUNK, CHUNK), 1)
    gamma = jnp.where((row_ids >= col_ids) & same, jnp.exp(jnp.minimum(cum - cum_row, 0.0)), 0.0)
    strict = jnp.where(row_ids > col_ids, gamma, 0.0)
    carry = jnp.exp(cum) * cols[rows, 4:5]
    last = jnp.exp(cum[CHUNK - 1 :, :] - cum) * cols[rows, 5:6]
    return gamma, strict, carry, last


def unit_lower_inverses(systems):
    size = systems[0].shape[0]
    row_ids, col_ids = iota2((size, size), 0), iota2((size, size), 1)
    eye = (row_ids == col_ids).astype(F32)
    found = [eye - jnp.where(row_ids // 2 == col_ids // 2, low, 0.0) for low in systems]
    width = 2
    while width < size:
        joined = (row_ids // (2 * width) == col_ids // (2 * width)) & (
            row_ids // width != col_ids // width
        )
        first = [mm_three(jnp.where(joined, low, 0.0), inv) for low, inv in zip(systems, found)]
        found = [inv - mm_three(inv, part) for inv, part in zip(found, first)]
        width *= 2
    return found


def device(planes=0, core=0, spot=0):
    place, here = lax.axis_index("dp"), lax.axis_index("seq")
    z = lax.rem(place // CORES + planes, PLANES)
    flip = lambda value, bits: value + sum(
        bit * (1 - 2 * lax.rem(value // bit, 2)) for bit in (1, 2) if bits & bit
    )
    return {"dp": z * CORES + flip(lax.rem(place, CORES), core), "seq": flip(here, spot)}


def greet(partners):
    barrier = pltpu.get_barrier_semaphore()
    for partner in partners:
        pl.semaphore_signal(barrier, inc=1, device_id=device(**partner), device_id_type=pl.DeviceIdType.MESH)
    pl.semaphore_wait(barrier, len(partners))


def gather_spans(inner):
    spans = [((H - 1) * HC, HC + LANES), ((H - 2) * HC, HC)]
    spans += [(h * HC, 2 * HC) for h in (4, 2, 0)]
    for at, size in ((AT_GATE, H * DV), (AT_OUT, H * DV)) + tuple((AT_FFN + i * inner, inner) for i in range(3)):
        spans += [(at + low, min(1024, size - low)) for low in range(0, size, 1024)]
    return spans


class Gathering:
    STAGES = (0, 1, 2, 3, 5, 7, 8)
    FIRST = ((0, 1, 2, 3, 4, 5, 6), (0, 1, 2, 3, 4, 6, 7))

    def __init__(self, spans, shard_ref, full_ref, sems):
        self.spans, self.shard, self.full = spans, shard_ref, full_ref
        self.send_sem, self.recv_sem, self.local_sem = sems
        self.piece = shard_ref.shape[0] // SPOTS
        self.half = full_ref.shape[0] // CORES
        self.z = lax.axis_index("dp") // CORES

    def own(self):
        piece = self.piece
        return [
            pltpu.make_async_copy(
                self.shard.at[q * piece : (q + 1) * piece],
                self.full.at[q * PLANES * piece : (q * PLANES + 1) * piece],
                self.local_sem.at[q],
            )
            for q in range(SPOTS)
        ]

    def copy(self, group, kind):
        at, size = self.spans[group]
        cols = pl.ds(at, size)
        piece, full = self.piece, self.full
        block = PLANES * piece
        rows = lambda quarter: pl.ds(quarter * block + piece, block - piece)
        if kind < 6:
            read, step, written = ((0, 1, 1), (0, -1, 3), (1, 1, 2), (3, -1, 2), (2, 1, 3), (2, -1, 1))[kind]
            source = self.shard.at[0:piece, cols] if read == 0 else full.at[read * piece : (read + 1) * piece, cols]
            target = full.at[written * piece : (written + 1) * piece, cols]
            to, arrival = device(planes=step % PLANES), written - 1
        elif kind < 8:
            source = full.at[rows(0), cols]
            target = full.at[rows(kind - 5), cols]
            to, arrival = device(spot=kind - 5), kind - 3
        elif kind == 8:
            by = 1 + group % 2
            source = full.at[rows(by), cols]
            target = full.at[rows(3), cols]
            to, arrival = device(spot=3 - by), 5
        else:
            source = full.at[0 : self.half, cols]
            target = full.at[self.half : 2 * self.half, cols]
            to, arrival = device(core=1), 6
        return pltpu.make_async_remote_copy(
            src_ref=source,
            dst_ref=target,
            send_sem=self.send_sem.at[group, kind],
            recv_sem=self.recv_sem.at[group, arrival],
            device_id=to,
            device_id_type=pl.DeviceIdType.MESH,
        )

    def sends(self, kind):
        z = self.z
        return (z < 3, z > 0, (z > 0) & (z < 3), (z > 0) & (z < 3), z == 2, z == 1)[kind]

    def start(self, group, kind):
        @pl.when(self.sends(kind))
        def _():
            self.copy(group, kind).start()

    def arrive(self, group, kind, condition):
        @pl.when(condition)
        def _():
            self.copy(group, kind).wait_recv()

    def tick(self, at):
        z = self.z
        due = []
        for group in range(len(self.spans)):
            stages = (self.FIRST + (self.STAGES,) * len(self.spans))[group]
            due += [(stage, group) for stage in range(len(stages)) if group + stages[stage] == at]
        for stage, group in sorted(due, reverse=True):
            by = 1 + group % 2
            if stage == 0:
                self.start(group, 0)
                self.start(group, 1)
            elif stage == 1:
                self.arrive(group, 0, z > 0)
                self.start(group, 2)
                self.arrive(group, 1, z < 3)
                self.start(group, 3)
            elif stage == 2:
                self.copy(group, 2).wait_recv()
                self.start(group, 4)
                self.start(group, 5)
            elif stage == 3:
                self.arrive(group, 0, z == 0)
                self.arrive(group, 1, z == 3)
                self.copy(group, 5 + by).start()
                self.copy(group, 8 - by).start()
            elif stage == 4:
                self.copy(group, 5 + by).wait_recv()
                self.copy(group, 8).start()
            elif stage == 5:
                self.copy(group, 8 - by).wait_recv()
                self.copy(group, 8).wait_recv()
                if group == 0:
                    for local in self.own():
                        local.wait()
                self.copy(group, 9).start()
            else:
                self.copy(group, 9).wait_recv()

    def finish(self):
        for group in range(len(self.spans)):
            for kind in range(6):

                @pl.when(self.sends(kind))
                def _(group=group, kind=kind):
                    self.copy(group, kind).wait_send()

            for kind in range(6, 10):
                self.copy(group, kind).wait_send()


def forward_kernel(*refs, planned, spans):
    h_ref, shard_ref, taps_ref, par_ref, cols_ref, segr_ref = refs[:6]
    refs = refs[6:]
    full_ref = shard_ref
    if planned:
        full_ref, refs = refs[0], refs[1:]
    (
        p_ref, logit_ref, part_ref, resp_ref, exch_ref, inv_ref, upd_ref, st_ref, stm_ref, amap_ref, rmap_ref,
        beta_ref, decay_ref, cum_ref, pf_ref, mix_ref, w_ref, wl_ref, load_sem,
    ) = refs[:19]
    head = pl.program_id(0)

    def load(slot, at, size, to):
        return pltpu.make_async_copy(full_ref.at[:, pl.ds(at, size)], to, load_sem.at[slot])

    if planned:
        stage_ref, send_sem, recv_sem, local_sem, exch_send, exch_recv, exch_local = refs[19:]
        gathering = Gathering(spans, shard_ref, full_ref, (send_sem, recv_sem, local_sem))
        lead = gathering.FIRST[0][-1] + 1
        final_tick = len(spans) + gathering.STAGES[-1]

        @pl.when(head == 0)
        def _():
            greet([dict(planes=d) for d in (1, 2, 3)] + [dict(spot=s) for s in (1, 2, 3)] + [dict(core=1)])
            for local in gathering.own():
                local.start()
            for at in range(lead):
                gathering.tick(at)

        for h in range(1, H):

            @pl.when(head == h)
            def _(h=h):
                gathering.tick(lead + 2 * h - 1)

    mine = load(0, pl.multiple_of((H - 1 - head) * HC, HC), HC, w_ref)
    mine.start()

    @pl.when(head == 0)
    def _():
        gates = load(1, AT_LOGIT, LANES, wl_ref)
        gates.start()
        gates.wait()
        logit_ref[...] = mm(h_ref[...], wl_ref[...])
        gate_tables(logit_ref, par_ref, beta_ref, decay_ref, cum_ref)

    mine.wait()
    p_ref[...] = mm(h_ref[...], w_ref[...]).astype(BF16)
    cols = cols_ref[...]
    tokens = cols.shape[0]
    total = mix_taps(p_ref, taps_ref, cols, pf_ref)
    mix_ref[...] = total * jax.nn.sigmoid(total)
    if planned:
        for h in range(H):

            @pl.when(head == h)
            def _(h=h):
                gathering.tick(lead + 2 * h)

    beta = lane(beta_ref[...], head + H)
    chunks = range(tokens // CHUNK)
    tables, lows, keys, queries = [], [], [], []
    for c in chunks:
        rows = slice(c * CHUNK, (c + 1) * CHUNK)
        query = mix_ref[rows, :DK]
        query = query * (lax.rsqrt(jnp.sum(query * query, axis=1, keepdims=True) + 1e-06) * DK**-0.5)
        key = mix_ref[rows, DK : 2 * DK]
        key = key * lax.rsqrt(jnp.sum(key * key, axis=1, keepdims=True) + 1e-06)
        gamma, strict, carry, last = chunk_tables(c, head, cols, segr_ref, cum_ref)
        dots = mm(jnp.concatenate([key, query], axis=0), key, NT)
        lows.append(beta[rows] * strict * dots[:CHUNK])
        tables.append((gamma * dots[CHUNK:], carry, last))
        keys.append(key)
        queries.append(query)
    inverses = unit_lower_inverses(lows)
    state = None
    for c in chunks:
        rows = slice(c * CHUNK, (c + 1) * CHUNK)
        scores, carry, last = tables[c]
        key, query = keys[c], queries[c]
        target = jnp.concatenate([mix_ref[rows, 2 * DK :], carry * key], axis=1) * beta[rows]
        updates = mm(inverses[c], target)
        inv_ref[0, c] = inverses[c].astype(BF16)
        upd_ref[0, rows, :] = updates
        weighted_t = jnp.transpose(last * key)
        both = mm(jnp.concatenate([weighted_t, scores], axis=0), updates)
        eye = (iota2((DK, DK), 0) == iota2((DK, DK), 1)).astype(F32)
        step_map = carry[CHUNK - 1 :, :] * eye - both[:DK, DV:]
        read_map = carry * query - both[DK:, DV:]
        amap_ref[0, c] = step_map.astype(BF16)
        rmap_ref[0, c] = read_map.astype(BF16)
        if c == 0:
            st_ref[0, c] = jnp.zeros((DK, DV), F32)
            stm_ref[0, c] = eye.astype(BF16)
            part_ref[rows, :] = both[DK:, :DV]
            resp_ref[rows, :] = read_map.astype(BF16)
            state = jnp.concatenate([both[:DK, :DV], step_map], axis=1)
        else:
            st_ref[0, c] = state[:, :DV]
            stm_ref[0, c] = state[:, DV:].astype(BF16)
            moved = mm(jnp.concatenate([step_map, read_map], axis=0), state)
            part_ref[rows, :] = both[DK:, :DV] + moved[DK:, :DV]
            resp_ref[rows, :] = moved[DK:, DV:].astype(BF16)
            state = moved[:DK] + jnp.concatenate(
                [both[:DK, :DV], jnp.zeros((DK, DK), F32)], axis=1
            )
    if not planned:
        exch_ref[0, 0] = state.astype(BF16)
        return
    stage_ref[head] = state.astype(BF16)

    def keep(h):
        return pltpu.make_async_copy(stage_ref.at[h], exch_ref.at[0, h], exch_local.at[h])

    def give(h, spot):
        return pltpu.make_async_remote_copy(
            src_ref=stage_ref.at[h],
            dst_ref=exch_ref.at[spot, h],
            send_sem=exch_send.at[spot - 1, h],
            recv_sem=exch_recv.at[spot - 1, h],
            device_id=device(spot=spot),
            device_id_type=pl.DeviceIdType.MESH,
        )

    keep(head).start()
    for spot in range(1, SPOTS):
        give(head, spot).start()

    @pl.when(head == H - 1)
    def _():
        for at in range(lead + 2 * H - 1, final_tick):
            gathering.tick(at)
        gathering.finish()
        for h in range(H):
            keep(h).wait()
            for spot in range(1, SPOTS):
                give(h, spot).wait()


def delta_forward(hidden, weights, taps, par, cols, segr, planned, inner):
    rows, width = hidden.shape
    tokens = rows - HALO
    chunks = tokens // CHUNK
    whole = lambda shape: pl.BlockSpec(shape, lambda h: (0,) * len(shape))
    by_head = lambda shape: pl.BlockSpec(shape, lambda h: (h,) + (0,) * (len(shape) - 1))
    anywhere = pl.BlockSpec(memory_space=pl.ANY)
    spans = gather_spans(inner)
    out_specs = [
        pl.BlockSpec((rows, HC), lambda h: (0, h)),
        whole((rows, LANES)),
        pl.BlockSpec((tokens, DV), lambda h: (0, h)),
        pl.BlockSpec((tokens, DK), lambda h: (0, h)),
        anywhere if planned else pl.BlockSpec((1, 1, DK, DV + DK), lambda h: (0, h, 0, 0)),
        by_head((1, chunks, CHUNK, CHUNK)),
        by_head((1, tokens, DV + DK)),
        by_head((1, chunks, DK, DV)),
        by_head((1, chunks, DK, DK)),
        by_head((1, chunks, DK, DK)),
        by_head((1, chunks, CHUNK, DK)),
    ]
    out_shape = [
        jax.ShapeDtypeStruct((rows, H * HC), BF16),
        jax.ShapeDtypeStruct((rows, LANES), F32),
        jax.ShapeDtypeStruct((tokens, H * DV), F32),
        jax.ShapeDtypeStruct((tokens, H * DK), BF16),
        jax.ShapeDtypeStruct((SPOTS if planned else 1, H, DK, DV + DK), BF16),
        jax.ShapeDtypeStruct((H, chunks, CHUNK, CHUNK), BF16),
        jax.ShapeDtypeStruct((H, tokens, DV + DK), F32),
        jax.ShapeDtypeStruct((H, chunks, DK, DV), F32),
        jax.ShapeDtypeStruct((H, chunks, DK, DK), BF16),
        jax.ShapeDtypeStruct((H, chunks, DK, DK), BF16),
        jax.ShapeDtypeStruct((H, chunks, CHUNK, DK), BF16),
    ]
    scratch = [
        pltpu.VMEM((tokens, LANES), F32),
        pltpu.VMEM((tokens, LANES), F32),
        pltpu.VMEM((tokens, LANES), F32),
        pltpu.VMEM((rows, HC), F32),
        pltpu.VMEM((tokens, HC), F32),
        pltpu.VMEM((width, HC), BF16),
        pltpu.VMEM((width, LANES), BF16),
        pltpu.SemaphoreType.DMA((2,)),
    ]
    more = {}
    if planned:
        out_specs = [anywhere] + out_specs
        out_shape = [jax.ShapeDtypeStruct((width, weights.shape[1]), BF16)] + out_shape
        scratch += [
            pltpu.VMEM((H, DK, DV + DK), BF16),
            pltpu.SemaphoreType.DMA((len(spans), 10)),
            pltpu.SemaphoreType.DMA((len(spans), 7)),
            pltpu.SemaphoreType.DMA((SPOTS,)),
            pltpu.SemaphoreType.DMA((SPOTS - 1, H)),
            pltpu.SemaphoreType.DMA((SPOTS - 1, H)),
            pltpu.SemaphoreType.DMA((H,)),
        ]
        more = dict(collective_id=0, has_side_effects=True)
    return pl.pallas_call(
        functools.partial(forward_kernel, planned=planned, spans=spans),
        grid=(H,),
        in_specs=[
            whole((rows, width)),
            pl.BlockSpec(memory_space=pltpu.VMEM) if planned else anywhere,
            pl.BlockSpec((8, HC), lambda h: (0, h)),
            whole((8, LANES)),
            whole((tokens, LANES)),
            whole((8, tokens)),
        ],
        out_specs=out_specs,
        out_shape=out_shape,
        scratch_shapes=scratch,
        compiler_params=params(**more),
        cost_estimate=cost(6e9 * H, 5e6 * H),
        name="delta_forward",
    )(hidden, weights, taps, par, cols, segr)


def backward_kernel(place_ref, slot_ref, *refs):
    grads_ref, refs = refs[10], refs[:10] + refs[11:]
    exch_ref = refs[9]

    def behind(source, grad):
        slot = slot_ref[source]
        return jnp.where(
            source > place_ref[0],
            grads_ref[slot, 0].astype(F32) + mm(exch_ref[slot, 0], grad, TN),
            grad,
        )

    places = exch_ref.shape[0]
    d_state = lax.fori_loop(
        0, places - 1, lambda lap, grad: behind(places - 1 - lap, grad), jnp.zeros((DK, DV), F32)
    )
    backward_head(pl.program_id(0), d_state, *refs)


def backward_head(
    head, d_state, p_ref, taps_ref, logit_ref, par_ref, cols_ref, back_ref, segr_ref,
    dattn_ref, sin_ref, exch_ref,
    inv_ref, upd_ref, st_ref, stm_ref, amap_ref, rmap_ref,
    dp_ref, dlogit_ref, dtaps_ref, dpar_ref,
    beta_ref, decay_ref, cum_ref, pf_ref, pre_ref, dmix_ref,
):
    @pl.when(head == 0)
    def _():
        gate_tables(logit_ref, par_ref, beta_ref, decay_ref, cum_ref)
        dlogit_ref[...] = jnp.zeros_like(dlogit_ref)
        dpar_ref[...] = jnp.zeros_like(dpar_ref)

    cols = cols_ref[...]
    tokens = cols.shape[0]
    chunks = range(tokens // CHUNK)
    pre = mix_taps(p_ref, taps_ref, cols, pf_ref)
    pre_ref[...] = pre
    beta = lane(beta_ref[...], head + H)

    state_in = sin_ref[0]
    d_states = [None] * len(chunks)
    for c in reversed(chunks):
        rows = slice(c * CHUNK, (c + 1) * CHUNK)
        d_states[c] = d_state
        if c > 0:
            d_state = mm(amap_ref[0, c], d_state, TN) + mm(rmap_ref[0, c], dattn_ref[rows, :], TN)

    row_ids, col_ids = iota2((CHUNK, CHUNK), 0), iota2((CHUNK, CHUNK), 1)
    d_beta_all, d_decay_all = [], []
    for c in chunks:
        rows = slice(c * CHUNK, (c + 1) * CHUNK)
        mixed = pre_ref[rows, :]
        gate = jax.nn.sigmoid(mixed)
        slope = gate * (1.0 + mixed * (1.0 - gate))
        mixed = mixed * gate
        query_raw, key_raw, value = mixed[:, :DK], mixed[:, DK : 2 * DK], mixed[:, 2 * DK :]
        query_size = lax.rsqrt(jnp.sum(query_raw * query_raw, axis=1, keepdims=True) + 1e-06)
        key_size = lax.rsqrt(jnp.sum(key_raw * key_raw, axis=1, keepdims=True) + 1e-06)
        query_unit, key = query_raw * query_size, key_raw * key_size
        query = query_unit * DK**-0.5
        gamma, strict, carry, last = chunk_tables(c, head, cols, segr_ref, cum_ref)
        strength = beta[rows]
        dots = mm(jnp.concatenate([key, query], axis=0), key, NT)
        weights = strict * dots[:CHUNK]
        low = strength * weights
        scores = gamma * dots[CHUNK:]
        if c == 0:
            state = state_in
        else:
            state = st_ref[0, c] + mm(stm_ref[0, c], state_in)
        updates = upd_ref[0, rows, :DV] - mm(upd_ref[0, rows, DV:], state)
        d_attn = dattn_ref[rows, :]
        d_state = d_states[c]
        d_updates = mm(scores, d_attn, TN) + mm(last * key, d_state)
        solved = mm(inv_ref[0, c], d_updates, TN)
        both = jnp.concatenate([d_attn, solved.astype(BF16)], axis=0)
        by_updates = mm(both, updates, NT)
        by_state = mm(both, state, NT)
        d_scores = by_updates[:CHUNK]
        d_low = -by_updates[CHUNK:]
        d_query = carry * by_state[:CHUNK]
        key_state = jnp.sum(key * by_state[CHUNK:], axis=1, keepdims=True)
        d_carry = jnp.sum(query * by_state[:CHUNK], axis=1, keepdims=True) - strength * key_state
        d_beta = (
            jnp.sum(solved * value, axis=1, keepdims=True)
            - carry * key_state
            + jnp.sum(d_low * weights, axis=1, keepdims=True)
        )
        d_dots_q = d_scores * gamma
        d_dots_k = d_low * strength * strict
        by_key = mm(jnp.concatenate([d_dots_q, d_dots_k], axis=0), key)
        d_query += by_key[:CHUNK]
        from_state = mm(updates, d_state, NT)
        d_key = (
            by_key[CHUNK:]
            + mm(
                jnp.concatenate([d_dots_q, d_dots_k], axis=0),
                jnp.concatenate([query, key], axis=0),
                TN,
            )
            - strength * carry * by_state[CHUNK:]
            + last * from_state
        )
        d_last = jnp.sum(key * from_state, axis=1, keepdims=True) * last
        d_spread = d_scores * scores + d_low * low
        final = (iota2((CHUNK, 1), 0) == CHUNK - 1).astype(F32)
        d_carry += final * jnp.sum(d_state * state)
        d_cum = (
            jnp.sum(d_spread, axis=1, keepdims=True)
            - to_column(jnp.sum(d_spread, axis=0, keepdims=True))
            + final * jnp.sum(d_last)
            - d_last
            + d_carry * carry
        )
        d_decay = jnp.sum(
            jnp.where(row_ids <= col_ids, to_row(d_cum), 0.0), axis=1, keepdims=True
        )
        d_beta_all.append(d_beta)
        d_decay_all.append(d_decay)
        d_query = d_query * DK**-0.5
        d_query = query_size * (
            d_query - query_unit * jnp.sum(d_query * query_unit, axis=1, keepdims=True)
        )
        d_key = key_size * (d_key - key * jnp.sum(d_key * key, axis=1, keepdims=True))
        d_value = strength * solved
        dmix_ref[HALO + c * CHUNK : HALO + (c + 1) * CHUNK, :] = slope * jnp.concatenate(
            [d_query, d_key, d_value], axis=1
        )

    d_beta = jnp.concatenate(d_beta_all, axis=0)
    d_decay = jnp.concatenate(d_decay_all, axis=0)
    lanes = iota2((tokens, LANES), 1)
    slope = jax.nn.sigmoid(logit_ref[HALO:, :] + par_ref[1:2, :]) * -jnp.exp(par_ref[0:1, :])
    here = jnp.where(lanes == head, d_decay, 0.0)
    d_first = here * slope
    strengths = beta_ref[...]
    d_second = jnp.where(lanes == head + H, d_beta, 0.0) * strengths * (1.0 - strengths)
    dlogit_ref[...] += d_first + d_second
    dpar_ref[0:1, :] += jnp.sum(here * decay_ref[...], axis=0, keepdims=True)
    dpar_ref[1:2, :] += jnp.sum(d_first, axis=0, keepdims=True)

    dmix_ref[:HALO, :] = jnp.zeros((HALO, HC), F32)
    dmix_ref[HALO + tokens :, :] = jnp.zeros((8, HC), F32)
    d_mix = dmix_ref[HALO : HALO + tokens, :]
    dtaps_ref[...] = jnp.zeros_like(dtaps_ref)
    dtaps_ref[0:1, :] = jnp.sum(d_mix * pf_ref[HALO:, :], axis=0, keepdims=True)
    total = dmix_ref[: HALO + tokens, :] * taps_ref[0:1, :]
    for j in range(1, CONV):
        total += dmix_ref[j : j + HALO + tokens, :] * taps_ref[j : j + 1, :] * back_ref[:, j : j + 1]
        dtaps_ref[j : j + 1, :] = jnp.sum(
            d_mix * cols[:, j : j + 1] * pf_ref[HALO - j : HALO - j + tokens, :],
            axis=0,
            keepdims=True,
        )
    dp_ref[...] = total.astype(BF16)


def delta_backward(
    place, slots, proj, taps, logits, par, cols, back, segr, d_attn, state_in, exch, grads, saved
):
    rows = proj.shape[0]
    tokens = rows - HALO
    chunks = tokens // CHUNK
    places = exch.shape[0]
    whole = lambda shape: pl.BlockSpec(shape, lambda h: (0,) * len(shape))
    by_head = lambda shape: pl.BlockSpec(shape, lambda h: (h,) + (0,) * (len(shape) - 1))
    return pl.pallas_call(
        backward_kernel,
        grid=(H,),
        in_specs=[
            pl.BlockSpec(memory_space=pltpu.SMEM),
            pl.BlockSpec(memory_space=pltpu.SMEM),
            pl.BlockSpec((rows, HC), lambda h: (0, h)),
            pl.BlockSpec((8, HC), lambda h: (0, h)),
            whole((rows, LANES)),
            whole((8, LANES)),
            whole((tokens, LANES)),
            whole((rows, LANES)),
            whole((8, tokens)),
            pl.BlockSpec((tokens, DV), lambda h: (0, h)),
            by_head((1, DK, DV)),
            pl.BlockSpec((places, 1, DK, DK), lambda h: (0, h, 0, DV // DK)),
            pl.BlockSpec((places, 1, DK, DV), lambda h: (0, h, 0, 0)),
            by_head((1, chunks, CHUNK, CHUNK)),
            by_head((1, tokens, DV + DK)),
            by_head((1, chunks, DK, DV)),
            by_head((1, chunks, DK, DK)),
            by_head((1, chunks, DK, DK)),
            by_head((1, chunks, CHUNK, DK)),
        ],
        out_specs=[
            pl.BlockSpec((rows, HC), lambda h: (0, h)),
            whole((tokens, LANES)),
            pl.BlockSpec((8, HC), lambda h: (0, h)),
            whole((8, LANES)),
        ],
        out_shape=[
            jax.ShapeDtypeStruct((rows, H * HC), BF16),
            jax.ShapeDtypeStruct((tokens, LANES), F32),
            jax.ShapeDtypeStruct((8, H * HC), F32),
            jax.ShapeDtypeStruct((8, LANES), F32),
        ],
        scratch_shapes=[
            pltpu.VMEM((tokens, LANES), F32),
            pltpu.VMEM((tokens, LANES), F32),
            pltpu.VMEM((tokens, LANES), F32),
            pltpu.VMEM((rows, HC), F32),
            pltpu.VMEM((tokens, HC), F32),
            pltpu.VMEM((rows + 8, HC), F32),
        ],
        compiler_params=params(),
        cost_estimate=cost(8e9 * H, 5e6 * H),
        name="delta_backward",
    )(place, slots, proj, taps, logits, par, cols, back, segr, d_attn, state_in, exch, grads, *saved)


def mixer_kernel(
    place_ref, slot_ref, part_ref, resp_ref, exch_ref, gpre_ref, gain_ref, w_ref, x_ref, gain2_ref,
    sin_ref, attn_ref, gated_ref, y_ref, h_ref,
):
    head = pl.program_id(0)
    place = place_ref[0]
    places = exch_ref.shape[0]

    def ahead(source, state):
        slot = slot_ref[source]
        return jnp.where(
            source < place,
            exch_ref[slot, 0, :, :DV].astype(F32) + mm(exch_ref[slot, 0, :, DV:], state),
            state,
        )

    state = lax.fori_loop(0, places - 1, ahead, jnp.zeros((DK, DV), F32))
    sin_ref[0] = state
    attn = part_ref[...] + mm(resp_ref[...], state)
    attn_ref[...] = attn
    scale = lax.rsqrt(jnp.mean(attn * attn, axis=-1, keepdims=True) + 1e-05)
    gate = gpre_ref[...]
    gated = (attn * scale * gain_ref[...] * (gate * jax.nn.sigmoid(gate))).astype(BF16)
    gated_ref[...] = gated

    @pl.when(head == 0)
    def _():
        y_ref[...] = x_ref[...].astype(F32)

    y_ref[...] += mm(gated, w_ref[...], NT)

    @pl.when(head == pl.num_programs(0) - 1)
    def _():
        value = y_ref[...]
        size = lax.rsqrt(jnp.mean(value * value, axis=-1, keepdims=True) + 1e-06)
        h_ref[...] = (value * size * gain2_ref[...]).astype(BF16)


def mixer_out(place, slots, part, resp, exch, gpre, gain, weights, x, gain2):
    tokens, width = x.shape
    places = exch.shape[0]
    whole = lambda shape: pl.BlockSpec(shape, lambda h: (0,) * len(shape))
    return pl.pallas_call(
        mixer_kernel,
        grid=(H,),
        in_specs=[
            pl.BlockSpec(memory_space=pltpu.SMEM),
            pl.BlockSpec(memory_space=pltpu.SMEM),
            pl.BlockSpec((tokens, DV), lambda h: (0, h)),
            pl.BlockSpec((tokens, DK), lambda h: (0, h)),
            pl.BlockSpec((places, 1, DK, DV + DK), lambda h: (0, h, 0, 0)),
            pl.BlockSpec((tokens, DV), lambda h: (0, h)),
            whole((1, DV)),
            pl.BlockSpec((width, DV), lambda h: (0, h + AT_OUT // DV)),
            whole((tokens, width)),
            whole((1, width)),
        ],
        out_specs=[
            pl.BlockSpec((1, DK, DV), lambda h: (h, 0, 0)),
            pl.BlockSpec((tokens, DV), lambda h: (0, h)),
            pl.BlockSpec((tokens, DV), lambda h: (0, h)),
            whole((tokens, width)),
            whole((tokens, width)),
        ],
        out_shape=[
            jax.ShapeDtypeStruct((H, DK, DV), F32),
            jax.ShapeDtypeStruct((tokens, H * DV), F32),
            jax.ShapeDtypeStruct((tokens, H * DV), BF16),
            jax.ShapeDtypeStruct((tokens, width), F32),
            jax.ShapeDtypeStruct((tokens, width), BF16),
        ],
        compiler_params=params(),
        cost_estimate=cost(2 * tokens * width * H * DV, 2e7),
        name="mixer_out",
    )(place, slots, part, resp, exch, gpre, gain, weights, x, gain2)


def mixer_back_kernel(
    dmix_ref, w_ref, attn_ref, gpre_ref, gain_ref, resp_ref,
    dattn_ref, dgpre_ref, grad_ref, dgain_ref,
):
    @pl.when(pl.program_id(0) == 0)
    def _():
        dgain_ref[...] = jnp.zeros_like(dgain_ref)

    d_gated = mm(dmix_ref[...], w_ref[...])
    attn = attn_ref[...]
    size = lax.rsqrt(jnp.mean(attn * attn, axis=-1, keepdims=True) + 1e-05)
    unit = attn * size
    gate = gpre_ref[...]
    slope = jax.nn.sigmoid(gate)
    swish = gate * slope
    gain = gain_ref[...]
    dgpre_ref[...] = (d_gated * (unit * gain) * (slope * (1.0 + gate * (1.0 - slope)))).astype(BF16)
    d_normed = d_gated * swish
    dgain_ref[0:1, :] += jnp.sum(d_normed * unit, axis=0, keepdims=True)
    d_unit = d_normed * gain
    d_attn = size * (d_unit - unit * jnp.mean(d_unit * unit, axis=-1, keepdims=True))
    d_attn = d_attn.astype(BF16)
    dattn_ref[...] = d_attn
    grad_ref[0] = mm(resp_ref[...], d_attn, TN).astype(BF16)


def mixer_back(d_mixer, weights, attn, gpre, gain, resp):
    tokens, width = d_mixer.shape
    whole = lambda shape: pl.BlockSpec(shape, lambda h: (0,) * len(shape))
    return pl.pallas_call(
        mixer_back_kernel,
        grid=(H,),
        in_specs=[
            whole((tokens, width)),
            pl.BlockSpec((width, DV), lambda h: (0, h + AT_OUT // DV)),
            pl.BlockSpec((tokens, DV), lambda h: (0, h)),
            pl.BlockSpec((tokens, DV), lambda h: (0, h)),
            whole((1, DV)),
            pl.BlockSpec((tokens, DK), lambda h: (0, h)),
        ],
        out_specs=[
            pl.BlockSpec((tokens, DV), lambda h: (0, h)),
            pl.BlockSpec((tokens, DV), lambda h: (0, h)),
            pl.BlockSpec((1, DK, DV), lambda h: (h, 0, 0)),
            whole((8, DV)),
        ],
        out_shape=[
            jax.ShapeDtypeStruct((tokens, H * DV), BF16),
            jax.ShapeDtypeStruct((tokens, H * DV), BF16),
            jax.ShapeDtypeStruct((H, DK, DV), BF16),
            jax.ShapeDtypeStruct((8, DV), F32),
        ],
        compiler_params=params(),
        cost_estimate=cost(2 * tokens * width * H * DV, 2e7),
        name="mixer_back",
    )(d_mixer, weights, attn, gpre, gain, resp)


def ffn_kernel(
    h_ref, dout_ref, y_ref, gain_ref, wg_ref, wu_ref, wd_ref,
    out_ref, act_ref, dgu_ref, dy_ref, dmix_ref, dgain_ref, res_ref, dh_ref,
):
    step = pl.program_id(0)

    @pl.when(step == 0)
    def _():
        res_ref[...] = y_ref[...]
        dh_ref[...] = jnp.zeros_like(dh_ref)

    hidden = h_ref[...]
    w_gate, w_up, w_down = wg_ref[...], wu_ref[...], wd_ref[...]
    gate = mm(hidden, w_gate)
    up = mm(hidden, w_up)
    d_act = mm(dout_ref[...], w_down)
    slope = jax.nn.sigmoid(gate)
    swish = gate * slope
    act = (swish * up).astype(BF16)
    act_ref[...] = act
    d_gate = (d_act * up * slope * (1.0 + gate * (1.0 - slope))).astype(BF16)
    d_up = (d_act * swish).astype(BF16)
    dgu_ref[0] = d_gate
    dgu_ref[1] = d_up
    res_ref[...] += mm(act, w_down, NT)
    dh_ref[...] += mm(d_gate, w_gate, NT) + mm(d_up, w_up, NT)

    @pl.when(step == pl.num_programs(0) - 1)
    def _():
        out_ref[...] = res_ref[...].astype(BF16)
        value = y_ref[...]
        size = lax.rsqrt(jnp.mean(value * value, axis=-1, keepdims=True) + 1e-06)
        unit = value * size
        d_hidden = dh_ref[...]
        dgain_ref[...] = jnp.zeros_like(dgain_ref)
        dgain_ref[0:1, :] = jnp.sum(d_hidden * unit, axis=0, keepdims=True)
        d_unit = d_hidden * gain_ref[...]
        d_y = dout_ref[...].astype(F32) + size * (
            d_unit - unit * jnp.mean(d_unit * unit, axis=-1, keepdims=True)
        )
        dy_ref[...] = d_y
        dmix_ref[...] = d_y.astype(BF16)


def feed_forward(hidden, d_out, y1, gain, weights, inner):
    tokens, width = hidden.shape
    block = 256
    weight = lambda at: pl.BlockSpec((width, block), lambda j: (0, j + at // block))
    whole = lambda shape: pl.BlockSpec(shape, lambda j: (0,) * len(shape))
    across = pl.BlockSpec((tokens, block), lambda j: (0, j))
    return pl.pallas_call(
        ffn_kernel,
        grid=(inner // block,),
        in_specs=[
            whole((tokens, width)),
            whole((tokens, width)),
            whole((tokens, width)),
            whole((1, width)),
        ]
        + [weight(AT_FFN + i * inner) for i in range(3)],
        out_specs=[
            whole((tokens, width)), across, pl.BlockSpec((2, tokens, block), lambda j: (0, 0, j)),
            whole((tokens, width)), whole((tokens, width)), whole((8, width)),
        ],
        out_shape=[
            jax.ShapeDtypeStruct((tokens, width), BF16),
            jax.ShapeDtypeStruct((tokens, inner), BF16),
            jax.ShapeDtypeStruct((2, tokens, inner), BF16),
            jax.ShapeDtypeStruct((tokens, width), F32),
            jax.ShapeDtypeStruct((tokens, width), BF16),
            jax.ShapeDtypeStruct((8, width), F32),
        ],
        scratch_shapes=[pltpu.VMEM((tokens, width), F32), pltpu.VMEM((tokens, width), F32)],
        compiler_params=params(),
        cost_estimate=cost(12 * tokens * width * inner, 3e7),
        name="feed_forward",
    )(hidden, d_out, y1, gain, weights, weights, weights)


BLOCK = HC
LEAD, EVERY = 4, 3


def other_index(step):
    return step - jnp.clip((step - LEAD + EVERY - 1) // EVERY, 0, H)


class Blocks:
    def __init__(self, inner):
        self.ups, self.downs = inner // (BLOCK // 2), inner // BLOCK
        self.outs = H * DV // BLOCK
        self.others = self.ups + self.downs + 2 * self.outs
        self.count = self.others + H + 1
        self.starts = [0, self.ups, self.ups + self.downs, self.ups + self.downs + self.outs, self.others]
        self.tail = inner - self.downs * BLOCK
        heads = [LEAD + EVERY * h for h in range(H)]
        rest = [n for n in range(self.count - 1) if n not in heads]
        parts = [rest[low:high] for low, high in zip(self.starts, self.starts[1:])]
        self.up_at, self.down_at, self.out_at, self.gate_at = parts
        self.head_at = heads

    def index(self, kind):
        low, high = self.starts[kind], self.starts[kind + 1]
        return lambda s: jnp.clip(other_index(s) - low, 0, high - low - 1)


def dot_blocks(left, right):
    return lax.dot_general(left, right, (NN, ((), ())), preferred_element_type=F32)


def flip_to(bit):
    here = lax.axis_index("seq")
    along_x = here + 1 - 2 * lax.rem(here, 2)
    along_y = here + 2 - 4 * (here // 2)
    return {"dp": lax.axis_index("dp"), "seq": (2 - bit) * along_x + (bit - 1) * along_y}


def reduce_kernel(
    dout_ref, hmid_ref, dres_ref, hidden_ref, act_ref, tail_ref, dgu_ref, gated_ref, dgpre_ref, lgrad_ref,
    p_ref, taps_ref, logit_ref, par_ref, cols_ref, back_ref, segr_ref, dattn_ref, sin_ref, exch_ref,
    inv_ref, upd_ref, st_ref, stm_ref, amap_ref, rmap_ref,
    sum_ref, dp_ref, dlogit_ref, dtaps_ref, dpar_ref,
    beta_ref, decay_ref, cum_ref, pf_ref, pre_ref, dmix_ref,
    turn_ref, dps_ref, halo_ref, grads_ref,
    core_keep, core_send, core_recv, near_keep, near_send, near_recv,
    far_keep, far_send, far_recv, z_keep, z_send, z_recv, done_ref,
    core_ss, core_rs, near_ss, near_rs, far_ss, far_rs, z_ss, z_rs, done_ss, done_rs, own_sem,
    halo_ss, halo_rs, grads_ss, grads_rs, *, blocks,
):
    step = pl.program_id(0)
    steps = pl.num_programs(0)
    place = lax.axis_index("seq")
    count = blocks.count
    half = core_keep.shape[1] * core_keep.shape[2]
    quarter = half // SPOTS
    piece = quarter // PLANES
    mesh = dict(device_id_type=pl.DeviceIdType.MESH)

    def remote(source, target, send, recv, to):
        return pltpu.make_async_remote_copy(
            src_ref=source, dst_ref=target, send_sem=send, recv_sem=recv, device_id=to, **mesh
        )

    def to_core(n):
        slot = lax.rem(n, 2)
        return remote(core_send.at[slot], core_recv.at[slot], core_ss.at[slot], core_rs.at[slot], device(core=1))

    def to_near(n):
        slot = lax.rem(n, 4)
        return remote(
            near_send.at[slot], near_recv.at[slot], near_ss.at[slot], near_rs.at[slot], flip_to(1 + lax.rem(n, 2))
        )

    def to_far(n):
        slot = lax.rem(n, 4)
        return remote(
            far_send.at[slot], far_recv.at[slot], far_ss.at[slot], far_rs.at[slot], flip_to(2 - lax.rem(n, 2))
        )

    def along_z(n, d):
        slot = lax.rem(n, 4)
        return remote(
            z_send.at[slot, d - 1], z_recv.at[slot, d - 1], z_ss.at[slot, d - 1], z_rs.at[slot, d - 1],
            device(planes=PLANES - d),
        )

    def target(n):
        return sum_ref.at[
            pl.ds(pl.multiple_of(place * piece, piece), piece), pl.ds(pl.multiple_of(n * BLOCK, BLOCK), BLOCK)
        ]

    def spread(n, spot):
        slot = lax.rem(n, 4)
        return remote(
            done_ref.at[slot], target(n), done_ss.at[slot, spot - 1], done_rs.at[n, spot - 1], device(spot=spot)
        )

    def keep(n):
        slot = lax.rem(n, 4)
        return pltpu.make_async_copy(done_ref.at[slot], target(n), own_sem.at[slot])

    def give_grads(spot):
        return remote(
            lgrad_ref, grads_ref.at[spot - 1], grads_ss.at[spot - 1], grads_rs.at[spot - 1], device(spot=spot)
        )

    def give_halo(head):
        to = {"dp": lax.axis_index("dp"), "seq": lax.rem(place + SPOTS - 1, SPOTS)}
        return remote(dps_ref.at[0:HALO], halo_ref.at[head], halo_ss.at[head], halo_rs.at[head], to)

    @pl.when(step == 0)
    def _():
        greet([dict(planes=d) for d in (1, 2, 3)] + [dict(spot=s) for s in (1, 2, 3)] + [dict(core=1)])
        for spot in range(1, SPOTS):
            give_grads(spot).start()
        for at, ref in enumerate((dout_ref, hmid_ref, dres_ref)):
            turn_ref[at] = jnp.transpose(ref[...])
        turn_ref[3] = jnp.transpose(hidden_ref[HALO:, :])

    def at_stage(lag, sent):
        n = step - lag

        def run(body):
            @pl.when((n >= 0) & (n < count))
            def _():
                @pl.when(n >= sent)
                def _():
                    body(n, True)

                body(n, False)

        return run

    @at_stage(7, 4)
    def _(n, free):
        if free:
            for spot in range(1, SPOTS):
                spread(n - 4, spot).wait_send()
            keep(n - 4).wait()
            return
        slot = lax.rem(n, 4)
        total = z_keep[slot]
        for d in range(1, PLANES):
            along_z(n, d).wait_recv()
            total += z_recv[slot, d - 1].astype(F32)
        done_ref[slot] = total.astype(BF16)
        keep(n).start()
        for spot in range(1, SPOTS):
            spread(n, spot).start()

    @at_stage(5, 4)
    def _(n, free):
        if free:
            for d in range(1, PLANES):
                along_z(n - 4, d).wait_send()
            return
        slot = lax.rem(n, 4)
        to_far(n).wait_recv()
        total = far_keep[slot] + far_recv[slot].astype(F32)
        z_keep[slot] = total[:piece]
        for d in range(1, PLANES):
            z_send[slot, d - 1] = total[d * piece : (d + 1) * piece].astype(BF16)
            along_z(n, d).start()

    @at_stage(3, 4)
    def _(n, free):
        if free:
            to_far(n - 4).wait_send()
            return
        slot = lax.rem(n, 4)
        to_near(n).wait_recv()
        far_keep[slot] = near_keep[slot, 0] + near_recv[slot, 0].astype(F32)
        far_send[slot] = (near_keep[slot, 1] + near_recv[slot, 1].astype(F32)).astype(BF16)
        to_far(n).start()

    @at_stage(1, 4)
    def _(n, free):
        if free:
            to_near(n - 4).wait_send()
            return
        slot, pair = lax.rem(n, 4), lax.rem(n, 2)
        first = 1 + pair
        to_core(n).wait_recv()
        whole = lambda quarter: core_keep[pair, quarter] + core_recv[pair, quarter].astype(F32)
        near_keep[slot, 0] = whole(0)
        near_keep[slot, 1] = whole(3 - first)
        near_send[slot, 0] = whole(first).astype(BF16)
        near_send[slot, 1] = whole(3).astype(BF16)
        to_near(n).start()

    since = step - LEAD
    heads_turn = (since >= 0) & (since < EVERY * H) & (lax.rem(jnp.maximum(since, 0), EVERY) == 0)
    other = other_index(step)

    def put(product):
        pair = lax.rem(step, 2)

        @pl.when(step >= 2)
        def _():
            to_core(step - 2).wait_send()

        for q in range(SPOTS):
            core_keep[pair, q] = product[q * quarter : (q + 1) * quarter]
            core_send[pair, q] = product[half + q * quarter : half + (q + 1) * quarter].astype(BF16)
        to_core(step).start()

    def on(kind):
        low, high = blocks.starts[kind], blocks.starts[kind + 1]
        return pl.when((other >= low) & (other < high) & jnp.logical_not(heads_turn))

    @on(0)
    def _():
        put(dot_blocks(turn_ref[1], jnp.concatenate([dgu_ref[0], dgu_ref[1]], axis=1)))

    @on(1)
    def _():
        put(dot_blocks(turn_ref[0], act_ref[...]))

    @on(2)
    def _():
        put(dot_blocks(turn_ref[2], gated_ref[...]))

    @on(3)
    def _():
        put(dot_blocks(turn_ref[3], dgpre_ref[...]))

    @pl.when(step == count - 1)
    def _():
        down = dot_blocks(turn_ref[0], tail_ref[...])
        gates = dot_blocks(turn_ref[3], dlogit_ref[...].astype(BF16))
        rest = jnp.zeros((down.shape[0], BLOCK - down.shape[1] - LANES), F32)
        put(jnp.concatenate([down, gates, rest], axis=1))

    @pl.when(heads_turn)
    def _():
        head = since // EVERY

        @pl.when(place > 0)
        def _():
            give_halo(head).wait_send()

        @pl.when(place < SPOTS - 1)
        def _():
            give_halo(head).wait_recv()
            tokens = dps_ref.shape[0] - HALO
            dps_ref[tokens:, :] = (
                dps_ref[tokens:, :].astype(F32) + halo_ref[head].astype(F32)
            ).astype(BF16)

        value = dps_ref[HALO:, :]
        dp_ref[...] = value
        put(dot_blocks(turn_ref[3], value))

    @pl.when((since >= -1) & (since < EVERY * H - 1) & (lax.rem(jnp.maximum(since + 1, 0), EVERY) == 0))
    def _():
        head = (since + 1) // EVERY

        @pl.when(head == 0)
        def _():
            for spot in range(1, SPOTS):
                give_grads(spot).wait()

        d_state = jnp.zeros((DK, DV), F32)
        for source in range(SPOTS - 1, 0, -1):
            low = lax.rem(place, 2) * (1 - 2 * (source % 2)) + source % 2
            high = (place // 2) * (1 - 2 * (source // 2)) + source // 2
            slot = low + 2 * high
            grads = grads_ref[jnp.maximum(slot - 1, 0), head].astype(F32)
            d_state = jnp.where(source > place, grads + mm(exch_ref[slot, 0], d_state, TN), d_state)
        backward_head(
            head, d_state, p_ref, taps_ref, logit_ref, par_ref, cols_ref, back_ref, segr_ref,
            dattn_ref, sin_ref, exch_ref, inv_ref, upd_ref, st_ref, stm_ref, amap_ref, rmap_ref,
            dps_ref, dlogit_ref, dtaps_ref, dpar_ref, beta_ref, decay_ref, cum_ref, pf_ref, pre_ref, dmix_ref,
        )

        @pl.when(place > 0)
        def _():
            give_halo(head).start()

    @pl.when(step == steps - 1)
    def _():
        for n in range(count - 4, count):
            if n >= count - 2:
                to_core(n).wait_send()
            to_near(n).wait_send()
            to_far(n).wait_send()
            for d in range(1, PLANES):
                along_z(n, d).wait_send()
            for spot in range(1, SPOTS):
                spread(n, spot).wait_send()
            keep(n).wait()

        def arrived(n, carry):
            for spot in range(1, SPOTS):
                spread(n, spot).wait_recv()
            return carry

        lax.fori_loop(0, count, arrived, 0)


def reduce_gradients(
    d_out, hidden_mid, d_mixer, hidden, act, d_gu, gated, d_gpre, local_grad,
    proj, taps, logits, par, cols, back, segr, d_attn, state_in, exch, saved,
):
    tokens, width = d_out.shape
    rows = hidden.shape[0]
    chunks = tokens // CHUNK
    blocks = Blocks(act.shape[1])
    half = width // CORES
    quarter = half // SPOTS
    piece = quarter // PLANES
    whole = lambda shape: pl.BlockSpec(shape, lambda s: (0,) * len(shape))
    coming = lambda s: jnp.clip((s + EVERY - LEAD) // EVERY, 0, H - 1)
    running = lambda s: jnp.clip((s + 1 - LEAD) // EVERY, 0, H - 1)
    leaving = lambda s: jnp.clip((s - LEAD) // EVERY, 0, H - 1)
    by_head = lambda shape: pl.BlockSpec(shape, lambda s: (coming(s),) + (0,) * (len(shape) - 1))
    across = lambda shape, at: pl.BlockSpec(shape, lambda s: (0, at(s)))
    sem = pltpu.SemaphoreType.DMA
    up, down, out, gate = (blocks.index(kind) for kind in range(4))
    return blocks, pl.pallas_call(
        functools.partial(reduce_kernel, blocks=blocks),
        grid=(blocks.count + 7,),
        in_specs=[
            whole((tokens, width)),
            whole((tokens, width)),
            whole((tokens, width)),
            whole((rows, width)),
            across((tokens, BLOCK), down),
            pl.BlockSpec((tokens, blocks.tail), lambda s: (0, blocks.downs * BLOCK // blocks.tail)),
            pl.BlockSpec((2, tokens, BLOCK // 2), lambda s: (0, 0, up(s))),
            across((tokens, BLOCK), out),
            across((tokens, BLOCK), gate),
            whole((H, DK, DV)),
            across((rows, HC), coming),
            across((8, HC), coming),
            whole((rows, LANES)),
            whole((8, LANES)),
            whole((tokens, LANES)),
            whole((rows, LANES)),
            whole((8, tokens)),
            across((tokens, DV), coming),
            by_head((1, DK, DV)),
            pl.BlockSpec((SPOTS, 1, DK, DK), lambda s: (0, coming(s), 0, DV // DK)),
            by_head((1, chunks, CHUNK, CHUNK)),
            by_head((1, tokens, DV + DK)),
            by_head((1, chunks, DK, DV)),
            by_head((1, chunks, DK, DK)),
            by_head((1, chunks, DK, DK)),
            by_head((1, chunks, CHUNK, DK)),
        ],
        out_specs=[
            pl.BlockSpec(memory_space=pl.ANY),
            across((tokens, HC), leaving),
            whole((tokens, LANES)),
            across((8, HC), running),
            whole((8, LANES)),
        ],
        out_shape=[
            jax.ShapeDtypeStruct((SPOTS * piece, blocks.count * BLOCK), BF16),
            jax.ShapeDtypeStruct((tokens, H * HC), BF16),
            jax.ShapeDtypeStruct((tokens, LANES), F32),
            jax.ShapeDtypeStruct((8, H * HC), F32),
            jax.ShapeDtypeStruct((8, LANES), F32),
        ],
        scratch_shapes=[
            pltpu.VMEM((tokens, LANES), F32),
            pltpu.VMEM((tokens, LANES), F32),
            pltpu.VMEM((tokens, LANES), F32),
            pltpu.VMEM((rows, HC), F32),
            pltpu.VMEM((tokens, HC), F32),
            pltpu.VMEM((rows + 8, HC), F32),
            pltpu.VMEM((4, width, tokens), BF16),
            pltpu.VMEM((rows, HC), BF16),
            pltpu.VMEM((H, HALO, HC), BF16),
            pltpu.VMEM((SPOTS - 1, H, DK, DV), BF16),
            pltpu.VMEM((2, SPOTS, quarter, BLOCK), F32),
            pltpu.VMEM((2, SPOTS, quarter, BLOCK), BF16),
            pltpu.VMEM((2, SPOTS, quarter, BLOCK), BF16),
            pltpu.VMEM((4, 2, quarter, BLOCK), F32),
            pltpu.VMEM((4, 2, quarter, BLOCK), BF16),
            pltpu.VMEM((4, 2, quarter, BLOCK), BF16),
            pltpu.VMEM((4, quarter, BLOCK), F32),
            pltpu.VMEM((4, quarter, BLOCK), BF16),
            pltpu.VMEM((4, quarter, BLOCK), BF16),
            pltpu.VMEM((4, piece, BLOCK), F32),
            pltpu.VMEM((4, PLANES - 1, piece, BLOCK), BF16),
            pltpu.VMEM((4, PLANES - 1, piece, BLOCK), BF16),
            pltpu.VMEM((4, piece, BLOCK), BF16),
            sem((2,)), sem((2,)), sem((4,)), sem((4,)), sem((4,)), sem((4,)),
            sem((4, PLANES - 1)), sem((4, PLANES - 1)),
            sem((4, SPOTS - 1)), sem((blocks.count, SPOTS - 1)), sem((4,)),
            sem((H,)), sem((H,)), sem((SPOTS - 1,)), sem((SPOTS - 1,)),
        ],
        compiler_params=params(collective_id=1, has_side_effects=True),
        cost_estimate=cost(1e11, 1e8),
        name="reduce_gradients",
    )(
        d_out, hidden_mid, d_mixer, hidden, act, act, d_gu, gated, d_gpre, local_grad,
        proj, taps, logits, par, cols, back, segr, d_attn, state_in, exch, *saved,
    )


def unpack_gradients(blocks, sums):
    sums = sums.astype(F32)
    part = lambda n, low, high: sums[:, n * BLOCK + low : n * BLOCK + high]
    join = lambda at, low=0, high=BLOCK: jnp.concatenate([part(n, low, high) for n in at], axis=1)
    last = blocks.count - 1
    heads = [from_heads(part(n, 0, BLOCK), 1) for n in blocks.head_at]
    query, key, value = (jnp.concatenate(parts, axis=1) for parts in zip(*heads))
    down = jnp.concatenate([join(blocks.down_at), part(last, 0, blocks.tail)], axis=1)
    logits = part(last, blocks.tail, blocks.tail + 2 * H)
    return (
        query, key, value, join(blocks.gate_at), logits, join(blocks.out_at),
        join(blocks.up_at, 0, BLOCK // 2), join(blocks.up_at, BLOCK // 2, BLOCK), down,
    )


def input_grad_kernel(
    dp_ref, dg_ref, dl_ref, w_ref, wl_ref, x_ref, gain_ref, dy_ref, turn_ref, out_ref, dgain_ref, acc_ref
):
    step = pl.program_id(0)

    @pl.when(step == 0)
    def _():
        acc_ref[...] = mm(dl_ref[...], wl_ref[...], NT)

    @pl.when(step < H)
    def _():
        acc_ref[...] += mm(dp_ref[...], w_ref[...], NT)

    @pl.when(step >= H)
    def _():
        acc_ref[...] += mm(dg_ref[...], w_ref[...], NT)

    @pl.when(step == pl.num_programs(0) - 1)
    def _():
        value = x_ref[...].astype(F32)
        size = lax.rsqrt(jnp.mean(value * value, axis=-1, keepdims=True) + 1e-06)
        unit = value * size
        d_hidden = acc_ref[...]
        dgain_ref[...] = jnp.zeros_like(dgain_ref)
        dgain_ref[0:1, :] = jnp.sum(d_hidden * unit, axis=0, keepdims=True)
        d_unit = d_hidden * gain_ref[...]
        total = dy_ref[...] + size * (
            d_unit - unit * jnp.mean(d_unit * unit, axis=-1, keepdims=True)
        )
        high, low = halves(total)
        out_ref[...] = mm(high, turn_ref[...], NT) + mm(low, turn_ref[...], NT)


def input_grad(d_proj, d_gpre, d_logit, weights, x, gain, d_y, turn):
    tokens, width = x.shape
    block = HC
    second = d_gpre.shape[1] // block
    steps = H + second
    whole = lambda shape: pl.BlockSpec(shape, lambda j: (0,) * len(shape))
    late = lambda j: (0, jnp.maximum(j - H, 0))
    weight = lambda j: (0, jnp.where(j < H, H - 1 - j, j - H + AT_GATE // block))
    in_specs = [
        pl.BlockSpec((tokens, block), lambda j: (0, jnp.minimum(j, H - 1))),
        pl.BlockSpec((tokens, block), late),
        whole((tokens, LANES)),
        pl.BlockSpec((width, block), weight),
        pl.BlockSpec((width, LANES), lambda j: (0, AT_LOGIT // LANES)),
        whole((tokens, width)),
        whole((1, width)),
        whole((tokens, width)),
        whole((width, width)),
    ]
    return pl.pallas_call(
        input_grad_kernel,
        grid=(steps,),
        in_specs=in_specs,
        out_specs=[whole((tokens, width)), whole((8, width))],
        out_shape=[
            jax.ShapeDtypeStruct((tokens, width), F32),
            jax.ShapeDtypeStruct((8, width), F32),
        ],
        scratch_shapes=[pltpu.VMEM((tokens, width), F32)],
        compiler_params=params(),
        cost_estimate=cost(2 * tokens * width * steps * block, 3e7),
        name="input_grad",
    )(d_proj, d_gpre, d_logit, weights, weights, x, gain, d_y, turn)


def shifted(block, axis, distance):
    devices = range(lax.axis_size(axis))
    route = [(i - distance, i) for i in devices if i - distance in devices]
    return lax.ppermute(block, axis, route)


def send(value, planes=0, core=0, spot=0):
    route = []
    for z in range(PLANES):
        for c in range(CORES):
            for s in range(SPOTS):
                target = (((z + planes) % PLANES) * CORES + (c ^ core)) * SPOTS + (s ^ spot)
                route.append(((z * CORES + c) * SPOTS + s, target))
    return lax.ppermute(value, ("dp", "seq"), route)


def flipped(stack, spot):
    pairs = stack.reshape((2, 2) + stack.shape[1:])
    pairs = jnp.where(spot % 2 == 1, pairs[:, ::-1], pairs)
    pairs = jnp.where(spot // 2 == 1, pairs[::-1], pairs)
    return pairs.reshape(stack.shape)


class Torus:
    def __init__(self, spot, width):
        self.spot = spot
        place = lax.axis_index("dp")
        z, c = place // CORES, place % CORES
        piece = width // (PLANES * CORES * SPOTS)
        at = jnp.arange(width)
        core, rest = at // (width // 2), at % (width // 2)
        quarter, plane, low = rest // (PLANES * piece), rest // piece % PLANES, rest % piece
        self.order = (
            ((z - plane) % PLANES * CORES + (c ^ core)) * SPOTS + (spot ^ quarter)
        ) * piece + low
        self.turn = (jnp.arange(width)[:, None] == self.order[None, :]).astype(BF16)
        self.slots = jnp.arange(SPOTS, dtype=jnp.int32) ^ spot

    def mine(self, value):
        return lax.dot(value, self.turn, preferred_element_type=BF16)

    def natural(self, value):
        return lax.dot_general(value, self.turn, (NT, ((), ())), preferred_element_type=BF16)

    def vector(self, value):
        return jnp.take(value, self.order)

    def vector_back(self, value):
        return jnp.dot(value[None], self.turn.T.astype(F32), precision=lax.Precision.HIGHEST)[0]

    def share(self, shard):
        rows, cols = shard.shape
        return flipped(shard.reshape(SPOTS, rows // SPOTS, cols), self.spot).reshape(rows, cols)

    def total(self, value):
        value = value + send(value, core=1)
        value = value + send(value, spot=1)
        value = value + send(value, spot=2)
        return value + (send(value, planes=1) + send(value, planes=2) + send(value, planes=3))


class Plain:
    def __init__(self, spot, width):
        self.turn = jnp.eye(width, dtype=BF16)
        self.slots = jnp.arange(lax.axis_size("seq"), dtype=jnp.int32)

    def mine(self, value):
        return value

    natural = vector = vector_back = mine

    def share(self, shard):
        return lax.all_gather(shard, "dp", axis=0, tiled=True)

    def reduce(self, left, right, skip_left=0):
        full = outer(left, right, skip_left)
        part = lax.psum_scatter(full, "dp", scatter_dimension=0, tiled=True)
        return lax.psum(part, "seq").astype(F32)

    def along(self, value):
        return lax.all_gather(value, "seq")

    def total(self, value):
        return lax.psum(value, ("dp", "seq"))


def by_heads(query, key, value):
    lead = query.shape[:-1]
    parts = [query.reshape(lead + (H, DK)), key.reshape(lead + (H, DK)), value.reshape(lead + (H, DV))]
    return jnp.concatenate(parts, axis=-1).reshape(lead + (H * HC,))


def from_heads(value, heads=H):
    lead = value.shape[:-1]
    parts = value.reshape(lead + (heads, HC))
    return (
        parts[..., :DK].reshape(lead + (heads * DK,)),
        parts[..., DK : 2 * DK].reshape(lead + (heads * DK,)),
        parts[..., 2 * DK :].reshape(lead + (heads * DV,)),
    )


def token_tables(segments, place, tokens):
    seg_pad = jnp.concatenate([jnp.full((HALO,), -1, jnp.int32), segments, jnp.full((8,), -2, jnp.int32)])
    ext = lax.dynamic_slice_in_dim(seg_pad, place * tokens, tokens + HALO + 8)
    seg = ext[HALO : HALO + tokens]
    columns = [seg.astype(F32)]
    for j in range(1, CONV):
        columns.append((ext[HALO - j : HALO - j + tokens] == seg).astype(F32))
    blocks = seg.reshape(-1, CHUNK)
    before = ext[HALO - 1 : HALO - 1 + tokens : CHUNK]
    columns.append((blocks == before[:, None]).astype(F32).reshape(-1))
    columns.append((blocks == blocks[:, -1:]).astype(F32).reshape(-1))
    columns += [jnp.zeros_like(columns[0])] * (LANES - len(columns))
    cols = jnp.stack(columns, axis=1)
    rows = tokens + HALO
    back = [jnp.zeros((rows,), F32)]
    for j in range(1, CONV):
        back.append((ext[j : j + rows] == ext[:rows]).astype(F32))
    back += [jnp.zeros((rows,), F32)] * (LANES - len(back))
    segr = jnp.broadcast_to(seg.astype(F32)[None], (8, tokens))
    return cols, jnp.stack(back, axis=1), segr


def wide(value):
    return jnp.pad(value, ((0, 0), (0, LANES - value.shape[1])))


def local(
    inputs, segments, cotangent, norm_gain_mix, w_query, w_key, w_value, w_outgate, w_gates,
    conv_weight, decay_log, dt_bias, out_norm_gain, w_out, norm_gain_ffn, w_ffn_gate, w_ffn_up, w_ffn_down,
):
    tokens, width = inputs.shape[1:]
    place = lax.axis_index("seq")
    place_arr = place.reshape((1,)).astype(jnp.int32)
    planned = (lax.axis_size("dp"), lax.axis_size("seq")) == (PLANES * CORES, SPOTS)
    comm = (Torus if planned else Plain)(place, width)
    slots = comm.slots
    low = lambda a: a.astype(BF16)

    qkv = by_heads(low(w_query), low(w_key), low(w_value))
    qkv = jnp.concatenate([qkv[:, h * HC : (h + 1) * HC] for h in reversed(range(H))], axis=1)
    shard = jnp.concatenate(
        [
            qkv, jnp.pad(low(w_gates), ((0, 0), (0, AT_GATE - AT_LOGIT - 2 * H))), low(w_outgate), low(w_out).T,
            low(w_ffn_gate), low(w_ffn_up), low(w_ffn_down).T,
        ],
        axis=1,
    )
    inner = w_ffn_gate.shape[1]
    weights = comm.share(shard)

    gain_mix, gain_ffn = comm.vector(norm_gain_mix)[None], comm.vector(norm_gain_ffn)[None]
    gain_out = out_norm_gain[None]
    taps_parts = by_heads(conv_weight[:, : H * DK], conv_weight[:, H * DK : 2 * H * DK], conv_weight[:, 2 * H * DK :])
    taps = jnp.pad(taps_parts, ((0, 8 - CONV), (0, 0)))
    par = jnp.pad(jnp.stack([decay_log, dt_bias]), ((0, 6), (0, LANES - H)))
    cols, back, segr = token_tables(segments[0], place, tokens)

    halo = shifted(inputs[0, tokens - HALO :], "seq", 1)
    x_ext = comm.mine(jnp.concatenate([halo, inputs[0]], axis=0))
    x = x_ext[HALO:]
    d_out = comm.mine(cotangent[0])
    value = x_ext.astype(F32)
    size = lax.rsqrt(jnp.mean(value * value, axis=-1, keepdims=True) + 1e-06)
    hidden = low(value * size * gain_mix)

    outs = delta_forward(hidden, weights, taps, par, cols, segr, planned, inner)
    if planned:
        weights, outs = outs[0], outs[1:]
    proj, logits, part, resp, exch, *saved = outs
    if not planned:
        exch = comm.along(exch[0])
    gpre = outgate(hidden, weights)
    state_in, attn, gated, y1, hidden_mid = mixer_out(
        place_arr, slots, part, resp, exch, gpre, gain_out, weights, x, gain_ffn
    )
    result, act, d_gu, d_y, d_mixer, d_gain_ffn = feed_forward(
        hidden_mid, d_out, y1, gain_ffn, weights, inner
    )
    d_attn, d_gpre, local_grad, d_gain_out = mixer_back(d_mixer, weights, attn, gpre, gain_out, resp)
    if planned:
        blocks, outs = reduce_gradients(
            d_out, hidden_mid, d_mixer, hidden, act, d_gu, gated, d_gpre, local_grad,
            proj, taps, logits, par, cols, back, segr, d_attn, state_in, exch, saved,
        )
        sums, d_proj, d_logits, d_taps, d_par = outs
        d_logit = low(d_logits)
        g_query, g_key, g_value, g_og, g_gates, g_out, g_gate, g_up, g_down = unpack_gradients(blocks, sums)
    else:
        grads = comm.along(local_grad)
        d_proj, d_logits, d_taps, d_par = delta_backward(
            place_arr, slots, proj, taps, logits, par, cols, back, segr, d_attn, state_in, exch, grads, saved
        )
        sent_back = shifted(d_proj[:HALO], "seq", -1)
        d_proj = d_proj.at[tokens:].add(sent_back)[HALO:]
        d_logit = low(d_logits)
        g_down = comm.reduce(d_out, act)
        g_gate = comm.reduce(hidden_mid, d_gu[0])
        g_up = comm.reduce(hidden_mid, d_gu[1])
        g_out = comm.reduce(d_mixer, gated)
        g_og = comm.reduce(hidden, d_gpre, HALO)
        g_query, g_key, g_value = from_heads(comm.reduce(hidden, d_proj, HALO))
        g_gates = comm.reduce(hidden, d_logit, HALO)[:, : 2 * H]
    d_inputs, d_gain_mix = input_grad(
        d_proj, d_gpre, d_logit, weights, x, gain_mix, d_y, comm.turn
    )

    d_conv = jnp.concatenate(from_heads(d_taps[:CONV]), axis=1)
    pieces = [
        comm.vector_back(d_gain_mix[0]), d_conv.reshape(-1), d_par[0, :H], d_par[1, :H],
        d_gain_out[0], comm.vector_back(d_gain_ffn[0]),
    ]
    flat = jnp.concatenate(pieces)
    flat = comm.total(jnp.pad(flat, (0, -flat.shape[0] % 1024)).reshape(-1, LANES)).reshape(-1)
    small, at = [], 0
    for one in pieces:
        small.append(flat[at : at + one.shape[0]])
        at += one.shape[0]
    return (
        comm.natural(result)[None], d_inputs[None], small[0], g_query, g_key, g_value, g_og,
        g_gates, small[1].reshape(d_conv.shape), small[2], small[3], small[4], g_out.T,
        small[5], g_gate, g_up, g_down.T,
    )


def solution(mesh):
    rows, cols, copied = P("dp", None), P(None, "dp"), P()
    tokens = P("dp", "seq", None)
    in_specs = (
        tokens, rows, tokens, copied, rows, rows, rows, rows, rows,
        copied, copied, copied, copied, cols, copied, rows, rows, cols,
    )
    out_specs = (
        tokens, tokens, copied, rows, rows, rows, rows, rows,
        copied, copied, copied, copied, cols, copied, rows, rows, cols,
    )
    return jax.shard_map(local, mesh=mesh, in_specs=in_specs, out_specs=out_specs, check_vma=False)
```

```python
import functools

import jax
import jax.numpy as jnp
from jax import lax
from jax.experimental import pallas as pl
from jax.experimental.pallas import tpu as pltpu
from jax.sharding import PartitionSpec as P

H = 8
DK = 128
DV = 256
CONV = 4
HALO = 16
CHUNK = 128
HC = 2 * DK + DV
LANES = 128
PLANES, CORES, SPOTS = 4, 2, 4

AT_LOGIT = H * HC
AT_GATE = AT_LOGIT + 512
AT_OUT = AT_GATE + H * DV
AT_FFN = AT_OUT + H * DV
VMEM_LIMIT = 56 * 2**20

F32 = jnp.float32
BF16 = jnp.bfloat16
NN = ((1,), (0,))
NT = ((1,), (1,))
TN = ((0,), (0,))


def mm(left, right, dims=NN):
    return lax.dot_general(
        left.astype(BF16), right.astype(BF16), (dims, ((), ())), preferred_element_type=F32
    )


def mm_exact(left, right, dims=NN):
    return lax.dot_general(
        left, right, (dims, ((), ())), precision=lax.Precision.HIGHEST, preferred_element_type=F32
    )


def halves(value):
    high = value.astype(BF16)
    return high, (value - high.astype(F32)).astype(BF16)


def mm_three(left, right):
    left_high, left_low = halves(left)
    right_high, right_low = halves(right)
    return mm(left_high, right_high) + (mm(left_high, right_low) + mm(left_low, right_high))


def params(**more):
    return pltpu.CompilerParams(vmem_limit_bytes=VMEM_LIMIT, **more)


def cost(flops, nbytes):
    return pl.CostEstimate(flops=int(flops), bytes_accessed=int(nbytes), transcendentals=0)


def iota2(shape, axis):
    return lax.broadcasted_iota(jnp.int32, shape, axis)


def lane(value, index):
    picked = jnp.where(iota2(value.shape, 1) == index, value, 0.0)
    return jnp.sum(picked, axis=1, keepdims=True)


def to_row(column):
    size = column.shape[0]
    same = iota2((size, size), 0) == iota2((size, size), 1)
    return jnp.sum(jnp.where(same, column, 0.0), axis=0, keepdims=True)


def to_column(row):
    size = row.shape[1]
    same = iota2((size, size), 0) == iota2((size, size), 1)
    return jnp.sum(jnp.where(same, row, 0.0), axis=1, keepdims=True)


def outgate_kernel(h_ref, w_ref, g_ref):
    g_ref[...] = mm(h_ref[HALO:, :], w_ref[...])


def outgate(hidden, weights):
    rows, width = hidden.shape
    cols = H * DV
    block = 512
    return pl.pallas_call(
        outgate_kernel,
        grid=(cols // block,),
        in_specs=[
            pl.BlockSpec((rows, width), lambda j: (0, 0)),
            pl.BlockSpec((width, block), lambda j: (0, j + AT_GATE // block)),
        ],
        out_specs=pl.BlockSpec((rows - HALO, block), lambda j: (0, j)),
        out_shape=jax.ShapeDtypeStruct((rows - HALO, cols), F32),
        compiler_params=params(),
        cost_estimate=cost(2 * rows * width * cols, 2 * width * cols + 4 * rows * cols),
        name="outgate",
    )(hidden, weights)


def outer_kernel(left_ref, right_ref, out_ref, turn_ref, *, skip):
    @pl.when(pl.program_id(0) == 0)
    def _():
        turn_ref[...] = jnp.transpose(left_ref[skip:, :])

    out_ref[...] = mm(turn_ref[...], right_ref[...]).astype(BF16)


def outer(left, right, skip):
    rows, width = left.shape
    cols = right.shape[1]
    block = next(b for b in (512, 256, 128) if cols % b == 0)
    return pl.pallas_call(
        functools.partial(outer_kernel, skip=skip),
        grid=(cols // block,),
        in_specs=[
            pl.BlockSpec((rows, width), lambda j: (0, 0)),
            pl.BlockSpec((rows - skip, block), lambda j: (0, j)),
        ],
        out_specs=pl.BlockSpec((width, block), lambda j: (0, j)),
        out_shape=jax.ShapeDtypeStruct((width, cols), BF16),
        scratch_shapes=[pltpu.VMEM((width, rows - skip), BF16)],
        compiler_params=params(),
        cost_estimate=cost(2 * rows * width * cols, 2 * width * cols + 2 * rows * cols),
        name="outer",
    )(left, right)


def gate_tables(logit_ref, par_ref, beta_ref, decay_ref, cum_ref):
    logits = logit_ref[HALO:, :]
    beta_ref[...] = jax.nn.sigmoid(logits)
    shifted = logits + par_ref[1:2, :]
    soft = jnp.maximum(shifted, 0.0) + jnp.log1p(jnp.exp(-jnp.abs(shifted)))
    decay_ref[...] = -jnp.exp(par_ref[0:1, :]) * soft
    lower = (iota2((CHUNK, CHUNK), 0) >= iota2((CHUNK, CHUNK), 1)).astype(F32)
    for c in range(logits.shape[0] // CHUNK):
        part = decay_ref[c * CHUNK : (c + 1) * CHUNK, :]
        cum_ref[c * CHUNK : (c + 1) * CHUNK, :] = mm_exact(lower, part)


def mix_taps(p_ref, taps_ref, cols, pf_ref):
    tokens = cols.shape[0]
    pf_ref[...] = p_ref[...].astype(F32)
    total = pf_ref[HALO:, :] * taps_ref[0:1, :]
    for j in range(1, CONV):
        total += pf_ref[HALO - j : HALO - j + tokens, :] * taps_ref[j : j + 1, :] * cols[:, j : j + 1]
    return total


def chunk_tables(c, head, cols, segr_ref, cum_ref):
    rows = slice(c * CHUNK, (c + 1) * CHUNK)
    cum = lane(cum_ref[rows, :], head)
    cum_row = to_row(cum)
    same = cols[rows, 0:1] == segr_ref[0:1, rows]
    row_ids, col_ids = iota2((CHUNK, CHUNK), 0), iota2((CHUNK, CHUNK), 1)
    gamma = jnp.where((row_ids >= col_ids) & same, jnp.exp(jnp.minimum(cum - cum_row, 0.0)), 0.0)
    strict = jnp.where(row_ids > col_ids, gamma, 0.0)
    carry = jnp.exp(cum) * cols[rows, 4:5]
    last = jnp.exp(cum[CHUNK - 1 :, :] - cum) * cols[rows, 5:6]
    return gamma, strict, carry, last


def unit_lower_inverses(systems):
    size = systems[0].shape[0]
    row_ids, col_ids = iota2((size, size), 0), iota2((size, size), 1)
    eye = (row_ids == col_ids).astype(F32)
    found = [eye - jnp.where(row_ids // 2 == col_ids // 2, low, 0.0) for low in systems]
    width = 2
    while width < size:
        joined = (row_ids // (2 * width) == col_ids // (2 * width)) & (
            row_ids // width != col_ids // width
        )
        first = [mm_three(jnp.where(joined, low, 0.0), inv) for low, inv in zip(systems, found)]
        found = [inv - mm_three(inv, part) for inv, part in zip(found, first)]
        width *= 2
    return found


def flip_spot(value, bits):
    low, high = lax.rem(value, 2), value // 2
    flip = lambda one, other: one + other - 2 * one * other
    return flip(low, bits % 2) + 2 * flip(high, bits // 2)


def device(planes=0, core=0, spot=0):
    place, here = lax.axis_index("dp"), lax.axis_index("seq")
    z = lax.rem(place // CORES + planes, PLANES)
    return {"dp": z * CORES + flip_spot(lax.rem(place, CORES), core), "seq": flip_spot(here, spot)}


def greet(partners):
    barrier = pltpu.get_barrier_semaphore()
    for partner in partners:
        pl.semaphore_signal(barrier, inc=1, device_id=device(**partner), device_id_type=pl.DeviceIdType.MESH)
    pl.semaphore_wait(barrier, len(partners))


def gather_spans(inner):
    spans = [((H - 1) * HC, HC + LANES), ((H - 2) * HC, HC)]
    spans += [(h * HC, 2 * HC) for h in (4, 2, 0)]
    for at, size in ((AT_GATE, H * DV), (AT_OUT, H * DV)) + tuple((AT_FFN + i * inner, inner) for i in range(3)):
        spans += [(at + low, min(1024, size - low)) for low in range(0, size, 1024)]
    return spans


class Gathering:
    STAGES = (0, 1, 2, 3, 5, 7, 8)
    FIRST = ((0, 1, 2, 3, 4, 5, 6), (0, 1, 2, 3, 4, 6, 7))

    def __init__(self, spans, shard_ref, full_ref, sems, pack):
        self.spans, self.shard, self.full, self.pack = spans, shard_ref, full_ref, pack
        self.send_sem, self.recv_sem, self.local_sem = sems
        self.piece = shard_ref.shape[0] // SPOTS
        self.half = full_ref.shape[0] // CORES
        self.z = lax.axis_index("dp") // CORES

    def quarter(self, spot, cols):
        row = flip_spot(lax.axis_index("seq"), spot) * self.piece
        return self.shard.at[pl.ds(pl.multiple_of(row, self.piece), self.piece), cols]

    def own(self, group):
        at, size = self.spans[group]
        cols = pl.ds(at, size)
        block = PLANES * self.piece
        return [
            pltpu.make_async_copy(
                self.quarter(q, cols),
                self.full.at[q * block : q * block + self.piece, cols],
                self.local_sem.at[group, q],
            )
            for q in range(SPOTS)
        ]

    def copy(self, group, kind):
        at, size = self.spans[group]
        cols = pl.ds(at, size)
        piece, full = self.piece, self.full
        block = PLANES * piece
        rows = lambda quarter: pl.ds(quarter * block + piece, block - piece)
        if kind < 6:
            read, step, written = ((0, 1, 1), (0, -1, 3), (1, 1, 2), (3, -1, 2), (2, 1, 3), (2, -1, 1))[kind]
            source = self.quarter(0, cols) if read == 0 else full.at[read * piece : (read + 1) * piece, cols]
            target = full.at[written * piece : (written + 1) * piece, cols]
            to, arrival = device(planes=step % PLANES), written - 1
        elif kind < 8:
            source = full.at[rows(0), cols]
            target = full.at[rows(kind - 5), cols]
            to, arrival = device(spot=kind - 5), kind - 3
        elif kind == 8:
            by = 1 + group % 2
            source = full.at[rows(by), cols]
            target = full.at[rows(3), cols]
            to, arrival = device(spot=3 - by), 5
        else:
            source = full.at[0 : self.half, cols]
            target = full.at[self.half : 2 * self.half, cols]
            to, arrival = device(core=1), 6
        return pltpu.make_async_remote_copy(
            src_ref=source,
            dst_ref=target,
            send_sem=self.send_sem.at[group, kind],
            recv_sem=self.recv_sem.at[group, arrival],
            device_id=to,
            device_id_type=pl.DeviceIdType.MESH,
        )

    def sends(self, kind):
        z = self.z
        return (z < 3, z > 0, (z > 0) & (z < 3), (z > 0) & (z < 3), z == 2, z == 1)[kind]

    def start(self, group, kind):
        @pl.when(self.sends(kind))
        def _():
            self.copy(group, kind).start()

    def arrive(self, group, kind, condition):
        @pl.when(condition)
        def _():
            self.copy(group, kind).wait_recv()

    def tick(self, at):
        z = self.z
        due = []
        for group in range(len(self.spans)):
            stages = (self.FIRST + (self.STAGES,) * len(self.spans))[group]
            due += [(stage, group) for stage in range(len(stages)) if group + stages[stage] == at]
        for stage, group in sorted(due, reverse=True):
            by = 1 + group % 2
            if stage == 0:
                self.pack(*self.spans[group])
                self.start(group, 0)
                self.start(group, 1)
                for local in self.own(group):
                    local.start()
            elif stage == 1:
                self.arrive(group, 0, z > 0)
                self.start(group, 2)
                self.arrive(group, 1, z < 3)
                self.start(group, 3)
            elif stage == 2:
                self.copy(group, 2).wait_recv()
                self.start(group, 4)
                self.start(group, 5)
            elif stage == 3:
                self.arrive(group, 0, z == 0)
                self.arrive(group, 1, z == 3)
                self.copy(group, 5 + by).start()
                self.copy(group, 8 - by).start()
            elif stage == 4:
                self.copy(group, 5 + by).wait_recv()
                self.copy(group, 8).start()
            elif stage == 5:
                self.copy(group, 8 - by).wait_recv()
                self.copy(group, 8).wait_recv()
                for local in self.own(group):
                    local.wait()
                self.copy(group, 9).start()
            else:
                self.copy(group, 9).wait_recv()

    def finish(self):
        for group in range(len(self.spans)):
            for kind in range(6):

                @pl.when(self.sends(kind))
                def _(group=group, kind=kind):
                    self.copy(group, kind).wait_send()

            for kind in range(6, 10):
                self.copy(group, kind).wait_send()


def forward_kernel(
    h_ref, full_ref, taps_ref, par_ref, cols_ref, segr_ref,
    p_ref, logit_ref, part_ref, resp_ref, exch_ref, inv_ref, upd_ref, st_ref, stm_ref, amap_ref, rmap_ref,
    beta_ref, decay_ref, cum_ref, pf_ref, mix_ref, w_ref, wl_ref, load_sem,
):
    head = pl.program_id(0)
    load_head(head, h_ref, full_ref, par_ref, p_ref, logit_ref, beta_ref, decay_ref, cum_ref, w_ref, wl_ref, load_sem)
    state = forward_head(
        head, p_ref, taps_ref, cols_ref, segr_ref, part_ref, resp_ref, inv_ref, upd_ref, st_ref, stm_ref,
        amap_ref, rmap_ref, beta_ref, cum_ref, pf_ref, mix_ref, lambda: None,
    )
    exch_ref[0, 0] = state.astype(BF16)


def load_head(
    head, h_ref, full_ref, par_ref, p_ref, logit_ref, beta_ref, decay_ref, cum_ref, w_ref, wl_ref, load_sem
):
    def load(slot, at, size, to):
        return pltpu.make_async_copy(full_ref.at[:, pl.ds(at, size)], to, load_sem.at[slot])

    mine = load(0, pl.multiple_of((H - 1 - head) * HC, HC), HC, w_ref)
    mine.start()

    @pl.when(head == 0)
    def _():
        gates = load(1, AT_LOGIT, LANES, wl_ref)
        gates.start()
        gates.wait()
        logit_ref[...] = mm(h_ref[...], wl_ref[...])
        gate_tables(logit_ref, par_ref, beta_ref, decay_ref, cum_ref)

    mine.wait()
    p_ref[...] = mm(h_ref[...], w_ref[...]).astype(BF16)


def forward_head(
    head, p_ref, taps_ref, cols_ref, segr_ref, part_ref, resp_ref, inv_ref, upd_ref, st_ref, stm_ref,
    amap_ref, rmap_ref, beta_ref, cum_ref, pf_ref, mix_ref, between,
):
    cols = cols_ref[...]
    tokens = cols.shape[0]
    total = mix_taps(p_ref, taps_ref, cols, pf_ref)
    mix_ref[...] = total * jax.nn.sigmoid(total)
    between()
    beta = lane(beta_ref[...], head + H)
    chunks = range(tokens // CHUNK)
    tables, lows, keys, queries = [], [], [], []
    for c in chunks:
        rows = slice(c * CHUNK, (c + 1) * CHUNK)
        query = mix_ref[rows, :DK]
        query = query * (lax.rsqrt(jnp.sum(query * query, axis=1, keepdims=True) + 1e-06) * DK**-0.5)
        key = mix_ref[rows, DK : 2 * DK]
        key = key * lax.rsqrt(jnp.sum(key * key, axis=1, keepdims=True) + 1e-06)
        gamma, strict, carry, last = chunk_tables(c, head, cols, segr_ref, cum_ref)
        dots = mm(jnp.concatenate([key, query], axis=0), key, NT)
        lows.append(beta[rows] * strict * dots[:CHUNK])
        tables.append((gamma * dots[CHUNK:], carry, last))
        keys.append(key)
        queries.append(query)
    inverses = unit_lower_inverses(lows)
    state = None
    for c in chunks:
        rows = slice(c * CHUNK, (c + 1) * CHUNK)
        scores, carry, last = tables[c]
        key, query = keys[c], queries[c]
        target = jnp.concatenate([mix_ref[rows, 2 * DK :], carry * key], axis=1) * beta[rows]
        updates = mm(inverses[c], target)
        inv_ref[0, c] = inverses[c].astype(BF16)
        upd_ref[0, rows, :] = updates
        weighted_t = jnp.transpose(last * key)
        both = mm(jnp.concatenate([weighted_t, scores], axis=0), updates)
        eye = (iota2((DK, DK), 0) == iota2((DK, DK), 1)).astype(F32)
        step_map = carry[CHUNK - 1 :, :] * eye - both[:DK, DV:]
        read_map = carry * query - both[DK:, DV:]
        amap_ref[0, c] = step_map.astype(BF16)
        rmap_ref[0, c] = read_map.astype(BF16)
        if c == 0:
            st_ref[0, c] = jnp.zeros((DK, DV), F32)
            stm_ref[0, c] = eye.astype(BF16)
            part_ref[rows, :] = both[DK:, :DV]
            resp_ref[rows, :] = read_map.astype(BF16)
            state = jnp.concatenate([both[:DK, :DV], step_map], axis=1)
        else:
            st_ref[0, c] = state[:, :DV]
            stm_ref[0, c] = state[:, DV:].astype(BF16)
            moved = mm(jnp.concatenate([step_map, read_map], axis=0), state)
            part_ref[rows, :] = both[DK:, :DV] + moved[DK:, :DV]
            resp_ref[rows, :] = moved[DK:, DV:].astype(BF16)
            state = moved[:DK] + jnp.concatenate(
                [both[:DK, :DV], jnp.zeros((DK, DK), F32)], axis=1
            )
    return state


def delta_forward(hidden, weights, taps, par, cols, segr):
    rows, width = hidden.shape
    tokens = rows - HALO
    chunks = tokens // CHUNK
    whole = lambda shape: pl.BlockSpec(shape, lambda h: (0,) * len(shape))
    by_head = lambda shape: pl.BlockSpec(shape, lambda h: (h,) + (0,) * (len(shape) - 1))
    return pl.pallas_call(
        forward_kernel,
        grid=(H,),
        in_specs=[
            whole((rows, width)),
            pl.BlockSpec(memory_space=pl.ANY),
            pl.BlockSpec((8, HC), lambda h: (0, h)),
            whole((8, LANES)),
            whole((tokens, LANES)),
            whole(segr.shape),
        ],
        out_specs=[
            pl.BlockSpec((rows, HC), lambda h: (0, h)),
            whole((rows, LANES)),
            pl.BlockSpec((tokens, DV), lambda h: (0, h)),
            pl.BlockSpec((tokens, DK), lambda h: (0, h)),
            pl.BlockSpec((1, 1, DK, DV + DK), lambda h: (0, h, 0, 0)),
            by_head((1, chunks, CHUNK, CHUNK)),
            by_head((1, tokens, DV + DK)),
            by_head((1, chunks, DK, DV)),
            by_head((1, chunks, DK, DK)),
            by_head((1, chunks, DK, DK)),
            by_head((1, chunks, CHUNK, DK)),
        ],
        out_shape=[
            jax.ShapeDtypeStruct((rows, H * HC), BF16),
            jax.ShapeDtypeStruct((rows, LANES), F32),
            jax.ShapeDtypeStruct((tokens, H * DV), F32),
            jax.ShapeDtypeStruct((tokens, H * DK), BF16),
            jax.ShapeDtypeStruct((1, H, DK, DV + DK), BF16),
        ]
        + saved_shapes(chunks),
        scratch_shapes=[
            pltpu.VMEM((tokens, LANES), F32),
            pltpu.VMEM((tokens, LANES), F32),
            pltpu.VMEM((tokens, LANES), F32),
            pltpu.VMEM((rows, HC), F32),
            pltpu.VMEM((tokens, HC), F32),
            pltpu.VMEM((width, HC), BF16),
            pltpu.VMEM((width, LANES), BF16),
            pltpu.SemaphoreType.DMA((2,)),
        ],
        compiler_params=params(),
        cost_estimate=cost(6e9 * H, 5e6 * H),
        name="delta_forward",
    )(hidden, weights, taps, par, cols, segr)


def saved_shapes(chunks):
    return [
        jax.ShapeDtypeStruct((H, chunks, CHUNK, CHUNK), BF16),
        jax.ShapeDtypeStruct((H, chunks * CHUNK, DV + DK), F32),
        jax.ShapeDtypeStruct((H, chunks, DK, DV), F32),
        jax.ShapeDtypeStruct((H, chunks, DK, DK), BF16),
        jax.ShapeDtypeStruct((H, chunks, DK, DK), BF16),
        jax.ShapeDtypeStruct((H, chunks, CHUNK, DK), BF16),
    ]


def mixer_forward_kernel(
    x_ref, cot_ref, wq_ref, wk_ref, wv_ref, wo_ref, wl_in, wm_ref, wg_ref, wu_ref, wd_ref,
    gains_ref, gain_ref, taps_ref, par_ref, near_ref, later_ref,
    full_ref, hidden_out, x_out, cot_out, turn_out, y_out, mid_out,
    gains_out, cols_ref, back_ref, p_ref, logit_ref, resp_out,
    inv_ref, upd_ref, st_ref, stm_ref, amap_ref, rmap_ref, maps_ref, sin_ref, attn_ref, gpre_ref, gated_ref,
    shard_ref, hidden_ref, xs_ref, cots_ref, turn_ref, y_ref, mid_ref, xh_ref, part_ref, resp_ref, exch_ref, stage_ref,
    beta_ref, decay_ref, cum_ref, pf_ref, mix_ref, w_ref, wl_ref, wb_ref,
    send_sem, recv_sem, local_sem, exch_send, exch_recv, load_sem, pair_sem, out_sem, halo_sem, *, spans, inner,
):
    step = pl.program_id(0)
    place = lax.axis_index("seq")
    tokens, width = x_ref.shape

    def pack(at, size):
        while size > 0:
            if at < AT_LOGIT:
                head, span = H - 1 - at // HC, HC
                shard_ref[:, at : at + DK] = wq_ref[:, head * DK : (head + 1) * DK].astype(BF16)
                shard_ref[:, at + DK : at + 2 * DK] = wk_ref[:, head * DK : (head + 1) * DK].astype(BF16)
                shard_ref[:, at + 2 * DK : at + HC] = wv_ref[:, head * DV : (head + 1) * DV].astype(BF16)
            elif at < AT_GATE:
                span = LANES
                shard_ref[:, at : at + LANES] = jnp.zeros((shard_ref.shape[0], LANES), BF16)
                shard_ref[:, at : at + 2 * H] = wl_in[...].astype(BF16)
            elif at < AT_OUT:
                span, low = size, at - AT_GATE
                shard_ref[:, at : at + span] = wo_ref[:, low : low + span].astype(BF16)
            elif at < AT_FFN:
                span, low = size, at - AT_OUT
                shard_ref[:, at : at + span] = jnp.transpose(wm_ref[low : low + span, :]).astype(BF16)
            else:
                span, which, low = size, (at - AT_FFN) // inner, (at - AT_FFN) % inner
                if which < 2:
                    shard_ref[:, at : at + span] = (wg_ref, wu_ref)[which][:, low : low + span].astype(BF16)
                else:
                    shard_ref[:, at : at + span] = jnp.transpose(wd_ref[low : low + span, :]).astype(BF16)
            at, size = at + span, size - span

    gathering = Gathering(spans, shard_ref, full_ref, (send_sem, recv_sem, local_sem), pack)
    lead = gathering.FIRST[0][-1] + 1
    final_tick = len(spans) + gathering.STAGES[-1]

    def give(h, spot):
        return pltpu.make_async_remote_copy(
            src_ref=stage_ref.at[h],
            dst_ref=exch_ref.at[spot - 1, h],
            send_sem=exch_send.at[spot - 1, h],
            recv_sem=exch_recv.at[spot - 1, h],
            device_id=device(spot=spot),
            device_id_type=pl.DeviceIdType.MESH,
        )

    def give_halo():
        return pltpu.make_async_remote_copy(
            src_ref=x_ref.at[tokens - HALO : tokens],
            dst_ref=xh_ref,
            send_sem=halo_sem.at[0],
            recv_sem=halo_sem.at[1],
            device_id={"dp": lax.axis_index("dp"), "seq": lax.rem(place + 1, SPOTS)},
            device_id_type=pl.DeviceIdType.MESH,
        )

    def keep(which):
        source, to = (
            (hidden_ref, hidden_out), (xs_ref, x_out), (cots_ref, cot_out), (turn_ref, turn_out),
            (y_ref, y_out), (mid_ref, mid_out),
        )[which]
        return pltpu.make_async_copy(source, to, out_sem.at[which])

    def load_pair(h):
        slot = lax.rem(h, 2)
        return [
            pltpu.make_async_copy(
                full_ref.at[:, pl.ds(pl.multiple_of(at + h * DV, DV), DV)], wb_ref.at[slot, i], pair_sem.at[slot, i]
            )
            for i, at in enumerate((AT_GATE, AT_OUT))
        ]

    @pl.when(step == 0)
    def _():
        greet([dict(planes=d) for d in (1, 2, 3)] + [dict(spot=s) for s in (1, 2, 3)] + [dict(core=1)])

        @pl.when(place < SPOTS - 1)
        def _():
            give_halo().start()

        gathering.tick(0)
        at = iota2((1, width), 1)
        piece = width // (PLANES * CORES * SPOTS)
        core, rest = at // (width // 2), at % (width // 2)
        quarter, plane, low = rest // (PLANES * piece), rest // piece % PLANES, rest % piece
        place_dp = lax.axis_index("dp")
        z, c = place_dp // CORES, lax.rem(place_dp, CORES)
        chip = ((z - plane + PLANES) % PLANES) * CORES + (c + core - 2 * c * core)
        order = (chip * SPOTS + flip_spot(quarter, place)) * piece + low
        turn_ref[...] = jnp.where(iota2((width, width), 0) == order, 1.0, 0.0).astype(BF16)
        keep(3).start()
        gathering.tick(1)
        cots_ref[...] = mm(cot_ref[...], turn_ref[...]).astype(BF16)
        keep(2).start()
        high, mid = halves(gains_ref[...])
        rest = (gains_ref[...] - high.astype(F32)) - mid.astype(F32)
        gains_out[...] = mm(high, turn_ref[...]) + mm(mid, turn_ref[...]) + mm(rest, turn_ref[...])
        gathering.tick(2)
        blank = jnp.zeros((LANES - near_ref.shape[0], LANES), F32)
        for n in range(tokens // LANES):
            span = slice(n * LANES, (n + 1) * LANES)
            cols_ref[span, :] = jnp.transpose(jnp.concatenate([near_ref[:, span], blank], axis=0))
        for n in range(tokens // LANES + 1):
            span = slice(n * LANES, (n + 1) * LANES)
            turned = jnp.transpose(jnp.concatenate([later_ref[:, span], blank], axis=0))
            kept = min(LANES, tokens + HALO - n * LANES)
            back_ref[n * LANES : n * LANES + kept, :] = turned[:kept]
        gathering.tick(3)

        @pl.when(place > 0)
        def _():
            give_halo().wait_recv()

        @pl.when(place == 0)
        def _():
            xh_ref[...] = jnp.zeros_like(xh_ref)

        value = mm(jnp.concatenate([xh_ref[...], x_ref[...]], axis=0), turn_ref[...])
        xs_ref[...] = value[HALO:].astype(BF16)
        keep(1).start()
        size = lax.rsqrt(jnp.mean(value * value, axis=-1, keepdims=True) + 1e-06)
        hidden_ref[...] = (value * size * gains_out[0:1, :]).astype(BF16)
        keep(0).start()
        for at in range(4, lead):
            gathering.tick(at)

    @pl.when(step < H)
    def _():
        head = step
        for h in range(1, H):

            @pl.when(head == h)
            def _(h=h):
                gathering.tick(lead + 2 * h - 1)

        load_head(
            head, hidden_ref, full_ref, par_ref, p_ref, logit_ref, beta_ref, decay_ref, cum_ref, w_ref, wl_ref, load_sem
        )

        def between():
            for h in range(H):

                @pl.when(head == h)
                def _(h=h):
                    gathering.tick(lead + 2 * h)

        state = forward_head(
            head, p_ref, taps_ref, cols_ref, near_ref, part_ref.at[head], resp_ref.at[head], inv_ref, upd_ref,
            st_ref, stm_ref, amap_ref, rmap_ref, beta_ref, cum_ref, pf_ref, mix_ref, between,
        )
        resp_out[...] = resp_ref[head]
        stage_ref[head] = state.astype(BF16)
        for spot in range(1, SPOTS):
            give(head, spot).start()

        @pl.when(head == H - 1)
        def _():
            for copy in load_pair(0):
                copy.start()

    @pl.when(step >= H)
    def _():
        head = step - H
        for n, at in enumerate(range(lead + 2 * H - 1, final_tick)):

            @pl.when(head == min(n, H - 1))
            def _(at=at):
                gathering.tick(at)

        @pl.when(head < H - 1)
        def _():
            for copy in load_pair(head + 1):
                copy.start()

        for copy in load_pair(head):
            copy.wait()
        for spot in range(1, SPOTS):
            give(head, spot).wait()
        slot = lax.rem(head, 2)
        gate = mm(hidden_ref[HALO:, :], wb_ref[slot, 0])
        gpre_ref[...] = gate
        maps_ref[0, 0] = stage_ref[head, :, DV:]
        for spot in range(1, SPOTS):
            maps_ref[spot, 0] = exch_ref[spot - 1, head, :, DV:]
        state = jnp.zeros((DK, DV), F32)
        for source in range(SPOTS - 1):
            theirs = exch_ref[jnp.maximum(flip_spot(place, source) - 1, 0), head]
            moved = theirs[:, :DV].astype(F32) + mm(theirs[:, DV:], state)
            state = jnp.where(source < place, moved, state)
        sin_ref[0] = state
        attn = part_ref[head] + mm(resp_ref[head], state)
        attn_ref[...] = attn
        scale = lax.rsqrt(jnp.mean(attn * attn, axis=-1, keepdims=True) + 1e-05)
        gated = (attn * scale * gain_ref[...] * (gate * jax.nn.sigmoid(gate))).astype(BF16)
        gated_ref[...] = gated

        @pl.when(head == 0)
        def _():
            y_ref[...] = xs_ref[...].astype(F32)

        y_ref[...] += mm(gated, wb_ref[slot, 1], NT)

        @pl.when(head == H - 1)
        def _():
            keep(4).start()
            value = y_ref[...]
            size = lax.rsqrt(jnp.mean(value * value, axis=-1, keepdims=True) + 1e-06)
            mid_ref[...] = (value * size * gains_out[1:2, :]).astype(BF16)
            keep(5).start()
            gathering.finish()

            @pl.when(place < SPOTS - 1)
            def _():
                give_halo().wait_send()

            for which in range(6):
                keep(which).wait()


def mixer_forward(x, cotangent, shards, gains, gain, taps, par, near, later):
    tokens, width = x.shape
    rows = tokens + HALO
    chunks = tokens // CHUNK
    inner = shards[-1].shape[0]
    spans = gather_spans(inner)
    total = AT_FFN + 3 * inner
    once = lambda array: pl.BlockSpec(
        array.shape, lambda s: (0,) * array.ndim, pipeline_mode=pl.Buffered(1)
    )
    whole = lambda shape: pl.BlockSpec(shape, lambda s: (0,) * len(shape))
    early = lambda s: jnp.minimum(s, H - 1)
    late = lambda s: jnp.maximum(s - H, 0)
    by_head = lambda shape, at: pl.BlockSpec(shape, lambda s: (at(s),) + (0,) * (len(shape) - 1))
    across = lambda shape, at: pl.BlockSpec(shape, lambda s: (0, at(s)))
    anywhere = pl.BlockSpec(memory_space=pl.ANY)
    shape = jax.ShapeDtypeStruct
    sem = pltpu.SemaphoreType.DMA
    saved = saved_shapes(chunks)
    return pl.pallas_call(
        functools.partial(mixer_forward_kernel, spans=spans, inner=inner),
        grid=(2 * H,),
        in_specs=[once(a) for a in (x, cotangent, *shards, gains, gain)]
        + [across((8, HC), early)]
        + [once(a) for a in (par, near, later)],
        out_specs=[anywhere] * 7
        + [
            whole((8, width)),
            whole((tokens, LANES)),
            whole((rows, LANES)),
            across((rows, HC), early),
            whole((rows, LANES)),
            across((tokens, DK), early),
        ]
        + [by_head((1,) + one.shape[1:], early) for one in saved]
        + [
            pl.BlockSpec((SPOTS, 1, DK, DK), lambda s: (0, late(s), 0, 0)),
            by_head((1, DK, DV), late),
            across((tokens, DV), late),
            across((tokens, DV), late),
            across((tokens, DV), late),
        ],
        out_shape=[
            shape((width, total), BF16),
            shape((rows, width), BF16),
            shape((tokens, width), BF16),
            shape((tokens, width), BF16),
            shape((width, width), BF16),
            shape((tokens, width), F32),
            shape((tokens, width), BF16),
            shape((8, width), F32),
            shape((tokens, LANES), F32),
            shape((rows, LANES), F32),
            shape((rows, H * HC), BF16),
            shape((rows, LANES), F32),
            shape((tokens, H * DK), BF16),
        ]
        + saved
        + [
            shape((SPOTS, H, DK, DK), BF16),
            shape((H, DK, DV), F32),
            shape((tokens, H * DV), F32),
            shape((tokens, H * DV), F32),
            shape((tokens, H * DV), BF16),
        ],
        scratch_shapes=[
            pltpu.VMEM((shards[0].shape[0], total), BF16),
            pltpu.VMEM((rows, width), BF16),
            pltpu.VMEM((tokens, width), BF16),
            pltpu.VMEM((tokens, width), BF16),
            pltpu.VMEM((width, width), BF16),
            pltpu.VMEM((tokens, width), F32),
            pltpu.VMEM((tokens, width), BF16),
            pltpu.VMEM((HALO, width), BF16),
            pltpu.VMEM((H, tokens, DV), F32),
            pltpu.VMEM((H, tokens, DK), BF16),
            pltpu.VMEM((SPOTS - 1, H, DK, DV + DK), BF16),
            pltpu.VMEM((H, DK, DV + DK), BF16),
            pltpu.VMEM((tokens, LANES), F32),
            pltpu.VMEM((tokens, LANES), F32),
            pltpu.VMEM((tokens, LANES), F32),
            pltpu.VMEM((rows, HC), F32),
            pltpu.VMEM((tokens, HC), F32),
            pltpu.VMEM((width, HC), BF16),
            pltpu.VMEM((width, LANES), BF16),
            pltpu.VMEM((2, 2, width, DV), BF16),
            sem((len(spans), 10)),
            sem((len(spans), 7)),
            sem((len(spans), SPOTS)),
            sem((SPOTS - 1, H)),
            sem((SPOTS - 1, H)),
            sem((2,)),
            sem((2, 2)),
            sem((6,)),
            sem((2,)),
        ],
        compiler_params=params(collective_id=0, has_side_effects=True),
        cost_estimate=cost(1e11, 1e8),
        name="mixer_forward",
    )(x, cotangent, *shards, gains, gain, taps, par, near, later)


def backward_kernel(place_ref, slot_ref, *refs):
    grads_ref, refs = refs[10], refs[:10] + refs[11:]
    exch_ref = refs[9]

    def behind(source, grad):
        slot = slot_ref[source]
        return jnp.where(
            source > place_ref[0],
            grads_ref[slot, 0].astype(F32) + mm(exch_ref[slot, 0], grad, TN),
            grad,
        )

    places = exch_ref.shape[0]
    d_state = lax.fori_loop(
        0, places - 1, lambda lap, grad: behind(places - 1 - lap, grad), jnp.zeros((DK, DV), F32)
    )
    backward_head(pl.program_id(0), d_state, *refs)


def backward_head(
    head, d_state, p_ref, taps_ref, logit_ref, par_ref, cols_ref, back_ref, segr_ref,
    dattn_ref, sin_ref, exch_ref,
    inv_ref, upd_ref, st_ref, stm_ref, amap_ref, rmap_ref,
    dp_ref, dlogit_ref, dtaps_ref, dpar_ref,
    beta_ref, decay_ref, cum_ref, pf_ref, pre_ref, dmix_ref,
):
    @pl.when(head == 0)
    def _():
        gate_tables(logit_ref, par_ref, beta_ref, decay_ref, cum_ref)
        dlogit_ref[...] = jnp.zeros_like(dlogit_ref)
        dpar_ref[...] = jnp.zeros_like(dpar_ref)

    cols = cols_ref[...]
    tokens = cols.shape[0]
    chunks = range(tokens // CHUNK)
    pre = mix_taps(p_ref, taps_ref, cols, pf_ref)
    pre_ref[...] = pre
    beta = lane(beta_ref[...], head + H)

    state_in = sin_ref[0]
    d_states = [None] * len(chunks)
    for c in reversed(chunks):
        rows = slice(c * CHUNK, (c + 1) * CHUNK)
        d_states[c] = d_state
        if c > 0:
            d_state = mm(amap_ref[0, c], d_state, TN) + mm(rmap_ref[0, c], dattn_ref[rows, :], TN)

    row_ids, col_ids = iota2((CHUNK, CHUNK), 0), iota2((CHUNK, CHUNK), 1)
    d_beta_all, d_decay_all = [], []
    for c in chunks:
        rows = slice(c * CHUNK, (c + 1) * CHUNK)
        mixed = pre_ref[rows, :]
        gate = jax.nn.sigmoid(mixed)
        slope = gate * (1.0 + mixed * (1.0 - gate))
        mixed = mixed * gate
        query_raw, key_raw, value = mixed[:, :DK], mixed[:, DK : 2 * DK], mixed[:, 2 * DK :]
        query_size = lax.rsqrt(jnp.sum(query_raw * query_raw, axis=1, keepdims=True) + 1e-06)
        key_size = lax.rsqrt(jnp.sum(key_raw * key_raw, axis=1, keepdims=True) + 1e-06)
        query_unit, key = query_raw * query_size, key_raw * key_size
        query = query_unit * DK**-0.5
        gamma, strict, carry, last = chunk_tables(c, head, cols, segr_ref, cum_ref)
        strength = beta[rows]
        dots = mm(jnp.concatenate([key, query], axis=0), key, NT)
        weights = strict * dots[:CHUNK]
        low = strength * weights
        scores = gamma * dots[CHUNK:]
        if c == 0:
            state = state_in
        else:
            state = st_ref[0, c] + mm(stm_ref[0, c], state_in)
        updates = upd_ref[0, rows, :DV] - mm(upd_ref[0, rows, DV:], state)
        d_attn = dattn_ref[rows, :]
        d_state = d_states[c]
        d_updates = mm(scores, d_attn, TN) + mm(last * key, d_state)
        solved = mm(inv_ref[0, c], d_updates, TN)
        both = jnp.concatenate([d_attn, solved.astype(BF16)], axis=0)
        by_updates = mm(both, updates, NT)
        by_state = mm(both, state, NT)
        d_scores = by_updates[:CHUNK]
        d_low = -by_updates[CHUNK:]
        d_query = carry * by_state[:CHUNK]
        key_state = jnp.sum(key * by_state[CHUNK:], axis=1, keepdims=True)
        d_carry = jnp.sum(query * by_state[:CHUNK], axis=1, keepdims=True) - strength * key_state
        d_beta = (
            jnp.sum(solved * value, axis=1, keepdims=True)
            - carry * key_state
            + jnp.sum(d_low * weights, axis=1, keepdims=True)
        )
        d_dots_q = d_scores * gamma
        d_dots_k = d_low * strength * strict
        by_key = mm(jnp.concatenate([d_dots_q, d_dots_k], axis=0), key)
        d_query += by_key[:CHUNK]
        from_state = mm(updates, d_state, NT)
        d_key = (
            by_key[CHUNK:]
            + mm(
                jnp.concatenate([d_dots_q, d_dots_k], axis=0),
                jnp.concatenate([query, key], axis=0),
                TN,
            )
            - strength * carry * by_state[CHUNK:]
            + last * from_state
        )
        d_last = jnp.sum(key * from_state, axis=1, keepdims=True) * last
        d_spread = d_scores * scores + d_low * low
        final = (iota2((CHUNK, 1), 0) == CHUNK - 1).astype(F32)
        d_carry += final * jnp.sum(d_state * state)
        d_cum = (
            jnp.sum(d_spread, axis=1, keepdims=True)
            - to_column(jnp.sum(d_spread, axis=0, keepdims=True))
            + final * jnp.sum(d_last)
            - d_last
            + d_carry * carry
        )
        d_decay = jnp.sum(
            jnp.where(row_ids <= col_ids, to_row(d_cum), 0.0), axis=1, keepdims=True
        )
        d_beta_all.append(d_beta)
        d_decay_all.append(d_decay)
        d_query = d_query * DK**-0.5
        d_query = query_size * (
            d_query - query_unit * jnp.sum(d_query * query_unit, axis=1, keepdims=True)
        )
        d_key = key_size * (d_key - key * jnp.sum(d_key * key, axis=1, keepdims=True))
        d_value = strength * solved
        dmix_ref[HALO + c * CHUNK : HALO + (c + 1) * CHUNK, :] = slope * jnp.concatenate(
            [d_query, d_key, d_value], axis=1
        )

    d_beta = jnp.concatenate(d_beta_all, axis=0)
    d_decay = jnp.concatenate(d_decay_all, axis=0)
    lanes = iota2((tokens, LANES), 1)
    slope = jax.nn.sigmoid(logit_ref[HALO:, :] + par_ref[1:2, :]) * -jnp.exp(par_ref[0:1, :])
    here = jnp.where(lanes == head, d_decay, 0.0)
    d_first = here * slope
    strengths = beta_ref[...]
    d_second = jnp.where(lanes == head + H, d_beta, 0.0) * strengths * (1.0 - strengths)
    dlogit_ref[...] += d_first + d_second
    dpar_ref[0:1, :] += jnp.sum(here * decay_ref[...], axis=0, keepdims=True)
    dpar_ref[1:2, :] += jnp.sum(d_first, axis=0, keepdims=True)

    dmix_ref[:HALO, :] = jnp.zeros((HALO, HC), F32)
    dmix_ref[HALO + tokens :, :] = jnp.zeros((8, HC), F32)
    d_mix = dmix_ref[HALO : HALO + tokens, :]
    dtaps_ref[...] = jnp.zeros_like(dtaps_ref)
    dtaps_ref[0:1, :] = jnp.sum(d_mix * pf_ref[HALO:, :], axis=0, keepdims=True)
    total = dmix_ref[: HALO + tokens, :] * taps_ref[0:1, :]
    for j in range(1, CONV):
        total += dmix_ref[j : j + HALO + tokens, :] * taps_ref[j : j + 1, :] * back_ref[:, j : j + 1]
        dtaps_ref[j : j + 1, :] = jnp.sum(
            d_mix * cols[:, j : j + 1] * pf_ref[HALO - j : HALO - j + tokens, :],
            axis=0,
            keepdims=True,
        )
    dp_ref[...] = total.astype(BF16)


def delta_backward(
    place, slots, proj, taps, logits, par, cols, back, segr, d_attn, state_in, exch, grads, saved
):
    rows = proj.shape[0]
    tokens = rows - HALO
    chunks = tokens // CHUNK
    places = exch.shape[0]
    whole = lambda shape: pl.BlockSpec(shape, lambda h: (0,) * len(shape))
    by_head = lambda shape: pl.BlockSpec(shape, lambda h: (h,) + (0,) * (len(shape) - 1))
    return pl.pallas_call(
        backward_kernel,
        grid=(H,),
        in_specs=[
            pl.BlockSpec(memory_space=pltpu.SMEM),
            pl.BlockSpec(memory_space=pltpu.SMEM),
            pl.BlockSpec((rows, HC), lambda h: (0, h)),
            pl.BlockSpec((8, HC), lambda h: (0, h)),
            whole((rows, LANES)),
            whole((8, LANES)),
            whole((tokens, LANES)),
            whole((rows, LANES)),
            whole(segr.shape),
            pl.BlockSpec((tokens, DV), lambda h: (0, h)),
            by_head((1, DK, DV)),
            pl.BlockSpec((places, 1, DK, DK), lambda h: (0, h, 0, DV // DK)),
            pl.BlockSpec((places, 1, DK, DV), lambda h: (0, h, 0, 0)),
            by_head((1, chunks, CHUNK, CHUNK)),
            by_head((1, tokens, DV + DK)),
            by_head((1, chunks, DK, DV)),
            by_head((1, chunks, DK, DK)),
            by_head((1, chunks, DK, DK)),
            by_head((1, chunks, CHUNK, DK)),
        ],
        out_specs=[
            pl.BlockSpec((rows, HC), lambda h: (0, h)),
            whole((tokens, LANES)),
            pl.BlockSpec((8, HC), lambda h: (0, h)),
            whole((8, LANES)),
        ],
        out_shape=[
            jax.ShapeDtypeStruct((rows, H * HC), BF16),
            jax.ShapeDtypeStruct((tokens, LANES), F32),
            jax.ShapeDtypeStruct((8, H * HC), F32),
            jax.ShapeDtypeStruct((8, LANES), F32),
        ],
        scratch_shapes=[
            pltpu.VMEM((tokens, LANES), F32),
            pltpu.VMEM((tokens, LANES), F32),
            pltpu.VMEM((tokens, LANES), F32),
            pltpu.VMEM((rows, HC), F32),
            pltpu.VMEM((tokens, HC), F32),
            pltpu.VMEM((rows + 8, HC), F32),
        ],
        compiler_params=params(),
        cost_estimate=cost(8e9 * H, 5e6 * H),
        name="delta_backward",
    )(place, slots, proj, taps, logits, par, cols, back, segr, d_attn, state_in, exch, grads, *saved)


def mixer_kernel(
    place_ref, slot_ref, part_ref, resp_ref, exch_ref, gpre_ref, gain_ref, w_ref, x_ref, gain2_ref,
    sin_ref, attn_ref, gated_ref, y_ref, h_ref,
):
    head = pl.program_id(0)
    place = place_ref[0]
    places = exch_ref.shape[0]

    def ahead(source, state):
        slot = slot_ref[source]
        return jnp.where(
            source < place,
            exch_ref[slot, 0, :, :DV].astype(F32) + mm(exch_ref[slot, 0, :, DV:], state),
            state,
        )

    state = lax.fori_loop(0, places - 1, ahead, jnp.zeros((DK, DV), F32))
    sin_ref[0] = state
    attn = part_ref[...] + mm(resp_ref[...], state)
    attn_ref[...] = attn
    scale = lax.rsqrt(jnp.mean(attn * attn, axis=-1, keepdims=True) + 1e-05)
    gate = gpre_ref[...]
    gated = (attn * scale * gain_ref[...] * (gate * jax.nn.sigmoid(gate))).astype(BF16)
    gated_ref[...] = gated

    @pl.when(head == 0)
    def _():
        y_ref[...] = x_ref[...].astype(F32)

    y_ref[...] += mm(gated, w_ref[...], NT)

    @pl.when(head == pl.num_programs(0) - 1)
    def _():
        value = y_ref[...]
        size = lax.rsqrt(jnp.mean(value * value, axis=-1, keepdims=True) + 1e-06)
        h_ref[...] = (value * size * gain2_ref[...]).astype(BF16)


def mixer_out(place, slots, part, resp, exch, gpre, gain, weights, x, gain2):
    tokens, width = x.shape
    places = exch.shape[0]
    whole = lambda shape: pl.BlockSpec(shape, lambda h: (0,) * len(shape))
    return pl.pallas_call(
        mixer_kernel,
        grid=(H,),
        in_specs=[
            pl.BlockSpec(memory_space=pltpu.SMEM),
            pl.BlockSpec(memory_space=pltpu.SMEM),
            pl.BlockSpec((tokens, DV), lambda h: (0, h)),
            pl.BlockSpec((tokens, DK), lambda h: (0, h)),
            pl.BlockSpec((places, 1, DK, DV + DK), lambda h: (0, h, 0, 0)),
            pl.BlockSpec((tokens, DV), lambda h: (0, h)),
            whole((1, DV)),
            pl.BlockSpec((width, DV), lambda h: (0, h + AT_OUT // DV)),
            whole((tokens, width)),
            whole((1, width)),
        ],
        out_specs=[
            pl.BlockSpec((1, DK, DV), lambda h: (h, 0, 0)),
            pl.BlockSpec((tokens, DV), lambda h: (0, h)),
            pl.BlockSpec((tokens, DV), lambda h: (0, h)),
            whole((tokens, width)),
            whole((tokens, width)),
        ],
        out_shape=[
            jax.ShapeDtypeStruct((H, DK, DV), F32),
            jax.ShapeDtypeStruct((tokens, H * DV), F32),
            jax.ShapeDtypeStruct((tokens, H * DV), BF16),
            jax.ShapeDtypeStruct((tokens, width), F32),
            jax.ShapeDtypeStruct((tokens, width), BF16),
        ],
        compiler_params=params(),
        cost_estimate=cost(2 * tokens * width * H * DV, 2e7),
        name="mixer_out",
    )(place, slots, part, resp, exch, gpre, gain, weights, x, gain2)


def mixer_back_kernel(
    dmix_ref, w_ref, attn_ref, gpre_ref, gain_ref, resp_ref,
    dattn_ref, dgpre_ref, grad_ref, dgain_ref,
):
    @pl.when(pl.program_id(0) == 0)
    def _():
        dgain_ref[...] = jnp.zeros_like(dgain_ref)

    d_gated = mm(dmix_ref[...], w_ref[...])
    attn = attn_ref[...]
    size = lax.rsqrt(jnp.mean(attn * attn, axis=-1, keepdims=True) + 1e-05)
    unit = attn * size
    gate = gpre_ref[...]
    slope = jax.nn.sigmoid(gate)
    swish = gate * slope
    gain = gain_ref[...]
    dgpre_ref[...] = (d_gated * (unit * gain) * (slope * (1.0 + gate * (1.0 - slope)))).astype(BF16)
    d_normed = d_gated * swish
    dgain_ref[0:1, :] += jnp.sum(d_normed * unit, axis=0, keepdims=True)
    d_unit = d_normed * gain
    d_attn = size * (d_unit - unit * jnp.mean(d_unit * unit, axis=-1, keepdims=True))
    d_attn = d_attn.astype(BF16)
    dattn_ref[...] = d_attn
    grad_ref[0] = mm(resp_ref[...], d_attn, TN).astype(BF16)


def mixer_back(d_mixer, weights, attn, gpre, gain, resp):
    tokens, width = d_mixer.shape
    whole = lambda shape: pl.BlockSpec(shape, lambda h: (0,) * len(shape))
    return pl.pallas_call(
        mixer_back_kernel,
        grid=(H,),
        in_specs=[
            whole((tokens, width)),
            pl.BlockSpec((width, DV), lambda h: (0, h + AT_OUT // DV)),
            pl.BlockSpec((tokens, DV), lambda h: (0, h)),
            pl.BlockSpec((tokens, DV), lambda h: (0, h)),
            whole((1, DV)),
            pl.BlockSpec((tokens, DK), lambda h: (0, h)),
        ],
        out_specs=[
            pl.BlockSpec((tokens, DV), lambda h: (0, h)),
            pl.BlockSpec((tokens, DV), lambda h: (0, h)),
            pl.BlockSpec((1, DK, DV), lambda h: (h, 0, 0)),
            whole((8, DV)),
        ],
        out_shape=[
            jax.ShapeDtypeStruct((tokens, H * DV), BF16),
            jax.ShapeDtypeStruct((tokens, H * DV), BF16),
            jax.ShapeDtypeStruct((H, DK, DV), BF16),
            jax.ShapeDtypeStruct((8, DV), F32),
        ],
        compiler_params=params(),
        cost_estimate=cost(2 * tokens * width * H * DV, 2e7),
        name="mixer_back",
    )(d_mixer, weights, attn, gpre, gain, resp)


def ffn_kernel(
    h_ref, dout_ref, y_ref, gain_ref, wg_ref, wu_ref, wd_ref,
    out_ref, act_ref, dgu_ref, dy_ref, dmix_ref, dgain_ref, res_ref, dh_ref,
):
    step = pl.program_id(0)

    @pl.when(step == 0)
    def _():
        res_ref[...] = y_ref[...]
        dh_ref[...] = jnp.zeros_like(dh_ref)

    hidden = h_ref[...]
    w_gate, w_up, w_down = wg_ref[...], wu_ref[...], wd_ref[...]
    gate = mm(hidden, w_gate)
    up = mm(hidden, w_up)
    d_act = mm(dout_ref[...], w_down)
    slope = jax.nn.sigmoid(gate)
    swish = gate * slope
    act = (swish * up).astype(BF16)
    act_ref[...] = act
    d_gate = (d_act * up * slope * (1.0 + gate * (1.0 - slope))).astype(BF16)
    d_up = (d_act * swish).astype(BF16)
    dgu_ref[0] = d_gate
    dgu_ref[1] = d_up
    res_ref[...] += mm(act, w_down, NT)
    dh_ref[...] += mm(d_gate, w_gate, NT) + mm(d_up, w_up, NT)

    @pl.when(step == pl.num_programs(0) - 1)
    def _():
        out_ref[...] = res_ref[...].astype(BF16)
        value = y_ref[...]
        size = lax.rsqrt(jnp.mean(value * value, axis=-1, keepdims=True) + 1e-06)
        unit = value * size
        d_hidden = dh_ref[...]
        dgain_ref[...] = jnp.zeros_like(dgain_ref)
        dgain_ref[0:1, :] = jnp.sum(d_hidden * unit, axis=0, keepdims=True)
        d_unit = d_hidden * gain_ref[...]
        d_y = dout_ref[...].astype(F32) + size * (
            d_unit - unit * jnp.mean(d_unit * unit, axis=-1, keepdims=True)
        )
        dy_ref[...] = d_y
        dmix_ref[...] = d_y.astype(BF16)


def feed_forward(hidden, d_out, y1, gain, weights, inner):
    tokens, width = hidden.shape
    block = 256
    weight = lambda at: pl.BlockSpec((width, block), lambda j: (0, j + at // block))
    whole = lambda shape: pl.BlockSpec(shape, lambda j: (0,) * len(shape))
    across = pl.BlockSpec((tokens, block), lambda j: (0, j))
    return pl.pallas_call(
        ffn_kernel,
        grid=(inner // block,),
        in_specs=[
            whole((tokens, width)),
            whole((tokens, width)),
            whole((tokens, width)),
            whole((1, width)),
        ]
        + [weight(AT_FFN + i * inner) for i in range(3)],
        out_specs=[
            whole((tokens, width)), across, pl.BlockSpec((2, tokens, block), lambda j: (0, 0, j)),
            whole((tokens, width)), whole((tokens, width)), whole((8, width)),
        ],
        out_shape=[
            jax.ShapeDtypeStruct((tokens, width), BF16),
            jax.ShapeDtypeStruct((tokens, inner), BF16),
            jax.ShapeDtypeStruct((2, tokens, inner), BF16),
            jax.ShapeDtypeStruct((tokens, width), F32),
            jax.ShapeDtypeStruct((tokens, width), BF16),
            jax.ShapeDtypeStruct((8, width), F32),
        ],
        scratch_shapes=[pltpu.VMEM((tokens, width), F32), pltpu.VMEM((tokens, width), F32)],
        compiler_params=params(),
        cost_estimate=cost(12 * tokens * width * inner, 3e7),
        name="feed_forward",
    )(hidden, d_out, y1, gain, weights, weights, weights)


BLOCK = HC
LEAD, EVERY = 4, 3


def other_index(step):
    return step - jnp.clip((step - LEAD + EVERY - 1) // EVERY, 0, H)


class Blocks:
    def __init__(self, inner):
        self.ups, self.downs = inner // (BLOCK // 2), inner // BLOCK
        self.outs = H * DV // BLOCK
        self.others = self.ups + self.downs + 2 * self.outs
        self.count = self.others + H + 1
        self.starts = [0, self.ups, self.ups + self.downs, self.ups + self.downs + self.outs, self.others]
        self.tail = inner - self.downs * BLOCK
        heads = [LEAD + EVERY * h for h in range(H)]
        rest = [n for n in range(self.count - 1) if n not in heads]
        parts = [rest[low:high] for low, high in zip(self.starts, self.starts[1:])]
        self.up_at, self.down_at, self.out_at, self.gate_at = parts
        self.head_at = heads

    def index(self, kind):
        low, high = self.starts[kind], self.starts[kind + 1]
        return lambda s: jnp.clip(other_index(s) - low, 0, high - low - 1)


def dot_blocks(left, right):
    return lax.dot_general(left, right, (NN, ((), ())), preferred_element_type=F32)


def flip_to(bit):
    here = lax.axis_index("seq")
    along_x = here + 1 - 2 * lax.rem(here, 2)
    along_y = here + 2 - 4 * (here // 2)
    return {"dp": lax.axis_index("dp"), "seq": (2 - bit) * along_x + (bit - 1) * along_y}


def reduce_kernel(
    dout_ref, hmid_ref, dres_ref, hidden_ref, act_ref, tail_ref, dgu_ref, gated_ref, dgpre_ref, lgrad_ref,
    p_ref, taps_ref, logit_ref, par_ref, cols_ref, back_ref, segr_ref, dattn_ref, sin_ref, exch_ref,
    inv_ref, upd_ref, st_ref, stm_ref, amap_ref, rmap_ref,
    sum_ref, dp_ref, dlogit_ref, dtaps_ref, dpar_ref,
    beta_ref, decay_ref, cum_ref, pf_ref, pre_ref, dmix_ref,
    turn_ref, dps_ref, halo_ref, grads_ref,
    core_keep, core_send, core_recv, near_keep, near_send, near_recv,
    far_keep, far_send, far_recv, z_keep, z_send, z_recv, done_ref,
    core_ss, core_rs, near_ss, near_rs, far_ss, far_rs, z_ss, z_rs, done_ss, done_rs, own_sem,
    halo_ss, halo_rs, grads_ss, grads_rs, *, blocks,
):
    step = pl.program_id(0)
    steps = pl.num_programs(0)
    place = lax.axis_index("seq")
    count = blocks.count
    half = core_keep.shape[1] * core_keep.shape[2]
    quarter = half // SPOTS
    piece = quarter // PLANES
    mesh = dict(device_id_type=pl.DeviceIdType.MESH)

    def remote(source, target, send, recv, to):
        return pltpu.make_async_remote_copy(
            src_ref=source, dst_ref=target, send_sem=send, recv_sem=recv, device_id=to, **mesh
        )

    def to_core(n):
        slot = lax.rem(n, 2)
        return remote(core_send.at[slot], core_recv.at[slot], core_ss.at[slot], core_rs.at[slot], device(core=1))

    def to_near(n):
        slot = lax.rem(n, 4)
        return remote(
            near_send.at[slot], near_recv.at[slot], near_ss.at[slot], near_rs.at[slot], flip_to(1 + lax.rem(n, 2))
        )

    def to_far(n):
        slot = lax.rem(n, 4)
        return remote(
            far_send.at[slot], far_recv.at[slot], far_ss.at[slot], far_rs.at[slot], flip_to(2 - lax.rem(n, 2))
        )

    def along_z(n, d):
        slot = lax.rem(n, 4)
        return remote(
            z_send.at[slot, d - 1], z_recv.at[slot, d - 1], z_ss.at[slot, d - 1], z_rs.at[slot, d - 1],
            device(planes=PLANES - d),
        )

    def target(n):
        return sum_ref.at[
            pl.ds(pl.multiple_of(place * piece, piece), piece), pl.ds(pl.multiple_of(n * BLOCK, BLOCK), BLOCK)
        ]

    def spread(n, spot):
        slot = lax.rem(n, 4)
        return remote(
            done_ref.at[slot], target(n), done_ss.at[slot, spot - 1], done_rs.at[n, spot - 1], device(spot=spot)
        )

    def keep(n):
        slot = lax.rem(n, 4)
        return pltpu.make_async_copy(done_ref.at[slot], target(n), own_sem.at[slot])

    def give_grads(spot):
        return remote(
            lgrad_ref, grads_ref.at[spot - 1], grads_ss.at[spot - 1], grads_rs.at[spot - 1], device(spot=spot)
        )

    def give_halo(head):
        to = {"dp": lax.axis_index("dp"), "seq": lax.rem(place + SPOTS - 1, SPOTS)}
        return remote(dps_ref.at[0:HALO], halo_ref.at[head], halo_ss.at[head], halo_rs.at[head], to)

    @pl.when(step == 0)
    def _():
        greet([dict(planes=d) for d in (1, 2, 3)] + [dict(spot=s) for s in (1, 2, 3)] + [dict(core=1)])
        for spot in range(1, SPOTS):
            give_grads(spot).start()
        for at, ref in enumerate((dout_ref, hmid_ref, dres_ref)):
            turn_ref[at] = jnp.transpose(ref[...])
        turn_ref[3] = jnp.transpose(hidden_ref[HALO:, :])

    def at_stage(lag, sent):
        n = step - lag

        def run(body):
            @pl.when((n >= 0) & (n < count))
            def _():
                @pl.when(n >= sent)
                def _():
                    body(n, True)

                body(n, False)

        return run

    @at_stage(7, 4)
    def _(n, free):
        if free:
            for spot in range(1, SPOTS):
                spread(n - 4, spot).wait_send()
            keep(n - 4).wait()
            return
        slot = lax.rem(n, 4)
        total = z_keep[slot]
        for d in range(1, PLANES):
            along_z(n, d).wait_recv()
            total += z_recv[slot, d - 1].astype(F32)
        done_ref[slot] = total.astype(BF16)
        keep(n).start()
        for spot in range(1, SPOTS):
            spread(n, spot).start()

    @at_stage(5, 4)
    def _(n, free):
        if free:
            for d in range(1, PLANES):
                along_z(n - 4, d).wait_send()
            return
        slot = lax.rem(n, 4)
        to_far(n).wait_recv()
        total = far_keep[slot] + far_recv[slot].astype(F32)
        z_keep[slot] = total[:piece]
        for d in range(1, PLANES):
            z_send[slot, d - 1] = total[d * piece : (d + 1) * piece].astype(BF16)
            along_z(n, d).start()

    @at_stage(3, 4)
    def _(n, free):
        if free:
            to_far(n - 4).wait_send()
            return
        slot = lax.rem(n, 4)
        to_near(n).wait_recv()
        far_keep[slot] = near_keep[slot, 0] + near_recv[slot, 0].astype(F32)
        far_send[slot] = (near_keep[slot, 1] + near_recv[slot, 1].astype(F32)).astype(BF16)
        to_far(n).start()

    @at_stage(1, 4)
    def _(n, free):
        if free:
            to_near(n - 4).wait_send()
            return
        slot, pair = lax.rem(n, 4), lax.rem(n, 2)
        first = 1 + pair
        to_core(n).wait_recv()
        whole = lambda quarter: core_keep[pair, quarter] + core_recv[pair, quarter].astype(F32)
        near_keep[slot, 0] = whole(0)
        near_keep[slot, 1] = whole(3 - first)
        near_send[slot, 0] = whole(first).astype(BF16)
        near_send[slot, 1] = whole(3).astype(BF16)
        to_near(n).start()

    since = step - LEAD
    heads_turn = (since >= 0) & (since < EVERY * H) & (lax.rem(jnp.maximum(since, 0), EVERY) == 0)
    other = other_index(step)

    def put(product):
        pair = lax.rem(step, 2)

        @pl.when(step >= 2)
        def _():
            to_core(step - 2).wait_send()

        for q in range(SPOTS):
            core_keep[pair, q] = product[q * quarter : (q + 1) * quarter]
            core_send[pair, q] = product[half + q * quarter : half + (q + 1) * quarter].astype(BF16)
        to_core(step).start()

    def on(kind):
        low, high = blocks.starts[kind], blocks.starts[kind + 1]
        return pl.when((other >= low) & (other < high) & jnp.logical_not(heads_turn))

    @on(0)
    def _():
        put(dot_blocks(turn_ref[1], jnp.concatenate([dgu_ref[0], dgu_ref[1]], axis=1)))

    @on(1)
    def _():
        put(dot_blocks(turn_ref[0], act_ref[...]))

    @on(2)
    def _():
        put(dot_blocks(turn_ref[2], gated_ref[...]))

    @on(3)
    def _():
        put(dot_blocks(turn_ref[3], dgpre_ref[...]))

    @pl.when(step == count - 1)
    def _():
        down = dot_blocks(turn_ref[0], tail_ref[...])
        gates = dot_blocks(turn_ref[3], dlogit_ref[...].astype(BF16))
        rest = jnp.zeros((down.shape[0], BLOCK - down.shape[1] - LANES), F32)
        put(jnp.concatenate([down, gates, rest], axis=1))

    @pl.when(heads_turn)
    def _():
        head = since // EVERY

        @pl.when(place > 0)
        def _():
            give_halo(head).wait_send()

        @pl.when(place < SPOTS - 1)
        def _():
            give_halo(head).wait_recv()
            tokens = dps_ref.shape[0] - HALO
            dps_ref[tokens:, :] = (
                dps_ref[tokens:, :].astype(F32) + halo_ref[head].astype(F32)
            ).astype(BF16)

        value = dps_ref[HALO:, :]
        dp_ref[...] = value
        put(dot_blocks(turn_ref[3], value))

    @pl.when((since >= -1) & (since < EVERY * H - 1) & (lax.rem(jnp.maximum(since + 1, 0), EVERY) == 0))
    def _():
        head = (since + 1) // EVERY

        @pl.when(head == 0)
        def _():
            for spot in range(1, SPOTS):
                give_grads(spot).wait()

        d_state = jnp.zeros((DK, DV), F32)
        for source in range(SPOTS - 1, 0, -1):
            slot = flip_spot(place, source)
            grads = grads_ref[jnp.maximum(slot - 1, 0), head].astype(F32)
            d_state = jnp.where(source > place, grads + mm(exch_ref[slot, 0], d_state, TN), d_state)
        backward_head(
            head, d_state, p_ref, taps_ref, logit_ref, par_ref, cols_ref, back_ref, segr_ref,
            dattn_ref, sin_ref, exch_ref, inv_ref, upd_ref, st_ref, stm_ref, amap_ref, rmap_ref,
            dps_ref, dlogit_ref, dtaps_ref, dpar_ref, beta_ref, decay_ref, cum_ref, pf_ref, pre_ref, dmix_ref,
        )

        @pl.when(place > 0)
        def _():
            give_halo(head).start()

    @pl.when(step == steps - 1)
    def _():
        for n in range(count - 4, count):
            if n >= count - 2:
                to_core(n).wait_send()
            to_near(n).wait_send()
            to_far(n).wait_send()
            for d in range(1, PLANES):
                along_z(n, d).wait_send()
            for spot in range(1, SPOTS):
                spread(n, spot).wait_send()
            keep(n).wait()

        def arrived(n, carry):
            for spot in range(1, SPOTS):
                spread(n, spot).wait_recv()
            return carry

        lax.fori_loop(0, count, arrived, 0)


def reduce_gradients(
    d_out, hidden_mid, d_mixer, hidden, act, d_gu, gated, d_gpre, local_grad,
    proj, taps, logits, par, cols, back, segr, d_attn, state_in, exch, saved,
):
    tokens, width = d_out.shape
    rows = hidden.shape[0]
    chunks = tokens // CHUNK
    blocks = Blocks(act.shape[1])
    half = width // CORES
    quarter = half // SPOTS
    piece = quarter // PLANES
    whole = lambda shape: pl.BlockSpec(shape, lambda s: (0,) * len(shape))
    coming = lambda s: jnp.clip((s + EVERY - LEAD) // EVERY, 0, H - 1)
    running = lambda s: jnp.clip((s + 1 - LEAD) // EVERY, 0, H - 1)
    leaving = lambda s: jnp.clip((s - LEAD) // EVERY, 0, H - 1)
    by_head = lambda shape: pl.BlockSpec(shape, lambda s: (coming(s),) + (0,) * (len(shape) - 1))
    across = lambda shape, at: pl.BlockSpec(shape, lambda s: (0, at(s)))
    sem = pltpu.SemaphoreType.DMA
    up, down, out, gate = (blocks.index(kind) for kind in range(4))
    return blocks, pl.pallas_call(
        functools.partial(reduce_kernel, blocks=blocks),
        grid=(blocks.count + 7,),
        in_specs=[
            whole((tokens, width)),
            whole((tokens, width)),
            whole((tokens, width)),
            whole((rows, width)),
            across((tokens, BLOCK), down),
            pl.BlockSpec((tokens, blocks.tail), lambda s: (0, blocks.downs * BLOCK // blocks.tail)),
            pl.BlockSpec((2, tokens, BLOCK // 2), lambda s: (0, 0, up(s))),
            across((tokens, BLOCK), out),
            across((tokens, BLOCK), gate),
            whole((H, DK, DV)),
            across((rows, HC), coming),
            across((8, HC), coming),
            whole((rows, LANES)),
            whole((8, LANES)),
            whole((tokens, LANES)),
            whole((rows, LANES)),
            whole(segr.shape),
            across((tokens, DV), coming),
            by_head((1, DK, DV)),
            pl.BlockSpec((SPOTS, 1, DK, DK), lambda s: (0, coming(s), 0, 0)),
            by_head((1, chunks, CHUNK, CHUNK)),
            by_head((1, tokens, DV + DK)),
            by_head((1, chunks, DK, DV)),
            by_head((1, chunks, DK, DK)),
            by_head((1, chunks, DK, DK)),
            by_head((1, chunks, CHUNK, DK)),
        ],
        out_specs=[
            pl.BlockSpec(memory_space=pl.ANY),
            across((tokens, HC), leaving),
            whole((tokens, LANES)),
            across((8, HC), running),
            whole((8, LANES)),
        ],
        out_shape=[
            jax.ShapeDtypeStruct((SPOTS * piece, blocks.count * BLOCK), BF16),
            jax.ShapeDtypeStruct((tokens, H * HC), BF16),
            jax.ShapeDtypeStruct((tokens, LANES), F32),
            jax.ShapeDtypeStruct((8, H * HC), F32),
            jax.ShapeDtypeStruct((8, LANES), F32),
        ],
        scratch_shapes=[
            pltpu.VMEM((tokens, LANES), F32),
            pltpu.VMEM((tokens, LANES), F32),
            pltpu.VMEM((tokens, LANES), F32),
            pltpu.VMEM((rows, HC), F32),
            pltpu.VMEM((tokens, HC), F32),
            pltpu.VMEM((rows + 8, HC), F32),
            pltpu.VMEM((4, width, tokens), BF16),
            pltpu.VMEM((rows, HC), BF16),
            pltpu.VMEM((H, HALO, HC), BF16),
            pltpu.VMEM((SPOTS - 1, H, DK, DV), BF16),
            pltpu.VMEM((2, SPOTS, quarter, BLOCK), F32),
            pltpu.VMEM((2, SPOTS, quarter, BLOCK), BF16),
            pltpu.VMEM((2, SPOTS, quarter, BLOCK), BF16),
            pltpu.VMEM((4, 2, quarter, BLOCK), F32),
            pltpu.VMEM((4, 2, quarter, BLOCK), BF16),
            pltpu.VMEM((4, 2, quarter, BLOCK), BF16),
            pltpu.VMEM((4, quarter, BLOCK), F32),
            pltpu.VMEM((4, quarter, BLOCK), BF16),
            pltpu.VMEM((4, quarter, BLOCK), BF16),
            pltpu.VMEM((4, piece, BLOCK), F32),
            pltpu.VMEM((4, PLANES - 1, piece, BLOCK), BF16),
            pltpu.VMEM((4, PLANES - 1, piece, BLOCK), BF16),
            pltpu.VMEM((4, piece, BLOCK), BF16),
            sem((2,)), sem((2,)), sem((4,)), sem((4,)), sem((4,)), sem((4,)),
            sem((4, PLANES - 1)), sem((4, PLANES - 1)),
            sem((4, SPOTS - 1)), sem((blocks.count, SPOTS - 1)), sem((4,)),
            sem((H,)), sem((H,)), sem((SPOTS - 1,)), sem((SPOTS - 1,)),
        ],
        compiler_params=params(collective_id=1, has_side_effects=True),
        cost_estimate=cost(1e11, 1e8),
        name="reduce_gradients",
    )(
        d_out, hidden_mid, d_mixer, hidden, act, act, d_gu, gated, d_gpre, local_grad,
        proj, taps, logits, par, cols, back, segr, d_attn, state_in, exch, *saved,
    )


def unpack_gradients(blocks, sums):
    sums = sums.astype(F32)
    part = lambda n, low, high: sums[:, n * BLOCK + low : n * BLOCK + high]
    join = lambda at, low=0, high=BLOCK: jnp.concatenate([part(n, low, high) for n in at], axis=1)
    last = blocks.count - 1
    heads = [from_heads(part(n, 0, BLOCK), 1) for n in blocks.head_at]
    query, key, value = (jnp.concatenate(parts, axis=1) for parts in zip(*heads))
    down = jnp.concatenate([join(blocks.down_at), part(last, 0, blocks.tail)], axis=1)
    logits = part(last, blocks.tail, blocks.tail + 2 * H)
    return (
        query, key, value, join(blocks.gate_at), logits, join(blocks.out_at),
        join(blocks.up_at, 0, BLOCK // 2), join(blocks.up_at, BLOCK // 2, BLOCK), down,
    )


def input_grad_kernel(
    dp_ref, dg_ref, dl_ref, w_ref, wl_ref, x_ref, gain_ref, dy_ref, turn_ref, out_ref, dgain_ref, acc_ref
):
    step = pl.program_id(0)

    @pl.when(step == 0)
    def _():
        acc_ref[...] = mm(dl_ref[...], wl_ref[...], NT)

    @pl.when(step < H)
    def _():
        acc_ref[...] += mm(dp_ref[...], w_ref[...], NT)

    @pl.when(step >= H)
    def _():
        acc_ref[...] += mm(dg_ref[...], w_ref[...], NT)

    @pl.when(step == pl.num_programs(0) - 1)
    def _():
        value = x_ref[...].astype(F32)
        size = lax.rsqrt(jnp.mean(value * value, axis=-1, keepdims=True) + 1e-06)
        unit = value * size
        d_hidden = acc_ref[...]
        dgain_ref[...] = jnp.zeros_like(dgain_ref)
        dgain_ref[0:1, :] = jnp.sum(d_hidden * unit, axis=0, keepdims=True)
        d_unit = d_hidden * gain_ref[...]
        total = dy_ref[...] + size * (
            d_unit - unit * jnp.mean(d_unit * unit, axis=-1, keepdims=True)
        )
        high, low = halves(total)
        out_ref[...] = mm(high, turn_ref[...], NT) + mm(low, turn_ref[...], NT)


def input_grad(d_proj, d_gpre, d_logit, weights, x, gain, d_y, turn):
    tokens, width = x.shape
    block = HC
    second = d_gpre.shape[1] // block
    steps = H + second
    whole = lambda shape: pl.BlockSpec(shape, lambda j: (0,) * len(shape))
    late = lambda j: (0, jnp.maximum(j - H, 0))
    weight = lambda j: (0, jnp.where(j < H, H - 1 - j, j - H + AT_GATE // block))
    in_specs = [
        pl.BlockSpec((tokens, block), lambda j: (0, jnp.minimum(j, H - 1))),
        pl.BlockSpec((tokens, block), late),
        whole((tokens, LANES)),
        pl.BlockSpec((width, block), weight),
        pl.BlockSpec((width, LANES), lambda j: (0, AT_LOGIT // LANES)),
        whole((tokens, width)),
        whole((1, width)),
        whole((tokens, width)),
        whole((width, width)),
    ]
    return pl.pallas_call(
        input_grad_kernel,
        grid=(steps,),
        in_specs=in_specs,
        out_specs=[whole((tokens, width)), whole((8, width))],
        out_shape=[
            jax.ShapeDtypeStruct((tokens, width), F32),
            jax.ShapeDtypeStruct((8, width), F32),
        ],
        scratch_shapes=[pltpu.VMEM((tokens, width), F32)],
        compiler_params=params(),
        cost_estimate=cost(2 * tokens * width * steps * block, 3e7),
        name="input_grad",
    )(d_proj, d_gpre, d_logit, weights, weights, x, gain, d_y, turn)


def shifted(block, axis, distance):
    devices = range(lax.axis_size(axis))
    route = [(i - distance, i) for i in devices if i - distance in devices]
    return lax.ppermute(block, axis, route)


def send(value, planes=0, core=0, spot=0):
    route = []
    for z in range(PLANES):
        for c in range(CORES):
            for s in range(SPOTS):
                target = (((z + planes) % PLANES) * CORES + (c ^ core)) * SPOTS + (s ^ spot)
                route.append(((z * CORES + c) * SPOTS + s, target))
    return lax.ppermute(value, ("dp", "seq"), route)


def total_of(value):
    value = value + send(value, core=1)
    value = value + send(value, spot=1)
    value = value + send(value, spot=2)
    return value + (send(value, planes=1) + send(value, planes=2) + send(value, planes=3))


def plain_sum(left, right, skip_left=0):
    part = lax.psum_scatter(outer(left, right, skip_left), "dp", scatter_dimension=0, tiled=True)
    return lax.psum(part, "seq").astype(F32)


def by_heads(query, key, value):
    lead = query.shape[:-1]
    parts = [query.reshape(lead + (H, DK)), key.reshape(lead + (H, DK)), value.reshape(lead + (H, DV))]
    return jnp.concatenate(parts, axis=-1).reshape(lead + (H * HC,))


def from_heads(value, heads=H):
    lead = value.shape[:-1]
    parts = value.reshape(lead + (heads, HC))
    return (
        parts[..., :DK].reshape(lead + (heads * DK,)),
        parts[..., DK : 2 * DK].reshape(lead + (heads * DK,)),
        parts[..., 2 * DK :].reshape(lead + (heads * DV,)),
    )


def token_rows(segments, place, tokens):
    ext = jnp.pad(segments, (HALO, LANES), constant_values=-1)
    ext = lax.dynamic_slice_in_dim(ext, place * tokens, tokens + LANES)
    seg = ext[HALO : HALO + tokens]
    blocks = seg.reshape(-1, CHUNK)
    before = ext[HALO - 1 : HALO - 1 + tokens : CHUNK]
    near = [seg] + [ext[HALO - j : HALO - j + tokens] == seg for j in range(1, CONV)]
    near += [(blocks == before[:, None]).reshape(-1), (blocks == blocks[:, -1:]).reshape(-1)]
    near = jnp.stack([row.astype(F32) for row in near])
    later = jnp.stack([(jnp.roll(ext, -j) == ext).astype(F32) for j in range(CONV)])
    return jnp.pad(near, ((0, 8 - near.shape[0]), (0, 0))), jnp.pad(later, ((0, 8 - CONV), (0, 0)))


def wide(value):
    return jnp.pad(value, ((0, 0), (0, LANES - value.shape[1])))


def local(
    inputs, segments, cotangent, norm_gain_mix, w_query, w_key, w_value, w_outgate, w_gates,
    conv_weight, decay_log, dt_bias, out_norm_gain, w_out, norm_gain_ffn, w_ffn_gate, w_ffn_up, w_ffn_down,
):
    tokens, width = inputs.shape[1:]
    place = lax.axis_index("seq")
    planned = (lax.axis_size("dp"), lax.axis_size("seq")) == (PLANES * CORES, SPOTS)
    low = lambda a: a.astype(BF16)
    inner = w_ffn_gate.shape[1]
    gain_out = out_norm_gain[None]
    taps_parts = by_heads(conv_weight[:, : H * DK], conv_weight[:, H * DK : 2 * H * DK], conv_weight[:, 2 * H * DK :])
    taps = jnp.pad(taps_parts, ((0, 8 - CONV), (0, 0)))
    par = jnp.pad(jnp.stack([decay_log, dt_bias]), ((0, 6), (0, LANES - H)))
    segr, later = token_rows(segments[0], place, tokens)

    if planned:
        gains = jnp.pad(jnp.stack([norm_gain_mix, norm_gain_ffn]), ((0, 6), (0, 0)))
        shards = (w_query, w_key, w_value, w_outgate, w_gates, w_out, w_ffn_gate, w_ffn_up, w_ffn_down)
        outs = mixer_forward(inputs[0], cotangent[0], shards, gains, gain_out, taps, par, segr, later)
        weights, hidden, x, d_out, turn, y1, hidden_mid, gains, cols, back, proj, logits, resp, *outs = outs
        saved, (maps, state_in, attn, gpre, gated) = outs[:6], outs[6:]
        gain_mix, gain_ffn = gains[0:1], gains[1:2]
    else:
        turn = jnp.eye(width, dtype=BF16)
        qkv = by_heads(low(w_query), low(w_key), low(w_value))
        qkv = jnp.concatenate([qkv[:, h * HC : (h + 1) * HC] for h in reversed(range(H))], axis=1)
        gates = jnp.pad(low(w_gates), ((0, 0), (0, AT_GATE - AT_LOGIT - 2 * H)))
        shard = [qkv, gates, low(w_outgate), low(w_out).T, low(w_ffn_gate), low(w_ffn_up), low(w_ffn_down).T]
        weights = lax.all_gather(jnp.concatenate(shard, axis=1), "dp", axis=0, tiled=True)
        gain_mix, gain_ffn = norm_gain_mix[None], norm_gain_ffn[None]
        cols = jnp.pad(segr.T, ((0, 0), (0, LANES - segr.shape[0])))
        back = jnp.pad(later.T[: tokens + HALO], ((0, 0), (0, LANES - later.shape[0])))
        x, d_out = inputs[0], cotangent[0]
        value = jnp.concatenate([shifted(x[tokens - HALO :], "seq", 1), x], axis=0).astype(F32)
        size = lax.rsqrt(jnp.mean(value * value, axis=-1, keepdims=True) + 1e-06)
        hidden = low(value * size * gain_mix)
        proj, logits, part, resp, exch, *saved = delta_forward(hidden, weights, taps, par, cols, segr)
        exch = lax.all_gather(exch[0], "seq")
        slots = jnp.arange(exch.shape[0], dtype=jnp.int32)
        place_arr = place.reshape((1,)).astype(jnp.int32)
        gpre = outgate(hidden, weights)
        state_in, attn, gated, y1, hidden_mid = mixer_out(
            place_arr, slots, part, resp, exch, gpre, gain_out, weights, x, gain_ffn
        )
    result, act, d_gu, d_y, d_mixer, d_gain_ffn = feed_forward(
        hidden_mid, d_out, y1, gain_ffn, weights, inner
    )
    d_attn, d_gpre, local_grad, d_gain_out = mixer_back(d_mixer, weights, attn, gpre, gain_out, resp)
    if planned:
        blocks, outs = reduce_gradients(
            d_out, hidden_mid, d_mixer, hidden, act, d_gu, gated, d_gpre, local_grad,
            proj, taps, logits, par, cols, back, segr, d_attn, state_in, maps, saved,
        )
        sums, d_proj, d_logits, d_taps, d_par = outs
        d_logit = low(d_logits)
        g_query, g_key, g_value, g_og, g_gates, g_out, g_gate, g_up, g_down = unpack_gradients(blocks, sums)
    else:
        grads = lax.all_gather(local_grad, "seq")
        d_proj, d_logits, d_taps, d_par = delta_backward(
            place_arr, slots, proj, taps, logits, par, cols, back, segr, d_attn, state_in, exch, grads, saved
        )
        sent_back = shifted(d_proj[:HALO], "seq", -1)
        d_proj = d_proj.at[tokens:].add(sent_back)[HALO:]
        d_logit = low(d_logits)
        g_down = plain_sum(d_out, act)
        g_gate = plain_sum(hidden_mid, d_gu[0])
        g_up = plain_sum(hidden_mid, d_gu[1])
        g_out = plain_sum(d_mixer, gated)
        g_og = plain_sum(hidden, d_gpre, HALO)
        g_query, g_key, g_value = from_heads(plain_sum(hidden, d_proj, HALO))
        g_gates = plain_sum(hidden, d_logit, HALO)[:, : 2 * H]
    d_inputs, d_gain_mix = input_grad(
        d_proj, d_gpre, d_logit, weights, x, gain_mix, d_y, turn
    )

    d_conv = jnp.concatenate(from_heads(d_taps[:CONV]), axis=1)
    exact = lambda value: jnp.dot(value, turn.T.astype(F32), precision=lax.Precision.HIGHEST)
    natural = (lambda gains: exact(gains)) if planned else (lambda gains: gains)
    d_gains = natural(jnp.concatenate([d_gain_mix[:1], d_gain_ffn[:1]]))
    pieces = [d_gains[0], d_conv.reshape(-1), d_par[0, :H], d_par[1, :H], d_gain_out[0], d_gains[1]]
    flat = jnp.concatenate(pieces)
    flat = jnp.pad(flat, (0, -flat.shape[0] % 1024)).reshape(-1, LANES)
    flat = (total_of(flat) if planned else lax.psum(flat, ("dp", "seq"))).reshape(-1)
    if planned:
        result = lax.dot_general(result, turn, (NT, ((), ())), preferred_element_type=BF16)
    small, at = [], 0
    for one in pieces:
        small.append(flat[at : at + one.shape[0]])
        at += one.shape[0]
    return (
        result[None], d_inputs[None], small[0], g_query, g_key, g_value, g_og,
        g_gates, small[1].reshape(d_conv.shape), small[2], small[3], small[4], g_out.T,
        small[5], g_gate, g_up, g_down.T,
    )


def solution(mesh):
    rows, cols, copied = P("dp", None), P(None, "dp"), P()
    tokens = P("dp", "seq", None)
    in_specs = (
        tokens, rows, tokens, copied, rows, rows, rows, rows, rows,
        copied, copied, copied, copied, cols, copied, rows, rows, cols,
    )
    out_specs = (
        tokens, tokens, copied, rows, rows, rows, rows, rows,
        copied, copied, copied, copied, cols, copied, rows, rows, cols,
    )
    return jax.shard_map(local, mesh=mesh, in_specs=in_specs, out_specs=out_specs, check_vma=False)
```

```python
import functools

import jax
import jax.numpy as jnp
from jax import lax
from jax.experimental import pallas as pl
from jax.experimental.pallas import tpu as pltpu
from jax.sharding import PartitionSpec as P

H = 8
DK = 128
DV = 256
CONV = 4
HALO = 16
CHUNK = 128
HC = 2 * DK + DV
LANES = 128
PLANES, CORES, SPOTS = 4, 2, 4

AT_LOGIT = H * HC
AT_GATE = AT_LOGIT + 512
AT_OUT = AT_GATE + H * DV
AT_FFN = AT_OUT + H * DV
VMEM_LIMIT = 62 * 2**20

F32 = jnp.float32
BF16 = jnp.bfloat16
NN = ((1,), (0,))
NT = ((1,), (1,))
TN = ((0,), (0,))


def mm(left, right, dims=NN):
    return lax.dot_general(
        left.astype(BF16), right.astype(BF16), (dims, ((), ())), preferred_element_type=F32
    )


def mm_exact(left, right, dims=NN):
    return lax.dot_general(
        left, right, (dims, ((), ())), precision=lax.Precision.HIGHEST, preferred_element_type=F32
    )


def halves(value):
    high = value.astype(BF16)
    return high, (value - high.astype(F32)).astype(BF16)


def mm_three(left, right):
    left_high, left_low = halves(left)
    right_high, right_low = halves(right)
    return mm(left_high, right_high) + (mm(left_high, right_low) + mm(left_low, right_high))


def params(**more):
    return pltpu.CompilerParams(vmem_limit_bytes=VMEM_LIMIT, **more)


def cost(flops, nbytes):
    return pl.CostEstimate(flops=int(flops), bytes_accessed=int(nbytes), transcendentals=0)


def iota2(shape, axis):
    return lax.broadcasted_iota(jnp.int32, shape, axis)


def lane(value, index):
    picked = jnp.where(iota2(value.shape, 1) == index, value, 0.0)
    return jnp.sum(picked, axis=1, keepdims=True)


def to_row(column):
    size = column.shape[0]
    same = iota2((size, size), 0) == iota2((size, size), 1)
    return jnp.sum(jnp.where(same, column, 0.0), axis=0, keepdims=True)


def to_column(row):
    size = row.shape[1]
    same = iota2((size, size), 0) == iota2((size, size), 1)
    return jnp.sum(jnp.where(same, row, 0.0), axis=1, keepdims=True)


def outgate_kernel(h_ref, w_ref, g_ref):
    g_ref[...] = mm(h_ref[HALO:, :], w_ref[...])


def outgate(hidden, weights):
    rows, width = hidden.shape
    cols = H * DV
    block = 512
    return pl.pallas_call(
        outgate_kernel,
        grid=(cols // block,),
        in_specs=[
            pl.BlockSpec((rows, width), lambda j: (0, 0)),
            pl.BlockSpec((width, block), lambda j: (0, j + AT_GATE // block)),
        ],
        out_specs=pl.BlockSpec((rows - HALO, block), lambda j: (0, j)),
        out_shape=jax.ShapeDtypeStruct((rows - HALO, cols), F32),
        compiler_params=params(),
        cost_estimate=cost(2 * rows * width * cols, 2 * width * cols + 4 * rows * cols),
        name="outgate",
    )(hidden, weights)


def outer_kernel(left_ref, right_ref, out_ref, turn_ref, *, skip):
    @pl.when(pl.program_id(0) == 0)
    def _():
        turn_ref[...] = jnp.transpose(left_ref[skip:, :])

    out_ref[...] = mm(turn_ref[...], right_ref[...]).astype(BF16)


def outer(left, right, skip):
    rows, width = left.shape
    cols = right.shape[1]
    block = next(b for b in (512, 256, 128) if cols % b == 0)
    return pl.pallas_call(
        functools.partial(outer_kernel, skip=skip),
        grid=(cols // block,),
        in_specs=[
            pl.BlockSpec((rows, width), lambda j: (0, 0)),
            pl.BlockSpec((rows - skip, block), lambda j: (0, j)),
        ],
        out_specs=pl.BlockSpec((width, block), lambda j: (0, j)),
        out_shape=jax.ShapeDtypeStruct((width, cols), BF16),
        scratch_shapes=[pltpu.VMEM((width, rows - skip), BF16)],
        compiler_params=params(),
        cost_estimate=cost(2 * rows * width * cols, 2 * width * cols + 2 * rows * cols),
        name="outer",
    )(left, right)


def gate_tables(logit_ref, par_ref, beta_ref, decay_ref, cum_ref):
    logits = logit_ref[HALO:, :]
    beta_ref[...] = jax.nn.sigmoid(logits)
    shifted = logits + par_ref[1:2, :]
    soft = jnp.maximum(shifted, 0.0) + jnp.log1p(jnp.exp(-jnp.abs(shifted)))
    decay_ref[...] = -jnp.exp(par_ref[0:1, :]) * soft
    lower = (iota2((CHUNK, CHUNK), 0) >= iota2((CHUNK, CHUNK), 1)).astype(F32)
    for c in range(logits.shape[0] // CHUNK):
        part = decay_ref[c * CHUNK : (c + 1) * CHUNK, :]
        cum_ref[c * CHUNK : (c + 1) * CHUNK, :] = mm_exact(lower, part)


def mix_taps(p_ref, taps_ref, cols, pf_ref):
    tokens = cols.shape[0]
    pf_ref[...] = p_ref[...].astype(F32)
    total = pf_ref[HALO:, :] * taps_ref[0:1, :]
    for j in range(1, CONV):
        total += pf_ref[HALO - j : HALO - j + tokens, :] * taps_ref[j : j + 1, :] * cols[:, j : j + 1]
    return total


def chunk_tables(c, head, cols, segr_ref, cum_ref):
    rows = slice(c * CHUNK, (c + 1) * CHUNK)
    cum = lane(cum_ref[rows, :], head)
    cum_row = to_row(cum)
    same = cols[rows, 0:1] == segr_ref[0:1, rows]
    row_ids, col_ids = iota2((CHUNK, CHUNK), 0), iota2((CHUNK, CHUNK), 1)
    gamma = jnp.where((row_ids >= col_ids) & same, jnp.exp(jnp.minimum(cum - cum_row, 0.0)), 0.0)
    strict = jnp.where(row_ids > col_ids, gamma, 0.0)
    carry = jnp.exp(cum) * cols[rows, 4:5]
    last = jnp.exp(cum[CHUNK - 1 :, :] - cum) * cols[rows, 5:6]
    return gamma, strict, carry, last


def unit_lower_inverses(systems):
    size = systems[0].shape[0]
    row_ids, col_ids = iota2((size, size), 0), iota2((size, size), 1)
    eye = (row_ids == col_ids).astype(F32)
    found = [eye - jnp.where(row_ids // 2 == col_ids // 2, low, 0.0) for low in systems]
    width = 2
    while width < size:
        joined = (row_ids // (2 * width) == col_ids // (2 * width)) & (
            row_ids // width != col_ids // width
        )
        first = [mm_three(jnp.where(joined, low, 0.0), inv) for low, inv in zip(systems, found)]
        found = [inv - mm_three(inv, part) for inv, part in zip(found, first)]
        width *= 2
    return found


def flip_spot(value, bits):
    low, high = lax.rem(value, 2), value // 2
    flip = lambda one, other: one + other - 2 * one * other
    return flip(low, bits % 2) + 2 * flip(high, bits // 2)


def device(planes=0, core=0, spot=0):
    place, here = lax.axis_index("dp"), lax.axis_index("seq")
    z = lax.rem(place // CORES + planes, PLANES)
    return {"dp": z * CORES + flip_spot(lax.rem(place, CORES), core), "seq": flip_spot(here, spot)}


def greet(partners):
    barrier = pltpu.get_barrier_semaphore()
    for partner in partners:
        pl.semaphore_signal(barrier, inc=1, device_id=device(**partner), device_id_type=pl.DeviceIdType.MESH)
    pl.semaphore_wait(barrier, len(partners))


def gather_spans(inner):
    spans = [((H - 1) * HC, HC + LANES), ((H - 2) * HC, HC)]
    spans += [(h * HC, 2 * HC) for h in (4, 2, 0)]
    for at, size in ((AT_GATE, H * DV), (AT_OUT, H * DV)) + tuple((AT_FFN + i * inner, inner) for i in range(3)):
        spans += [(at + low, min(1024, size - low)) for low in range(0, size, 1024)]
    return spans


class Gathering:
    STAGES = (0, 1, 2, 3, 5, 7, 8)
    FIRST = ((0, 1, 2, 3, 4, 5, 6), (0, 1, 2, 3, 4, 6, 7))

    def __init__(self, spans, shard_ref, full_ref, sems, pack):
        self.spans, self.shard, self.full, self.pack = spans, shard_ref, full_ref, pack
        self.send_sem, self.recv_sem, self.local_sem = sems
        self.piece = shard_ref.shape[0] // SPOTS
        self.half = full_ref.shape[0] // CORES
        self.z = lax.axis_index("dp") // CORES

    def quarter(self, spot, cols):
        row = flip_spot(lax.axis_index("seq"), spot) * self.piece
        return self.shard.at[pl.ds(pl.multiple_of(row, self.piece), self.piece), cols]

    def own(self, group):
        at, size = self.spans[group]
        cols = pl.ds(at, size)
        block = PLANES * self.piece
        return [
            pltpu.make_async_copy(
                self.quarter(q, cols),
                self.full.at[q * block : q * block + self.piece, cols],
                self.local_sem.at[group, q],
            )
            for q in range(SPOTS)
        ]

    def copy(self, group, kind):
        at, size = self.spans[group]
        cols = pl.ds(at, size)
        piece, full = self.piece, self.full
        block = PLANES * piece
        rows = lambda quarter: pl.ds(quarter * block + piece, block - piece)
        if kind < 6:
            read, step, written = ((0, 1, 1), (0, -1, 3), (1, 1, 2), (3, -1, 2), (2, 1, 3), (2, -1, 1))[kind]
            source = self.quarter(0, cols) if read == 0 else full.at[read * piece : (read + 1) * piece, cols]
            target = full.at[written * piece : (written + 1) * piece, cols]
            to, arrival = device(planes=step % PLANES), written - 1
        elif kind < 8:
            source = full.at[rows(0), cols]
            target = full.at[rows(kind - 5), cols]
            to, arrival = device(spot=kind - 5), kind - 3
        elif kind == 8:
            by = 1 + group % 2
            source = full.at[rows(by), cols]
            target = full.at[rows(3), cols]
            to, arrival = device(spot=3 - by), 5
        else:
            source = full.at[0 : self.half, cols]
            target = full.at[self.half : 2 * self.half, cols]
            to, arrival = device(core=1), 6
        return pltpu.make_async_remote_copy(
            src_ref=source,
            dst_ref=target,
            send_sem=self.send_sem.at[group, kind],
            recv_sem=self.recv_sem.at[group, arrival],
            device_id=to,
            device_id_type=pl.DeviceIdType.MESH,
        )

    def sends(self, kind):
        z = self.z
        return (z < 3, z > 0, (z > 0) & (z < 3), (z > 0) & (z < 3), z == 2, z == 1)[kind]

    def start(self, group, kind):
        @pl.when(self.sends(kind))
        def _():
            self.copy(group, kind).start()

    def arrive(self, group, kind, condition):
        @pl.when(condition)
        def _():
            self.copy(group, kind).wait_recv()

    def tick(self, at):
        z = self.z
        due = []
        for group in range(len(self.spans)):
            stages = (self.FIRST + (self.STAGES,) * len(self.spans))[group]
            due += [(stage, group) for stage in range(len(stages)) if group + stages[stage] == at]
        for stage, group in sorted(due, reverse=True):
            by = 1 + group % 2
            if stage == 0:
                self.pack(*self.spans[group])
                self.start(group, 0)
                self.start(group, 1)
                for local in self.own(group):
                    local.start()
            elif stage == 1:
                self.arrive(group, 0, z > 0)
                self.start(group, 2)
                self.arrive(group, 1, z < 3)
                self.start(group, 3)
            elif stage == 2:
                self.copy(group, 2).wait_recv()
                self.start(group, 4)
                self.start(group, 5)
            elif stage == 3:
                self.arrive(group, 0, z == 0)
                self.arrive(group, 1, z == 3)
                self.copy(group, 5 + by).start()
                self.copy(group, 8 - by).start()
            elif stage == 4:
                self.copy(group, 5 + by).wait_recv()
                self.copy(group, 8).start()
            elif stage == 5:
                self.copy(group, 8 - by).wait_recv()
                self.copy(group, 8).wait_recv()
                for local in self.own(group):
                    local.wait()
                self.copy(group, 9).start()
            else:
                self.copy(group, 9).wait_recv()

    def finish(self):
        for group in range(len(self.spans)):
            for kind in range(6):

                @pl.when(self.sends(kind))
                def _(group=group, kind=kind):
                    self.copy(group, kind).wait_send()

            for kind in range(6, 10):
                self.copy(group, kind).wait_send()


def forward_kernel(
    h_ref, full_ref, taps_ref, par_ref, cols_ref, segr_ref,
    p_ref, logit_ref, part_ref, resp_ref, exch_ref, inv_ref, upd_ref, st_ref, stm_ref, amap_ref, rmap_ref,
    beta_ref, decay_ref, cum_ref, pf_ref, mix_ref, w_ref, wl_ref, load_sem,
):
    head = pl.program_id(0)
    load_head(head, h_ref, full_ref, par_ref, p_ref, logit_ref, beta_ref, decay_ref, cum_ref, w_ref, wl_ref, load_sem)
    state = forward_head(
        head, p_ref, taps_ref, cols_ref, segr_ref, part_ref, resp_ref, inv_ref, upd_ref, st_ref, stm_ref,
        amap_ref, rmap_ref, beta_ref, cum_ref, pf_ref, mix_ref, lambda: None,
    )
    exch_ref[0, 0] = state.astype(BF16)


def load_head(
    head, h_ref, full_ref, par_ref, p_ref, logit_ref, beta_ref, decay_ref, cum_ref, w_ref, wl_ref, load_sem
):
    def load(slot, at, size, to):
        return pltpu.make_async_copy(full_ref.at[:, pl.ds(at, size)], to, load_sem.at[slot])

    mine = load(0, pl.multiple_of((H - 1 - head) * HC, HC), HC, w_ref)
    mine.start()

    @pl.when(head == 0)
    def _():
        gates = load(1, AT_LOGIT, LANES, wl_ref)
        gates.start()
        gates.wait()
        logit_ref[...] = mm(h_ref[...], wl_ref[...])
        gate_tables(logit_ref, par_ref, beta_ref, decay_ref, cum_ref)

    mine.wait()
    p_ref[...] = mm(h_ref[...], w_ref[...]).astype(BF16)


def forward_head(
    head, p_ref, taps_ref, cols_ref, segr_ref, part_ref, resp_ref, inv_ref, upd_ref, st_ref, stm_ref,
    amap_ref, rmap_ref, beta_ref, cum_ref, pf_ref, mix_ref, between,
):
    cols = cols_ref[...]
    tokens = cols.shape[0]
    total = mix_taps(p_ref, taps_ref, cols, pf_ref)
    mix_ref[...] = total * jax.nn.sigmoid(total)
    between()
    beta = lane(beta_ref[...], head + H)
    chunks = range(tokens // CHUNK)
    tables, lows, keys, queries = [], [], [], []
    for c in chunks:
        rows = slice(c * CHUNK, (c + 1) * CHUNK)
        query = mix_ref[rows, :DK]
        query = query * (lax.rsqrt(jnp.sum(query * query, axis=1, keepdims=True) + 1e-06) * DK**-0.5)
        key = mix_ref[rows, DK : 2 * DK]
        key = key * lax.rsqrt(jnp.sum(key * key, axis=1, keepdims=True) + 1e-06)
        gamma, strict, carry, last = chunk_tables(c, head, cols, segr_ref, cum_ref)
        dots = mm(jnp.concatenate([key, query], axis=0), key, NT)
        lows.append(beta[rows] * strict * dots[:CHUNK])
        tables.append((gamma * dots[CHUNK:], carry, last))
        keys.append(key)
        queries.append(query)
    inverses = unit_lower_inverses(lows)
    state = None
    for c in chunks:
        rows = slice(c * CHUNK, (c + 1) * CHUNK)
        scores, carry, last = tables[c]
        key, query = keys[c], queries[c]
        target = jnp.concatenate([mix_ref[rows, 2 * DK :], carry * key], axis=1) * beta[rows]
        updates = mm(inverses[c], target)
        inv_ref[0, c] = inverses[c].astype(BF16)
        upd_ref[0, rows, :] = updates
        weighted_t = jnp.transpose(last * key)
        both = mm(jnp.concatenate([weighted_t, scores], axis=0), updates)
        eye = (iota2((DK, DK), 0) == iota2((DK, DK), 1)).astype(F32)
        step_map = carry[CHUNK - 1 :, :] * eye - both[:DK, DV:]
        read_map = carry * query - both[DK:, DV:]
        amap_ref[0, c] = step_map.astype(BF16)
        rmap_ref[0, c] = read_map.astype(BF16)
        if c == 0:
            st_ref[0, c] = jnp.zeros((DK, DV), F32)
            stm_ref[0, c] = eye.astype(BF16)
            part_ref[rows, :] = both[DK:, :DV]
            resp_ref[rows, :] = read_map.astype(BF16)
            state = jnp.concatenate([both[:DK, :DV], step_map], axis=1)
        else:
            st_ref[0, c] = state[:, :DV]
            stm_ref[0, c] = state[:, DV:].astype(BF16)
            moved = mm(jnp.concatenate([step_map, read_map], axis=0), state)
            part_ref[rows, :] = both[DK:, :DV] + moved[DK:, :DV]
            resp_ref[rows, :] = moved[DK:, DV:].astype(BF16)
            state = moved[:DK] + jnp.concatenate(
                [both[:DK, :DV], jnp.zeros((DK, DK), F32)], axis=1
            )
    return state


def delta_forward(hidden, weights, taps, par, cols, segr):
    rows, width = hidden.shape
    tokens = rows - HALO
    chunks = tokens // CHUNK
    whole = lambda shape: pl.BlockSpec(shape, lambda h: (0,) * len(shape))
    by_head = lambda shape: pl.BlockSpec(shape, lambda h: (h,) + (0,) * (len(shape) - 1))
    return pl.pallas_call(
        forward_kernel,
        grid=(H,),
        in_specs=[
            whole((rows, width)),
            pl.BlockSpec(memory_space=pl.ANY),
            pl.BlockSpec((8, HC), lambda h: (0, h)),
            whole((8, LANES)),
            whole((tokens, LANES)),
            whole(segr.shape),
        ],
        out_specs=[
            pl.BlockSpec((rows, HC), lambda h: (0, h)),
            whole((rows, LANES)),
            pl.BlockSpec((tokens, DV), lambda h: (0, h)),
            pl.BlockSpec((tokens, DK), lambda h: (0, h)),
            pl.BlockSpec((1, 1, DK, DV + DK), lambda h: (0, h, 0, 0)),
            by_head((1, chunks, CHUNK, CHUNK)),
            by_head((1, tokens, DV + DK)),
            by_head((1, chunks, DK, DV)),
            by_head((1, chunks, DK, DK)),
            by_head((1, chunks, DK, DK)),
            by_head((1, chunks, CHUNK, DK)),
        ],
        out_shape=[
            jax.ShapeDtypeStruct((rows, H * HC), BF16),
            jax.ShapeDtypeStruct((rows, LANES), F32),
            jax.ShapeDtypeStruct((tokens, H * DV), F32),
            jax.ShapeDtypeStruct((tokens, H * DK), BF16),
            jax.ShapeDtypeStruct((1, H, DK, DV + DK), BF16),
        ]
        + saved_shapes(chunks),
        scratch_shapes=[
            pltpu.VMEM((tokens, LANES), F32),
            pltpu.VMEM((tokens, LANES), F32),
            pltpu.VMEM((tokens, LANES), F32),
            pltpu.VMEM((rows, HC), F32),
            pltpu.VMEM((tokens, HC), F32),
            pltpu.VMEM((width, HC), BF16),
            pltpu.VMEM((width, LANES), BF16),
            pltpu.SemaphoreType.DMA((2,)),
        ],
        compiler_params=params(),
        cost_estimate=cost(6e9 * H, 5e6 * H),
        name="delta_forward",
    )(hidden, weights, taps, par, cols, segr)


def saved_shapes(chunks):
    return [
        jax.ShapeDtypeStruct((H, chunks, CHUNK, CHUNK), BF16),
        jax.ShapeDtypeStruct((H, chunks * CHUNK, DV + DK), F32),
        jax.ShapeDtypeStruct((H, chunks, DK, DV), F32),
        jax.ShapeDtypeStruct((H, chunks, DK, DK), BF16),
        jax.ShapeDtypeStruct((H, chunks, DK, DK), BF16),
        jax.ShapeDtypeStruct((H, chunks, CHUNK, DK), BF16),
    ]


def mixer_forward_kernel(
    x_ref, cot_ref, wq_ref, wk_ref, wv_ref, wo_ref, wl_in, wm_ref, wg_ref, wu_ref, wd_ref,
    gains_ref, gain_ref, taps_ref, par_ref, near_ref, later_ref,
    full_ref, hidden_out, x_out, cot_out, turn_out, y_out, mid_out,
    gains_out, cols_ref, back_ref, p_ref, logit_ref, resp_out,
    inv_ref, upd_ref, st_ref, stm_ref, amap_ref, rmap_ref, maps_ref, sin_ref, attn_ref, gpre_ref, gated_ref,
    shard_ref, hidden_ref, xs_ref, cots_ref, turn_ref, y_ref, mid_ref, xh_ref, part_ref, resp_ref, exch_ref, stage_ref, half_ref, low_ref,
    beta_ref, decay_ref, cum_ref, pf_ref, mix_ref, w_ref, wl_ref, wb_ref,
    send_sem, recv_sem, local_sem, exch_send, exch_recv, load_sem, pair_sem, out_sem, halo_sem, *, spans, inner,
):
    step = pl.program_id(0)
    place = lax.axis_index("seq")
    tokens, width = x_ref.shape

    def pack(at, size):
        while size > 0:
            if at < AT_LOGIT:
                head, span = H - 1 - at // HC, HC
                shard_ref[:, at : at + DK] = wq_ref[:, head * DK : (head + 1) * DK].astype(BF16)
                shard_ref[:, at + DK : at + 2 * DK] = wk_ref[:, head * DK : (head + 1) * DK].astype(BF16)
                shard_ref[:, at + 2 * DK : at + HC] = wv_ref[:, head * DV : (head + 1) * DV].astype(BF16)
            elif at < AT_GATE:
                span = LANES
                shard_ref[:, at : at + LANES] = jnp.zeros((shard_ref.shape[0], LANES), BF16)
                shard_ref[:, at : at + 2 * H] = wl_in[...].astype(BF16)
            elif at < AT_OUT:
                span, low = size, at - AT_GATE
                shard_ref[:, at : at + span] = wo_ref[:, low : low + span].astype(BF16)
            elif at < AT_FFN:
                span, low = size, at - AT_OUT
                shard_ref[:, at : at + span] = jnp.transpose(wm_ref[low : low + span, :]).astype(BF16)
            else:
                span, which, low = size, (at - AT_FFN) // inner, (at - AT_FFN) % inner
                if which < 2:
                    shard_ref[:, at : at + span] = (wg_ref, wu_ref)[which][:, low : low + span].astype(BF16)
                else:
                    shard_ref[:, at : at + span] = jnp.transpose(wd_ref[low : low + span, :]).astype(BF16)
            at, size = at + span, size - span

    gathering = Gathering(spans, shard_ref, full_ref, (send_sem, recv_sem, local_sem), pack)
    lead = gathering.FIRST[0][-1] + 1
    final_tick = len(spans) + gathering.STAGES[-1]

    upper = place // 2 == 1
    second = lax.rem(place, 2) == 1

    def give(h):
        return pltpu.make_async_remote_copy(
            src_ref=stage_ref.at[h],
            dst_ref=exch_ref.at[h],
            send_sem=exch_send.at[0, h],
            recv_sem=exch_recv.at[0, h],
            device_id=device(spot=1),
            device_id_type=pl.DeviceIdType.MESH,
        )

    def give_half(h):
        return pltpu.make_async_remote_copy(
            src_ref=half_ref.at[h],
            dst_ref=low_ref.at[h],
            send_sem=exch_send.at[1, h],
            recv_sem=exch_recv.at[1, h],
            device_id=device(spot=2),
            device_id_type=pl.DeviceIdType.MESH,
        )

    def join(h):
        give(h).wait()

        @pl.when(jnp.logical_not(upper))
        def _():
            mine, theirs = stage_ref[h], exch_ref[h]
            later = jnp.where(second, mine, theirs)
            earlier = jnp.where(second, theirs, mine)
            half_ref[h] = (later[:, :DV].astype(F32) + mm(later[:, DV:], earlier[:, :DV])).astype(BF16)
            give_half(h).start()

    def give_halo():
        return pltpu.make_async_remote_copy(
            src_ref=x_ref.at[tokens - HALO : tokens],
            dst_ref=xh_ref,
            send_sem=halo_sem.at[0],
            recv_sem=halo_sem.at[1],
            device_id={"dp": lax.axis_index("dp"), "seq": lax.rem(place + 1, SPOTS)},
            device_id_type=pl.DeviceIdType.MESH,
        )

    def keep(which):
        source, to = (
            (hidden_ref, hidden_out), (xs_ref, x_out), (cots_ref, cot_out), (turn_ref, turn_out),
            (y_ref, y_out), (mid_ref, mid_out),
        )[which]
        return pltpu.make_async_copy(source, to, out_sem.at[which])

    def load_pair(h):
        slot = lax.rem(h, 2)
        return [
            pltpu.make_async_copy(
                full_ref.at[:, pl.ds(pl.multiple_of(at + h * DV, DV), DV)], wb_ref.at[slot, i], pair_sem.at[slot, i]
            )
            for i, at in enumerate((AT_GATE, AT_OUT))
        ]

    @pl.when(step == 0)
    def _():
        greet([dict(planes=d) for d in (1, 2, 3)] + [dict(spot=s) for s in (1, 2, 3)] + [dict(core=1)])

        @pl.when(place < SPOTS - 1)
        def _():
            give_halo().start()

        gathering.tick(0)
        at = iota2((1, width), 1)
        piece = width // (PLANES * CORES * SPOTS)
        core, rest = at // (width // 2), at % (width // 2)
        quarter, plane, low = rest // (PLANES * piece), rest // piece % PLANES, rest % piece
        place_dp = lax.axis_index("dp")
        z, c = place_dp // CORES, lax.rem(place_dp, CORES)
        chip = ((z - plane + PLANES) % PLANES) * CORES + (c + core - 2 * c * core)
        order = (chip * SPOTS + flip_spot(quarter, place)) * piece + low
        turn_ref[...] = jnp.where(iota2((width, width), 0) == order, 1.0, 0.0).astype(BF16)
        keep(3).start()
        gathering.tick(1)
        cots_ref[...] = mm(cot_ref[...], turn_ref[...]).astype(BF16)
        keep(2).start()
        high, mid = halves(gains_ref[...])
        rest = (gains_ref[...] - high.astype(F32)) - mid.astype(F32)
        gains_out[...] = mm(high, turn_ref[...]) + mm(mid, turn_ref[...]) + mm(rest, turn_ref[...])
        gathering.tick(2)
        blank = jnp.zeros((LANES - near_ref.shape[0], LANES), F32)
        for n in range(tokens // LANES):
            span = slice(n * LANES, (n + 1) * LANES)
            cols_ref[span, :] = jnp.transpose(jnp.concatenate([near_ref[:, span], blank], axis=0))
        for n in range(tokens // LANES + 1):
            span = slice(n * LANES, (n + 1) * LANES)
            turned = jnp.transpose(jnp.concatenate([later_ref[:, span], blank], axis=0))
            kept = min(LANES, tokens + HALO - n * LANES)
            back_ref[n * LANES : n * LANES + kept, :] = turned[:kept]
        gathering.tick(3)

        @pl.when(place > 0)
        def _():
            give_halo().wait_recv()

        @pl.when(place == 0)
        def _():
            xh_ref[...] = jnp.zeros_like(xh_ref)

        value = mm(jnp.concatenate([xh_ref[...], x_ref[...]], axis=0), turn_ref[...])
        xs_ref[...] = value[HALO:].astype(BF16)
        keep(1).start()
        size = lax.rsqrt(jnp.mean(value * value, axis=-1, keepdims=True) + 1e-06)
        hidden_ref[...] = (value * size * gains_out[0:1, :]).astype(BF16)
        keep(0).start()
        for at in range(4, lead):
            gathering.tick(at)

    @pl.when((step >= 2) & (step < H + 2))
    def _():
        join(step - 2)

    @pl.when(step < H)
    def _():
        head = step
        for h in range(1, H):

            @pl.when(head == h)
            def _(h=h):
                gathering.tick(lead + 2 * h - 1)

        load_head(
            head, hidden_ref, full_ref, par_ref, p_ref, logit_ref, beta_ref, decay_ref, cum_ref, w_ref, wl_ref, load_sem
        )

        def between():
            for h in range(H):

                @pl.when(head == h)
                def _(h=h):
                    gathering.tick(lead + 2 * h)

        state = forward_head(
            head, p_ref, taps_ref, cols_ref, near_ref, part_ref.at[head], resp_ref.at[head], inv_ref, upd_ref,
            st_ref, stm_ref, amap_ref, rmap_ref, beta_ref, cum_ref, pf_ref, mix_ref, between,
        )
        resp_out[...] = resp_ref[head]
        stage_ref[head] = state.astype(BF16)
        give(head).start()

        @pl.when(head == H - 1)
        def _():
            for copy in load_pair(0):
                copy.start()

    @pl.when(step >= H)
    def _():
        head = step - H
        for n, at in enumerate(range(lead + 2 * H - 1, final_tick)):

            @pl.when(head == min(n, H - 1))
            def _(at=at):
                gathering.tick(at)

        @pl.when(head < H - 1)
        def _():
            for copy in load_pair(head + 1):
                copy.start()

        for copy in load_pair(head):
            copy.wait()
        @pl.when(upper)
        def _():
            give_half(head).wait_recv()

        @pl.when(jnp.logical_not(upper))
        def _():
            low_ref[head] = jnp.zeros((DK, DV), BF16)
            give_half(head).wait_send()

        slot = lax.rem(head, 2)
        gate = mm(hidden_ref[HALO:, :], wb_ref[slot, 0])
        gpre_ref[...] = gate
        theirs = exch_ref[head]
        maps_ref[0, 0] = stage_ref[head, :, DV:]
        maps_ref[1, 0] = theirs[:, DV:]
        state = low_ref[head].astype(F32)
        state = jnp.where(second, theirs[:, :DV].astype(F32) + mm(theirs[:, DV:], state), state)
        sin_ref[0] = state
        attn = part_ref[head] + mm(resp_ref[head], state)
        attn_ref[...] = attn
        scale = lax.rsqrt(jnp.mean(attn * attn, axis=-1, keepdims=True) + 1e-05)
        gated = (attn * scale * gain_ref[...] * (gate * jax.nn.sigmoid(gate))).astype(BF16)
        gated_ref[...] = gated

        @pl.when(head == 0)
        def _():
            y_ref[...] = xs_ref[...].astype(F32)

        y_ref[...] += mm(gated, wb_ref[slot, 1], NT)

        @pl.when(head == H - 1)
        def _():
            keep(4).start()
            value = y_ref[...]
            size = lax.rsqrt(jnp.mean(value * value, axis=-1, keepdims=True) + 1e-06)
            mid_ref[...] = (value * size * gains_out[1:2, :]).astype(BF16)
            keep(5).start()
            gathering.finish()

            @pl.when(place < SPOTS - 1)
            def _():
                give_halo().wait_send()

            for which in range(6):
                keep(which).wait()


def mixer_forward(x, cotangent, shards, gains, gain, taps, par, near, later):
    tokens, width = x.shape
    rows = tokens + HALO
    chunks = tokens // CHUNK
    inner = shards[-1].shape[0]
    spans = gather_spans(inner)
    total = AT_FFN + 3 * inner
    once = lambda array: pl.BlockSpec(
        array.shape, lambda s: (0,) * array.ndim, pipeline_mode=pl.Buffered(1)
    )
    whole = lambda shape: pl.BlockSpec(shape, lambda s: (0,) * len(shape))
    early = lambda s: jnp.minimum(s, H - 1)
    late = lambda s: jnp.maximum(s - H, 0)
    by_head = lambda shape, at: pl.BlockSpec(shape, lambda s: (at(s),) + (0,) * (len(shape) - 1))
    across = lambda shape, at: pl.BlockSpec(shape, lambda s: (0, at(s)))
    anywhere = pl.BlockSpec(memory_space=pl.ANY)
    shape = jax.ShapeDtypeStruct
    sem = pltpu.SemaphoreType.DMA
    saved = saved_shapes(chunks)
    return pl.pallas_call(
        functools.partial(mixer_forward_kernel, spans=spans, inner=inner),
        grid=(2 * H,),
        in_specs=[once(a) for a in (x, cotangent, *shards, gains, gain)]
        + [across((8, HC), early)]
        + [once(a) for a in (par, near, later)],
        out_specs=[anywhere] * 7
        + [
            whole((8, width)),
            whole((tokens, LANES)),
            whole((rows, LANES)),
            across((rows, HC), early),
            whole((rows, LANES)),
            across((tokens, DK), early),
        ]
        + [by_head((1,) + one.shape[1:], early) for one in saved]
        + [
            pl.BlockSpec((2, 1, DK, DK), lambda s: (0, late(s), 0, 0)),
            by_head((1, DK, DV), late),
            across((tokens, DV), late),
            across((tokens, DV), late),
            across((tokens, DV), late),
        ],
        out_shape=[
            shape((width, total), BF16),
            shape((rows, width), BF16),
            shape((tokens, width), BF16),
            shape((tokens, width), BF16),
            shape((width, width), BF16),
            shape((tokens, width), F32),
            shape((tokens, width), BF16),
            shape((8, width), F32),
            shape((tokens, LANES), F32),
            shape((rows, LANES), F32),
            shape((rows, H * HC), BF16),
            shape((rows, LANES), F32),
            shape((tokens, H * DK), BF16),
        ]
        + saved
        + [
            shape((2, H, DK, DK), BF16),
            shape((H, DK, DV), F32),
            shape((tokens, H * DV), F32),
            shape((tokens, H * DV), F32),
            shape((tokens, H * DV), BF16),
        ],
        scratch_shapes=[
            pltpu.VMEM((shards[0].shape[0], total), BF16),
            pltpu.VMEM((rows, width), BF16),
            pltpu.VMEM((tokens, width), BF16),
            pltpu.VMEM((tokens, width), BF16),
            pltpu.VMEM((width, width), BF16),
            pltpu.VMEM((tokens, width), F32),
            pltpu.VMEM((tokens, width), BF16),
            pltpu.VMEM((HALO, width), BF16),
            pltpu.VMEM((H, tokens, DV), F32),
            pltpu.VMEM((H, tokens, DK), BF16),
            pltpu.VMEM((H, DK, DV + DK), BF16),
            pltpu.VMEM((H, DK, DV + DK), BF16),
            pltpu.VMEM((H, DK, DV), BF16),
            pltpu.VMEM((H, DK, DV), BF16),
            pltpu.VMEM((tokens, LANES), F32),
            pltpu.VMEM((tokens, LANES), F32),
            pltpu.VMEM((tokens, LANES), F32),
            pltpu.VMEM((rows, HC), F32),
            pltpu.VMEM((tokens, HC), F32),
            pltpu.VMEM((width, HC), BF16),
            pltpu.VMEM((width, LANES), BF16),
            pltpu.VMEM((2, 2, width, DV), BF16),
            sem((len(spans), 10)),
            sem((len(spans), 7)),
            sem((len(spans), SPOTS)),
            sem((2, H)),
            sem((2, H)),
            sem((2,)),
            sem((2, 2)),
            sem((6,)),
            sem((2,)),
        ],
        compiler_params=params(collective_id=0, has_side_effects=True),
        cost_estimate=cost(1e11, 1e8),
        name="mixer_forward",
    )(x, cotangent, *shards, gains, gain, taps, par, near, later)


def backward_kernel(place_ref, slot_ref, *refs):
    exch_ref, grads_ref, refs = refs[9], refs[10], refs[:9] + refs[11:]

    def behind(source, grad):
        slot = slot_ref[source]
        return jnp.where(
            source > place_ref[0],
            grads_ref[slot, 0].astype(F32) + mm(exch_ref[slot, 0], grad, TN),
            grad,
        )

    places = exch_ref.shape[0]
    d_state = lax.fori_loop(
        0, places - 1, lambda lap, grad: behind(places - 1 - lap, grad), jnp.zeros((DK, DV), F32)
    )
    backward_head(pl.program_id(0), d_state, *refs)


def backward_head(
    head, d_state, p_ref, taps_ref, logit_ref, par_ref, cols_ref, back_ref, segr_ref,
    dattn_ref, sin_ref,
    inv_ref, upd_ref, st_ref, stm_ref, amap_ref, rmap_ref,
    dp_ref, dlogit_ref, dtaps_ref, dpar_ref,
    beta_ref, decay_ref, cum_ref, pf_ref, pre_ref, dmix_ref,
):
    @pl.when(head == 0)
    def _():
        gate_tables(logit_ref, par_ref, beta_ref, decay_ref, cum_ref)
        dlogit_ref[...] = jnp.zeros_like(dlogit_ref)
        dpar_ref[...] = jnp.zeros_like(dpar_ref)

    cols = cols_ref[...]
    tokens = cols.shape[0]
    chunks = range(tokens // CHUNK)
    pre = mix_taps(p_ref, taps_ref, cols, pf_ref)
    pre_ref[...] = pre
    beta = lane(beta_ref[...], head + H)

    state_in = sin_ref[0]
    d_states = [None] * len(chunks)
    for c in reversed(chunks):
        rows = slice(c * CHUNK, (c + 1) * CHUNK)
        d_states[c] = d_state
        if c > 0:
            d_state = mm(amap_ref[0, c], d_state, TN) + mm(rmap_ref[0, c], dattn_ref[rows, :], TN)

    row_ids, col_ids = iota2((CHUNK, CHUNK), 0), iota2((CHUNK, CHUNK), 1)
    d_beta_all, d_decay_all = [], []
    for c in chunks:
        rows = slice(c * CHUNK, (c + 1) * CHUNK)
        mixed = pre_ref[rows, :]
        gate = jax.nn.sigmoid(mixed)
        slope = gate * (1.0 + mixed * (1.0 - gate))
        mixed = mixed * gate
        query_raw, key_raw, value = mixed[:, :DK], mixed[:, DK : 2 * DK], mixed[:, 2 * DK :]
        query_size = lax.rsqrt(jnp.sum(query_raw * query_raw, axis=1, keepdims=True) + 1e-06)
        key_size = lax.rsqrt(jnp.sum(key_raw * key_raw, axis=1, keepdims=True) + 1e-06)
        query_unit, key = query_raw * query_size, key_raw * key_size
        query = query_unit * DK**-0.5
        gamma, strict, carry, last = chunk_tables(c, head, cols, segr_ref, cum_ref)
        strength = beta[rows]
        dots = mm(jnp.concatenate([key, query], axis=0), key, NT)
        weights = strict * dots[:CHUNK]
        low = strength * weights
        scores = gamma * dots[CHUNK:]
        if c == 0:
            state = state_in
        else:
            state = st_ref[0, c] + mm(stm_ref[0, c], state_in)
        updates = upd_ref[0, rows, :DV] - mm(upd_ref[0, rows, DV:], state)
        d_attn = dattn_ref[rows, :]
        d_state = d_states[c]
        d_updates = mm(scores, d_attn, TN) + mm(last * key, d_state)
        solved = mm(inv_ref[0, c], d_updates, TN)
        both = jnp.concatenate([d_attn, solved.astype(BF16)], axis=0)
        by_updates = mm(both, updates, NT)
        by_state = mm(both, state, NT)
        d_scores = by_updates[:CHUNK]
        d_low = -by_updates[CHUNK:]
        d_query = carry * by_state[:CHUNK]
        key_state = jnp.sum(key * by_state[CHUNK:], axis=1, keepdims=True)
        d_carry = jnp.sum(query * by_state[:CHUNK], axis=1, keepdims=True) - strength * key_state
        d_beta = (
            jnp.sum(solved * value, axis=1, keepdims=True)
            - carry * key_state
            + jnp.sum(d_low * weights, axis=1, keepdims=True)
        )
        d_dots_q = d_scores * gamma
        d_dots_k = d_low * strength * strict
        by_key = mm(jnp.concatenate([d_dots_q, d_dots_k], axis=0), key)
        d_query += by_key[:CHUNK]
        from_state = mm(updates, d_state, NT)
        d_key = (
            by_key[CHUNK:]
            + mm(
                jnp.concatenate([d_dots_q, d_dots_k], axis=0),
                jnp.concatenate([query, key], axis=0),
                TN,
            )
            - strength * carry * by_state[CHUNK:]
            + last * from_state
        )
        d_last = jnp.sum(key * from_state, axis=1, keepdims=True) * last
        d_spread = d_scores * scores + d_low * low
        final = (iota2((CHUNK, 1), 0) == CHUNK - 1).astype(F32)
        d_carry += final * jnp.sum(d_state * state)
        d_cum = (
            jnp.sum(d_spread, axis=1, keepdims=True)
            - to_column(jnp.sum(d_spread, axis=0, keepdims=True))
            + final * jnp.sum(d_last)
            - d_last
            + d_carry * carry
        )
        d_decay = jnp.sum(
            jnp.where(row_ids <= col_ids, to_row(d_cum), 0.0), axis=1, keepdims=True
        )
        d_beta_all.append(d_beta)
        d_decay_all.append(d_decay)
        d_query = d_query * DK**-0.5
        d_query = query_size * (
            d_query - query_unit * jnp.sum(d_query * query_unit, axis=1, keepdims=True)
        )
        d_key = key_size * (d_key - key * jnp.sum(d_key * key, axis=1, keepdims=True))
        d_value = strength * solved
        dmix_ref[HALO + c * CHUNK : HALO + (c + 1) * CHUNK, :] = slope * jnp.concatenate(
            [d_query, d_key, d_value], axis=1
        )

    d_beta = jnp.concatenate(d_beta_all, axis=0)
    d_decay = jnp.concatenate(d_decay_all, axis=0)
    lanes = iota2((tokens, LANES), 1)
    slope = jax.nn.sigmoid(logit_ref[HALO:, :] + par_ref[1:2, :]) * -jnp.exp(par_ref[0:1, :])
    here = jnp.where(lanes == head, d_decay, 0.0)
    d_first = here * slope
    strengths = beta_ref[...]
    d_second = jnp.where(lanes == head + H, d_beta, 0.0) * strengths * (1.0 - strengths)
    dlogit_ref[...] += d_first + d_second
    dpar_ref[0:1, :] += jnp.sum(here * decay_ref[...], axis=0, keepdims=True)
    dpar_ref[1:2, :] += jnp.sum(d_first, axis=0, keepdims=True)

    dmix_ref[:HALO, :] = jnp.zeros((HALO, HC), F32)
    dmix_ref[HALO + tokens :, :] = jnp.zeros((8, HC), F32)
    d_mix = dmix_ref[HALO : HALO + tokens, :]
    dtaps_ref[...] = jnp.zeros_like(dtaps_ref)
    dtaps_ref[0:1, :] = jnp.sum(d_mix * pf_ref[HALO:, :], axis=0, keepdims=True)
    total = dmix_ref[: HALO + tokens, :] * taps_ref[0:1, :]
    for j in range(1, CONV):
        total += dmix_ref[j : j + HALO + tokens, :] * taps_ref[j : j + 1, :] * back_ref[:, j : j + 1]
        dtaps_ref[j : j + 1, :] = jnp.sum(
            d_mix * cols[:, j : j + 1] * pf_ref[HALO - j : HALO - j + tokens, :],
            axis=0,
            keepdims=True,
        )
    dp_ref[...] = total.astype(BF16)


def delta_backward(
    place, slots, proj, taps, logits, par, cols, back, segr, d_attn, state_in, exch, grads, saved
):
    rows = proj.shape[0]
    tokens = rows - HALO
    chunks = tokens // CHUNK
    places = exch.shape[0]
    whole = lambda shape: pl.BlockSpec(shape, lambda h: (0,) * len(shape))
    by_head = lambda shape: pl.BlockSpec(shape, lambda h: (h,) + (0,) * (len(shape) - 1))
    return pl.pallas_call(
        backward_kernel,
        grid=(H,),
        in_specs=[
            pl.BlockSpec(memory_space=pltpu.SMEM),
            pl.BlockSpec(memory_space=pltpu.SMEM),
            pl.BlockSpec((rows, HC), lambda h: (0, h)),
            pl.BlockSpec((8, HC), lambda h: (0, h)),
            whole((rows, LANES)),
            whole((8, LANES)),
            whole((tokens, LANES)),
            whole((rows, LANES)),
            whole(segr.shape),
            pl.BlockSpec((tokens, DV), lambda h: (0, h)),
            by_head((1, DK, DV)),
            pl.BlockSpec((places, 1, DK, DK), lambda h: (0, h, 0, DV // DK)),
            pl.BlockSpec((places, 1, DK, DV), lambda h: (0, h, 0, 0)),
            by_head((1, chunks, CHUNK, CHUNK)),
            by_head((1, tokens, DV + DK)),
            by_head((1, chunks, DK, DV)),
            by_head((1, chunks, DK, DK)),
            by_head((1, chunks, DK, DK)),
            by_head((1, chunks, CHUNK, DK)),
        ],
        out_specs=[
            pl.BlockSpec((rows, HC), lambda h: (0, h)),
            whole((tokens, LANES)),
            pl.BlockSpec((8, HC), lambda h: (0, h)),
            whole((8, LANES)),
        ],
        out_shape=[
            jax.ShapeDtypeStruct((rows, H * HC), BF16),
            jax.ShapeDtypeStruct((tokens, LANES), F32),
            jax.ShapeDtypeStruct((8, H * HC), F32),
            jax.ShapeDtypeStruct((8, LANES), F32),
        ],
        scratch_shapes=[
            pltpu.VMEM((tokens, LANES), F32),
            pltpu.VMEM((tokens, LANES), F32),
            pltpu.VMEM((tokens, LANES), F32),
            pltpu.VMEM((rows, HC), F32),
            pltpu.VMEM((tokens, HC), F32),
            pltpu.VMEM((rows + 8, HC), F32),
        ],
        compiler_params=params(),
        cost_estimate=cost(8e9 * H, 5e6 * H),
        name="delta_backward",
    )(place, slots, proj, taps, logits, par, cols, back, segr, d_attn, state_in, exch, grads, *saved)


def mixer_kernel(
    place_ref, slot_ref, part_ref, resp_ref, exch_ref, gpre_ref, gain_ref, w_ref, x_ref, gain2_ref,
    sin_ref, attn_ref, gated_ref, y_ref, h_ref,
):
    head = pl.program_id(0)
    place = place_ref[0]
    places = exch_ref.shape[0]

    def ahead(source, state):
        slot = slot_ref[source]
        return jnp.where(
            source < place,
            exch_ref[slot, 0, :, :DV].astype(F32) + mm(exch_ref[slot, 0, :, DV:], state),
            state,
        )

    state = lax.fori_loop(0, places - 1, ahead, jnp.zeros((DK, DV), F32))
    sin_ref[0] = state
    attn = part_ref[...] + mm(resp_ref[...], state)
    attn_ref[...] = attn
    scale = lax.rsqrt(jnp.mean(attn * attn, axis=-1, keepdims=True) + 1e-05)
    gate = gpre_ref[...]
    gated = (attn * scale * gain_ref[...] * (gate * jax.nn.sigmoid(gate))).astype(BF16)
    gated_ref[...] = gated

    @pl.when(head == 0)
    def _():
        y_ref[...] = x_ref[...].astype(F32)

    y_ref[...] += mm(gated, w_ref[...], NT)

    @pl.when(head == pl.num_programs(0) - 1)
    def _():
        value = y_ref[...]
        size = lax.rsqrt(jnp.mean(value * value, axis=-1, keepdims=True) + 1e-06)
        h_ref[...] = (value * size * gain2_ref[...]).astype(BF16)


def mixer_out(place, slots, part, resp, exch, gpre, gain, weights, x, gain2):
    tokens, width = x.shape
    places = exch.shape[0]
    whole = lambda shape: pl.BlockSpec(shape, lambda h: (0,) * len(shape))
    return pl.pallas_call(
        mixer_kernel,
        grid=(H,),
        in_specs=[
            pl.BlockSpec(memory_space=pltpu.SMEM),
            pl.BlockSpec(memory_space=pltpu.SMEM),
            pl.BlockSpec((tokens, DV), lambda h: (0, h)),
            pl.BlockSpec((tokens, DK), lambda h: (0, h)),
            pl.BlockSpec((places, 1, DK, DV + DK), lambda h: (0, h, 0, 0)),
            pl.BlockSpec((tokens, DV), lambda h: (0, h)),
            whole((1, DV)),
            pl.BlockSpec((width, DV), lambda h: (0, h + AT_OUT // DV)),
            whole((tokens, width)),
            whole((1, width)),
        ],
        out_specs=[
            pl.BlockSpec((1, DK, DV), lambda h: (h, 0, 0)),
            pl.BlockSpec((tokens, DV), lambda h: (0, h)),
            pl.BlockSpec((tokens, DV), lambda h: (0, h)),
            whole((tokens, width)),
            whole((tokens, width)),
        ],
        out_shape=[
            jax.ShapeDtypeStruct((H, DK, DV), F32),
            jax.ShapeDtypeStruct((tokens, H * DV), F32),
            jax.ShapeDtypeStruct((tokens, H * DV), BF16),
            jax.ShapeDtypeStruct((tokens, width), F32),
            jax.ShapeDtypeStruct((tokens, width), BF16),
        ],
        compiler_params=params(),
        cost_estimate=cost(2 * tokens * width * H * DV, 2e7),
        name="mixer_out",
    )(place, slots, part, resp, exch, gpre, gain, weights, x, gain2)


def mixer_back_kernel(
    dmix_ref, w_ref, attn_ref, gpre_ref, gain_ref, resp_ref,
    dattn_ref, dgpre_ref, grad_ref, dgain_ref,
):
    @pl.when(pl.program_id(0) == 0)
    def _():
        dgain_ref[...] = jnp.zeros_like(dgain_ref)

    d_gain, dattn_ref[...], dgpre_ref[...], grad_ref[0] = mixer_back_head(
        dmix_ref, w_ref, attn_ref, gpre_ref, gain_ref, resp_ref
    )
    dgain_ref[0:1, :] += d_gain


def mixer_back_head(dmix_ref, w_ref, attn_ref, gpre_ref, gain_ref, resp_ref):
    d_gated = mm(dmix_ref[...], w_ref[...])
    attn = attn_ref[...]
    size = lax.rsqrt(jnp.mean(attn * attn, axis=-1, keepdims=True) + 1e-05)
    unit = attn * size
    gate = gpre_ref[...]
    slope = jax.nn.sigmoid(gate)
    swish = gate * slope
    gain = gain_ref[...]
    d_gpre = (d_gated * (unit * gain) * (slope * (1.0 + gate * (1.0 - slope)))).astype(BF16)
    d_normed = d_gated * swish
    d_gain = jnp.sum(d_normed * unit, axis=0, keepdims=True)
    d_unit = d_normed * gain
    d_attn = size * (d_unit - unit * jnp.mean(d_unit * unit, axis=-1, keepdims=True))
    d_attn = d_attn.astype(BF16)
    return d_gain, d_attn, d_gpre, mm(resp_ref[...], d_attn, TN).astype(BF16)


def mixer_back(d_mixer, weights, attn, gpre, gain, resp):
    tokens, width = d_mixer.shape
    whole = lambda shape: pl.BlockSpec(shape, lambda h: (0,) * len(shape))
    return pl.pallas_call(
        mixer_back_kernel,
        grid=(H,),
        in_specs=[
            whole((tokens, width)),
            pl.BlockSpec((width, DV), lambda h: (0, h + AT_OUT // DV)),
            pl.BlockSpec((tokens, DV), lambda h: (0, h)),
            pl.BlockSpec((tokens, DV), lambda h: (0, h)),
            whole((1, DV)),
            pl.BlockSpec((tokens, DK), lambda h: (0, h)),
        ],
        out_specs=[
            pl.BlockSpec((tokens, DV), lambda h: (0, h)),
            pl.BlockSpec((tokens, DV), lambda h: (0, h)),
            pl.BlockSpec((1, DK, DV), lambda h: (h, 0, 0)),
            whole((8, DV)),
        ],
        out_shape=[
            jax.ShapeDtypeStruct((tokens, H * DV), BF16),
            jax.ShapeDtypeStruct((tokens, H * DV), BF16),
            jax.ShapeDtypeStruct((H, DK, DV), BF16),
            jax.ShapeDtypeStruct((8, DV), F32),
        ],
        compiler_params=params(),
        cost_estimate=cost(2 * tokens * width * H * DV, 2e7),
        name="mixer_back",
    )(d_mixer, weights, attn, gpre, gain, resp)


def ffn_kernel(
    h_ref, dout_ref, y_ref, gain_ref, turn_ref, wg_ref, wu_ref, wd_ref,
    out_ref, act_ref, dgu_ref, dy_ref, dmix_ref, dgain_ref, res_ref, dh_ref,
):
    step = pl.program_id(0)

    @pl.when(step == 0)
    def _():
        res_ref[...] = y_ref[...]
        dh_ref[...] = jnp.zeros_like(dh_ref)

    hidden = h_ref[...]
    w_gate, w_up, w_down = wg_ref[...], wu_ref[...], wd_ref[...]
    gate = mm(hidden, w_gate)
    up = mm(hidden, w_up)
    d_act = mm(dout_ref[...], w_down)
    slope = jax.nn.sigmoid(gate)
    swish = gate * slope
    act = (swish * up).astype(BF16)
    act_ref[...] = act
    d_gate = (d_act * up * slope * (1.0 + gate * (1.0 - slope))).astype(BF16)
    d_up = (d_act * swish).astype(BF16)
    dgu_ref[0] = d_gate
    dgu_ref[1] = d_up
    res_ref[...] += mm(act, w_down, NT)
    dh_ref[...] += mm(d_gate, w_gate, NT) + mm(d_up, w_up, NT)

    @pl.when(step == pl.num_programs(0) - 1)
    def _():
        out_ref[...] = mm(res_ref[...], turn_ref[...], NT).astype(BF16)
        value = y_ref[...]
        size = lax.rsqrt(jnp.mean(value * value, axis=-1, keepdims=True) + 1e-06)
        unit = value * size
        d_hidden = dh_ref[...]
        dgain_ref[...] = jnp.zeros_like(dgain_ref)
        dgain_ref[0:1, :] = jnp.sum(d_hidden * unit, axis=0, keepdims=True)
        d_unit = d_hidden * gain_ref[...]
        d_y = dout_ref[...].astype(F32) + size * (
            d_unit - unit * jnp.mean(d_unit * unit, axis=-1, keepdims=True)
        )
        dy_ref[...] = d_y
        dmix_ref[...] = d_y.astype(BF16)


def feed_forward(hidden, d_out, y1, gain, turn, weights, inner):
    tokens, width = hidden.shape
    block = 256
    weight = lambda at: pl.BlockSpec((width, block), lambda j: (0, j + at // block))
    whole = lambda shape: pl.BlockSpec(shape, lambda j: (0,) * len(shape))
    across = pl.BlockSpec((tokens, block), lambda j: (0, j))
    return pl.pallas_call(
        ffn_kernel,
        grid=(inner // block,),
        in_specs=[
            whole((tokens, width)),
            whole((tokens, width)),
            whole((tokens, width)),
            whole((1, width)),
            pl.BlockSpec((width, width), lambda j: (0, 0), pipeline_mode=pl.Buffered(1)),
        ]
        + [weight(AT_FFN + i * inner) for i in range(3)],
        out_specs=[
            whole((tokens, width)), across, pl.BlockSpec((2, tokens, block), lambda j: (0, 0, j)),
            whole((tokens, width)), whole((tokens, width)), whole((8, width)),
        ],
        out_shape=[
            jax.ShapeDtypeStruct((tokens, width), BF16),
            jax.ShapeDtypeStruct((tokens, inner), BF16),
            jax.ShapeDtypeStruct((2, tokens, inner), BF16),
            jax.ShapeDtypeStruct((tokens, width), F32),
            jax.ShapeDtypeStruct((tokens, width), BF16),
            jax.ShapeDtypeStruct((8, width), F32),
        ],
        scratch_shapes=[pltpu.VMEM((tokens, width), F32), pltpu.VMEM((tokens, width), F32)],
        compiler_params=params(),
        cost_estimate=cost(12 * tokens * width * inner, 3e7),
        name="feed_forward",
    )(hidden, d_out, y1, gain, turn, weights, weights, weights)


BLOCK = HC
LEAD, EVERY = 5, 3


def other_index(step):
    return step - jnp.clip((step - LEAD + EVERY - 1) // EVERY, 0, H)


class Blocks:
    def __init__(self, inner):
        self.ups, self.downs = inner // (BLOCK // 2), inner // BLOCK
        self.outs = H * DV // BLOCK
        self.others = self.ups + self.downs + 2 * self.outs
        self.count = self.others + H + 1
        self.starts = [0, self.ups, self.ups + self.downs, self.ups + self.downs + self.outs, self.others]
        self.tail = inner - self.downs * BLOCK
        heads = [LEAD + EVERY * h for h in range(H)]
        rest = [n for n in range(self.count - 1) if n not in heads]
        parts = [rest[low:high] for low, high in zip(self.starts, self.starts[1:])]
        self.up_at, self.down_at, self.out_at, self.gate_at = parts
        self.head_at = heads

    def index(self, kind):
        low, high = self.starts[kind], self.starts[kind + 1]
        return lambda s: jnp.clip(other_index(s) - low, 0, high - low - 1)


def dot_blocks(left, right):
    return lax.dot_general(left, right, (NN, ((), ())), preferred_element_type=F32)


def flip_to(bit):
    here = lax.axis_index("seq")
    along_x = here + 1 - 2 * lax.rem(here, 2)
    along_y = here + 2 - 4 * (here // 2)
    return {"dp": lax.axis_index("dp"), "seq": (2 - bit) * along_x + (bit - 1) * along_y}


def reduce_kernel(
    dout_any, hmid_any, hidden_any, x_any, dy_any, turn_any, dres_ref,
    act_ref, tail_ref, dgu_ref, gated_ref, wout_ref, attn_ref, gpre_ref, gain_ref, resp_ref, win_ref, wl_ref,
    gains_ref, dffn_ref,
    p_ref, taps_ref, logit_ref, par_ref, cols_ref, back_ref, segr_ref, sin_ref, maps_ref,
    inv_ref, upd_ref, st_ref, stm_ref, amap_ref, rmap_ref,
    sum_ref, dx_ref, small_ref,
    dlogit_ref, dtaps_ref, dpar_ref, dgain_ref, dattn_ref, dgpre_ref, lgrad_ref, acc_ref, left_ref,
    total_ref, other_ref,
    beta_ref, decay_ref, cum_ref, pf_ref, pre_ref, dmix_ref,
    turn_ref, dps_ref, halo_ref, grads_ref, halves_ref,
    core_keep, core_send, core_recv, near_keep, near_send, near_recv,
    z_keep, pair_send, pair_recv, cross_send, cross_recv, far_send, far_recv, done_ref,
    core_ss, core_rs, near_ss, near_rs, pair_ss, pair_rs, cross_ss, cross_rs, far_ss, far_rs, done_ss, done_rs, own_sem,
    halo_ss, halo_rs, grads_ss, grads_rs, load_sem, small_ss, small_rs, *, blocks,
):
    step = pl.program_id(0)
    steps = pl.num_programs(0)
    place = lax.axis_index("seq")
    count = blocks.count
    half = core_keep.shape[1] * core_keep.shape[2]
    quarter = half // SPOTS
    piece = quarter // PLANES
    mesh = dict(device_id_type=pl.DeviceIdType.MESH)

    def remote(source, target, send, recv, to):
        return pltpu.make_async_remote_copy(
            src_ref=source, dst_ref=target, send_sem=send, recv_sem=recv, device_id=to, **mesh
        )

    def to_core(n):
        mine, slot = lax.rem(n, 3), lax.rem(n, 4)
        return remote(core_send.at[mine], core_recv.at[slot], core_ss.at[mine], core_rs.at[slot], device(core=1))

    def to_near(n):
        slot = lax.rem(n, 4)
        return remote(
            near_send.at[slot], near_recv.at[slot], near_ss.at[slot], near_rs.at[slot], flip_to(1 + lax.rem(n, 2))
        )

    def to_far(n):
        slot = lax.rem(n, 4)
        return remote(
            far_send.at[slot], far_recv.at[slot], far_ss.at[slot], far_rs.at[slot], flip_to(2 - lax.rem(n, 2))
        )

    z = lax.axis_index("dp") // CORES
    inner = (z > 0) & (z < PLANES - 1)
    outer_plane = (z == 0) | (z == PLANES - 1)

    def to_pair(n, pieces):
        slot = lax.rem(n, 4)
        return remote(
            pair_send.at[slot, 0:pieces], pair_recv.at[slot, 0:pieces], pair_ss.at[slot], pair_rs.at[slot],
            device(planes=1 + 2 * lax.rem(z, 2)),
        )

    def to_cross(n, outside):
        planes = 2 if outside else 2 * z - 1
        slot = lax.rem(n, 4)
        return remote(
            cross_send.at[slot, outside], cross_recv.at[n], cross_ss.at[slot, outside], cross_rs.at[n],
            device(planes=planes),
        )

    def target(n, which):
        spot = place if which == 0 else flip_spot(place, 2 - lax.rem(n, 2))
        return sum_ref.at[
            pl.ds(pl.multiple_of(spot * piece, piece), piece), pl.ds(pl.multiple_of(n * BLOCK, BLOCK), BLOCK)
        ]

    def spread(n, which):
        slot = lax.rem(n, 4)
        return remote(
            done_ref.at[slot, which], target(n, which), done_ss.at[slot, which], done_rs.at[n, which],
            flip_to(1 + lax.rem(n, 2)),
        )

    def keep(n, which):
        slot = lax.rem(n, 4)
        return pltpu.make_async_copy(done_ref.at[slot, which], target(n, which), own_sem.at[slot, which])

    upper = place // 2 == 1
    second = lax.rem(place, 2) == 1

    def give_grads(head):
        return remote(
            lgrad_ref.at[head], grads_ref.at[0, head], grads_ss.at[0, head], grads_rs.at[0, head], device(spot=1)
        )

    def give_half(head):
        return remote(
            halves_ref.at[head], grads_ref.at[1, head], grads_ss.at[1, head], grads_rs.at[1, head], device(spot=2)
        )

    def give_small(stage):
        to = (dict(core=1), dict(spot=1), dict(spot=2), dict(planes=1), dict(planes=2), dict(planes=3))[stage]
        return remote(
            total_ref.at[min(stage, 3)], other_ref.at[stage], small_ss.at[stage], small_rs.at[stage], device(**to)
        )

    def load(at, source, to):
        return pltpu.make_async_copy(source, to, load_sem.at[at])

    def final_loads():
        width = turn_any.shape[0]
        copies = []
        for n in range(2):
            cols = slice(n * (width // 2), (n + 1) * (width // 2))
            copies.append(load(n, turn_any.at[:, cols], turn_ref.at[n]))
            rows = x_any.shape[0]
            copies.append(load(2 + n, x_any.at[:, cols], turn_ref.at[2, n * rows : (n + 1) * rows]))
            for q in range(SPOTS):
                copies.append(
                    load(4 + n * SPOTS + q, dy_any.at[q * quarter : (q + 1) * quarter, cols], core_keep.at[n, q])
                )
        return copies

    def final_stores():
        width = dx_ref.shape[1]
        return [
            load(
                n * SPOTS + q,
                core_keep.at[n, q],
                dx_ref.at[q * quarter : (q + 1) * quarter, n * (width // 2) : (n + 1) * (width // 2)],
            )
            for n in range(2)
            for q in range(SPOTS)
        ]

    def give_halo(head):
        to = {"dp": lax.axis_index("dp"), "seq": lax.rem(place + SPOTS - 1, SPOTS)}
        return remote(dps_ref.at[0:HALO], halo_ref.at[head], halo_ss.at[head], halo_rs.at[head], to)

    @pl.when(step == 0)
    def _():
        greet([dict(planes=d) for d in (1, 2, 3)] + [dict(spot=s) for s in (1, 2, 3)] + [dict(core=1)])
        dgain_ref[...] = jnp.zeros_like(dgain_ref)
        acc_ref[...] = jnp.zeros_like(acc_ref)

    def left(n):
        tokens = dres_ref.shape[0]
        source = (hmid_any, dout_any, hidden_any.at[HALO : HALO + tokens])[n]
        return load(n, source, left_ref.at[n % 2])

    for n, at in enumerate((1, 0, 3, 2)):

        @pl.when(step == n)
        def _(n=n, at=at):
            if n == 0:
                left(0).start()
            if n < 2:
                left(n + 1).start()
            if n < 3:
                left(n).wait()
                turn_ref[at] = jnp.transpose(left_ref[n % 2])
            else:
                turn_ref[at] = jnp.transpose(dres_ref[...])

    def at_stage(lag, sent):
        n = step - lag

        def run(body):
            @pl.when((n >= 0) & (n < count))
            def _():
                @pl.when(n >= sent)
                def _():
                    body(n, True)

                body(n, False)

        return run

    @at_stage(10, 4)
    def _(n, free):
        if free:
            for which in range(2):
                spread(n - 4, which).wait_send()
                keep(n - 4, which).wait()
            return
        slot = lax.rem(n, 4)
        to_far(n).wait_recv()
        for which in range(2):
            total = far_send[slot, which].astype(F32) + far_recv[slot, 1 - which].astype(F32)
            done_ref[slot, which] = total.astype(BF16)
            keep(n, which).start()
            spread(n, which).start()

    @at_stage(8, 4)
    def _(n, free):
        if free:
            to_far(n - 4).wait_send()
            return
        slot = lax.rem(n, 4)
        to_cross(n, 0).wait_recv()
        total = (z_keep[slot, 0] + cross_recv[n].astype(F32)).astype(BF16)
        far_send[slot, 0], far_send[slot, 1] = total[:piece], total[piece:]
        to_far(n).start()

    @at_stage(6, 4)
    def _(n, free):
        slot = lax.rem(n, 4)
        if free:

            @pl.when(inner)
            def _():
                to_cross(n - 4, 0).wait_send()
                to_cross(n - 4, 1).wait_send()

            return

        @pl.when(outer_plane)
        def _():
            to_pair(n, 1).wait_recv()

        @pl.when(inner)
        def _():
            to_pair(n, 3).wait_recv()
            for outside, at in enumerate((5 - 2 * z, 2)):
                cross_send[slot, outside] = (
                    z_keep[slot, at] + pair_recv[slot, 1 + outside].astype(F32)
                ).astype(BF16)
                to_cross(n, outside).start()

        z_keep[slot, 0] += pair_recv[slot, 0].astype(F32)

    @at_stage(4, 4)
    def _(n, free):
        slot = lax.rem(n, 4)
        if free:

            @pl.when(outer_plane)
            def _():
                to_pair(n - 4, 3).wait_send()

            @pl.when(inner)
            def _():
                to_pair(n - 4, 1).wait_send()

            return
        to_near(n).wait_recv()
        for which in range(2):
            total = near_keep[slot, which] + near_recv[slot, which].astype(F32)
            for d in range(PLANES):
                z_keep[slot, d, which * piece : (which + 1) * piece] = total[d * piece : (d + 1) * piece]

        @pl.when(outer_plane)
        def _():
            up = 1 - z // 3
            for k in range(3):
                pair_send[slot, k] = z_keep[slot, up * (3 - k) + (1 - up) * (1 + k)].astype(BF16)
            to_pair(n, 3).start()

        @pl.when(inner)
        def _():
            pair_send[slot, 0] = z_keep[slot, 2 * z - 1].astype(BF16)
            to_pair(n, 1).start()

    @at_stage(2, 4)
    def _(n, free):
        if free:
            to_near(n - 4).wait_send()
            return
        slot, mine = lax.rem(n, 4), lax.rem(n, 3)
        first = 1 + lax.rem(n, 2)
        to_core(n).wait_recv()
        whole = lambda quarter: core_keep[mine, quarter] + core_recv[slot, quarter].astype(F32)
        near_keep[slot, 0] = whole(0)
        near_keep[slot, 1] = whole(3 - first)
        near_send[slot, 0] = whole(first).astype(BF16)
        near_send[slot, 1] = whole(3).astype(BF16)
        to_near(n).start()

    since = step - LEAD
    heads_turn = (since >= 0) & (since < EVERY * H) & (lax.rem(jnp.maximum(since, 0), EVERY) == 0)
    other = other_index(step)

    def put(product):
        mine = lax.rem(step, 3)

        @pl.when(step >= 3)
        def _():
            to_core(step - 3).wait_send()

        for q in range(SPOTS):
            core_keep[mine, q] = product[q * quarter : (q + 1) * quarter]
            core_send[mine, q] = product[half + q * quarter : half + (q + 1) * quarter].astype(BF16)
        to_core(step).start()

    def on(kind):
        low, high = blocks.starts[kind], blocks.starts[kind + 1]
        return pl.when((other >= low) & (other < high) & jnp.logical_not(heads_turn))

    @on(0)
    def _():
        put(dot_blocks(turn_ref[1], jnp.concatenate([dgu_ref[0], dgu_ref[1]], axis=1)))

    @on(1)
    def _():
        put(dot_blocks(turn_ref[0], act_ref[...]))

    @on(2)
    def _():
        put(dot_blocks(turn_ref[2], gated_ref[...]))

    @on(3)
    def _():
        gate = other - blocks.starts[3]
        value = jnp.concatenate([dgpre_ref[2 * gate], dgpre_ref[2 * gate + 1]], axis=1)
        acc_ref[...] += mm(value, win_ref[...], NT)
        put(dot_blocks(turn_ref[3], value))

    @pl.when(step == count - 1)
    def _():
        down = dot_blocks(turn_ref[0], tail_ref[...])
        gates = dot_blocks(turn_ref[3], dlogit_ref[...].astype(BF16))
        acc_ref[...] += mm(dlogit_ref[...], wl_ref[...], NT)
        rest = jnp.zeros((down.shape[0], BLOCK - down.shape[1] - LANES), F32)
        put(jnp.concatenate([down, gates, rest], axis=1))

    @pl.when(heads_turn)
    def _():
        head = since // EVERY

        @pl.when(place > 0)
        def _():
            give_halo(head).wait_send()

        @pl.when(place < SPOTS - 1)
        def _():
            give_halo(head).wait_recv()
            tokens = dps_ref.shape[0] - HALO
            dps_ref[tokens:, :] = (
                dps_ref[tokens:, :].astype(F32) + halo_ref[head].astype(F32)
            ).astype(BF16)

        value = dps_ref[HALO:, :]
        acc_ref[...] += mm(value, win_ref[...], NT)
        put(dot_blocks(turn_ref[3], value))

    @pl.when(step < H)
    def _():
        d_gain, dattn_ref[step], dgpre_ref[step], lgrad_ref[step] = mixer_back_head(
            dres_ref, wout_ref, attn_ref, gpre_ref, gain_ref, resp_ref
        )
        dgain_ref[...] += d_gain
        give_grads(step).start()

    @pl.when((step >= 2) & (step < H + 2))
    def _():
        head = step - 2
        give_grads(head).wait()

        @pl.when(upper)
        def _():
            mine, theirs = lgrad_ref[head], grads_ref[0, head]
            earlier = jnp.where(second, theirs, mine)
            later = jnp.where(second, mine, theirs)
            through = jnp.where(second, maps_ref[1, head], maps_ref[0, head])
            halves_ref[head] = (earlier.astype(F32) + mm(through, later, TN)).astype(BF16)
            give_half(head).start()

    @pl.when((since >= -1) & (since < EVERY * H - 1) & (lax.rem(jnp.maximum(since + 1, 0), EVERY) == 0))
    def _():
        head = (since + 1) // EVERY

        @pl.when(upper)
        def _():
            grads_ref[1, head] = jnp.zeros((DK, DV), BF16)
            give_half(head).wait_send()

        @pl.when(jnp.logical_not(upper))
        def _():
            give_half(head).wait_recv()

        d_state = grads_ref[1, head].astype(F32)
        nearer = grads_ref[0, head].astype(F32) + mm(maps_ref[1, head], d_state, TN)
        d_state = jnp.where(second, d_state, nearer)
        backward_head(
            head, d_state, p_ref, taps_ref, logit_ref, par_ref, cols_ref, back_ref, segr_ref,
            dattn_ref.at[head], sin_ref, inv_ref, upd_ref, st_ref, stm_ref, amap_ref, rmap_ref,
            dps_ref, dlogit_ref, dtaps_ref, dpar_ref, beta_ref, decay_ref, cum_ref, pf_ref, pre_ref, dmix_ref,
        )
        total_ref[0, pl.ds(pl.multiple_of(head * 8, 8), 8), :] = dtaps_ref[...]

        @pl.when(place > 0)
        def _():
            give_halo(head).start()

    @pl.when(step == count)
    def _():
        for copy in final_loads():
            copy.start()

    @pl.when(step == count + 2)
    def _():
        for copy in final_loads():
            copy.wait()
        tokens, width = acc_ref.shape
        middle = width // 2
        halves_of = lambda ref: jnp.concatenate([ref[0], ref[1]], axis=1)
        value = jnp.concatenate([turn_ref[2, :tokens], turn_ref[2, tokens:]], axis=1).astype(F32)
        size = lax.rsqrt(jnp.mean(value * value, axis=-1, keepdims=True) + 1e-06)
        unit = value * size
        d_hidden = acc_ref[...]
        d_gain = jnp.sum(d_hidden * unit, axis=0, keepdims=True)
        d_unit = d_hidden * gains_ref[0:1, :]
        through = size * (d_unit - unit * jnp.mean(d_unit * unit, axis=-1, keepdims=True))
        d_y = [jnp.concatenate([core_keep[n, q] for q in range(SPOTS)], axis=0) for n in range(2)]
        total = jnp.concatenate(d_y, axis=1) + through

        def natural(part):
            return mm(part[:, :middle], turn_ref[0], NT) + mm(part[:, middle:], turn_ref[1], NT)

        high, low = halves(total)
        total = natural(high) + natural(low)
        for n in range(2):
            for q in range(SPOTS):
                core_keep[n, q] = total[q * quarter : (q + 1) * quarter, n * middle : (n + 1) * middle]
        for copy in final_stores():
            copy.start()
        gains = jnp.concatenate([d_gain, dffn_ref[0:1, :], jnp.zeros((6, width), F32)], axis=0)
        high, mid = halves(gains)
        gains = natural(high) + natural(mid) + natural((gains - high.astype(F32)) - mid.astype(F32))
        base = 8 * H
        total_ref[0, base : base + 8, :] = gains[:, :middle]
        total_ref[0, base + 8 : base + 16, :] = gains[:, middle:]
        total_ref[0, base + 16 : base + 24, : dgain_ref.shape[1]] = dgain_ref[...]
        total_ref[0, base + 16 : base + 24, dgain_ref.shape[1] : dgain_ref.shape[1] + LANES] = dpar_ref[...]
        total_ref[0, base + 16 : base + 24, dgain_ref.shape[1] + LANES :] = jnp.zeros((8, LANES), F32)
        give_small(0).start()

    for stage in range(3):

        @pl.when(step == count + 3 + stage)
        def _(stage=stage):
            give_small(stage).wait_recv()
            total_ref[stage + 1] = total_ref[stage] + other_ref[stage]
            for later in (stage + 1,) if stage < 2 else (3, 4, 5):
                give_small(later).start()

    @pl.when(step == count + 6)
    def _():
        total = total_ref[3]
        for stage in (3, 4, 5):
            give_small(stage).wait_recv()
            total += other_ref[stage]
        small_ref[...] = total
        for stage in range(6):
            give_small(stage).wait_send()
        for copy in final_stores():
            copy.wait()

    @pl.when(step == steps - 1)
    def _():
        for n in range(count - 4, count):
            if n >= count - 3:
                to_core(n).wait_send()
            to_near(n).wait_send()
            to_far(n).wait_send()

            @pl.when(outer_plane)
            def _(n=n):
                to_pair(n, 3).wait_send()

            @pl.when(inner)
            def _(n=n):
                to_pair(n, 1).wait_send()
                to_cross(n, 0).wait_send()
                to_cross(n, 1).wait_send()

            for which in range(2):
                spread(n, which).wait_send()
                keep(n, which).wait()

        def arrived(n, carry):
            for which in range(2):
                spread(n, which).wait_recv()
            return carry

        lax.fori_loop(0, count, arrived, 0)


def reduce_gradients(
    d_out, hidden_mid, hidden, x, d_y, turn, d_mixer, act, d_gu, gated, weights, attn, gpre, gain_out, resp, gains,
    d_ffn, proj, taps, logits, par, cols, back, segr, state_in, maps, saved,
):
    tokens, width = d_mixer.shape
    rows = hidden.shape[0]
    chunks = tokens // CHUNK
    blocks = Blocks(act.shape[1])
    half = width // CORES
    quarter = half // SPOTS
    piece = quarter // PLANES
    small = 8 * H + 24
    anywhere = pl.BlockSpec(memory_space=pl.ANY)
    whole = lambda shape: pl.BlockSpec(shape, lambda s: (0,) * len(shape))
    once = lambda shape: pl.BlockSpec(shape, lambda s: (0,) * len(shape), pipeline_mode=pl.Buffered(1))
    coming = lambda s: jnp.clip((s + EVERY - LEAD) // EVERY, 0, H - 1)
    starting = lambda s: jnp.minimum(s, H - 1)
    by_head = lambda shape: pl.BlockSpec(shape, lambda s: (coming(s),) + (0,) * (len(shape) - 1))
    across = lambda shape, at: pl.BlockSpec(shape, lambda s: (0, at(s)))
    sem = pltpu.SemaphoreType.DMA
    up, down, out, gate = (blocks.index(kind) for kind in range(4))
    first_gate = blocks.gate_at[0]

    def win(s):
        no_head = ((s - LEAD) % EVERY != 0) | (s > blocks.head_at[-1])
        is_gate = (s >= first_gate) & (s <= blocks.gate_at[-1]) & no_head
        head = jnp.clip((s - LEAD + EVERY - 1) // EVERY, 0, H - 1)
        return jnp.where(is_gate, AT_GATE // BLOCK + gate(s), H - 1 - head)

    return blocks, pl.pallas_call(
        functools.partial(reduce_kernel, blocks=blocks),
        grid=(blocks.count + 10,),
        in_specs=[anywhere] * 6
        + [
            once((tokens, width)),
            across((tokens, BLOCK), down),
            pl.BlockSpec(
                (tokens, blocks.tail), lambda s: (0, blocks.downs * BLOCK // blocks.tail), pipeline_mode=pl.Buffered(1)
            ),
            pl.BlockSpec((2, tokens, BLOCK // 2), lambda s: (0, 0, up(s))),
            across((tokens, BLOCK), out),
            pl.BlockSpec((width, DV), lambda s: (0, AT_OUT // DV + starting(s))),
            across((tokens, DV), starting),
            across((tokens, DV), starting),
            once((1, DV)),
            across((tokens, DK), starting),
            across((width, BLOCK), win),
            pl.BlockSpec((width, LANES), lambda s: (0, AT_LOGIT // LANES), pipeline_mode=pl.Buffered(1)),
            once((8, width)),
            once((8, width)),
            across((rows, HC), coming),
            across((8, HC), coming),
            once((rows, LANES)),
            once((8, LANES)),
            once((tokens, LANES)),
            once((rows, LANES)),
            once(segr.shape),
            by_head((1, DK, DV)),
            once((2, H, DK, DK)),
            by_head((1, chunks, CHUNK, CHUNK)),
            by_head((1, tokens, DV + DK)),
            by_head((1, chunks, DK, DV)),
            by_head((1, chunks, DK, DK)),
            by_head((1, chunks, DK, DK)),
            by_head((1, chunks, CHUNK, DK)),
        ],
        out_specs=[anywhere, anywhere, whole((small, BLOCK))],
        out_shape=[
            jax.ShapeDtypeStruct((SPOTS * piece, blocks.count * BLOCK), BF16),
            jax.ShapeDtypeStruct((tokens, width), F32),
            jax.ShapeDtypeStruct((small, BLOCK), F32),
        ],
        scratch_shapes=[
            pltpu.VMEM((tokens, LANES), F32),
            pltpu.VMEM((8, HC), F32),
            pltpu.VMEM((8, LANES), F32),
            pltpu.VMEM((8, DV), F32),
            pltpu.VMEM((H, tokens, DV), BF16),
            pltpu.VMEM((H, tokens, DV), BF16),
            pltpu.VMEM((H, DK, DV), BF16),
            pltpu.VMEM((tokens, width), F32),
            pltpu.VMEM((2, tokens, width), BF16),
            pltpu.VMEM((4, small, BLOCK), F32),
            pltpu.VMEM((6, small, BLOCK), F32),
            pltpu.VMEM((tokens, LANES), F32),
            pltpu.VMEM((tokens, LANES), F32),
            pltpu.VMEM((tokens, LANES), F32),
            pltpu.VMEM((rows, HC), F32),
            pltpu.VMEM((tokens, HC), F32),
            pltpu.VMEM((rows + 8, HC), F32),
            pltpu.VMEM((4, width, tokens), BF16),
            pltpu.VMEM((rows, HC), BF16),
            pltpu.VMEM((H, HALO, HC), BF16),
            pltpu.VMEM((2, H, DK, DV), BF16),
            pltpu.VMEM((H, DK, DV), BF16),
            pltpu.VMEM((3, SPOTS, quarter, BLOCK), F32),
            pltpu.VMEM((3, SPOTS, quarter, BLOCK), BF16),
            pltpu.VMEM((4, SPOTS, quarter, BLOCK), BF16),
            pltpu.VMEM((4, 2, quarter, BLOCK), F32),
            pltpu.VMEM((4, 2, quarter, BLOCK), BF16),
            pltpu.VMEM((4, 2, quarter, BLOCK), BF16),
            pltpu.VMEM((4, PLANES, 2 * piece, BLOCK), F32),
            pltpu.VMEM((4, PLANES - 1, 2 * piece, BLOCK), BF16),
            pltpu.VMEM((4, PLANES - 1, 2 * piece, BLOCK), BF16),
            pltpu.VMEM((4, 2, 2 * piece, BLOCK), BF16),
            pltpu.VMEM((blocks.count, 2 * piece, BLOCK), BF16),
            pltpu.VMEM((4, 2, piece, BLOCK), BF16),
            pltpu.VMEM((4, 2, piece, BLOCK), BF16),
            pltpu.VMEM((4, 2, piece, BLOCK), BF16),
            sem((3,)), sem((4,)), sem((4,)), sem((4,)), sem((4,)), sem((4,)),
            sem((4, 2)), sem((blocks.count,)), sem((4,)), sem((4,)),
            sem((4, 2)), sem((blocks.count, 2)), sem((4, 2)),
            sem((H,)), sem((H,)), sem((2, H)), sem((2, H)),
            sem((4 + 2 * SPOTS,)), sem((6,)), sem((6,)),
        ],
        compiler_params=params(collective_id=1, has_side_effects=True),
        cost_estimate=cost(1e11, 1e8),
        name="reduce_gradients",
    )(
        d_out, hidden_mid, hidden, x, d_y, turn, d_mixer, act, act, d_gu, gated, weights, attn, gpre, gain_out, resp,
        weights, weights, gains, d_ffn, proj, taps, logits, par, cols, back, segr, state_in, maps, *saved,
    )


def unpack_kernel(
    sum_ref, query_ref, key_ref, value_ref, gate_ref, logit_ref, out_ref, wg_ref, wu_ref, wd_ref, *, blocks
):
    def part(n, low=0, high=BLOCK):
        return sum_ref[:, n * BLOCK + low : n * BLOCK + high].astype(F32)

    for h, n in enumerate(blocks.head_at):
        query_ref[:, h * DK : (h + 1) * DK] = part(n, 0, DK)
        key_ref[:, h * DK : (h + 1) * DK] = part(n, DK, 2 * DK)
        value_ref[:, h * DV : (h + 1) * DV] = part(n, 2 * DK, HC)
    for i, n in enumerate(blocks.gate_at):
        gate_ref[:, i * BLOCK : (i + 1) * BLOCK] = part(n)
    for i, n in enumerate(blocks.out_at):
        out_ref[i * BLOCK : (i + 1) * BLOCK, :] = jnp.transpose(part(n))
    middle = BLOCK // 2
    for i, n in enumerate(blocks.up_at):
        wg_ref[:, i * middle : (i + 1) * middle] = part(n, 0, middle)
        wu_ref[:, i * middle : (i + 1) * middle] = part(n, middle, BLOCK)
    for i, n in enumerate(blocks.down_at):
        wd_ref[i * BLOCK : (i + 1) * BLOCK, :] = jnp.transpose(part(n))
    last, tail = blocks.count - 1, blocks.tail
    wd_ref[blocks.downs * BLOCK :, :] = jnp.transpose(part(last, 0, tail))
    logit_ref[...] = part(last, tail, tail + LANES)


def unpack_gradients(blocks, sums):
    rows = sums.shape[0]
    inner = blocks.downs * BLOCK + blocks.tail
    shapes = [
        (rows, H * DK), (rows, H * DK), (rows, H * DV), (rows, H * DV), (rows, LANES), (H * DV, rows),
        (rows, inner), (rows, inner), (inner, rows),
    ]
    return pl.pallas_call(
        functools.partial(unpack_kernel, blocks=blocks),
        out_shape=[jax.ShapeDtypeStruct(shape, F32) for shape in shapes],
        compiler_params=params(),
        cost_estimate=cost(0, 6 * sums.size),
        name="unpack_gradients",
    )(sums)


def input_grad_kernel(
    dp_ref, dg_ref, dl_ref, w_ref, wl_ref, x_ref, gain_ref, dy_ref, out_ref, dgain_ref, acc_ref
):
    step = pl.program_id(0)

    @pl.when(step == 0)
    def _():
        acc_ref[...] = mm(dl_ref[...], wl_ref[...], NT)

    @pl.when(step < H)
    def _():
        acc_ref[...] += mm(dp_ref[...], w_ref[...], NT)

    @pl.when(step >= H)
    def _():
        acc_ref[...] += mm(dg_ref[...], w_ref[...], NT)

    @pl.when(step == pl.num_programs(0) - 1)
    def _():
        value = x_ref[...].astype(F32)
        size = lax.rsqrt(jnp.mean(value * value, axis=-1, keepdims=True) + 1e-06)
        unit = value * size
        d_hidden = acc_ref[...]
        dgain_ref[...] = jnp.zeros_like(dgain_ref)
        dgain_ref[0:1, :] = jnp.sum(d_hidden * unit, axis=0, keepdims=True)
        d_unit = d_hidden * gain_ref[...]
        out_ref[...] = dy_ref[...] + size * (
            d_unit - unit * jnp.mean(d_unit * unit, axis=-1, keepdims=True)
        )


def input_grad(d_proj, d_gpre, d_logit, weights, x, gain, d_y):
    tokens, width = x.shape
    block = HC
    second = d_gpre.shape[1] // block
    steps = H + second
    whole = lambda shape: pl.BlockSpec(shape, lambda j: (0,) * len(shape))
    late = lambda j: (0, jnp.maximum(j - H, 0))
    weight = lambda j: (0, jnp.where(j < H, H - 1 - j, j - H + AT_GATE // block))
    in_specs = [
        pl.BlockSpec((tokens, block), lambda j: (0, jnp.minimum(j, H - 1))),
        pl.BlockSpec((tokens, block), late),
        whole((tokens, LANES)),
        pl.BlockSpec((width, block), weight),
        pl.BlockSpec((width, LANES), lambda j: (0, AT_LOGIT // LANES)),
        whole((tokens, width)),
        whole((1, width)),
        whole((tokens, width)),
    ]
    return pl.pallas_call(
        input_grad_kernel,
        grid=(steps,),
        in_specs=in_specs,
        out_specs=[whole((tokens, width)), whole((8, width))],
        out_shape=[
            jax.ShapeDtypeStruct((tokens, width), F32),
            jax.ShapeDtypeStruct((8, width), F32),
        ],
        scratch_shapes=[pltpu.VMEM((tokens, width), F32)],
        compiler_params=params(),
        cost_estimate=cost(2 * tokens * width * steps * block, 3e7),
        name="input_grad",
    )(d_proj, d_gpre, d_logit, weights, weights, x, gain, d_y)


def shifted(block, axis, distance):
    devices = range(lax.axis_size(axis))
    route = [(i - distance, i) for i in devices if i - distance in devices]
    return lax.ppermute(block, axis, route)


def plain_sum(left, right, skip_left=0):
    part = lax.psum_scatter(outer(left, right, skip_left), "dp", scatter_dimension=0, tiled=True)
    return lax.psum(part, "seq").astype(F32)


def by_heads(query, key, value):
    lead = query.shape[:-1]
    parts = [query.reshape(lead + (H, DK)), key.reshape(lead + (H, DK)), value.reshape(lead + (H, DV))]
    return jnp.concatenate(parts, axis=-1).reshape(lead + (H * HC,))


def from_heads(value, heads=H):
    lead = value.shape[:-1]
    parts = value.reshape(lead + (heads, HC))
    return (
        parts[..., :DK].reshape(lead + (heads * DK,)),
        parts[..., DK : 2 * DK].reshape(lead + (heads * DK,)),
        parts[..., 2 * DK :].reshape(lead + (heads * DV,)),
    )


def token_rows(segments, place, tokens):
    ext = jnp.pad(segments, (HALO, LANES), constant_values=-1)
    ext = lax.dynamic_slice_in_dim(ext, place * tokens, tokens + LANES)
    seg = ext[HALO : HALO + tokens]
    blocks = seg.reshape(-1, CHUNK)
    before = ext[HALO - 1 : HALO - 1 + tokens : CHUNK]
    near = [seg] + [ext[HALO - j : HALO - j + tokens] == seg for j in range(1, CONV)]
    near += [(blocks == before[:, None]).reshape(-1), (blocks == blocks[:, -1:]).reshape(-1)]
    near = jnp.stack([row.astype(F32) for row in near])
    later = jnp.stack([(jnp.roll(ext, -j) == ext).astype(F32) for j in range(CONV)])
    return jnp.pad(near, ((0, 8 - near.shape[0]), (0, 0))), jnp.pad(later, ((0, 8 - CONV), (0, 0)))


def wide(value):
    return jnp.pad(value, ((0, 0), (0, LANES - value.shape[1])))


def local(
    inputs, segments, cotangent, norm_gain_mix, w_query, w_key, w_value, w_outgate, w_gates,
    conv_weight, decay_log, dt_bias, out_norm_gain, w_out, norm_gain_ffn, w_ffn_gate, w_ffn_up, w_ffn_down,
):
    tokens, width = inputs.shape[1:]
    place = lax.axis_index("seq")
    planned = (lax.axis_size("dp"), lax.axis_size("seq")) == (PLANES * CORES, SPOTS)
    low = lambda a: a.astype(BF16)
    inner = w_ffn_gate.shape[1]
    gain_out = out_norm_gain[None]
    taps_parts = by_heads(conv_weight[:, : H * DK], conv_weight[:, H * DK : 2 * H * DK], conv_weight[:, 2 * H * DK :])
    taps = jnp.pad(taps_parts, ((0, 8 - CONV), (0, 0)))
    par = jnp.pad(jnp.stack([decay_log, dt_bias]), ((0, 6), (0, LANES - H)))
    segr, later = token_rows(segments[0], place, tokens)

    if planned:
        gains = jnp.pad(jnp.stack([norm_gain_mix, norm_gain_ffn]), ((0, 6), (0, 0)))
        shards = (w_query, w_key, w_value, w_outgate, w_gates, w_out, w_ffn_gate, w_ffn_up, w_ffn_down)
        outs = mixer_forward(inputs[0], cotangent[0], shards, gains, gain_out, taps, par, segr, later)
        weights, hidden, x, d_out, turn, y1, hidden_mid, gains, cols, back, proj, logits, resp, *outs = outs
        saved, (maps, state_in, attn, gpre, gated) = outs[:6], outs[6:]
        gain_mix, gain_ffn = gains[0:1], gains[1:2]
    else:
        turn = jnp.eye(width, dtype=BF16)
        qkv = by_heads(low(w_query), low(w_key), low(w_value))
        qkv = jnp.concatenate([qkv[:, h * HC : (h + 1) * HC] for h in reversed(range(H))], axis=1)
        gates = jnp.pad(low(w_gates), ((0, 0), (0, AT_GATE - AT_LOGIT - 2 * H)))
        shard = [qkv, gates, low(w_outgate), low(w_out).T, low(w_ffn_gate), low(w_ffn_up), low(w_ffn_down).T]
        weights = lax.all_gather(jnp.concatenate(shard, axis=1), "dp", axis=0, tiled=True)
        gain_mix, gain_ffn = norm_gain_mix[None], norm_gain_ffn[None]
        cols = jnp.pad(segr.T, ((0, 0), (0, LANES - segr.shape[0])))
        back = jnp.pad(later.T[: tokens + HALO], ((0, 0), (0, LANES - later.shape[0])))
        x, d_out = inputs[0], cotangent[0]
        value = jnp.concatenate([shifted(x[tokens - HALO :], "seq", 1), x], axis=0).astype(F32)
        size = lax.rsqrt(jnp.mean(value * value, axis=-1, keepdims=True) + 1e-06)
        hidden = low(value * size * gain_mix)
        proj, logits, part, resp, exch, *saved = delta_forward(hidden, weights, taps, par, cols, segr)
        exch = lax.all_gather(exch[0], "seq")
        slots = jnp.arange(exch.shape[0], dtype=jnp.int32)
        place_arr = place.reshape((1,)).astype(jnp.int32)
        gpre = outgate(hidden, weights)
        state_in, attn, gated, y1, hidden_mid = mixer_out(
            place_arr, slots, part, resp, exch, gpre, gain_out, weights, x, gain_ffn
        )
    result, act, d_gu, d_y, d_mixer, d_gain_ffn = feed_forward(
        hidden_mid, d_out, y1, gain_ffn, turn, weights, inner
    )
    if planned:
        blocks, (sums, d_inputs, small) = reduce_gradients(
            d_out, hidden_mid, hidden, x, d_y, turn, d_mixer, act, d_gu, gated, weights, attn, gpre, gain_out, resp,
            gains, d_gain_ffn, proj, taps, logits, par, cols, back, segr, state_in, maps, saved,
        )
        g_query, g_key, g_value, g_og, g_gates, g_out, g_gate, g_up, g_down = unpack_gradients(blocks, sums)
        d_taps = small[: 8 * H].reshape(H, 8, HC)[:, :CONV].transpose(1, 0, 2).reshape(CONV, H * HC)
        rest = small[8 * H :]
        d_gains = jnp.concatenate([rest[:2], rest[8:10]], axis=1)
        d_gain_mix, d_gain_ffn = d_gains[0], d_gains[1]
        d_gain_out, d_par = rest[16, :DV], rest[16:18, DV : DV + H]
        d_conv = jnp.concatenate(from_heads(d_taps), axis=1)
        d_decay_log, d_dt_bias = d_par[0], d_par[1]
    else:
        d_attn, d_gpre, local_grad, d_gain_out = mixer_back(d_mixer, weights, attn, gpre, gain_out, resp)
        grads = lax.all_gather(local_grad, "seq")
        d_proj, d_logits, d_taps, d_par = delta_backward(
            place_arr, slots, proj, taps, logits, par, cols, back, segr, d_attn, state_in, exch, grads, saved
        )
        sent_back = shifted(d_proj[:HALO], "seq", -1)
        d_proj = d_proj.at[tokens:].add(sent_back)[HALO:]
        d_logit = low(d_logits)
        g_down = plain_sum(d_out, act).T
        g_gate = plain_sum(hidden_mid, d_gu[0])
        g_up = plain_sum(hidden_mid, d_gu[1])
        g_out = plain_sum(d_mixer, gated).T
        g_og = plain_sum(hidden, d_gpre, HALO)
        g_query, g_key, g_value = from_heads(plain_sum(hidden, d_proj, HALO))
        g_gates = plain_sum(hidden, d_logit, HALO)
        d_inputs, d_gain_mix = input_grad(d_proj, d_gpre, d_logit, weights, x, gain_mix, d_y)
        d_conv = jnp.concatenate(from_heads(d_taps[:CONV]), axis=1)
        d_gain_mix, d_conv, d_decay_log, d_dt_bias, d_gain_out, d_gain_ffn = lax.psum(
            (d_gain_mix[0], d_conv, d_par[0, :H], d_par[1, :H], d_gain_out[0], d_gain_ffn[0]), ("dp", "seq")
        )
    return (
        result[None], d_inputs[None], d_gain_mix, g_query, g_key, g_value, g_og,
        g_gates[:, : 2 * H], d_conv, d_decay_log, d_dt_bias, d_gain_out, g_out,
        d_gain_ffn, g_gate, g_up, g_down,
    )


def solution(mesh):
    rows, cols, copied = P("dp", None), P(None, "dp"), P()
    tokens = P("dp", "seq", None)
    in_specs = (
        tokens, rows, tokens, copied, rows, rows, rows, rows, rows,
        copied, copied, copied, copied, cols, copied, rows, rows, cols,
    )
    out_specs = (
        tokens, tokens, copied, rows, rows, rows, rows, rows,
        copied, copied, copied, copied, cols, copied, rows, rows, cols,
    )
    return jax.shard_map(local, mesh=mesh, in_specs=in_specs, out_specs=out_specs, check_vma=False)
```

```python
import functools

import jax
import jax.numpy as jnp
from jax import lax
from jax.experimental import pallas as pl
from jax.experimental.pallas import tpu as pltpu
from jax.sharding import PartitionSpec as P

H = 8
DK = 128
DV = 256
CONV = 4
HALO = 16
CHUNK = 128
HC = 2 * DK + DV
LANES = 128
PLANES, CORES, SPOTS = 4, 2, 4

AT_LOGIT = H * HC
AT_GATE = AT_LOGIT + 512
AT_OUT = AT_GATE + H * DV
AT_FFN = AT_OUT + H * DV
VMEM_LIMIT = 62 * 2**20

F32 = jnp.float32
BF16 = jnp.bfloat16
NN = ((1,), (0,))
NT = ((1,), (1,))
TN = ((0,), (0,))


def mm(left, right, dims=NN):
    return lax.dot_general(
        left.astype(BF16), right.astype(BF16), (dims, ((), ())), preferred_element_type=F32
    )


def mm_exact(left, right, dims=NN):
    return lax.dot_general(
        left, right, (dims, ((), ())), precision=lax.Precision.HIGHEST, preferred_element_type=F32
    )


def halves(value):
    high = value.astype(BF16)
    return high, (value - high.astype(F32)).astype(BF16)


def mm_three(left, right):
    left_high, left_low = halves(left)
    right_high, right_low = halves(right)
    return mm(left_high, right_high) + (mm(left_high, right_low) + mm(left_low, right_high))


def params(**more):
    return pltpu.CompilerParams(vmem_limit_bytes=VMEM_LIMIT, **more)


def cost(flops, nbytes):
    return pl.CostEstimate(flops=int(flops), bytes_accessed=int(nbytes), transcendentals=0)


def iota2(shape, axis):
    return lax.broadcasted_iota(jnp.int32, shape, axis)


def lane(value, index):
    picked = jnp.where(iota2(value.shape, 1) == index, value, 0.0)
    return jnp.sum(picked, axis=1, keepdims=True)


def to_row(column):
    size = column.shape[0]
    same = iota2((size, size), 0) == iota2((size, size), 1)
    return jnp.sum(jnp.where(same, column, 0.0), axis=0, keepdims=True)


def to_column(row):
    size = row.shape[1]
    same = iota2((size, size), 0) == iota2((size, size), 1)
    return jnp.sum(jnp.where(same, row, 0.0), axis=1, keepdims=True)


def outgate_kernel(h_ref, w_ref, g_ref):
    g_ref[...] = mm(h_ref[HALO:, :], w_ref[...])


def outgate(hidden, weights):
    rows, width = hidden.shape
    cols = H * DV
    block = 512
    return pl.pallas_call(
        outgate_kernel,
        grid=(cols // block,),
        in_specs=[
            pl.BlockSpec((rows, width), lambda j: (0, 0)),
            pl.BlockSpec((width, block), lambda j: (0, j + AT_GATE // block)),
        ],
        out_specs=pl.BlockSpec((rows - HALO, block), lambda j: (0, j)),
        out_shape=jax.ShapeDtypeStruct((rows - HALO, cols), F32),
        compiler_params=params(),
        cost_estimate=cost(2 * rows * width * cols, 2 * width * cols + 4 * rows * cols),
        name="outgate",
    )(hidden, weights)


def outer_kernel(left_ref, right_ref, out_ref, turn_ref, *, skip):
    @pl.when(pl.program_id(0) == 0)
    def _():
        turn_ref[...] = jnp.transpose(left_ref[skip:, :])

    out_ref[...] = mm(turn_ref[...], right_ref[...]).astype(BF16)


def outer(left, right, skip):
    rows, width = left.shape
    cols = right.shape[1]
    block = next(b for b in (512, 256, 128) if cols % b == 0)
    return pl.pallas_call(
        functools.partial(outer_kernel, skip=skip),
        grid=(cols // block,),
        in_specs=[
            pl.BlockSpec((rows, width), lambda j: (0, 0)),
            pl.BlockSpec((rows - skip, block), lambda j: (0, j)),
        ],
        out_specs=pl.BlockSpec((width, block), lambda j: (0, j)),
        out_shape=jax.ShapeDtypeStruct((width, cols), BF16),
        scratch_shapes=[pltpu.VMEM((width, rows - skip), BF16)],
        compiler_params=params(),
        cost_estimate=cost(2 * rows * width * cols, 2 * width * cols + 2 * rows * cols),
        name="outer",
    )(left, right)


def gate_tables(logit_ref, par_ref, beta_ref, decay_ref, cum_ref):
    logits = logit_ref[HALO:, :]
    beta_ref[...] = jax.nn.sigmoid(logits)
    shifted = logits + par_ref[1:2, :]
    soft = jnp.maximum(shifted, 0.0) + jnp.log1p(jnp.exp(-jnp.abs(shifted)))
    decay_ref[...] = -jnp.exp(par_ref[0:1, :]) * soft
    lower = (iota2((CHUNK, CHUNK), 0) >= iota2((CHUNK, CHUNK), 1)).astype(F32)
    for c in range(logits.shape[0] // CHUNK):
        part = decay_ref[c * CHUNK : (c + 1) * CHUNK, :]
        cum_ref[c * CHUNK : (c + 1) * CHUNK, :] = mm_exact(lower, part)


def join_taps(taps_ref, query_ref, key_ref, value_ref):
    taps_ref[0:CONV, :DK] = query_ref[...]
    taps_ref[0:CONV, DK : 2 * DK] = key_ref[...]
    taps_ref[0:CONV, 2 * DK :] = value_ref[...]


def taps_specs(at):
    return [
        pl.BlockSpec((CONV, DK), lambda s: (0, at(s))),
        pl.BlockSpec((CONV, DK), lambda s: (0, H + at(s))),
        pl.BlockSpec((CONV, DV), lambda s: (0, 2 * H * DK // DV + at(s))),
    ]


def mix_taps(p_ref, taps_ref, cols, pf_ref):
    tokens = cols.shape[0]
    pf_ref[...] = p_ref[...].astype(F32)
    total = pf_ref[HALO:, :] * taps_ref[0:1, :]
    for j in range(1, CONV):
        total += pf_ref[HALO - j : HALO - j + tokens, :] * taps_ref[j : j + 1, :] * cols[:, j : j + 1]
    return total


def chunk_tables(c, head, cols, segr_ref, cum_ref):
    rows = slice(c * CHUNK, (c + 1) * CHUNK)
    cum = lane(cum_ref[rows, :], head)
    cum_row = to_row(cum)
    same = cols[rows, 0:1] == segr_ref[0:1, rows]
    row_ids, col_ids = iota2((CHUNK, CHUNK), 0), iota2((CHUNK, CHUNK), 1)
    gamma = jnp.where((row_ids >= col_ids) & same, jnp.exp(jnp.minimum(cum - cum_row, 0.0)), 0.0)
    strict = jnp.where(row_ids > col_ids, gamma, 0.0)
    carry = jnp.exp(cum) * cols[rows, 4:5]
    last = jnp.exp(cum[CHUNK - 1 :, :] - cum) * cols[rows, 5:6]
    return gamma, strict, carry, last


def unit_lower_inverses(systems):
    size = systems[0].shape[0]
    row_ids, col_ids = iota2((size, size), 0), iota2((size, size), 1)
    eye = (row_ids == col_ids).astype(F32)
    found = [eye - jnp.where(row_ids // 2 == col_ids // 2, low, 0.0) for low in systems]
    width = 2
    while width < size:
        joined = (row_ids // (2 * width) == col_ids // (2 * width)) & (
            row_ids // width != col_ids // width
        )
        first = [mm_three(jnp.where(joined, low, 0.0), inv) for low, inv in zip(systems, found)]
        found = [inv - mm_three(inv, part) for inv, part in zip(found, first)]
        width *= 2
    return found


def flip_spot(value, bits):
    low, high = lax.rem(value, 2), value // 2
    flip = lambda one, other: one + other - 2 * one * other
    return flip(low, bits % 2) + 2 * flip(high, bits // 2)


def device(planes=0, core=0, spot=0):
    place, here = lax.axis_index("dp"), lax.axis_index("seq")
    z = lax.rem(place // CORES + planes, PLANES)
    return {"dp": z * CORES + flip_spot(lax.rem(place, CORES), core), "seq": flip_spot(here, spot)}


def greet(partners):
    barrier = pltpu.get_barrier_semaphore()
    for partner in partners:
        pl.semaphore_signal(barrier, inc=1, device_id=device(**partner), device_id_type=pl.DeviceIdType.MESH)
    pl.semaphore_wait(barrier, len(partners))


def gather_spans(inner):
    spans = [((H - 1) * HC, HC + LANES), ((H - 2) * HC, HC)]
    spans += [(h * HC, 2 * HC) for h in (4, 2, 0)]
    for at, size in ((AT_GATE, H * DV), (AT_OUT, H * DV)) + tuple((AT_FFN + i * inner, inner) for i in range(3)):
        spans += [(at + low, min(1024, size - low)) for low in range(0, size, 1024)]
    return spans


class Gathering:
    STAGES = (0, 1, 2, 3, 5, 7, 8)
    FIRST = ((0, 1, 2, 3, 4, 5, 6), (0, 1, 2, 3, 4, 6, 7))

    def __init__(self, spans, shard_ref, full_ref, sems, pack):
        self.spans, self.shard, self.full, self.pack = spans, shard_ref, full_ref, pack
        self.send_sem, self.recv_sem, self.local_sem = sems
        self.piece = shard_ref.shape[0] // SPOTS
        self.half = full_ref.shape[0] // CORES
        self.z = lax.axis_index("dp") // CORES

    def quarter(self, spot, cols):
        row = flip_spot(lax.axis_index("seq"), spot) * self.piece
        return self.shard.at[pl.ds(pl.multiple_of(row, self.piece), self.piece), cols]

    def own(self, group):
        at, size = self.spans[group]
        cols = pl.ds(at, size)
        block = PLANES * self.piece
        return [
            pltpu.make_async_copy(
                self.quarter(q, cols),
                self.full.at[q * block : q * block + self.piece, cols],
                self.local_sem.at[group, q],
            )
            for q in range(SPOTS)
        ]

    def copy(self, group, kind):
        at, size = self.spans[group]
        cols = pl.ds(at, size)
        piece, full = self.piece, self.full
        block = PLANES * piece
        rows = lambda quarter: pl.ds(quarter * block + piece, block - piece)
        if kind < 6:
            read, step, written = ((0, 1, 1), (0, -1, 3), (1, 1, 2), (3, -1, 2), (2, 1, 3), (2, -1, 1))[kind]
            source = self.quarter(0, cols) if read == 0 else full.at[read * piece : (read + 1) * piece, cols]
            target = full.at[written * piece : (written + 1) * piece, cols]
            to, arrival = device(planes=step % PLANES), written - 1
        elif kind < 8:
            source = full.at[rows(0), cols]
            target = full.at[rows(kind - 5), cols]
            to, arrival = device(spot=kind - 5), kind - 3
        elif kind == 8:
            by = 1 + group % 2
            source = full.at[rows(by), cols]
            target = full.at[rows(3), cols]
            to, arrival = device(spot=3 - by), 5
        else:
            source = full.at[0 : self.half, cols]
            target = full.at[self.half : 2 * self.half, cols]
            to, arrival = device(core=1), 6
        return pltpu.make_async_remote_copy(
            src_ref=source,
            dst_ref=target,
            send_sem=self.send_sem.at[group, kind],
            recv_sem=self.recv_sem.at[group, arrival],
            device_id=to,
            device_id_type=pl.DeviceIdType.MESH,
        )

    def sends(self, kind):
        z = self.z
        return (z < 3, z > 0, (z > 0) & (z < 3), (z > 0) & (z < 3), z == 2, z == 1)[kind]

    def start(self, group, kind):
        @pl.when(self.sends(kind))
        def _():
            self.copy(group, kind).start()

    def arrive(self, group, kind, condition):
        @pl.when(condition)
        def _():
            self.copy(group, kind).wait_recv()

    def tick(self, at):
        z = self.z
        due = []
        for group in range(len(self.spans)):
            stages = (self.FIRST + (self.STAGES,) * len(self.spans))[group]
            due += [(stage, group) for stage in range(len(stages)) if group + stages[stage] == at]
        for stage, group in sorted(due, reverse=True):
            by = 1 + group % 2
            if stage == 0:
                self.pack(*self.spans[group])
                self.start(group, 0)
                self.start(group, 1)
                for local in self.own(group):
                    local.start()
            elif stage == 1:
                self.arrive(group, 0, z > 0)
                self.start(group, 2)
                self.arrive(group, 1, z < 3)
                self.start(group, 3)
            elif stage == 2:
                self.copy(group, 2).wait_recv()
                self.start(group, 4)
                self.start(group, 5)
            elif stage == 3:
                self.arrive(group, 0, z == 0)
                self.arrive(group, 1, z == 3)
                self.copy(group, 5 + by).start()
                self.copy(group, 8 - by).start()
            elif stage == 4:
                self.copy(group, 5 + by).wait_recv()
                self.copy(group, 8).start()
            elif stage == 5:
                self.copy(group, 8 - by).wait_recv()
                self.copy(group, 8).wait_recv()
                for local in self.own(group):
                    local.wait()
                self.copy(group, 9).start()
            else:
                self.copy(group, 9).wait_recv()

    def finish(self):
        for group in range(len(self.spans)):
            for kind in range(6):

                @pl.when(self.sends(kind))
                def _(group=group, kind=kind):
                    self.copy(group, kind).wait_send()

            for kind in range(6, 10):
                self.copy(group, kind).wait_send()


def forward_kernel(
    h_ref, full_ref, taps_ref, par_ref, cols_ref, segr_ref,
    p_ref, logit_ref, part_ref, resp_ref, exch_ref, inv_ref, upd_ref, st_ref, stm_ref, amap_ref, rmap_ref,
    beta_ref, decay_ref, cum_ref, pf_ref, mix_ref, w_ref, wl_ref, load_sem,
):
    head = pl.program_id(0)
    load_head(head, h_ref, full_ref, par_ref, p_ref, logit_ref, beta_ref, decay_ref, cum_ref, w_ref, wl_ref, load_sem)
    state = forward_head(
        head, p_ref, taps_ref, cols_ref, segr_ref, part_ref, resp_ref, inv_ref, upd_ref, st_ref, stm_ref,
        amap_ref, rmap_ref, beta_ref, cum_ref, pf_ref, mix_ref, lambda: None,
    )
    exch_ref[0, 0] = state.astype(BF16)


def load_head(
    head, h_ref, full_ref, par_ref, p_ref, logit_ref, beta_ref, decay_ref, cum_ref, w_ref, wl_ref, load_sem
):
    def load(slot, at, size, to):
        return pltpu.make_async_copy(full_ref.at[:, pl.ds(at, size)], to, load_sem.at[slot])

    mine = load(0, pl.multiple_of((H - 1 - head) * HC, HC), HC, w_ref)
    mine.start()

    @pl.when(head == 0)
    def _():
        gates = load(1, AT_LOGIT, LANES, wl_ref)
        gates.start()
        gates.wait()
        logit_ref[...] = mm(h_ref[...], wl_ref[...])
        gate_tables(logit_ref, par_ref, beta_ref, decay_ref, cum_ref)

    mine.wait()
    p_ref[...] = mm(h_ref[...], w_ref[...]).astype(BF16)


def forward_head(
    head, p_ref, taps_ref, cols_ref, segr_ref, part_ref, resp_ref, inv_ref, upd_ref, st_ref, stm_ref,
    amap_ref, rmap_ref, beta_ref, cum_ref, pf_ref, mix_ref, between,
):
    cols = cols_ref[...]
    tokens = cols.shape[0]
    total = mix_taps(p_ref, taps_ref, cols, pf_ref)
    mix_ref[...] = total * jax.nn.sigmoid(total)
    between()
    beta = lane(beta_ref[...], head + H)
    chunks = range(tokens // CHUNK)
    tables, lows, keys, queries = [], [], [], []
    for c in chunks:
        rows = slice(c * CHUNK, (c + 1) * CHUNK)
        query = mix_ref[rows, :DK]
        query = query * (lax.rsqrt(jnp.sum(query * query, axis=1, keepdims=True) + 1e-06) * DK**-0.5)
        key = mix_ref[rows, DK : 2 * DK]
        key = key * lax.rsqrt(jnp.sum(key * key, axis=1, keepdims=True) + 1e-06)
        gamma, strict, carry, last = chunk_tables(c, head, cols, segr_ref, cum_ref)
        dots = mm(jnp.concatenate([key, query], axis=0), key, NT)
        lows.append(beta[rows] * strict * dots[:CHUNK])
        tables.append((gamma * dots[CHUNK:], carry, last))
        keys.append(key)
        queries.append(query)
    inverses = unit_lower_inverses(lows)
    state = None
    for c in chunks:
        rows = slice(c * CHUNK, (c + 1) * CHUNK)
        scores, carry, last = tables[c]
        key, query = keys[c], queries[c]
        target = jnp.concatenate([mix_ref[rows, 2 * DK :], carry * key], axis=1) * beta[rows]
        updates = mm(inverses[c], target)
        inv_ref[0, c] = inverses[c].astype(BF16)
        upd_ref[0, rows, :] = updates
        weighted_t = jnp.transpose(last * key)
        both = mm(jnp.concatenate([weighted_t, scores], axis=0), updates)
        eye = (iota2((DK, DK), 0) == iota2((DK, DK), 1)).astype(F32)
        step_map = carry[CHUNK - 1 :, :] * eye - both[:DK, DV:]
        read_map = carry * query - both[DK:, DV:]
        amap_ref[0, c] = step_map.astype(BF16)
        rmap_ref[0, c] = read_map.astype(BF16)
        if c == 0:
            st_ref[0, c] = jnp.zeros((DK, DV), F32)
            stm_ref[0, c] = eye.astype(BF16)
            part_ref[rows, :] = both[DK:, :DV]
            resp_ref[rows, :] = read_map.astype(BF16)
            state = jnp.concatenate([both[:DK, :DV], step_map], axis=1)
        else:
            st_ref[0, c] = state[:, :DV]
            stm_ref[0, c] = state[:, DV:].astype(BF16)
            moved = mm(jnp.concatenate([step_map, read_map], axis=0), state)
            part_ref[rows, :] = both[DK:, :DV] + moved[DK:, :DV]
            resp_ref[rows, :] = moved[DK:, DV:].astype(BF16)
            state = moved[:DK] + jnp.concatenate(
                [both[:DK, :DV], jnp.zeros((DK, DK), F32)], axis=1
            )
    return state


def delta_forward(hidden, weights, taps, par, cols, segr):
    rows, width = hidden.shape
    tokens = rows - HALO
    chunks = tokens // CHUNK
    whole = lambda shape: pl.BlockSpec(shape, lambda h: (0,) * len(shape))
    by_head = lambda shape: pl.BlockSpec(shape, lambda h: (h,) + (0,) * (len(shape) - 1))
    return pl.pallas_call(
        forward_kernel,
        grid=(H,),
        in_specs=[
            whole((rows, width)),
            pl.BlockSpec(memory_space=pl.ANY),
            pl.BlockSpec((8, HC), lambda h: (0, h)),
            whole((8, LANES)),
            whole((tokens, LANES)),
            whole(segr.shape),
        ],
        out_specs=[
            pl.BlockSpec((rows, HC), lambda h: (0, h)),
            whole((rows, LANES)),
            pl.BlockSpec((tokens, DV), lambda h: (0, h)),
            pl.BlockSpec((tokens, DK), lambda h: (0, h)),
            pl.BlockSpec((1, 1, DK, DV + DK), lambda h: (0, h, 0, 0)),
            by_head((1, chunks, CHUNK, CHUNK)),
            by_head((1, tokens, DV + DK)),
            by_head((1, chunks, DK, DV)),
            by_head((1, chunks, DK, DK)),
            by_head((1, chunks, DK, DK)),
            by_head((1, chunks, CHUNK, DK)),
        ],
        out_shape=[
            jax.ShapeDtypeStruct((rows, H * HC), BF16),
            jax.ShapeDtypeStruct((rows, LANES), F32),
            jax.ShapeDtypeStruct((tokens, H * DV), F32),
            jax.ShapeDtypeStruct((tokens, H * DK), BF16),
            jax.ShapeDtypeStruct((1, H, DK, DV + DK), BF16),
        ]
        + saved_shapes(chunks),
        scratch_shapes=[
            pltpu.VMEM((tokens, LANES), F32),
            pltpu.VMEM((tokens, LANES), F32),
            pltpu.VMEM((tokens, LANES), F32),
            pltpu.VMEM((rows, HC), F32),
            pltpu.VMEM((tokens, HC), F32),
            pltpu.VMEM((width, HC), BF16),
            pltpu.VMEM((width, LANES), BF16),
            pltpu.SemaphoreType.DMA((2,)),
        ],
        compiler_params=params(),
        cost_estimate=cost(6e9 * H, 5e6 * H),
        name="delta_forward",
    )(hidden, weights, taps, par, cols, segr)


def saved_shapes(chunks):
    return [
        jax.ShapeDtypeStruct((H, chunks, CHUNK, CHUNK), BF16),
        jax.ShapeDtypeStruct((H, chunks * CHUNK, DV + DK), F32),
        jax.ShapeDtypeStruct((H, chunks, DK, DV), F32),
        jax.ShapeDtypeStruct((H, chunks, DK, DK), BF16),
        jax.ShapeDtypeStruct((H, chunks, DK, DK), BF16),
        jax.ShapeDtypeStruct((H, chunks, CHUNK, DK), BF16),
    ]


def mixer_forward_kernel(
    x_ref, wq_ref, wk_ref, wv_ref, wl_in, gain_mix_ref, gain_ffn_ref, gain_ref, rate_ref, bias_ref, seg_ref,
    taps_q_ref, taps_k_ref, taps_v_ref, cot_any, wo_any, wm_any, wg_any, wu_any, wd_any,
    full_ref, hidden_out, x_out, cot_out, turn_out, y_out, mid_out,
    gains_out, near_ref, par_ref, cols_ref, back_ref, p_ref, logit_ref, resp_out,
    inv_ref, upd_ref, st_ref, stm_ref, amap_ref, rmap_ref, maps_ref, sin_ref, attn_ref, gpre_ref, gated_ref,
    shard_ref, hidden_ref, xs_ref, cots_ref, turn_ref, y_ref, mid_ref, xh_ref, part_ref, resp_ref, exch_ref, stage_ref, half_ref, low_ref,
    beta_ref, decay_ref, cum_ref, pf_ref, mix_ref, w_ref, wl_ref, wb_ref,
    cot_ref, wo_ref, wm_ref, wg_ref, wu_ref, wd_ref, taps_ref, row_ref, later_ref, late_sem,
    send_sem, recv_sem, local_sem, exch_send, exch_recv, load_sem, pair_sem, out_sem, halo_sem, *, spans, inner,
):
    step = pl.program_id(0)
    place = lax.axis_index("seq")
    tokens, width = x_ref.shape

    def late(which):
        source, to = (
            (wo_any, wo_ref), (wm_any, wm_ref), (wg_any, wg_ref), (wu_any, wu_ref), (wd_any, wd_ref), (cot_any, cot_ref),
        )[which]
        return pltpu.make_async_copy(source, to, late_sem.at[which])

    def pack(at, size):
        while size > 0:
            if at < AT_LOGIT:
                head, span = H - 1 - at // HC, HC
                shard_ref[:, at : at + DK] = wq_ref[:, head * DK : (head + 1) * DK].astype(BF16)
                shard_ref[:, at + DK : at + 2 * DK] = wk_ref[:, head * DK : (head + 1) * DK].astype(BF16)
                shard_ref[:, at + 2 * DK : at + HC] = wv_ref[:, head * DV : (head + 1) * DV].astype(BF16)
            elif at < AT_GATE:
                span = LANES
                rest = jnp.zeros((LANES - 2 * H, LANES), F32)
                turned = jnp.transpose(jnp.concatenate([wl_in[...], rest], axis=0))
                shard_ref[:, at : at + LANES] = turned.astype(BF16)
            elif at < AT_OUT:
                span, low = size, at - AT_GATE
                if low == 0:
                    late(0).wait()
                shard_ref[:, at : at + span] = wo_ref[:, low : low + span].astype(BF16)
            elif at < AT_FFN:
                span, low = size, at - AT_OUT
                if low == 0:
                    late(1).wait()
                shard_ref[:, at : at + span] = jnp.transpose(wm_ref[low : low + span, :]).astype(BF16)
            else:
                span, which, low = size, (at - AT_FFN) // inner, (at - AT_FFN) % inner
                if low == 0:
                    late(2 + which).wait()
                if which < 2:
                    shard_ref[:, at : at + span] = (wg_ref, wu_ref)[which][:, low : low + span].astype(BF16)
                else:
                    shard_ref[:, at : at + span] = jnp.transpose(wd_ref[low : low + span, :]).astype(BF16)
            at, size = at + span, size - span

    gathering = Gathering(spans, shard_ref, full_ref, (send_sem, recv_sem, local_sem), pack)
    lead = gathering.FIRST[0][-1] + 1
    final_tick = len(spans) + gathering.STAGES[-1]

    upper = place // 2 == 1
    second = lax.rem(place, 2) == 1

    def give(h):
        return pltpu.make_async_remote_copy(
            src_ref=stage_ref.at[h],
            dst_ref=exch_ref.at[h],
            send_sem=exch_send.at[0, h],
            recv_sem=exch_recv.at[0, h],
            device_id=device(spot=1),
            device_id_type=pl.DeviceIdType.MESH,
        )

    def give_half(h):
        return pltpu.make_async_remote_copy(
            src_ref=half_ref.at[h],
            dst_ref=low_ref.at[h],
            send_sem=exch_send.at[1, h],
            recv_sem=exch_recv.at[1, h],
            device_id=device(spot=2),
            device_id_type=pl.DeviceIdType.MESH,
        )

    def join(h):
        give(h).wait()

        @pl.when(jnp.logical_not(upper))
        def _():
            mine, theirs = stage_ref[h], exch_ref[h]
            later = jnp.where(second, mine, theirs)
            earlier = jnp.where(second, theirs, mine)
            half_ref[h] = (later[:, :DV].astype(F32) + mm(later[:, DV:], earlier[:, :DV])).astype(BF16)
            give_half(h).start()

    def give_halo():
        return pltpu.make_async_remote_copy(
            src_ref=x_ref.at[tokens - HALO : tokens],
            dst_ref=xh_ref,
            send_sem=halo_sem.at[0],
            recv_sem=halo_sem.at[1],
            device_id={"dp": lax.axis_index("dp"), "seq": lax.rem(place + 1, SPOTS)},
            device_id_type=pl.DeviceIdType.MESH,
        )

    def keep(which):
        source, to = (
            (hidden_ref, hidden_out), (xs_ref, x_out), (cots_ref, cot_out), (turn_ref, turn_out),
            (y_ref, y_out), (mid_ref, mid_out),
        )[which]
        return pltpu.make_async_copy(source, to, out_sem.at[which])

    def load_pair(h):
        slot = lax.rem(h, 2)
        return [
            pltpu.make_async_copy(
                full_ref.at[:, pl.ds(pl.multiple_of(at + h * DV, DV), DV)], wb_ref.at[slot, i], pair_sem.at[slot, i]
            )
            for i, at in enumerate((AT_GATE, AT_OUT))
        ]

    @pl.when(step == 0)
    def _():
        greet([dict(planes=d) for d in (1, 2, 3)] + [dict(spot=s) for s in (1, 2, 3)] + [dict(core=1)])

        @pl.when(place < SPOTS - 1)
        def _():
            give_halo().start()

        gathering.tick(0)
        for which in range(6):
            late(which).start()
        at = iota2((1, width), 1)
        piece = width // (PLANES * CORES * SPOTS)
        core, rest = at // (width // 2), at % (width // 2)
        quarter, plane, low = rest // (PLANES * piece), rest // piece % PLANES, rest % piece
        place_dp = lax.axis_index("dp")
        z, c = place_dp // CORES, lax.rem(place_dp, CORES)
        chip = ((z - plane + PLANES) % PLANES) * CORES + (c + core - 2 * c * core)
        order = (chip * SPOTS + flip_spot(quarter, place)) * piece + low
        turn_ref[...] = jnp.where(iota2((width, width), 0) == order, 1.0, 0.0).astype(BF16)
        keep(3).start()
        gathering.tick(1)
        gains = jnp.concatenate([gain_mix_ref[...], gain_ffn_ref[...], jnp.zeros((6, width), F32)], axis=0)
        high, mid = halves(gains)
        rest = (gains - high.astype(F32)) - mid.astype(F32)
        gains_out[...] = mm(high, turn_ref[...]) + mm(mid, turn_ref[...]) + mm(rest, turn_ref[...])
        par_ref[...] = jnp.zeros_like(par_ref)
        par_ref[0:1, :H] = rate_ref[...]
        par_ref[1:2, :H] = bias_ref[...]
        gathering.tick(2)

        row_ref[...] = jnp.full(row_ref.shape, -1.0, F32)
        row_ref[0:1, LANES : LANES + seg_ref.shape[1]] = seg_ref[...].astype(F32)
        row = row_ref[0:1, pl.ds(pl.multiple_of(place * tokens, LANES), tokens + 2 * LANES)]
        seg = row[:, LANES : LANES + tokens]
        near = [seg]
        for j in range(1, CONV):
            moved = pltpu.roll(row, j, 1)[:, LANES : LANES + tokens]
            near.append((moved == seg).astype(F32))
        before, last = [], []
        for n in range(tokens // CHUNK):
            part = seg[:, n * CHUNK : (n + 1) * CHUNK]
            before.append((part == row[:, LANES + n * CHUNK - 1 : LANES + n * CHUNK]).astype(F32))
            last.append((part == part[:, CHUNK - 1 :]).astype(F32))
        near += [jnp.concatenate(before, axis=1), jnp.concatenate(last, axis=1)]
        near.append(jnp.zeros((8 - len(near), tokens), F32))
        near_ref[...] = jnp.concatenate(near, axis=0)
        size = row.shape[1]
        ahead = pltpu.roll(row, size - (LANES - HALO), 1)
        later = [jnp.zeros((1, tokens + LANES), F32)]
        for j in range(1, CONV):
            later.append((pltpu.roll(ahead, size - j, 1) == ahead).astype(F32)[:, : tokens + LANES])
        later.append(jnp.zeros((8 - CONV, tokens + LANES), F32))
        later_ref[...] = jnp.concatenate(later, axis=0)
        blank = jnp.zeros((LANES - 8, LANES), F32)
        for n in range(tokens // LANES):
            span = slice(n * LANES, (n + 1) * LANES)
            cols_ref[span, :] = jnp.transpose(jnp.concatenate([near_ref[:, span], blank], axis=0))
        gathering.tick(3)

        @pl.when(place > 0)
        def _():
            give_halo().wait_recv()

        @pl.when(place == 0)
        def _():
            xh_ref[...] = jnp.zeros_like(xh_ref)

        value = mm(jnp.concatenate([xh_ref[...], x_ref[...]], axis=0), turn_ref[...])
        xs_ref[...] = value[HALO:].astype(BF16)
        keep(1).start()
        size = lax.rsqrt(jnp.mean(value * value, axis=-1, keepdims=True) + 1e-06)
        hidden_ref[...] = (value * size * gains_out[0:1, :]).astype(BF16)
        keep(0).start()
        for at in range(4, lead):
            gathering.tick(at)

    @pl.when((step >= 2) & (step < H + 2))
    def _():
        join(step - 2)

    @pl.when(step < H)
    def _():
        head = step
        for h in range(1, H):

            @pl.when(head == h)
            def _(h=h):
                gathering.tick(lead + 2 * h - 1)

        load_head(
            head, hidden_ref, full_ref, par_ref, p_ref, logit_ref, beta_ref, decay_ref, cum_ref, w_ref, wl_ref, load_sem
        )

        def between():
            for h in range(H):

                @pl.when(head == h)
                def _(h=h):
                    gathering.tick(lead + 2 * h)

        join_taps(taps_ref, taps_q_ref, taps_k_ref, taps_v_ref)
        state = forward_head(
            head, p_ref, taps_ref, cols_ref, near_ref, part_ref.at[head], resp_ref.at[head], inv_ref, upd_ref,
            st_ref, stm_ref, amap_ref, rmap_ref, beta_ref, cum_ref, pf_ref, mix_ref, between,
        )
        resp_out[...] = resp_ref[head]
        stage_ref[head] = state.astype(BF16)
        give(head).start()

        @pl.when(head == H - 1)
        def _():
            for copy in load_pair(0):
                copy.start()

    @pl.when(step >= H)
    def _():
        head = step - H
        for n, at in enumerate(range(lead + 2 * H - 1, final_tick)):

            @pl.when(head == min(n, H - 1))
            def _(at=at):
                gathering.tick(at)

        @pl.when(head < H - 1)
        def _():
            for copy in load_pair(head + 1):
                copy.start()

        for copy in load_pair(head):
            copy.wait()
        @pl.when(upper)
        def _():
            give_half(head).wait_recv()

        @pl.when(jnp.logical_not(upper))
        def _():
            low_ref[head] = jnp.zeros((DK, DV), BF16)
            give_half(head).wait_send()

        slot = lax.rem(head, 2)
        gate = mm(hidden_ref[HALO:, :], wb_ref[slot, 0])
        gpre_ref[...] = gate
        theirs = exch_ref[head]
        maps_ref[0, 0] = stage_ref[head, :, DV:]
        maps_ref[1, 0] = theirs[:, DV:]
        state = low_ref[head].astype(F32)
        state = jnp.where(second, theirs[:, :DV].astype(F32) + mm(theirs[:, DV:], state), state)
        sin_ref[0] = state
        attn = part_ref[head] + mm(resp_ref[head], state)
        attn_ref[...] = attn
        scale = lax.rsqrt(jnp.mean(attn * attn, axis=-1, keepdims=True) + 1e-05)
        gated = (attn * scale * gain_ref[...] * (gate * jax.nn.sigmoid(gate))).astype(BF16)
        gated_ref[...] = gated

        @pl.when(head == 0)
        def _():
            y_ref[...] = xs_ref[...].astype(F32)
            late(5).wait()
            cots_ref[...] = mm(cot_ref[...], turn_ref[...]).astype(BF16)
            keep(2).start()
            blank = jnp.zeros((LANES - 8, LANES), F32)
            for n in range(tokens // LANES + 1):
                span = slice(n * LANES, (n + 1) * LANES)
                turned = jnp.transpose(jnp.concatenate([later_ref[:, span], blank], axis=0))
                kept = min(LANES, tokens + HALO - n * LANES)
                back_ref[n * LANES : n * LANES + kept, :] = turned[:kept]

        y_ref[...] += mm(gated, wb_ref[slot, 1], NT)

        @pl.when(head == H - 1)
        def _():
            keep(4).start()
            value = y_ref[...]
            size = lax.rsqrt(jnp.mean(value * value, axis=-1, keepdims=True) + 1e-06)
            mid_ref[...] = (value * size * gains_out[1:2, :]).astype(BF16)
            keep(5).start()
            gathering.finish()

            @pl.when(place < SPOTS - 1)
            def _():
                give_halo().wait_send()

            for which in range(6):
                keep(which).wait()


def mixer_forward(x, cotangent, shards, gains, gain, rate, bias, segments, taps):
    tokens, width = x.shape
    rows = tokens + HALO
    chunks = tokens // CHUNK
    query, key, value, outgate_w, gates, out_w, gate_w, up_w, down_w = shards
    inner = down_w.shape[0]
    spans = gather_spans(inner)
    total = AT_FFN + 3 * inner
    once = lambda array: pl.BlockSpec(
        array.shape, lambda s: (0,) * array.ndim, pipeline_mode=pl.Buffered(1)
    )
    whole = lambda shape: pl.BlockSpec(shape, lambda s: (0,) * len(shape))
    early = lambda s: jnp.minimum(s, H - 1)
    late = lambda s: jnp.maximum(s - H, 0)
    by_head = lambda shape, at: pl.BlockSpec(shape, lambda s: (at(s),) + (0,) * (len(shape) - 1))
    across = lambda shape, at: pl.BlockSpec(shape, lambda s: (0, at(s)))
    anywhere = pl.BlockSpec(memory_space=pl.ANY)
    shape = jax.ShapeDtypeStruct
    sem = pltpu.SemaphoreType.DMA
    saved = saved_shapes(chunks)
    return pl.pallas_call(
        functools.partial(mixer_forward_kernel, spans=spans, inner=inner),
        grid=(2 * H,),
        in_specs=[once(a) for a in (x, query, key, value, gates, *gains, gain, rate, bias, segments)]
        + taps_specs(early)
        + [anywhere] * 6,
        out_specs=[anywhere] * 7
        + [
            whole((8, width)),
            whole((8, tokens)),
            whole((8, LANES)),
            whole((tokens, LANES)),
            whole((rows, LANES)),
            across((rows, HC), early),
            whole((rows, LANES)),
            across((tokens, DK), early),
        ]
        + [by_head((1,) + one.shape[1:], early) for one in saved]
        + [
            pl.BlockSpec((2, 1, DK, DK), lambda s: (0, late(s), 0, 0)),
            by_head((1, DK, DV), late),
            across((tokens, DV), late),
            across((tokens, DV), late),
            across((tokens, DV), late),
        ],
        out_shape=[
            shape((width, total), BF16),
            shape((rows, width), BF16),
            shape((tokens, width), BF16),
            shape((tokens, width), BF16),
            shape((width, width), BF16),
            shape((tokens, width), F32),
            shape((tokens, width), BF16),
            shape((8, width), F32),
            shape((8, tokens), F32),
            shape((8, LANES), F32),
            shape((tokens, LANES), F32),
            shape((rows, LANES), F32),
            shape((rows, H * HC), BF16),
            shape((rows, LANES), F32),
            shape((tokens, H * DK), BF16),
        ]
        + saved
        + [
            shape((2, H, DK, DK), BF16),
            shape((H, DK, DV), F32),
            shape((tokens, H * DV), F32),
            shape((tokens, H * DV), F32),
            shape((tokens, H * DV), BF16),
        ],
        scratch_shapes=[
            pltpu.VMEM((query.shape[0], total), BF16),
            pltpu.VMEM((rows, width), BF16),
            pltpu.VMEM((tokens, width), BF16),
            pltpu.VMEM((tokens, width), BF16),
            pltpu.VMEM((width, width), BF16),
            pltpu.VMEM((tokens, width), F32),
            pltpu.VMEM((tokens, width), BF16),
            pltpu.VMEM((HALO, width), BF16),
            pltpu.VMEM((H, tokens, DV), F32),
            pltpu.VMEM((H, tokens, DK), BF16),
            pltpu.VMEM((H, DK, DV + DK), BF16),
            pltpu.VMEM((H, DK, DV + DK), BF16),
            pltpu.VMEM((H, DK, DV), BF16),
            pltpu.VMEM((H, DK, DV), BF16),
            pltpu.VMEM((tokens, LANES), F32),
            pltpu.VMEM((tokens, LANES), F32),
            pltpu.VMEM((tokens, LANES), F32),
            pltpu.VMEM((rows, HC), F32),
            pltpu.VMEM((tokens, HC), F32),
            pltpu.VMEM((width, HC), BF16),
            pltpu.VMEM((width, LANES), BF16),
            pltpu.VMEM((2, 2, width, DV), BF16),
            pltpu.VMEM(cotangent.shape, BF16),
            pltpu.VMEM(outgate_w.shape, F32),
            pltpu.VMEM(out_w.shape, F32),
            pltpu.VMEM(gate_w.shape, F32),
            pltpu.VMEM(up_w.shape, F32),
            pltpu.VMEM(down_w.shape, F32),
            pltpu.VMEM((8, HC), F32),
            pltpu.VMEM((8, segments.shape[1] + 2 * LANES), F32),
            pltpu.VMEM((8, tokens + LANES), F32),
            sem((6,)),
            sem((len(spans), 10)),
            sem((len(spans), 7)),
            sem((len(spans), SPOTS)),
            sem((2, H)),
            sem((2, H)),
            sem((2,)),
            sem((2, 2)),
            sem((6,)),
            sem((2,)),
        ],
        compiler_params=params(collective_id=0, has_side_effects=True),
        cost_estimate=cost(1e11, 1e8),
        name="mixer_forward",
    )(
        x, query, key, value, gates, *gains, gain, rate, bias, segments, taps, taps, taps,
        cotangent, outgate_w, out_w, gate_w, up_w, down_w,
    )


def backward_kernel(place_ref, slot_ref, *refs):
    exch_ref, grads_ref, refs = refs[9], refs[10], refs[:9] + refs[11:]

    def behind(source, grad):
        slot = slot_ref[source]
        return jnp.where(
            source > place_ref[0],
            grads_ref[slot, 0].astype(F32) + mm(exch_ref[slot, 0], grad, TN),
            grad,
        )

    places = exch_ref.shape[0]
    d_state = lax.fori_loop(
        0, places - 1, lambda lap, grad: behind(places - 1 - lap, grad), jnp.zeros((DK, DV), F32)
    )
    for phase in range(PHASES):
        backward_head(phase, pl.program_id(0), lambda: d_state, *refs)


PHASES = 3


def backward_head(
    phase, head, entering, p_ref, taps_ref, logit_ref, par_ref, cols_ref, back_ref, segr_ref,
    dattn_ref, sin_ref,
    inv_ref, upd_ref, st_ref, stm_ref, amap_ref, rmap_ref,
    dp_ref, dlogit_ref, dtaps_ref, dpar_ref,
    beta_ref, decay_ref, cum_ref, pf_ref, pre_ref, dmix_ref, dstate_ref, dbeta_ref, ddecay_ref,
):
    tokens = cols_ref.shape[0]
    chunks = range(tokens // CHUNK)
    refs = (
        cols_ref, segr_ref, dattn_ref, sin_ref, inv_ref, upd_ref, st_ref, stm_ref, beta_ref, cum_ref, pre_ref,
        dmix_ref, dstate_ref, dbeta_ref, ddecay_ref,
    )
    if phase == 0:

        @pl.when(head == 0)
        def _():
            gate_tables(logit_ref, par_ref, beta_ref, decay_ref, cum_ref)
            dlogit_ref[...] = jnp.zeros_like(dlogit_ref)
            dpar_ref[...] = jnp.zeros_like(dpar_ref)

        pre_ref[...] = mix_taps(p_ref, taps_ref, cols_ref[...], pf_ref)
        d_state = entering()
        for c in reversed(chunks):
            rows = slice(c * CHUNK, (c + 1) * CHUNK)
            dstate_ref[c] = d_state
            if c > 0:
                d_state = mm(amap_ref[0, c], d_state, TN) + mm(rmap_ref[0, c], dattn_ref[rows, :], TN)
        backward_chunks(head, chunks[:1], *refs)
    elif phase == 1:
        backward_chunks(head, chunks[1:3], *refs)
    else:
        backward_chunks(head, chunks[3:], *refs)
        backward_ends(
            head, taps_ref, logit_ref, par_ref, cols_ref, back_ref, dp_ref, dlogit_ref, dtaps_ref, dpar_ref,
            beta_ref, decay_ref, pf_ref, dmix_ref, dbeta_ref, ddecay_ref,
        )


def backward_chunks(
    head, chunks, cols_ref, segr_ref, dattn_ref, sin_ref, inv_ref, upd_ref, st_ref, stm_ref, beta_ref, cum_ref, pre_ref,
    dmix_ref, dstate_ref, dbeta_ref, ddecay_ref,
):
    cols = cols_ref[...]
    beta = lane(beta_ref[...], head + H)
    state_in = sin_ref[0]
    row_ids, col_ids = iota2((CHUNK, CHUNK), 0), iota2((CHUNK, CHUNK), 1)
    for c in chunks:
        rows = slice(c * CHUNK, (c + 1) * CHUNK)
        mixed = pre_ref[rows, :]
        gate = jax.nn.sigmoid(mixed)
        slope = gate * (1.0 + mixed * (1.0 - gate))
        mixed = mixed * gate
        query_raw, key_raw, value = mixed[:, :DK], mixed[:, DK : 2 * DK], mixed[:, 2 * DK :]
        query_size = lax.rsqrt(jnp.sum(query_raw * query_raw, axis=1, keepdims=True) + 1e-06)
        key_size = lax.rsqrt(jnp.sum(key_raw * key_raw, axis=1, keepdims=True) + 1e-06)
        query_unit, key = query_raw * query_size, key_raw * key_size
        query = query_unit * DK**-0.5
        gamma, strict, carry, last = chunk_tables(c, head, cols, segr_ref, cum_ref)
        strength = beta[rows]
        dots = mm(jnp.concatenate([key, query], axis=0), key, NT)
        weights = strict * dots[:CHUNK]
        low = strength * weights
        scores = gamma * dots[CHUNK:]
        if c == 0:
            state = state_in
        else:
            state = st_ref[0, c] + mm(stm_ref[0, c], state_in)
        updates = upd_ref[0, rows, :DV] - mm(upd_ref[0, rows, DV:], state)
        d_attn = dattn_ref[rows, :]
        d_state = dstate_ref[c]
        d_updates = mm(scores, d_attn, TN) + mm(last * key, d_state)
        solved = mm(inv_ref[0, c], d_updates, TN)
        both = jnp.concatenate([d_attn, solved.astype(BF16)], axis=0)
        by_updates = mm(both, updates, NT)
        by_state = mm(both, state, NT)
        d_scores = by_updates[:CHUNK]
        d_low = -by_updates[CHUNK:]
        d_query = carry * by_state[:CHUNK]
        key_state = jnp.sum(key * by_state[CHUNK:], axis=1, keepdims=True)
        d_carry = jnp.sum(query * by_state[:CHUNK], axis=1, keepdims=True) - strength * key_state
        d_beta = (
            jnp.sum(solved * value, axis=1, keepdims=True)
            - carry * key_state
            + jnp.sum(d_low * weights, axis=1, keepdims=True)
        )
        d_dots_q = d_scores * gamma
        d_dots_k = d_low * strength * strict
        by_key = mm(jnp.concatenate([d_dots_q, d_dots_k], axis=0), key)
        d_query += by_key[:CHUNK]
        from_state = mm(updates, d_state, NT)
        d_key = (
            by_key[CHUNK:]
            + mm(
                jnp.concatenate([d_dots_q, d_dots_k], axis=0),
                jnp.concatenate([query, key], axis=0),
                TN,
            )
            - strength * carry * by_state[CHUNK:]
            + last * from_state
        )
        d_last = jnp.sum(key * from_state, axis=1, keepdims=True) * last
        d_spread = d_scores * scores + d_low * low
        final = (iota2((CHUNK, 1), 0) == CHUNK - 1).astype(F32)
        d_carry += final * jnp.sum(d_state * state)
        d_cum = (
            jnp.sum(d_spread, axis=1, keepdims=True)
            - to_column(jnp.sum(d_spread, axis=0, keepdims=True))
            + final * jnp.sum(d_last)
            - d_last
            + d_carry * carry
        )
        d_decay = jnp.sum(
            jnp.where(row_ids <= col_ids, to_row(d_cum), 0.0), axis=1, keepdims=True
        )
        dbeta_ref[rows, :] = jnp.broadcast_to(d_beta, (CHUNK, LANES))
        ddecay_ref[rows, :] = jnp.broadcast_to(d_decay, (CHUNK, LANES))
        d_query = d_query * DK**-0.5
        d_query = query_size * (
            d_query - query_unit * jnp.sum(d_query * query_unit, axis=1, keepdims=True)
        )
        d_key = key_size * (d_key - key * jnp.sum(d_key * key, axis=1, keepdims=True))
        d_value = strength * solved
        dmix_ref[HALO + c * CHUNK : HALO + (c + 1) * CHUNK, :] = slope * jnp.concatenate(
            [d_query, d_key, d_value], axis=1
        )


def backward_ends(
    head, taps_ref, logit_ref, par_ref, cols_ref, back_ref, dp_ref, dlogit_ref, dtaps_ref, dpar_ref,
    beta_ref, decay_ref, pf_ref, dmix_ref, dbeta_ref, ddecay_ref,
):
    cols = cols_ref[...]
    tokens = cols.shape[0]
    lanes = iota2((tokens, LANES), 1)
    slope = jax.nn.sigmoid(logit_ref[HALO:, :] + par_ref[1:2, :]) * -jnp.exp(par_ref[0:1, :])
    here = jnp.where(lanes == head, ddecay_ref[...], 0.0)
    d_first = here * slope
    strengths = beta_ref[...]
    d_second = jnp.where(lanes == head + H, dbeta_ref[...], 0.0) * strengths * (1.0 - strengths)
    dlogit_ref[...] += d_first + d_second
    dpar_ref[0:1, :] += jnp.sum(here * decay_ref[...], axis=0, keepdims=True)
    dpar_ref[1:2, :] += jnp.sum(d_first, axis=0, keepdims=True)

    dmix_ref[:HALO, :] = jnp.zeros((HALO, HC), F32)
    dmix_ref[HALO + tokens :, :] = jnp.zeros((8, HC), F32)
    d_mix = dmix_ref[HALO : HALO + tokens, :]
    dtaps_ref[...] = jnp.zeros_like(dtaps_ref)
    dtaps_ref[0:1, :] = jnp.sum(d_mix * pf_ref[HALO:, :], axis=0, keepdims=True)
    total = dmix_ref[: HALO + tokens, :] * taps_ref[0:1, :]
    for j in range(1, CONV):
        total += dmix_ref[j : j + HALO + tokens, :] * taps_ref[j : j + 1, :] * back_ref[:, j : j + 1]
        dtaps_ref[j : j + 1, :] = jnp.sum(
            d_mix * cols[:, j : j + 1] * pf_ref[HALO - j : HALO - j + tokens, :],
            axis=0,
            keepdims=True,
        )
    dp_ref[...] = total.astype(BF16)


def delta_backward(
    place, slots, proj, taps, logits, par, cols, back, segr, d_attn, state_in, exch, grads, saved
):
    rows = proj.shape[0]
    tokens = rows - HALO
    chunks = tokens // CHUNK
    places = exch.shape[0]
    whole = lambda shape: pl.BlockSpec(shape, lambda h: (0,) * len(shape))
    by_head = lambda shape: pl.BlockSpec(shape, lambda h: (h,) + (0,) * (len(shape) - 1))
    return pl.pallas_call(
        backward_kernel,
        grid=(H,),
        in_specs=[
            pl.BlockSpec(memory_space=pltpu.SMEM),
            pl.BlockSpec(memory_space=pltpu.SMEM),
            pl.BlockSpec((rows, HC), lambda h: (0, h)),
            pl.BlockSpec((8, HC), lambda h: (0, h)),
            whole((rows, LANES)),
            whole((8, LANES)),
            whole((tokens, LANES)),
            whole((rows, LANES)),
            whole(segr.shape),
            pl.BlockSpec((tokens, DV), lambda h: (0, h)),
            by_head((1, DK, DV)),
            pl.BlockSpec((places, 1, DK, DK), lambda h: (0, h, 0, DV // DK)),
            pl.BlockSpec((places, 1, DK, DV), lambda h: (0, h, 0, 0)),
            by_head((1, chunks, CHUNK, CHUNK)),
            by_head((1, tokens, DV + DK)),
            by_head((1, chunks, DK, DV)),
            by_head((1, chunks, DK, DK)),
            by_head((1, chunks, DK, DK)),
            by_head((1, chunks, CHUNK, DK)),
        ],
        out_specs=[
            pl.BlockSpec((rows, HC), lambda h: (0, h)),
            whole((tokens, LANES)),
            pl.BlockSpec((8, HC), lambda h: (0, h)),
            whole((8, LANES)),
        ],
        out_shape=[
            jax.ShapeDtypeStruct((rows, H * HC), BF16),
            jax.ShapeDtypeStruct((tokens, LANES), F32),
            jax.ShapeDtypeStruct((8, H * HC), F32),
            jax.ShapeDtypeStruct((8, LANES), F32),
        ],
        scratch_shapes=[
            pltpu.VMEM((tokens, LANES), F32),
            pltpu.VMEM((tokens, LANES), F32),
            pltpu.VMEM((tokens, LANES), F32),
            pltpu.VMEM((rows, HC), F32),
            pltpu.VMEM((tokens, HC), F32),
            pltpu.VMEM((rows + 8, HC), F32),
            pltpu.VMEM((chunks, DK, DV), F32),
            pltpu.VMEM((tokens, LANES), F32),
            pltpu.VMEM((tokens, LANES), F32),
        ],
        compiler_params=params(),
        cost_estimate=cost(8e9 * H, 5e6 * H),
        name="delta_backward",
    )(place, slots, proj, taps, logits, par, cols, back, segr, d_attn, state_in, exch, grads, *saved)


def mixer_kernel(
    place_ref, slot_ref, part_ref, resp_ref, exch_ref, gpre_ref, gain_ref, w_ref, x_ref, gain2_ref,
    sin_ref, attn_ref, gated_ref, y_ref, h_ref,
):
    head = pl.program_id(0)
    place = place_ref[0]
    places = exch_ref.shape[0]

    def ahead(source, state):
        slot = slot_ref[source]
        return jnp.where(
            source < place,
            exch_ref[slot, 0, :, :DV].astype(F32) + mm(exch_ref[slot, 0, :, DV:], state),
            state,
        )

    state = lax.fori_loop(0, places - 1, ahead, jnp.zeros((DK, DV), F32))
    sin_ref[0] = state
    attn = part_ref[...] + mm(resp_ref[...], state)
    attn_ref[...] = attn
    scale = lax.rsqrt(jnp.mean(attn * attn, axis=-1, keepdims=True) + 1e-05)
    gate = gpre_ref[...]
    gated = (attn * scale * gain_ref[...] * (gate * jax.nn.sigmoid(gate))).astype(BF16)
    gated_ref[...] = gated

    @pl.when(head == 0)
    def _():
        y_ref[...] = x_ref[...].astype(F32)

    y_ref[...] += mm(gated, w_ref[...], NT)

    @pl.when(head == pl.num_programs(0) - 1)
    def _():
        value = y_ref[...]
        size = lax.rsqrt(jnp.mean(value * value, axis=-1, keepdims=True) + 1e-06)
        h_ref[...] = (value * size * gain2_ref[...]).astype(BF16)


def mixer_out(place, slots, part, resp, exch, gpre, gain, weights, x, gain2):
    tokens, width = x.shape
    places = exch.shape[0]
    whole = lambda shape: pl.BlockSpec(shape, lambda h: (0,) * len(shape))
    return pl.pallas_call(
        mixer_kernel,
        grid=(H,),
        in_specs=[
            pl.BlockSpec(memory_space=pltpu.SMEM),
            pl.BlockSpec(memory_space=pltpu.SMEM),
            pl.BlockSpec((tokens, DV), lambda h: (0, h)),
            pl.BlockSpec((tokens, DK), lambda h: (0, h)),
            pl.BlockSpec((places, 1, DK, DV + DK), lambda h: (0, h, 0, 0)),
            pl.BlockSpec((tokens, DV), lambda h: (0, h)),
            whole((1, DV)),
            pl.BlockSpec((width, DV), lambda h: (0, h + AT_OUT // DV)),
            whole((tokens, width)),
            whole((1, width)),
        ],
        out_specs=[
            pl.BlockSpec((1, DK, DV), lambda h: (h, 0, 0)),
            pl.BlockSpec((tokens, DV), lambda h: (0, h)),
            pl.BlockSpec((tokens, DV), lambda h: (0, h)),
            whole((tokens, width)),
            whole((tokens, width)),
        ],
        out_shape=[
            jax.ShapeDtypeStruct((H, DK, DV), F32),
            jax.ShapeDtypeStruct((tokens, H * DV), F32),
            jax.ShapeDtypeStruct((tokens, H * DV), BF16),
            jax.ShapeDtypeStruct((tokens, width), F32),
            jax.ShapeDtypeStruct((tokens, width), BF16),
        ],
        compiler_params=params(),
        cost_estimate=cost(2 * tokens * width * H * DV, 2e7),
        name="mixer_out",
    )(place, slots, part, resp, exch, gpre, gain, weights, x, gain2)


def mixer_back_kernel(
    dmix_ref, w_ref, attn_ref, gpre_ref, gain_ref, resp_ref,
    dattn_ref, dgpre_ref, grad_ref, dgain_ref,
):
    @pl.when(pl.program_id(0) == 0)
    def _():
        dgain_ref[...] = jnp.zeros_like(dgain_ref)

    d_gain, dattn_ref[...], dgpre_ref[...], grad_ref[0] = mixer_back_head(
        dmix_ref, w_ref, attn_ref, gpre_ref, gain_ref, resp_ref
    )
    dgain_ref[0:1, :] += d_gain


def mixer_back_head(dmix_ref, w_ref, attn_ref, gpre_ref, gain_ref, resp_ref):
    d_gated = mm(dmix_ref[...], w_ref[...])
    attn = attn_ref[...]
    size = lax.rsqrt(jnp.mean(attn * attn, axis=-1, keepdims=True) + 1e-05)
    unit = attn * size
    gate = gpre_ref[...]
    slope = jax.nn.sigmoid(gate)
    swish = gate * slope
    gain = gain_ref[...]
    d_gpre = (d_gated * (unit * gain) * (slope * (1.0 + gate * (1.0 - slope)))).astype(BF16)
    d_normed = d_gated * swish
    d_gain = jnp.sum(d_normed * unit, axis=0, keepdims=True)
    d_unit = d_normed * gain
    d_attn = size * (d_unit - unit * jnp.mean(d_unit * unit, axis=-1, keepdims=True))
    d_attn = d_attn.astype(BF16)
    return d_gain, d_attn, d_gpre, mm(resp_ref[...], d_attn, TN).astype(BF16)


def mixer_back(d_mixer, weights, attn, gpre, gain, resp):
    tokens, width = d_mixer.shape
    whole = lambda shape: pl.BlockSpec(shape, lambda h: (0,) * len(shape))
    return pl.pallas_call(
        mixer_back_kernel,
        grid=(H,),
        in_specs=[
            whole((tokens, width)),
            pl.BlockSpec((width, DV), lambda h: (0, h + AT_OUT // DV)),
            pl.BlockSpec((tokens, DV), lambda h: (0, h)),
            pl.BlockSpec((tokens, DV), lambda h: (0, h)),
            whole((1, DV)),
            pl.BlockSpec((tokens, DK), lambda h: (0, h)),
        ],
        out_specs=[
            pl.BlockSpec((tokens, DV), lambda h: (0, h)),
            pl.BlockSpec((tokens, DV), lambda h: (0, h)),
            pl.BlockSpec((1, DK, DV), lambda h: (h, 0, 0)),
            whole((8, DV)),
        ],
        out_shape=[
            jax.ShapeDtypeStruct((tokens, H * DV), BF16),
            jax.ShapeDtypeStruct((tokens, H * DV), BF16),
            jax.ShapeDtypeStruct((H, DK, DV), BF16),
            jax.ShapeDtypeStruct((8, DV), F32),
        ],
        compiler_params=params(),
        cost_estimate=cost(2 * tokens * width * H * DV, 2e7),
        name="mixer_back",
    )(d_mixer, weights, attn, gpre, gain, resp)


def ffn_kernel(
    h_ref, dout_ref, y_ref, gain_ref, turn_ref, weights_ref,
    out_ref, act_ref, dgu_ref, dy_ref, dmix_ref, dgain_ref,
    w_ref, acts_ref, dg_ref, du_ref, res_ref, dh_ref, load_sem, *, inner, block, gain_row,
):
    step = pl.program_id(0)
    blocks = inner // block
    across = dh_ref.shape[1] // (pl.num_programs(0) - blocks)

    def load(which, n):
        cols = pl.multiple_of(n * block, block)
        return pltpu.make_async_copy(
            weights_ref.at[:, pl.ds(AT_FFN + which * inner + cols, block)],
            w_ref.at[which, :, pl.ds(cols, block)],
            load_sem.at[which, n],
        )

    @pl.when(step == 0)
    def _():
        for n in range(blocks):
            for which in range(3):
                load(which, n).start()

    @pl.when(step < blocks)
    def _():
        for which in range(3):
            load(which, step).wait()
        cols = pl.ds(pl.multiple_of(step * block, block), block)
        hidden = h_ref[...]
        gate = mm(hidden, w_ref[0, :, cols])
        up = mm(hidden, w_ref[1, :, cols])
        d_act = mm(dout_ref[...], w_ref[2, :, cols])
        slope = jax.nn.sigmoid(gate)
        swish = gate * slope
        act = (swish * up).astype(BF16)
        act_ref[...] = act
        acts_ref[:, cols] = act
        d_gate = (d_act * up * slope * (1.0 + gate * (1.0 - slope))).astype(BF16)
        d_up = (d_act * swish).astype(BF16)
        dgu_ref[0] = d_gate
        dg_ref[:, cols] = d_gate
        dgu_ref[1] = d_up
        du_ref[:, cols] = d_up

    @pl.when(step >= blocks)
    def _():
        rows = pl.ds(pl.multiple_of((step - blocks) * across, across), across)
        res_ref[:, rows] = y_ref[:, rows] + mm(acts_ref[...], w_ref[2, rows, :], NT)
        dh_ref[:, rows] = mm(dg_ref[...], w_ref[0, rows, :], NT) + mm(du_ref[...], w_ref[1, rows, :], NT)

    @pl.when(step == pl.num_programs(0) - 1)
    def _():
        out_ref[...] = mm(res_ref[...], turn_ref[...], NT).astype(BF16)
        value = y_ref[...]
        size = lax.rsqrt(jnp.mean(value * value, axis=-1, keepdims=True) + 1e-06)
        unit = value * size
        d_hidden = dh_ref[...]
        dgain_ref[...] = jnp.zeros_like(dgain_ref)
        dgain_ref[0:1, :] = jnp.sum(d_hidden * unit, axis=0, keepdims=True)
        d_unit = d_hidden * gain_ref[gain_row : gain_row + 1, :]
        d_y = dout_ref[...].astype(F32) + size * (
            d_unit - unit * jnp.mean(d_unit * unit, axis=-1, keepdims=True)
        )
        dy_ref[...] = d_y
        dmix_ref[...] = d_y.astype(BF16)


def feed_forward(hidden, d_out, y1, gains, gain_row, turn, weights, inner):
    tokens, width = hidden.shape
    block, across = 256, 256
    blocks = inner // block
    once = lambda shape: pl.BlockSpec(shape, lambda j: (0,) * len(shape), pipeline_mode=pl.Buffered(1))
    whole = lambda shape: pl.BlockSpec(shape, lambda j: (0,) * len(shape))
    at = lambda j: jnp.minimum(j, blocks - 1)
    return pl.pallas_call(
        functools.partial(ffn_kernel, inner=inner, block=block, gain_row=gain_row),
        grid=(blocks + width // across,),
        in_specs=[
            once((tokens, width)),
            once((tokens, width)),
            once((tokens, width)),
            once(gains.shape),
            once((width, width)),
            pl.BlockSpec(memory_space=pl.ANY),
        ],
        out_specs=[
            whole((tokens, width)),
            pl.BlockSpec((tokens, block), lambda j: (0, at(j))),
            pl.BlockSpec((2, tokens, block), lambda j: (0, 0, at(j))),
            whole((tokens, width)), whole((tokens, width)), whole((8, width)),
        ],
        out_shape=[
            jax.ShapeDtypeStruct((tokens, width), BF16),
            jax.ShapeDtypeStruct((tokens, inner), BF16),
            jax.ShapeDtypeStruct((2, tokens, inner), BF16),
            jax.ShapeDtypeStruct((tokens, width), F32),
            jax.ShapeDtypeStruct((tokens, width), BF16),
            jax.ShapeDtypeStruct((8, width), F32),
        ],
        scratch_shapes=[
            pltpu.VMEM((3, width, inner), BF16),
            pltpu.VMEM((tokens, inner), BF16),
            pltpu.VMEM((tokens, inner), BF16),
            pltpu.VMEM((tokens, inner), BF16),
            pltpu.VMEM((tokens, width), F32),
            pltpu.VMEM((tokens, width), F32),
            pltpu.SemaphoreType.DMA((3, blocks)),
        ],
        compiler_params=params(),
        cost_estimate=cost(12 * tokens * width * inner, 3e7),
        name="feed_forward",
    )(hidden, d_out, y1, gains, turn, weights)


BLOCK = HC
LEAD, EVERY = 7, 3


def other_index(step):
    return step - jnp.clip((step - LEAD + EVERY - 1) // EVERY, 0, H)


class Blocks:
    def __init__(self, inner):
        self.ups, self.downs = inner // (BLOCK // 2), inner // BLOCK
        self.outs = H * DV // BLOCK
        self.others = self.ups + self.downs + 2 * self.outs
        self.count = self.others + H + 1
        self.starts = [0, self.ups, self.ups + self.downs, self.ups + self.downs + self.outs, self.others]
        self.tail = inner - self.downs * BLOCK
        heads = [LEAD + EVERY * h for h in range(H)]
        rest = [n for n in range(self.count - 1) if n not in heads]
        parts = [rest[low:high] for low, high in zip(self.starts, self.starts[1:])]
        self.up_at, self.down_at, self.out_at, self.gate_at = parts
        self.head_at = heads

    def index(self, kind):
        low, high = self.starts[kind], self.starts[kind + 1]
        return lambda s: jnp.clip(other_index(s) - low, 0, high - low - 1)


def dot_blocks(left, right):
    return lax.dot_general(left, right, (NN, ((), ())), preferred_element_type=F32)


def flip_to(bit):
    here = lax.axis_index("seq")
    along_x = here + 1 - 2 * lax.rem(here, 2)
    along_y = here + 2 - 4 * (here // 2)
    return {"dp": lax.axis_index("dp"), "seq": (2 - bit) * along_x + (bit - 1) * along_y}


def reduce_kernel(
    dout_any, hmid_any, hidden_any, x_any, dy_any, turn_any, dres_ref,
    act_ref, tail_ref, dgu_ref, gated_ref, wout_ref, attn_ref, gpre_ref, gain_ref, resp_ref, win_ref, wl_ref,
    gains_ref, dffn_ref,
    p_ref, taps_q_ref, taps_k_ref, taps_v_ref, logit_ref, par_ref, cols_ref, back_ref, segr_ref, sin_ref, maps_ref,
    inv_ref, upd_ref, st_ref, stm_ref, amap_ref, rmap_ref,
    sum_ref, dx_ref, small_ref,
    taps_ref, dlogit_ref, dtaps_ref, dpar_ref, dgain_ref, dattn_ref, dgpre_ref, lgrad_ref, acc_ref, left_ref,
    total_ref, other_ref,
    beta_ref, decay_ref, cum_ref, pf_ref, pre_ref, dmix_ref, dstate_ref, dbeta_ref, ddecay_ref,
    turn_ref, dps_ref, halo_ref, grads_ref, halves_ref,
    core_keep, core_send, core_recv, near_keep, near_send, near_recv,
    z_keep, pair_send, pair_recv, cross_send, cross_recv, far_send, far_recv, done_ref,
    core_ss, core_rs, near_ss, near_rs, pair_ss, pair_rs, cross_ss, cross_rs, far_ss, far_rs, done_ss, done_rs, own_sem,
    halo_ss, halo_rs, grads_ss, grads_rs, load_sem, small_ss, small_rs, *, blocks,
):
    step = pl.program_id(0)
    steps = pl.num_programs(0)
    place = lax.axis_index("seq")
    count = blocks.count
    half = core_keep.shape[1] * core_keep.shape[2]
    quarter = half // SPOTS
    piece = quarter // PLANES
    mesh = dict(device_id_type=pl.DeviceIdType.MESH)

    def remote(source, target, send, recv, to):
        return pltpu.make_async_remote_copy(
            src_ref=source, dst_ref=target, send_sem=send, recv_sem=recv, device_id=to, **mesh
        )

    def to_core(n):
        mine, slot = lax.rem(n, 3), lax.rem(n, 4)
        return remote(core_send.at[mine], core_recv.at[slot], core_ss.at[mine], core_rs.at[slot], device(core=1))

    def to_near(n):
        slot = lax.rem(n, 4)
        return remote(
            near_send.at[slot], near_recv.at[slot], near_ss.at[slot], near_rs.at[slot], flip_to(1 + lax.rem(n, 2))
        )

    def to_far(n):
        slot = lax.rem(n, 4)
        return remote(
            far_send.at[slot], far_recv.at[slot], far_ss.at[slot], far_rs.at[slot], flip_to(2 - lax.rem(n, 2))
        )

    z = lax.axis_index("dp") // CORES
    inner = (z > 0) & (z < PLANES - 1)
    outer_plane = (z == 0) | (z == PLANES - 1)

    def to_pair(n, pieces):
        slot = lax.rem(n, 4)
        return remote(
            pair_send.at[slot, 0:pieces], pair_recv.at[slot, 0:pieces], pair_ss.at[slot], pair_rs.at[slot],
            device(planes=1 + 2 * lax.rem(z, 2)),
        )

    def to_cross(n, outside):
        planes = 2 if outside else 2 * z - 1
        slot = lax.rem(n, 4)
        return remote(
            cross_send.at[slot, outside], cross_recv.at[n], cross_ss.at[slot, outside], cross_rs.at[n],
            device(planes=planes),
        )

    def target(n, which):
        spot = place if which == 0 else flip_spot(place, 2 - lax.rem(n, 2))
        return sum_ref.at[
            pl.ds(pl.multiple_of(spot * piece, piece), piece), pl.ds(pl.multiple_of(n * BLOCK, BLOCK), BLOCK)
        ]

    def spread(n, which):
        slot = lax.rem(n, 4)
        return remote(
            done_ref.at[slot, which], target(n, which), done_ss.at[slot, which], done_rs.at[n, which],
            flip_to(1 + lax.rem(n, 2)),
        )

    def keep(n, which):
        slot = lax.rem(n, 4)
        return pltpu.make_async_copy(done_ref.at[slot, which], target(n, which), own_sem.at[slot, which])

    upper = place // 2 == 1
    second = lax.rem(place, 2) == 1

    def give_grads(head):
        return remote(
            lgrad_ref.at[head], grads_ref.at[0, head], grads_ss.at[0, head], grads_rs.at[0, head], device(spot=1)
        )

    def give_half(head):
        return remote(
            halves_ref.at[head], grads_ref.at[1, head], grads_ss.at[1, head], grads_rs.at[1, head], device(spot=2)
        )

    def give_small(stage):
        to = (dict(core=1), dict(spot=1), dict(spot=2), dict(planes=1), dict(planes=2), dict(planes=3))[stage]
        return remote(
            total_ref.at[min(stage, 3)], other_ref.at[stage], small_ss.at[stage], small_rs.at[stage], device(**to)
        )

    def load(at, source, to):
        return pltpu.make_async_copy(source, to, load_sem.at[at])

    def final_loads():
        width = turn_any.shape[0]
        copies = []
        for n in range(2):
            cols = slice(n * (width // 2), (n + 1) * (width // 2))
            copies.append(load(n, turn_any.at[:, cols], turn_ref.at[n]))
            rows = x_any.shape[0]
            copies.append(load(2 + n, x_any.at[:, cols], turn_ref.at[2, n * rows : (n + 1) * rows]))
            for q in range(SPOTS):
                copies.append(
                    load(4 + n * SPOTS + q, dy_any.at[q * quarter : (q + 1) * quarter, cols], core_keep.at[n, q])
                )
        return copies

    def final_stores():
        width = dx_ref.shape[1]
        return [
            load(
                n * SPOTS + q,
                core_keep.at[n, q],
                dx_ref.at[q * quarter : (q + 1) * quarter, n * (width // 2) : (n + 1) * (width // 2)],
            )
            for n in range(2)
            for q in range(SPOTS)
        ]

    def give_halo(head):
        to = {"dp": lax.axis_index("dp"), "seq": lax.rem(place + SPOTS - 1, SPOTS)}
        return remote(dps_ref.at[0:HALO], halo_ref.at[head], halo_ss.at[head], halo_rs.at[head], to)

    @pl.when(step == 0)
    def _():
        greet([dict(planes=d) for d in (1, 2, 3)] + [dict(spot=s) for s in (1, 2, 3)] + [dict(core=1)])
        dgain_ref[...] = jnp.zeros_like(dgain_ref)
        acc_ref[...] = jnp.zeros_like(acc_ref)

    def left(n):
        tokens = dres_ref.shape[0]
        source = (hmid_any, dout_any, hidden_any.at[HALO : HALO + tokens])[n]
        return load(n, source, left_ref.at[n % 2])

    for n, at in enumerate((1, 0, 3, 2)):

        @pl.when(step == n)
        def _(n=n, at=at):
            if n == 0:
                left(0).start()
            if n < 2:
                left(n + 1).start()
            if n < 3:
                left(n).wait()
                turn_ref[at] = jnp.transpose(left_ref[n % 2])
            else:
                turn_ref[at] = jnp.transpose(dres_ref[...])

    def at_stage(lag, sent):
        n = step - lag

        def run(body):
            @pl.when((n >= 0) & (n < count))
            def _():
                @pl.when(n >= sent)
                def _():
                    body(n, True)

                body(n, False)

        return run

    @at_stage(10, 4)
    def _(n, free):
        if free:
            for which in range(2):
                spread(n - 4, which).wait_send()
                keep(n - 4, which).wait()
            return
        slot = lax.rem(n, 4)
        to_far(n).wait_recv()
        for which in range(2):
            total = far_send[slot, which].astype(F32) + far_recv[slot, 1 - which].astype(F32)
            done_ref[slot, which] = total.astype(BF16)
            keep(n, which).start()
            spread(n, which).start()

    @at_stage(8, 4)
    def _(n, free):
        if free:
            to_far(n - 4).wait_send()
            return
        slot = lax.rem(n, 4)
        to_cross(n, 0).wait_recv()
        total = (z_keep[slot, 0] + cross_recv[n].astype(F32)).astype(BF16)
        far_send[slot, 0], far_send[slot, 1] = total[:piece], total[piece:]
        to_far(n).start()

    @at_stage(6, 4)
    def _(n, free):
        slot = lax.rem(n, 4)
        if free:

            @pl.when(inner)
            def _():
                to_cross(n - 4, 0).wait_send()
                to_cross(n - 4, 1).wait_send()

            return

        @pl.when(outer_plane)
        def _():
            to_pair(n, 1).wait_recv()

        @pl.when(inner)
        def _():
            to_pair(n, 3).wait_recv()
            for outside, at in enumerate((5 - 2 * z, 2)):
                cross_send[slot, outside] = (
                    z_keep[slot, at] + pair_recv[slot, 1 + outside].astype(F32)
                ).astype(BF16)
                to_cross(n, outside).start()

        z_keep[slot, 0] += pair_recv[slot, 0].astype(F32)

    @at_stage(4, 4)
    def _(n, free):
        slot = lax.rem(n, 4)
        if free:

            @pl.when(outer_plane)
            def _():
                to_pair(n - 4, 3).wait_send()

            @pl.when(inner)
            def _():
                to_pair(n - 4, 1).wait_send()

            return
        to_near(n).wait_recv()
        for which in range(2):
            total = near_keep[slot, which] + near_recv[slot, which].astype(F32)
            for d in range(PLANES):
                z_keep[slot, d, which * piece : (which + 1) * piece] = total[d * piece : (d + 1) * piece]

        @pl.when(outer_plane)
        def _():
            up = 1 - z // 3
            for k in range(3):
                pair_send[slot, k] = z_keep[slot, up * (3 - k) + (1 - up) * (1 + k)].astype(BF16)
            to_pair(n, 3).start()

        @pl.when(inner)
        def _():
            pair_send[slot, 0] = z_keep[slot, 2 * z - 1].astype(BF16)
            to_pair(n, 1).start()

    @at_stage(2, 4)
    def _(n, free):
        if free:
            to_near(n - 4).wait_send()
            return
        slot, mine = lax.rem(n, 4), lax.rem(n, 3)
        first = 1 + lax.rem(n, 2)
        to_core(n).wait_recv()
        whole = lambda quarter: core_keep[mine, quarter] + core_recv[slot, quarter].astype(F32)
        near_keep[slot, 0] = whole(0)
        near_keep[slot, 1] = whole(3 - first)
        near_send[slot, 0] = whole(first).astype(BF16)
        near_send[slot, 1] = whole(3).astype(BF16)
        to_near(n).start()

    since = step - LEAD
    heads_turn = (since >= 0) & (since < EVERY * H) & (lax.rem(jnp.maximum(since, 0), EVERY) == 0)
    other = other_index(step)

    def put(product):
        mine = lax.rem(step, 3)

        @pl.when(step >= 3)
        def _():
            to_core(step - 3).wait_send()

        for q in range(SPOTS):
            core_keep[mine, q] = product[q * quarter : (q + 1) * quarter]
            core_send[mine, q] = product[half + q * quarter : half + (q + 1) * quarter].astype(BF16)
        to_core(step).start()

    def on(kind):
        low, high = blocks.starts[kind], blocks.starts[kind + 1]
        return pl.when((other >= low) & (other < high) & jnp.logical_not(heads_turn))

    @on(0)
    def _():
        put(dot_blocks(turn_ref[1], jnp.concatenate([dgu_ref[0], dgu_ref[1]], axis=1)))

    @on(1)
    def _():
        put(dot_blocks(turn_ref[0], act_ref[...]))

    @on(2)
    def _():
        put(dot_blocks(turn_ref[2], gated_ref[...]))

    @on(3)
    def _():
        gate = other - blocks.starts[3]
        value = jnp.concatenate([dgpre_ref[2 * gate], dgpre_ref[2 * gate + 1]], axis=1)
        acc_ref[...] += mm(value, win_ref[...], NT)
        put(dot_blocks(turn_ref[3], value))

    @pl.when(step == count - 1)
    def _():
        down = dot_blocks(turn_ref[0], tail_ref[...])
        gates = dot_blocks(turn_ref[3], dlogit_ref[...].astype(BF16))
        acc_ref[...] += mm(dlogit_ref[...], wl_ref[...], NT)
        rest = jnp.zeros((down.shape[0], BLOCK - down.shape[1] - LANES), F32)
        put(jnp.concatenate([down, gates, rest], axis=1))

    @pl.when(heads_turn)
    def _():
        head = since // EVERY

        @pl.when(place > 0)
        def _():
            give_halo(head).wait_send()

        @pl.when(place < SPOTS - 1)
        def _():
            give_halo(head).wait_recv()
            tokens = dps_ref.shape[0] - HALO
            dps_ref[tokens:, :] = (
                dps_ref[tokens:, :].astype(F32) + halo_ref[head].astype(F32)
            ).astype(BF16)

        value = dps_ref[HALO:, :]
        acc_ref[...] += mm(value, win_ref[...], NT)
        put(dot_blocks(turn_ref[3], value))

    @pl.when(step < H)
    def _():
        d_gain, dattn_ref[step], dgpre_ref[step], lgrad_ref[step] = mixer_back_head(
            dres_ref, wout_ref, attn_ref, gpre_ref, gain_ref, resp_ref
        )
        dgain_ref[...] += d_gain
        give_grads(step).start()

    @pl.when((step >= 2) & (step < H + 2))
    def _():
        head = step - 2
        give_grads(head).wait()

        @pl.when(upper)
        def _():
            mine, theirs = lgrad_ref[head], grads_ref[0, head]
            earlier = jnp.where(second, theirs, mine)
            later = jnp.where(second, mine, theirs)
            through = jnp.where(second, maps_ref[1, head], maps_ref[0, head])
            halves_ref[head] = (earlier.astype(F32) + mm(through, later, TN)).astype(BF16)
            give_half(head).start()

    ahead = since + EVERY
    for phase in range(PHASES):

        @pl.when((ahead >= 0) & (ahead < EVERY * H) & (lax.rem(jnp.maximum(ahead, 0), EVERY) == phase))
        def _(phase=phase):
            head = ahead // EVERY

            def entering():
                @pl.when(upper)
                def _():
                    grads_ref[1, head] = jnp.zeros((DK, DV), BF16)
                    give_half(head).wait_send()

                @pl.when(jnp.logical_not(upper))
                def _():
                    give_half(head).wait_recv()

                d_state = grads_ref[1, head].astype(F32)
                nearer = grads_ref[0, head].astype(F32) + mm(maps_ref[1, head], d_state, TN)
                return jnp.where(second, d_state, nearer)

            if phase == 0:
                join_taps(taps_ref, taps_q_ref, taps_k_ref, taps_v_ref)
            backward_head(
                phase, head, entering, p_ref, taps_ref, logit_ref, par_ref, cols_ref, back_ref, segr_ref,
                dattn_ref.at[head], sin_ref, inv_ref, upd_ref, st_ref, stm_ref, amap_ref, rmap_ref,
                dps_ref, dlogit_ref, dtaps_ref, dpar_ref, beta_ref, decay_ref, cum_ref, pf_ref, pre_ref, dmix_ref,
                dstate_ref, dbeta_ref, ddecay_ref,
            )
            if phase == PHASES - 1:
                total_ref[0, pl.ds(pl.multiple_of(head * 8, 8), 8), :] = dtaps_ref[...]

                @pl.when(place > 0)
                def _():
                    give_halo(head).start()

    @pl.when(step == count)
    def _():
        for copy in final_loads():
            copy.start()

    @pl.when(step == count + 2)
    def _():
        for copy in final_loads():
            copy.wait()
        tokens, width = acc_ref.shape
        middle = width // 2
        halves_of = lambda ref: jnp.concatenate([ref[0], ref[1]], axis=1)
        value = jnp.concatenate([turn_ref[2, :tokens], turn_ref[2, tokens:]], axis=1).astype(F32)
        size = lax.rsqrt(jnp.mean(value * value, axis=-1, keepdims=True) + 1e-06)
        unit = value * size
        d_hidden = acc_ref[...]
        d_gain = jnp.sum(d_hidden * unit, axis=0, keepdims=True)
        d_unit = d_hidden * gains_ref[0:1, :]
        through = size * (d_unit - unit * jnp.mean(d_unit * unit, axis=-1, keepdims=True))
        d_y = [jnp.concatenate([core_keep[n, q] for q in range(SPOTS)], axis=0) for n in range(2)]
        total = jnp.concatenate(d_y, axis=1) + through

        def natural(part):
            return mm(part[:, :middle], turn_ref[0], NT) + mm(part[:, middle:], turn_ref[1], NT)

        high, low = halves(total)
        total = natural(high) + natural(low)
        for n in range(2):
            for q in range(SPOTS):
                core_keep[n, q] = total[q * quarter : (q + 1) * quarter, n * middle : (n + 1) * middle]
        for copy in final_stores():
            copy.start()
        gains = jnp.concatenate([d_gain, dffn_ref[0:1, :], jnp.zeros((6, width), F32)], axis=0)
        high, mid = halves(gains)
        gains = natural(high) + natural(mid) + natural((gains - high.astype(F32)) - mid.astype(F32))
        base = 8 * H
        total_ref[0, base : base + 8, :] = gains[:, :middle]
        total_ref[0, base + 8 : base + 16, :] = gains[:, middle:]
        total_ref[0, base + 16 : base + 24, : dgain_ref.shape[1]] = dgain_ref[...]
        total_ref[0, base + 16 : base + 24, dgain_ref.shape[1] : dgain_ref.shape[1] + LANES] = dpar_ref[...]
        total_ref[0, base + 16 : base + 24, dgain_ref.shape[1] + LANES :] = jnp.zeros((8, LANES), F32)
        give_small(0).start()

    for stage in range(3):

        @pl.when(step == count + 3 + stage)
        def _(stage=stage):
            give_small(stage).wait_recv()
            total_ref[stage + 1] = total_ref[stage] + other_ref[stage]
            for later in (stage + 1,) if stage < 2 else (3, 4, 5):
                give_small(later).start()

    @pl.when(step == count + 6)
    def _():
        total = total_ref[3]
        for stage in (3, 4, 5):
            give_small(stage).wait_recv()
            total += other_ref[stage]
        small_ref[...] = total
        for stage in range(6):
            give_small(stage).wait_send()
        for copy in final_stores():
            copy.wait()

    @pl.when(step == steps - 1)
    def _():
        for n in range(count - 4, count):
            if n >= count - 3:
                to_core(n).wait_send()
            to_near(n).wait_send()
            to_far(n).wait_send()

            @pl.when(outer_plane)
            def _(n=n):
                to_pair(n, 3).wait_send()

            @pl.when(inner)
            def _(n=n):
                to_pair(n, 1).wait_send()
                to_cross(n, 0).wait_send()
                to_cross(n, 1).wait_send()

            for which in range(2):
                spread(n, which).wait_send()
                keep(n, which).wait()

        def arrived(n, carry):
            for which in range(2):
                spread(n, which).wait_recv()
            return carry

        lax.fori_loop(0, count, arrived, 0)


def reduce_gradients(
    d_out, hidden_mid, hidden, x, d_y, turn, d_mixer, act, d_gu, gated, weights, attn, gpre, gain_out, resp, gains,
    d_ffn, proj, taps, logits, par, cols, back, segr, state_in, maps, saved,
):
    tokens, width = d_mixer.shape
    rows = hidden.shape[0]
    chunks = tokens // CHUNK
    blocks = Blocks(act.shape[1])
    half = width // CORES
    quarter = half // SPOTS
    piece = quarter // PLANES
    small = 8 * H + 24
    anywhere = pl.BlockSpec(memory_space=pl.ANY)
    whole = lambda shape: pl.BlockSpec(shape, lambda s: (0,) * len(shape))
    once = lambda shape: pl.BlockSpec(shape, lambda s: (0,) * len(shape), pipeline_mode=pl.Buffered(1))
    coming = lambda s: jnp.clip((s - (LEAD - EVERY)) // EVERY, 0, H - 1)
    starting = lambda s: jnp.minimum(s, H - 1)
    by_head = lambda shape: pl.BlockSpec(shape, lambda s: (coming(s),) + (0,) * (len(shape) - 1))
    across = lambda shape, at: pl.BlockSpec(shape, lambda s: (0, at(s)))
    sem = pltpu.SemaphoreType.DMA
    up, down, out, gate = (blocks.index(kind) for kind in range(4))
    first_gate = blocks.gate_at[0]

    def win(s):
        no_head = ((s - LEAD) % EVERY != 0) | (s > blocks.head_at[-1])
        is_gate = (s >= first_gate) & (s <= blocks.gate_at[-1]) & no_head
        head = jnp.clip((s - LEAD + EVERY - 1) // EVERY, 0, H - 1)
        return jnp.where(is_gate, AT_GATE // BLOCK + gate(s), H - 1 - head)

    return blocks, pl.pallas_call(
        functools.partial(reduce_kernel, blocks=blocks),
        grid=(blocks.count + 10,),
        in_specs=[anywhere] * 6
        + [
            once((tokens, width)),
            across((tokens, BLOCK), down),
            pl.BlockSpec(
                (tokens, blocks.tail), lambda s: (0, blocks.downs * BLOCK // blocks.tail), pipeline_mode=pl.Buffered(1)
            ),
            pl.BlockSpec((2, tokens, BLOCK // 2), lambda s: (0, 0, up(s))),
            across((tokens, BLOCK), out),
            pl.BlockSpec((width, DV), lambda s: (0, AT_OUT // DV + starting(s))),
            across((tokens, DV), starting),
            across((tokens, DV), starting),
            once((1, DV)),
            across((tokens, DK), starting),
            across((width, BLOCK), win),
            pl.BlockSpec((width, LANES), lambda s: (0, AT_LOGIT // LANES), pipeline_mode=pl.Buffered(1)),
            once((8, width)),
            once((8, width)),
            across((rows, HC), coming),
            *taps_specs(coming),
            once((rows, LANES)),
            once((8, LANES)),
            once((tokens, LANES)),
            once((rows, LANES)),
            once(segr.shape),
            by_head((1, DK, DV)),
            once((2, H, DK, DK)),
            by_head((1, chunks, CHUNK, CHUNK)),
            by_head((1, tokens, DV + DK)),
            by_head((1, chunks, DK, DV)),
            by_head((1, chunks, DK, DK)),
            by_head((1, chunks, DK, DK)),
            by_head((1, chunks, CHUNK, DK)),
        ],
        out_specs=[anywhere, anywhere, whole((small, BLOCK))],
        out_shape=[
            jax.ShapeDtypeStruct((SPOTS * piece, blocks.count * BLOCK), BF16),
            jax.ShapeDtypeStruct((tokens, width), F32),
            jax.ShapeDtypeStruct((small, BLOCK), F32),
        ],
        scratch_shapes=[
            pltpu.VMEM((8, HC), F32),
            pltpu.VMEM((tokens, LANES), F32),
            pltpu.VMEM((8, HC), F32),
            pltpu.VMEM((8, LANES), F32),
            pltpu.VMEM((8, DV), F32),
            pltpu.VMEM((H, tokens, DV), BF16),
            pltpu.VMEM((H, tokens, DV), BF16),
            pltpu.VMEM((H, DK, DV), BF16),
            pltpu.VMEM((tokens, width), F32),
            pltpu.VMEM((2, tokens, width), BF16),
            pltpu.VMEM((4, small, BLOCK), F32),
            pltpu.VMEM((6, small, BLOCK), F32),
            pltpu.VMEM((tokens, LANES), F32),
            pltpu.VMEM((tokens, LANES), F32),
            pltpu.VMEM((tokens, LANES), F32),
            pltpu.VMEM((rows, HC), F32),
            pltpu.VMEM((tokens, HC), F32),
            pltpu.VMEM((rows + 8, HC), F32),
            pltpu.VMEM((chunks, DK, DV), F32),
            pltpu.VMEM((tokens, LANES), F32),
            pltpu.VMEM((tokens, LANES), F32),
            pltpu.VMEM((4, width, tokens), BF16),
            pltpu.VMEM((rows, HC), BF16),
            pltpu.VMEM((H, HALO, HC), BF16),
            pltpu.VMEM((2, H, DK, DV), BF16),
            pltpu.VMEM((H, DK, DV), BF16),
            pltpu.VMEM((3, SPOTS, quarter, BLOCK), F32),
            pltpu.VMEM((3, SPOTS, quarter, BLOCK), BF16),
            pltpu.VMEM((4, SPOTS, quarter, BLOCK), BF16),
            pltpu.VMEM((4, 2, quarter, BLOCK), F32),
            pltpu.VMEM((4, 2, quarter, BLOCK), BF16),
            pltpu.VMEM((4, 2, quarter, BLOCK), BF16),
            pltpu.VMEM((4, PLANES, 2 * piece, BLOCK), F32),
            pltpu.VMEM((4, PLANES - 1, 2 * piece, BLOCK), BF16),
            pltpu.VMEM((4, PLANES - 1, 2 * piece, BLOCK), BF16),
            pltpu.VMEM((4, 2, 2 * piece, BLOCK), BF16),
            pltpu.VMEM((blocks.count, 2 * piece, BLOCK), BF16),
            pltpu.VMEM((4, 2, piece, BLOCK), BF16),
            pltpu.VMEM((4, 2, piece, BLOCK), BF16),
            pltpu.VMEM((4, 2, piece, BLOCK), BF16),
            sem((3,)), sem((4,)), sem((4,)), sem((4,)), sem((4,)), sem((4,)),
            sem((4, 2)), sem((blocks.count,)), sem((4,)), sem((4,)),
            sem((4, 2)), sem((blocks.count, 2)), sem((4, 2)),
            sem((H,)), sem((H,)), sem((2, H)), sem((2, H)),
            sem((4 + 2 * SPOTS,)), sem((6,)), sem((6,)),
        ],
        compiler_params=params(collective_id=1, has_side_effects=True),
        cost_estimate=cost(1e11, 1e8),
        name="reduce_gradients",
    )(
        d_out, hidden_mid, hidden, x, d_y, turn, d_mixer, act, act, d_gu, gated, weights, attn, gpre, gain_out, resp,
        weights, weights, gains, d_ffn, proj, taps, taps, taps, logits, par, cols, back, segr, state_in, maps, *saved,
    )


def unpack_kernel(
    sum_ref, small_ref, dx_ref, query_ref, key_ref, value_ref, gate_ref, logit_ref, out_ref, wg_ref, wu_ref, wd_ref,
    taps_ref, mix_ref, ffn_ref, norm_ref, par_ref, dx_out, *, blocks
):
    dx_out[...] = dx_ref[...]
    for h in range(H):
        part = small_ref[8 * h : 8 * h + CONV, :]
        taps_ref[:, h * DK : (h + 1) * DK] = part[:, :DK]
        taps_ref[:, (H + h) * DK : (H + h + 1) * DK] = part[:, DK : 2 * DK]
        taps_ref[:, 2 * H * DK + h * DV : 2 * H * DK + (h + 1) * DV] = part[:, 2 * DK :]
    for row, ref in enumerate((mix_ref, ffn_ref)):
        for n in range(2):
            at = 8 * H + 8 * n + row
            ref[:, n * small_ref.shape[1] : (n + 1) * small_ref.shape[1]] = small_ref[at : at + 1, :]
    norm_ref[...] = small_ref[8 * H + 16 : 8 * H + 17, :DV]
    par_ref[...] = small_ref[8 * H + 16 : 8 * H + 24, DV : DV + LANES]

    def part(n, low=0, high=BLOCK):
        return sum_ref[:, n * BLOCK + low : n * BLOCK + high].astype(F32)

    for h, n in enumerate(blocks.head_at):
        query_ref[:, h * DK : (h + 1) * DK] = part(n, 0, DK)
        key_ref[:, h * DK : (h + 1) * DK] = part(n, DK, 2 * DK)
        value_ref[:, h * DV : (h + 1) * DV] = part(n, 2 * DK, HC)
    for i, n in enumerate(blocks.gate_at):
        gate_ref[:, i * BLOCK : (i + 1) * BLOCK] = part(n)
    for i, n in enumerate(blocks.out_at):
        out_ref[i * BLOCK : (i + 1) * BLOCK, :] = jnp.transpose(part(n))
    middle = BLOCK // 2
    for i, n in enumerate(blocks.up_at):
        wg_ref[:, i * middle : (i + 1) * middle] = part(n, 0, middle)
        wu_ref[:, i * middle : (i + 1) * middle] = part(n, middle, BLOCK)
    for i, n in enumerate(blocks.down_at):
        wd_ref[i * BLOCK : (i + 1) * BLOCK, :] = jnp.transpose(part(n))
    last, tail = blocks.count - 1, blocks.tail
    wd_ref[blocks.downs * BLOCK :, :] = jnp.transpose(part(last, 0, tail))
    logit_ref[...] = jnp.transpose(part(last, tail, tail + LANES))[: 2 * H]


def unpack_gradients(blocks, sums, small, d_inputs):
    rows = sums.shape[0]
    inner = blocks.downs * BLOCK + blocks.tail
    width = d_inputs.shape[1]
    shapes = [
        (rows, H * DK), (rows, H * DK), (rows, H * DV), (rows, H * DV), (2 * H, rows), (H * DV, rows),
        (rows, inner), (rows, inner), (inner, rows), (CONV, H * HC), (1, width), (1, width), (1, DV), (8, LANES),
        d_inputs.shape,
    ]
    return pl.pallas_call(
        functools.partial(unpack_kernel, blocks=blocks),
        out_shape=[jax.ShapeDtypeStruct(shape, F32) for shape in shapes],
        compiler_params=params(),
        cost_estimate=cost(0, 6 * sums.size),
        name="unpack_gradients",
    )(sums, small, d_inputs)


def input_grad_kernel(
    dp_ref, dg_ref, dl_ref, w_ref, wl_ref, x_ref, gain_ref, dy_ref, out_ref, dgain_ref, acc_ref
):
    step = pl.program_id(0)

    @pl.when(step == 0)
    def _():
        acc_ref[...] = mm(dl_ref[...], wl_ref[...], NT)

    @pl.when(step < H)
    def _():
        acc_ref[...] += mm(dp_ref[...], w_ref[...], NT)

    @pl.when(step >= H)
    def _():
        acc_ref[...] += mm(dg_ref[...], w_ref[...], NT)

    @pl.when(step == pl.num_programs(0) - 1)
    def _():
        value = x_ref[...].astype(F32)
        size = lax.rsqrt(jnp.mean(value * value, axis=-1, keepdims=True) + 1e-06)
        unit = value * size
        d_hidden = acc_ref[...]
        dgain_ref[...] = jnp.zeros_like(dgain_ref)
        dgain_ref[0:1, :] = jnp.sum(d_hidden * unit, axis=0, keepdims=True)
        d_unit = d_hidden * gain_ref[...]
        out_ref[...] = dy_ref[...] + size * (
            d_unit - unit * jnp.mean(d_unit * unit, axis=-1, keepdims=True)
        )


def input_grad(d_proj, d_gpre, d_logit, weights, x, gain, d_y):
    tokens, width = x.shape
    block = HC
    second = d_gpre.shape[1] // block
    steps = H + second
    whole = lambda shape: pl.BlockSpec(shape, lambda j: (0,) * len(shape))
    late = lambda j: (0, jnp.maximum(j - H, 0))
    weight = lambda j: (0, jnp.where(j < H, H - 1 - j, j - H + AT_GATE // block))
    in_specs = [
        pl.BlockSpec((tokens, block), lambda j: (0, jnp.minimum(j, H - 1))),
        pl.BlockSpec((tokens, block), late),
        whole((tokens, LANES)),
        pl.BlockSpec((width, block), weight),
        pl.BlockSpec((width, LANES), lambda j: (0, AT_LOGIT // LANES)),
        whole((tokens, width)),
        whole((1, width)),
        whole((tokens, width)),
    ]
    return pl.pallas_call(
        input_grad_kernel,
        grid=(steps,),
        in_specs=in_specs,
        out_specs=[whole((tokens, width)), whole((8, width))],
        out_shape=[
            jax.ShapeDtypeStruct((tokens, width), F32),
            jax.ShapeDtypeStruct((8, width), F32),
        ],
        scratch_shapes=[pltpu.VMEM((tokens, width), F32)],
        compiler_params=params(),
        cost_estimate=cost(2 * tokens * width * steps * block, 3e7),
        name="input_grad",
    )(d_proj, d_gpre, d_logit, weights, weights, x, gain, d_y)


def shifted(block, axis, distance):
    devices = range(lax.axis_size(axis))
    route = [(i - distance, i) for i in devices if i - distance in devices]
    return lax.ppermute(block, axis, route)


def plain_sum(left, right, skip_left=0):
    part = lax.psum_scatter(outer(left, right, skip_left), "dp", scatter_dimension=0, tiled=True)
    return lax.psum(part, "seq").astype(F32)


def by_heads(query, key, value):
    lead = query.shape[:-1]
    parts = [query.reshape(lead + (H, DK)), key.reshape(lead + (H, DK)), value.reshape(lead + (H, DV))]
    return jnp.concatenate(parts, axis=-1).reshape(lead + (H * HC,))


def from_heads(value, heads=H):
    lead = value.shape[:-1]
    parts = value.reshape(lead + (heads, HC))
    return (
        parts[..., :DK].reshape(lead + (heads * DK,)),
        parts[..., DK : 2 * DK].reshape(lead + (heads * DK,)),
        parts[..., 2 * DK :].reshape(lead + (heads * DV,)),
    )


def token_rows(segments, place, tokens):
    ext = jnp.pad(segments, (HALO, LANES), constant_values=-1)
    ext = lax.dynamic_slice_in_dim(ext, place * tokens, tokens + LANES)
    seg = ext[HALO : HALO + tokens]
    blocks = seg.reshape(-1, CHUNK)
    before = ext[HALO - 1 : HALO - 1 + tokens : CHUNK]
    near = [seg] + [ext[HALO - j : HALO - j + tokens] == seg for j in range(1, CONV)]
    near += [(blocks == before[:, None]).reshape(-1), (blocks == blocks[:, -1:]).reshape(-1)]
    near = jnp.stack([row.astype(F32) for row in near])
    later = jnp.stack([(jnp.roll(ext, -j) == ext).astype(F32) for j in range(CONV)])
    return jnp.pad(near, ((0, 8 - near.shape[0]), (0, 0))), jnp.pad(later, ((0, 8 - CONV), (0, 0)))


def wide(value):
    return jnp.pad(value, ((0, 0), (0, LANES - value.shape[1])))


def local(
    inputs, segments, cotangent, norm_gain_mix, w_query, w_key, w_value, w_outgate, w_gates,
    conv_weight, decay_log, dt_bias, out_norm_gain, w_out, norm_gain_ffn, w_ffn_gate, w_ffn_up, w_ffn_down,
):
    tokens, width = inputs.shape[1:]
    place = lax.axis_index("seq")
    planned = (lax.axis_size("dp"), lax.axis_size("seq")) == (PLANES * CORES, SPOTS)
    low = lambda a: a.astype(BF16)
    inner = w_ffn_gate.shape[1]
    gain_out = out_norm_gain[None]

    if planned:
        taps = conv_weight
        shards = (w_query, w_key, w_value, w_outgate, w_gates.T, w_out, w_ffn_gate, w_ffn_up, w_ffn_down)
        outs = mixer_forward(
            inputs[0], cotangent[0], shards, (norm_gain_mix[None], norm_gain_ffn[None]), gain_out,
            decay_log[None], dt_bias[None], segments, conv_weight,
        )
        weights, hidden, x, d_out, turn, y1, hidden_mid, gains, segr, par, cols, back, *outs = outs
        proj, logits, resp, *outs = outs
        saved, (maps, state_in, attn, gpre, gated) = outs[:6], outs[6:]
        gain_row = 1
    else:
        taps = by_heads(conv_weight[:, : H * DK], conv_weight[:, H * DK : 2 * H * DK], conv_weight[:, 2 * H * DK :])
        taps = jnp.pad(taps, ((0, 8 - CONV), (0, 0)))
        par = jnp.pad(jnp.stack([decay_log, dt_bias]), ((0, 6), (0, LANES - H)))
        segr, later = token_rows(segments[0], place, tokens)
        turn = jnp.eye(width, dtype=BF16)
        qkv = by_heads(low(w_query), low(w_key), low(w_value))
        qkv = jnp.concatenate([qkv[:, h * HC : (h + 1) * HC] for h in reversed(range(H))], axis=1)
        gates = jnp.pad(low(w_gates), ((0, 0), (0, AT_GATE - AT_LOGIT - 2 * H)))
        shard = [qkv, gates, low(w_outgate), low(w_out).T, low(w_ffn_gate), low(w_ffn_up), low(w_ffn_down).T]
        weights = lax.all_gather(jnp.concatenate(shard, axis=1), "dp", axis=0, tiled=True)
        gain_mix, gain_ffn = norm_gain_mix[None], norm_gain_ffn[None]
        gains, gain_row = gain_ffn, 0
        cols = jnp.pad(segr.T, ((0, 0), (0, LANES - segr.shape[0])))
        back = jnp.pad(later.T[: tokens + HALO], ((0, 0), (0, LANES - later.shape[0])))
        x, d_out = inputs[0], cotangent[0]
        value = jnp.concatenate([shifted(x[tokens - HALO :], "seq", 1), x], axis=0).astype(F32)
        size = lax.rsqrt(jnp.mean(value * value, axis=-1, keepdims=True) + 1e-06)
        hidden = low(value * size * gain_mix)
        proj, logits, part, resp, exch, *saved = delta_forward(hidden, weights, taps, par, cols, segr)
        exch = lax.all_gather(exch[0], "seq")
        slots = jnp.arange(exch.shape[0], dtype=jnp.int32)
        place_arr = place.reshape((1,)).astype(jnp.int32)
        gpre = outgate(hidden, weights)
        state_in, attn, gated, y1, hidden_mid = mixer_out(
            place_arr, slots, part, resp, exch, gpre, gain_out, weights, x, gain_ffn
        )
    result, act, d_gu, d_y, d_mixer, d_gain_ffn = feed_forward(
        hidden_mid, d_out, y1, gains, gain_row, turn, weights, inner
    )
    if planned:
        blocks, (sums, d_inputs, small) = reduce_gradients(
            d_out, hidden_mid, hidden, x, d_y, turn, d_mixer, act, d_gu, gated, weights, attn, gpre, gain_out, resp,
            gains, d_gain_ffn, proj, taps, logits, par, cols, back, segr, state_in, maps, saved,
        )
        (
            g_query, g_key, g_value, g_og, g_gates, g_out, g_gate, g_up, g_down,
            d_conv, d_gain_mix, d_gain_ffn, d_gain_out, d_par, d_inputs,
        ) = unpack_gradients(blocks, sums, small, d_inputs)
        g_gates = g_gates.T
        d_gain_mix, d_gain_ffn, d_gain_out = d_gain_mix[0], d_gain_ffn[0], d_gain_out[0]
        d_decay_log, d_dt_bias = d_par[0, :H], d_par[1, :H]
    else:
        d_attn, d_gpre, local_grad, d_gain_out = mixer_back(d_mixer, weights, attn, gpre, gain_out, resp)
        grads = lax.all_gather(local_grad, "seq")
        d_proj, d_logits, d_taps, d_par = delta_backward(
            place_arr, slots, proj, taps, logits, par, cols, back, segr, d_attn, state_in, exch, grads, saved
        )
        sent_back = shifted(d_proj[:HALO], "seq", -1)
        d_proj = d_proj.at[tokens:].add(sent_back)[HALO:]
        d_logit = low(d_logits)
        g_down = plain_sum(d_out, act).T
        g_gate = plain_sum(hidden_mid, d_gu[0])
        g_up = plain_sum(hidden_mid, d_gu[1])
        g_out = plain_sum(d_mixer, gated).T
        g_og = plain_sum(hidden, d_gpre, HALO)
        g_query, g_key, g_value = from_heads(plain_sum(hidden, d_proj, HALO))
        g_gates = plain_sum(hidden, d_logit, HALO)
        d_inputs, d_gain_mix = input_grad(d_proj, d_gpre, d_logit, weights, x, gain_mix, d_y)
        d_conv = jnp.concatenate(from_heads(d_taps[:CONV]), axis=1)
        d_gain_mix, d_conv, d_decay_log, d_dt_bias, d_gain_out, d_gain_ffn = lax.psum(
            (d_gain_mix[0], d_conv, d_par[0, :H], d_par[1, :H], d_gain_out[0], d_gain_ffn[0]), ("dp", "seq")
        )
    return (
        result[None], d_inputs[None], d_gain_mix, g_query, g_key, g_value, g_og,
        g_gates[:, : 2 * H], d_conv, d_decay_log, d_dt_bias, d_gain_out, g_out,
        d_gain_ffn, g_gate, g_up, g_down,
    )


def solution(mesh):
    rows, cols, copied = P("dp", None), P(None, "dp"), P()
    tokens = P("dp", "seq", None)
    in_specs = (
        tokens, rows, tokens, copied, rows, rows, rows, rows, rows,
        copied, copied, copied, copied, cols, copied, rows, rows, cols,
    )
    out_specs = (
        tokens, tokens, copied, rows, rows, rows, rows, rows,
        copied, copied, copied, copied, cols, copied, rows, rows, cols,
    )
    return jax.shard_map(local, mesh=mesh, in_specs=in_specs, out_specs=out_specs, check_vma=False)
```

```python
import functools

import jax
import jax.numpy as jnp
from jax import lax
from jax.experimental import pallas as pl
from jax.experimental.pallas import tpu as pltpu
from jax.sharding import PartitionSpec as P

H = 8
DK = 128
DV = 256
CONV = 4
HALO = 16
CHUNK = 128
HC = 2 * DK + DV
LANES = 128
PLANES, CORES, SPOTS = 4, 2, 4

AT_LOGIT = H * HC
AT_GATE = AT_LOGIT + 512
AT_OUT = AT_GATE + H * DV
AT_FFN = AT_OUT + H * DV
VMEM_LIMIT = 62 * 2**20

F32 = jnp.float32
BF16 = jnp.bfloat16
NN = ((1,), (0,))
NT = ((1,), (1,))
TN = ((0,), (0,))


def mm(left, right, dims=NN):
    return lax.dot_general(
        left.astype(BF16), right.astype(BF16), (dims, ((), ())), preferred_element_type=F32
    )


def mm_exact(left, right, dims=NN):
    return lax.dot_general(
        left, right, (dims, ((), ())), precision=lax.Precision.HIGHEST, preferred_element_type=F32
    )


def halves(value):
    high = value.astype(BF16)
    return high, (value - high.astype(F32)).astype(BF16)


def mm_three(left, right):
    left_high, left_low = halves(left)
    right_high, right_low = halves(right)
    return mm(left_high, right_high) + (mm(left_high, right_low) + mm(left_low, right_high))


def params(**more):
    return pltpu.CompilerParams(vmem_limit_bytes=VMEM_LIMIT, **more)


def cost(flops, nbytes):
    return pl.CostEstimate(flops=int(flops), bytes_accessed=int(nbytes), transcendentals=0)


def iota2(shape, axis):
    return lax.broadcasted_iota(jnp.int32, shape, axis)


def lane(value, index):
    picked = jnp.where(iota2(value.shape, 1) == index, value, 0.0)
    return jnp.sum(picked, axis=1, keepdims=True)


def to_row(column):
    size = column.shape[0]
    same = iota2((size, size), 0) == iota2((size, size), 1)
    return jnp.sum(jnp.where(same, column, 0.0), axis=0, keepdims=True)


def to_column(row):
    size = row.shape[1]
    same = iota2((size, size), 0) == iota2((size, size), 1)
    return jnp.sum(jnp.where(same, row, 0.0), axis=1, keepdims=True)


def outgate_kernel(h_ref, w_ref, g_ref):
    g_ref[...] = mm(h_ref[HALO:, :], w_ref[...])


def outgate(hidden, weights):
    rows, width = hidden.shape
    cols = H * DV
    block = 512
    return pl.pallas_call(
        outgate_kernel,
        grid=(cols // block,),
        in_specs=[
            pl.BlockSpec((rows, width), lambda j: (0, 0)),
            pl.BlockSpec((width, block), lambda j: (0, j + AT_GATE // block)),
        ],
        out_specs=pl.BlockSpec((rows - HALO, block), lambda j: (0, j)),
        out_shape=jax.ShapeDtypeStruct((rows - HALO, cols), F32),
        compiler_params=params(),
        cost_estimate=cost(2 * rows * width * cols, 2 * width * cols + 4 * rows * cols),
        name="outgate",
    )(hidden, weights)


def outer_kernel(left_ref, right_ref, out_ref, turn_ref, *, skip):
    @pl.when(pl.program_id(0) == 0)
    def _():
        turn_ref[...] = jnp.transpose(left_ref[skip:, :])

    out_ref[...] = mm(turn_ref[...], right_ref[...]).astype(BF16)


def outer(left, right, skip):
    rows, width = left.shape
    cols = right.shape[1]
    block = next(b for b in (512, 256, 128) if cols % b == 0)
    return pl.pallas_call(
        functools.partial(outer_kernel, skip=skip),
        grid=(cols // block,),
        in_specs=[
            pl.BlockSpec((rows, width), lambda j: (0, 0)),
            pl.BlockSpec((rows - skip, block), lambda j: (0, j)),
        ],
        out_specs=pl.BlockSpec((width, block), lambda j: (0, j)),
        out_shape=jax.ShapeDtypeStruct((width, cols), BF16),
        scratch_shapes=[pltpu.VMEM((width, rows - skip), BF16)],
        compiler_params=params(),
        cost_estimate=cost(2 * rows * width * cols, 2 * width * cols + 2 * rows * cols),
        name="outer",
    )(left, right)


def gate_tables(logit_ref, par_ref, beta_ref, decay_ref, cum_ref):
    logits = logit_ref[HALO:, :]
    beta_ref[...] = jax.nn.sigmoid(logits)
    shifted = logits + par_ref[1:2, :]
    soft = jnp.maximum(shifted, 0.0) + jnp.log1p(jnp.exp(-jnp.abs(shifted)))
    decay_ref[...] = -jnp.exp(par_ref[0:1, :]) * soft
    lower = (iota2((CHUNK, CHUNK), 0) >= iota2((CHUNK, CHUNK), 1)).astype(F32)
    for c in range(logits.shape[0] // CHUNK):
        part = decay_ref[c * CHUNK : (c + 1) * CHUNK, :]
        cum_ref[c * CHUNK : (c + 1) * CHUNK, :] = mm_exact(lower, part)


def join_taps(taps_ref, query_ref, key_ref, value_ref):
    taps_ref[0:CONV, :DK] = query_ref[...]
    taps_ref[0:CONV, DK : 2 * DK] = key_ref[...]
    taps_ref[0:CONV, 2 * DK :] = value_ref[...]


def taps_specs(at):
    return [
        pl.BlockSpec((CONV, DK), lambda s: (0, at(s))),
        pl.BlockSpec((CONV, DK), lambda s: (0, H + at(s))),
        pl.BlockSpec((CONV, DV), lambda s: (0, 2 * H * DK // DV + at(s))),
    ]


def mix_taps(p_ref, taps_ref, cols, pf_ref):
    tokens = cols.shape[0]
    pf_ref[...] = p_ref[...].astype(F32)
    total = pf_ref[HALO:, :] * taps_ref[0:1, :]
    for j in range(1, CONV):
        total += pf_ref[HALO - j : HALO - j + tokens, :] * taps_ref[j : j + 1, :] * cols[:, j : j + 1]
    return total


def chunk_tables(c, head, cols, segr_ref, cum_ref):
    rows = slice(c * CHUNK, (c + 1) * CHUNK)
    cum = lane(cum_ref[rows, :], head)
    cum_row = to_row(cum)
    same = cols[rows, 0:1] == segr_ref[0:1, rows]
    row_ids, col_ids = iota2((CHUNK, CHUNK), 0), iota2((CHUNK, CHUNK), 1)
    gamma = jnp.where((row_ids >= col_ids) & same, jnp.exp(jnp.minimum(cum - cum_row, 0.0)), 0.0)
    strict = jnp.where(row_ids > col_ids, gamma, 0.0)
    carry = jnp.exp(cum) * cols[rows, 4:5]
    last = jnp.exp(cum[CHUNK - 1 :, :] - cum) * cols[rows, 5:6]
    return gamma, strict, carry, last


def unit_lower_inverses(systems):
    size = systems[0].shape[0]
    row_ids, col_ids = iota2((size, size), 0), iota2((size, size), 1)
    eye = (row_ids == col_ids).astype(F32)
    found = [eye - jnp.where(row_ids // 2 == col_ids // 2, low, 0.0) for low in systems]
    width = 2
    while width < size:
        joined = (row_ids // (2 * width) == col_ids // (2 * width)) & (
            row_ids // width != col_ids // width
        )
        first = [mm_three(jnp.where(joined, low, 0.0), inv) for low, inv in zip(systems, found)]
        found = [inv - mm_three(inv, part) for inv, part in zip(found, first)]
        width *= 2
    return found


def flip_spot(value, bits):
    low, high = lax.rem(value, 2), value // 2
    flip = lambda one, other: one + other - 2 * one * other
    return flip(low, bits % 2) + 2 * flip(high, bits // 2)


def device(planes=0, core=0, spot=0):
    place, here = lax.axis_index("dp"), lax.axis_index("seq")
    z = lax.rem(place // CORES + planes, PLANES)
    return {"dp": z * CORES + flip_spot(lax.rem(place, CORES), core), "seq": flip_spot(here, spot)}


def greet(partners):
    barrier = pltpu.get_barrier_semaphore()
    for partner in partners:
        pl.semaphore_signal(barrier, inc=1, device_id=device(**partner), device_id_type=pl.DeviceIdType.MESH)
    pl.semaphore_wait(barrier, len(partners))


def gather_spans(inner):
    spans = [((H - 1) * HC, HC + LANES), ((H - 2) * HC, HC)]
    spans += [(h * HC, 2 * HC) for h in (4, 2, 0)]
    for at, size in ((AT_GATE, H * DV), (AT_OUT, H * DV)) + tuple((AT_FFN + i * inner, inner) for i in range(3)):
        spans += [(at + low, min(1024, size - low)) for low in range(0, size, 1024)]
    return spans


TICKS = (((), (6,)), ((7,), (8,)), ((9,), (10,)), ((11,), (12,)), ((13,), ()), ((14,), ()), ((15,), ()), ((16,), (17,)), (18,), (19,), (20,), (21,), (22,), (23,), (24,), (25,))


class Gathering:
    HALVED = (0, 3, 5, 8, 10, 13, 15)
    STAGES = (0, 1, 2, 3, 5, 7, 8)
    FIRST = ((0, 1, 2, 3, 4, 4, 5), (0, 1, 2, 3, 4, 5, 6), (0, 1, 2, 3, 5, 6, 7))

    def __init__(self, spans, shard_ref, full_ref, sems, pack):
        self.spans, self.shard, self.full, self.pack = spans, shard_ref, full_ref, pack
        self.send_sem, self.recv_sem, self.local_sem = sems
        self.piece = shard_ref.shape[0] // SPOTS
        self.half = full_ref.shape[0] // CORES
        self.z = lax.axis_index("dp") // CORES

    def quarter(self, spot, cols):
        row = flip_spot(lax.axis_index("seq"), spot) * self.piece
        return self.shard.at[pl.ds(pl.multiple_of(row, self.piece), self.piece), cols]

    def own(self, group):
        at, size = self.spans[group]
        cols = pl.ds(at, size)
        block = PLANES * self.piece
        return [
            pltpu.make_async_copy(
                self.quarter(q, cols),
                self.full.at[q * block : q * block + self.piece, cols],
                self.local_sem.at[group, q],
            )
            for q in range(SPOTS)
        ]

    def axis(self, group):
        return 1 + self.HALVED.index(group) % 2 if group in self.HALVED else 0

    def parts(self, group):
        return (0, 3 - self.axis(group)) if self.axis(group) else (0,)

    def copy(self, group, kind, part=0):
        at, size = self.spans[group]
        cols = pl.ds(at, size)
        piece, full = self.piece, self.full
        block = PLANES * piece
        rows = lambda quarter: pl.ds(quarter * block + piece, block - piece)
        axis, sent = self.axis(group), kind
        if kind < 6:
            read, step, written = ((0, 1, 1), (0, -1, 3), (1, 1, 2), (3, -1, 2), (2, 1, 3), (2, -1, 1))[kind]
            quarter = self.parts(group)[part]
            slot = lambda n: full.at[quarter * block + n * piece : quarter * block + (n + 1) * piece, cols]
            source = self.quarter(quarter, cols) if read == 0 else slot(read)
            target = slot(written)
            to, arrival = device(planes=step % PLANES), written - 1 + 7 * part
            sent += 10 * part
        elif kind < 8 and axis:
            source = full.at[rows(self.parts(group)[kind - 6]), cols]
            target = full.at[rows((axis, 3)[kind - 6]), cols]
            to, arrival = device(spot=axis), kind - 3
        elif kind < 8:
            source = full.at[rows(0), cols]
            target = full.at[rows(kind - 5), cols]
            to, arrival = device(spot=kind - 5), kind - 3
        elif kind == 8:
            by = 1 + group % 2
            source = full.at[rows(by), cols]
            target = full.at[rows(3), cols]
            to, arrival = device(spot=3 - by), 5
        else:
            source = full.at[0 : self.half, cols]
            target = full.at[self.half : 2 * self.half, cols]
            to, arrival = device(core=1), 6
        return pltpu.make_async_remote_copy(
            src_ref=source,
            dst_ref=target,
            send_sem=self.send_sem.at[group, sent],
            recv_sem=self.recv_sem.at[group, arrival],
            device_id=to,
            device_id_type=pl.DeviceIdType.MESH,
        )

    def sends(self, kind):
        z = self.z
        return (z < 3, z > 0, (z > 0) & (z < 3), (z > 0) & (z < 3), z == 2, z == 1)[kind]

    def start(self, group, kind):
        @pl.when(self.sends(kind))
        def _():
            for part in range(len(self.parts(group))):
                self.copy(group, kind, part).start()

    def arrive(self, group, kind, condition=None):
        def wait():
            for part in range(len(self.parts(group))):
                self.copy(group, kind, part).wait_recv()

        wait() if condition is None else pl.when(condition)(wait)

    def tick(self, at):
        z = self.z
        due = []
        for group in range(len(self.spans)):
            stages = (self.FIRST + (self.STAGES,) * len(self.spans))[group]
            due += [(stage, group) for stage in range(len(stages)) if group + stages[stage] == at]
        for stage, group in sorted(due, reverse=True):
            by = 1 + group % 2
            if stage == 0:
                self.pack(*self.spans[group])
                self.start(group, 0)
                self.start(group, 1)
                for local in self.own(group):
                    local.start()
            elif stage == 1:
                self.arrive(group, 0, z > 0)
                self.start(group, 2)
                self.arrive(group, 1, z < 3)
                self.start(group, 3)
            elif stage == 2:
                self.arrive(group, 2)
                self.start(group, 4)
                self.start(group, 5)
            elif stage == 3:
                self.arrive(group, 0, z == 0)
                self.arrive(group, 1, z == 3)
                self.copy(group, 5 + by).start()
                self.copy(group, 8 - by).start()
            elif stage == 4:
                if not self.axis(group):
                    self.copy(group, 5 + by).wait_recv()
                    self.copy(group, 8).start()
            elif stage == 5:
                self.copy(group, 8 - by).wait_recv()
                self.copy(group, 5 + by if self.axis(group) else 8).wait_recv()
                for local in self.own(group):
                    local.wait()
                self.copy(group, 9).start()
            else:
                self.copy(group, 9).wait_recv()

    def finish(self):
        for group in range(len(self.spans)):
            for kind in range(6):

                @pl.when(self.sends(kind))
                def _(group=group, kind=kind):
                    for part in range(len(self.parts(group))):
                        self.copy(group, kind, part).wait_send()

            for kind in (6, 7, 9) if self.axis(group) else (6, 7, 8, 9):
                self.copy(group, kind).wait_send()


def forward_kernel(
    h_ref, full_ref, taps_ref, par_ref, cols_ref, segr_ref,
    p_ref, logit_ref, part_ref, resp_ref, exch_ref, inv_ref, upd_ref, st_ref, stm_ref, amap_ref, rmap_ref,
    beta_ref, decay_ref, cum_ref, pf_ref, mix_ref, w_ref, wl_ref, load_sem,
):
    head = pl.program_id(0)
    load_head(head, h_ref, full_ref, par_ref, p_ref, logit_ref, beta_ref, decay_ref, cum_ref, w_ref, wl_ref, load_sem)
    state = forward_head(
        head, p_ref, taps_ref, cols_ref, segr_ref, part_ref, resp_ref, inv_ref, upd_ref, st_ref, stm_ref,
        amap_ref, rmap_ref, beta_ref, cum_ref, pf_ref, mix_ref, lambda: None,
    )
    exch_ref[0, 0] = state.astype(BF16)


def load_head(
    head, h_ref, full_ref, par_ref, p_ref, logit_ref, beta_ref, decay_ref, cum_ref, w_ref, wl_ref, load_sem
):
    def load(slot, at, size, to):
        return pltpu.make_async_copy(full_ref.at[:, pl.ds(at, size)], to, load_sem.at[slot])

    mine = load(0, pl.multiple_of((H - 1 - head) * HC, HC), HC, w_ref)
    mine.start()

    @pl.when(head == 0)
    def _():
        gates = load(1, AT_LOGIT, LANES, wl_ref)
        gates.start()
        gates.wait()
        logit_ref[...] = mm(h_ref[...], wl_ref[...])
        gate_tables(logit_ref, par_ref, beta_ref, decay_ref, cum_ref)

    mine.wait()
    p_ref[...] = mm(h_ref[...], w_ref[...]).astype(BF16)


def forward_head(
    head, p_ref, taps_ref, cols_ref, segr_ref, part_ref, resp_ref, inv_ref, upd_ref, st_ref, stm_ref,
    amap_ref, rmap_ref, beta_ref, cum_ref, pf_ref, mix_ref, between,
):
    cols = cols_ref[...]
    tokens = cols.shape[0]
    total = mix_taps(p_ref, taps_ref, cols, pf_ref)
    mix_ref[...] = total * jax.nn.sigmoid(total)
    between()
    beta = lane(beta_ref[...], head + H)
    chunks = range(tokens // CHUNK)
    tables, lows, keys, queries = [], [], [], []
    for c in chunks:
        rows = slice(c * CHUNK, (c + 1) * CHUNK)
        query = mix_ref[rows, :DK]
        query = query * (lax.rsqrt(jnp.sum(query * query, axis=1, keepdims=True) + 1e-06) * DK**-0.5)
        key = mix_ref[rows, DK : 2 * DK]
        key = key * lax.rsqrt(jnp.sum(key * key, axis=1, keepdims=True) + 1e-06)
        gamma, strict, carry, last = chunk_tables(c, head, cols, segr_ref, cum_ref)
        dots = mm(jnp.concatenate([key, query], axis=0), key, NT)
        lows.append(beta[rows] * strict * dots[:CHUNK])
        tables.append((gamma * dots[CHUNK:], carry, last))
        keys.append(key)
        queries.append(query)
    inverses = unit_lower_inverses(lows)
    state = None
    for c in chunks:
        rows = slice(c * CHUNK, (c + 1) * CHUNK)
        scores, carry, last = tables[c]
        key, query = keys[c], queries[c]
        target = jnp.concatenate([mix_ref[rows, 2 * DK :], carry * key], axis=1) * beta[rows]
        updates = mm(inverses[c], target)
        inv_ref[0, c] = inverses[c].astype(BF16)
        upd_ref[0, rows, :] = updates
        weighted_t = jnp.transpose(last * key)
        both = mm(jnp.concatenate([weighted_t, scores], axis=0), updates)
        eye = (iota2((DK, DK), 0) == iota2((DK, DK), 1)).astype(F32)
        step_map = carry[CHUNK - 1 :, :] * eye - both[:DK, DV:]
        read_map = carry * query - both[DK:, DV:]
        amap_ref[0, c] = step_map.astype(BF16)
        rmap_ref[0, c] = read_map.astype(BF16)
        if c == 0:
            st_ref[0, c] = jnp.zeros((DK, DV), F32)
            stm_ref[0, c] = eye.astype(BF16)
            part_ref[rows, :] = both[DK:, :DV]
            resp_ref[rows, :] = read_map.astype(BF16)
            state = jnp.concatenate([both[:DK, :DV], step_map], axis=1)
        else:
            st_ref[0, c] = state[:, :DV]
            stm_ref[0, c] = state[:, DV:].astype(BF16)
            moved = mm(jnp.concatenate([step_map, read_map], axis=0), state)
            part_ref[rows, :] = both[DK:, :DV] + moved[DK:, :DV]
            resp_ref[rows, :] = moved[DK:, DV:].astype(BF16)
            state = moved[:DK] + jnp.concatenate(
                [both[:DK, :DV], jnp.zeros((DK, DK), F32)], axis=1
            )
    return state


def delta_forward(hidden, weights, taps, par, cols, segr):
    rows, width = hidden.shape
    tokens = rows - HALO
    chunks = tokens // CHUNK
    whole = lambda shape: pl.BlockSpec(shape, lambda h: (0,) * len(shape))
    by_head = lambda shape: pl.BlockSpec(shape, lambda h: (h,) + (0,) * (len(shape) - 1))
    return pl.pallas_call(
        forward_kernel,
        grid=(H,),
        in_specs=[
            whole((rows, width)),
            pl.BlockSpec(memory_space=pl.ANY),
            pl.BlockSpec((8, HC), lambda h: (0, h)),
            whole((8, LANES)),
            whole((tokens, LANES)),
            whole(segr.shape),
        ],
        out_specs=[
            pl.BlockSpec((rows, HC), lambda h: (0, h)),
            whole((rows, LANES)),
            pl.BlockSpec((tokens, DV), lambda h: (0, h)),
            pl.BlockSpec((tokens, DK), lambda h: (0, h)),
            pl.BlockSpec((1, 1, DK, DV + DK), lambda h: (0, h, 0, 0)),
            by_head((1, chunks, CHUNK, CHUNK)),
            by_head((1, tokens, DV + DK)),
            by_head((1, chunks, DK, DV)),
            by_head((1, chunks, DK, DK)),
            by_head((1, chunks, DK, DK)),
            by_head((1, chunks, CHUNK, DK)),
        ],
        out_shape=[
            jax.ShapeDtypeStruct((rows, H * HC), BF16),
            jax.ShapeDtypeStruct((rows, LANES), F32),
            jax.ShapeDtypeStruct((tokens, H * DV), F32),
            jax.ShapeDtypeStruct((tokens, H * DK), BF16),
            jax.ShapeDtypeStruct((1, H, DK, DV + DK), BF16),
        ]
        + saved_shapes(chunks),
        scratch_shapes=[
            pltpu.VMEM((tokens, LANES), F32),
            pltpu.VMEM((tokens, LANES), F32),
            pltpu.VMEM((tokens, LANES), F32),
            pltpu.VMEM((rows, HC), F32),
            pltpu.VMEM((tokens, HC), F32),
            pltpu.VMEM((width, HC), BF16),
            pltpu.VMEM((width, LANES), BF16),
            pltpu.SemaphoreType.DMA((2,)),
        ],
        compiler_params=params(),
        cost_estimate=cost(6e9 * H, 5e6 * H),
        name="delta_forward",
    )(hidden, weights, taps, par, cols, segr)


def saved_shapes(chunks):
    return [
        jax.ShapeDtypeStruct((H, chunks, CHUNK, CHUNK), BF16),
        jax.ShapeDtypeStruct((H, chunks * CHUNK, DV + DK), F32),
        jax.ShapeDtypeStruct((H, chunks, DK, DV), F32),
        jax.ShapeDtypeStruct((H, chunks, DK, DK), BF16),
        jax.ShapeDtypeStruct((H, chunks, DK, DK), BF16),
        jax.ShapeDtypeStruct((H, chunks, CHUNK, DK), BF16),
    ]


def mixer_forward_kernel(
    x_ref, wq_ref, wk_ref, wv_ref, wl_in, gain_mix_ref, gain_ffn_ref, gain_ref, rate_ref, bias_ref, seg_ref,
    taps_q_ref, taps_k_ref, taps_v_ref, cot_any, wo_any, wm_any, wg_any, wu_any, wd_any,
    full_ref, hidden_out, x_out, cot_out, turn_out, y_out, mid_out,
    gains_out, near_ref, par_ref, cols_ref, back_ref, p_ref, logit_ref, resp_out,
    inv_ref, upd_ref, st_ref, stm_ref, amap_ref, rmap_ref, maps_ref, sin_ref, attn_ref, gpre_ref, gated_ref,
    shard_ref, hidden_ref, xs_ref, cots_ref, turn_ref, y_ref, mid_ref, xh_ref, part_ref, resp_ref, exch_ref, stage_ref, half_ref, low_ref,
    beta_ref, decay_ref, cum_ref, pf_ref, mix_ref, w_ref, wl_ref, wb_ref,
    cot_ref, wo_ref, wm_ref, wg_ref, wu_ref, wd_ref, taps_ref, row_ref, later_ref, late_sem,
    send_sem, recv_sem, local_sem, exch_send, exch_recv, load_sem, pair_sem, out_sem, halo_sem, *, spans, inner,
):
    step = pl.program_id(0)
    place = lax.axis_index("seq")
    tokens, width = x_ref.shape

    def late(which):
        source, to = (
            (wo_any, wo_ref), (wm_any, wm_ref), (wg_any, wg_ref), (wu_any, wu_ref), (wd_any, wd_ref), (cot_any, cot_ref),
        )[which]
        return pltpu.make_async_copy(source, to, late_sem.at[which])

    def pack(at, size):
        while size > 0:
            if at < AT_LOGIT:
                head, span = H - 1 - at // HC, HC
                shard_ref[:, at : at + DK] = wq_ref[:, head * DK : (head + 1) * DK].astype(BF16)
                shard_ref[:, at + DK : at + 2 * DK] = wk_ref[:, head * DK : (head + 1) * DK].astype(BF16)
                shard_ref[:, at + 2 * DK : at + HC] = wv_ref[:, head * DV : (head + 1) * DV].astype(BF16)
            elif at < AT_GATE:
                span = LANES
                rest = jnp.zeros((LANES - 2 * H, LANES), F32)
                turned = jnp.transpose(jnp.concatenate([wl_in[...], rest], axis=0))
                shard_ref[:, at : at + LANES] = turned.astype(BF16)
            elif at < AT_OUT:
                span, low = size, at - AT_GATE
                if low == 0:
                    late(0).wait()
                shard_ref[:, at : at + span] = wo_ref[:, low : low + span].astype(BF16)
            elif at < AT_FFN:
                span, low = size, at - AT_OUT
                if low == 0:
                    late(1).wait()
                shard_ref[:, at : at + span] = jnp.transpose(wm_ref[low : low + span, :]).astype(BF16)
            else:
                span, which, low = size, (at - AT_FFN) // inner, (at - AT_FFN) % inner
                if low == 0:
                    late(2 + which).wait()
                if which < 2:
                    shard_ref[:, at : at + span] = (wg_ref, wu_ref)[which][:, low : low + span].astype(BF16)
                else:
                    shard_ref[:, at : at + span] = jnp.transpose(wd_ref[low : low + span, :]).astype(BF16)
            at, size = at + span, size - span

    gathering = Gathering(spans, shard_ref, full_ref, (send_sem, recv_sem, local_sem), pack)
    lead = gathering.FIRST[0][-1] + 1
    final_tick = len(spans) + gathering.STAGES[-1]

    upper = place // 2 == 1
    second = lax.rem(place, 2) == 1

    def give(h):
        return pltpu.make_async_remote_copy(
            src_ref=stage_ref.at[h],
            dst_ref=exch_ref.at[h],
            send_sem=exch_send.at[0, h],
            recv_sem=exch_recv.at[0, h],
            device_id=device(spot=1),
            device_id_type=pl.DeviceIdType.MESH,
        )

    def give_half(h):
        return pltpu.make_async_remote_copy(
            src_ref=half_ref.at[h],
            dst_ref=low_ref.at[h],
            send_sem=exch_send.at[1, h],
            recv_sem=exch_recv.at[1, h],
            device_id=device(spot=2),
            device_id_type=pl.DeviceIdType.MESH,
        )

    def join(h):
        give(h).wait()

        @pl.when(jnp.logical_not(upper))
        def _():
            mine, theirs = stage_ref[h], exch_ref[h]
            later = jnp.where(second, mine, theirs)
            earlier = jnp.where(second, theirs, mine)
            half_ref[h] = (later[:, :DV].astype(F32) + mm(later[:, DV:], earlier[:, :DV])).astype(BF16)
            give_half(h).start()

    def give_halo():
        return pltpu.make_async_remote_copy(
            src_ref=x_ref.at[tokens - HALO : tokens],
            dst_ref=xh_ref,
            send_sem=halo_sem.at[0],
            recv_sem=halo_sem.at[1],
            device_id={"dp": lax.axis_index("dp"), "seq": lax.rem(place + 1, SPOTS)},
            device_id_type=pl.DeviceIdType.MESH,
        )

    def keep(which):
        source, to = (
            (hidden_ref, hidden_out), (xs_ref, x_out), (cots_ref, cot_out), (turn_ref, turn_out),
            (y_ref, y_out), (mid_ref, mid_out),
        )[which]
        return pltpu.make_async_copy(source, to, out_sem.at[which])

    def load_pair(h):
        slot = lax.rem(h, 2)
        return [
            pltpu.make_async_copy(
                full_ref.at[:, pl.ds(pl.multiple_of(at + h * DV, DV), DV)], wb_ref.at[slot, i], pair_sem.at[slot, i]
            )
            for i, at in enumerate((AT_GATE, AT_OUT))
        ]

    @pl.when(step == 0)
    def _():
        greet([dict(planes=d) for d in (1, 2, 3)] + [dict(spot=s) for s in (1, 2, 3)] + [dict(core=1)])

        @pl.when(place < SPOTS - 1)
        def _():
            give_halo().start()

        gathering.tick(0)
        for which in range(6):
            late(which).start()
        at = iota2((1, width), 1)
        piece = width // (PLANES * CORES * SPOTS)
        core, rest = at // (width // 2), at % (width // 2)
        quarter, plane, low = rest // (PLANES * piece), rest // piece % PLANES, rest % piece
        place_dp = lax.axis_index("dp")
        z, c = place_dp // CORES, lax.rem(place_dp, CORES)
        chip = ((z - plane + PLANES) % PLANES) * CORES + (c + core - 2 * c * core)
        order = (chip * SPOTS + flip_spot(quarter, place)) * piece + low
        turn_ref[...] = jnp.where(iota2((width, width), 0) == order, 1.0, 0.0).astype(BF16)
        keep(3).start()
        gathering.tick(1)
        gains = jnp.concatenate([gain_mix_ref[...], gain_ffn_ref[...], jnp.zeros((6, width), F32)], axis=0)
        high, mid = halves(gains)
        rest = (gains - high.astype(F32)) - mid.astype(F32)
        gains_out[...] = mm(high, turn_ref[...]) + mm(mid, turn_ref[...]) + mm(rest, turn_ref[...])
        par_ref[...] = jnp.zeros_like(par_ref)
        par_ref[0:1, :H] = rate_ref[...]
        par_ref[1:2, :H] = bias_ref[...]
        gathering.tick(2)

        row_ref[...] = jnp.full(row_ref.shape, -1.0, F32)
        row_ref[0:1, LANES : LANES + seg_ref.shape[1]] = seg_ref[...].astype(F32)
        row = row_ref[0:1, pl.ds(pl.multiple_of(place * tokens, LANES), tokens + 2 * LANES)]
        seg = row[:, LANES : LANES + tokens]
        near = [seg]
        for j in range(1, CONV):
            moved = pltpu.roll(row, j, 1)[:, LANES : LANES + tokens]
            near.append((moved == seg).astype(F32))
        before, last = [], []
        for n in range(tokens // CHUNK):
            part = seg[:, n * CHUNK : (n + 1) * CHUNK]
            before.append((part == row[:, LANES + n * CHUNK - 1 : LANES + n * CHUNK]).astype(F32))
            last.append((part == part[:, CHUNK - 1 :]).astype(F32))
        near += [jnp.concatenate(before, axis=1), jnp.concatenate(last, axis=1)]
        near.append(jnp.zeros((8 - len(near), tokens), F32))
        near_ref[...] = jnp.concatenate(near, axis=0)
        size = row.shape[1]
        ahead = pltpu.roll(row, size - (LANES - HALO), 1)
        later = [jnp.zeros((1, tokens + LANES), F32)]
        for j in range(1, CONV):
            later.append((pltpu.roll(ahead, size - j, 1) == ahead).astype(F32)[:, : tokens + LANES])
        later.append(jnp.zeros((8 - CONV, tokens + LANES), F32))
        later_ref[...] = jnp.concatenate(later, axis=0)
        blank = jnp.zeros((LANES - 8, LANES), F32)
        for n in range(tokens // LANES):
            span = slice(n * LANES, (n + 1) * LANES)
            cols_ref[span, :] = jnp.transpose(jnp.concatenate([near_ref[:, span], blank], axis=0))
        gathering.tick(3)

        @pl.when(place > 0)
        def _():
            give_halo().wait_recv()

        @pl.when(place == 0)
        def _():
            xh_ref[...] = jnp.zeros_like(xh_ref)

        value = mm(jnp.concatenate([xh_ref[...], x_ref[...]], axis=0), turn_ref[...])
        xs_ref[...] = value[HALO:].astype(BF16)
        keep(1).start()
        size = lax.rsqrt(jnp.mean(value * value, axis=-1, keepdims=True) + 1e-06)
        hidden_ref[...] = (value * size * gains_out[0:1, :]).astype(BF16)
        keep(0).start()
        for at in range(4, lead):
            gathering.tick(at)

    @pl.when((step >= 2) & (step < H + 2))
    def _():
        join(step - 2)

    @pl.when(step < H)
    def _():
        head = step
        for h in range(1, H):

            @pl.when(head == h)
            def _(h=h):
                for at in TICKS[h][0]:
                    gathering.tick(at)

        load_head(
            head, hidden_ref, full_ref, par_ref, p_ref, logit_ref, beta_ref, decay_ref, cum_ref, w_ref, wl_ref, load_sem
        )

        def between():
            for h in range(H):

                @pl.when(head == h)
                def _(h=h):
                    for at in TICKS[h][1]:
                        gathering.tick(at)

        join_taps(taps_ref, taps_q_ref, taps_k_ref, taps_v_ref)
        state = forward_head(
            head, p_ref, taps_ref, cols_ref, near_ref, part_ref.at[head], resp_ref.at[head], inv_ref, upd_ref,
            st_ref, stm_ref, amap_ref, rmap_ref, beta_ref, cum_ref, pf_ref, mix_ref, between,
        )
        resp_out[...] = resp_ref[head]
        stage_ref[head] = state.astype(BF16)
        give(head).start()

        @pl.when(head == H - 1)
        def _():
            for copy in load_pair(0):
                copy.start()

    @pl.when(step >= H)
    def _():
        head = step - H
        for h in range(H):

            @pl.when(head == h)
            def _(h=h):
                for at in TICKS[H + h]:
                    gathering.tick(at)

        @pl.when(head < H - 1)
        def _():
            for copy in load_pair(head + 1):
                copy.start()

        for copy in load_pair(head):
            copy.wait()
        @pl.when(upper)
        def _():
            give_half(head).wait_recv()

        @pl.when(jnp.logical_not(upper))
        def _():
            low_ref[head] = jnp.zeros((DK, DV), BF16)
            give_half(head).wait_send()

        slot = lax.rem(head, 2)
        gate = mm(hidden_ref[HALO:, :], wb_ref[slot, 0])
        gpre_ref[...] = gate
        theirs = exch_ref[head]
        maps_ref[0, 0] = stage_ref[head, :, DV:]
        maps_ref[1, 0] = theirs[:, DV:]
        state = low_ref[head].astype(F32)
        state = jnp.where(second, theirs[:, :DV].astype(F32) + mm(theirs[:, DV:], state), state)
        sin_ref[0] = state
        attn = part_ref[head] + mm(resp_ref[head], state)
        attn_ref[...] = attn
        scale = lax.rsqrt(jnp.mean(attn * attn, axis=-1, keepdims=True) + 1e-05)
        gated = (attn * scale * gain_ref[...] * (gate * jax.nn.sigmoid(gate))).astype(BF16)
        gated_ref[...] = gated

        @pl.when(head == 0)
        def _():
            y_ref[...] = xs_ref[...].astype(F32)
            late(5).wait()
            cots_ref[...] = mm(cot_ref[...], turn_ref[...]).astype(BF16)
            keep(2).start()
            blank = jnp.zeros((LANES - 8, LANES), F32)
            for n in range(tokens // LANES + 1):
                span = slice(n * LANES, (n + 1) * LANES)
                turned = jnp.transpose(jnp.concatenate([later_ref[:, span], blank], axis=0))
                kept = min(LANES, tokens + HALO - n * LANES)
                back_ref[n * LANES : n * LANES + kept, :] = turned[:kept]

        y_ref[...] += mm(gated, wb_ref[slot, 1], NT)

        @pl.when(head == H - 1)
        def _():
            keep(4).start()
            value = y_ref[...]
            size = lax.rsqrt(jnp.mean(value * value, axis=-1, keepdims=True) + 1e-06)
            mid_ref[...] = (value * size * gains_out[1:2, :]).astype(BF16)
            keep(5).start()
            gathering.finish()

            @pl.when(place < SPOTS - 1)
            def _():
                give_halo().wait_send()

            for which in range(6):
                keep(which).wait()


def mixer_forward(x, cotangent, shards, gains, gain, rate, bias, segments, taps):
    tokens, width = x.shape
    rows = tokens + HALO
    chunks = tokens // CHUNK
    query, key, value, outgate_w, gates, out_w, gate_w, up_w, down_w = shards
    inner = down_w.shape[0]
    spans = gather_spans(inner)
    total = AT_FFN + 3 * inner
    once = lambda array: pl.BlockSpec(
        array.shape, lambda s: (0,) * array.ndim, pipeline_mode=pl.Buffered(1)
    )
    whole = lambda shape: pl.BlockSpec(shape, lambda s: (0,) * len(shape))
    early = lambda s: jnp.minimum(s, H - 1)
    late = lambda s: jnp.maximum(s - H, 0)
    by_head = lambda shape, at: pl.BlockSpec(shape, lambda s: (at(s),) + (0,) * (len(shape) - 1))
    across = lambda shape, at: pl.BlockSpec(shape, lambda s: (0, at(s)))
    anywhere = pl.BlockSpec(memory_space=pl.ANY)
    shape = jax.ShapeDtypeStruct
    sem = pltpu.SemaphoreType.DMA
    saved = saved_shapes(chunks)
    return pl.pallas_call(
        functools.partial(mixer_forward_kernel, spans=spans, inner=inner),
        grid=(2 * H,),
        in_specs=[once(a) for a in (x, query, key, value, gates, *gains, gain, rate, bias, segments)]
        + taps_specs(early)
        + [anywhere] * 6,
        out_specs=[anywhere] * 7
        + [
            whole((8, width)),
            whole((8, tokens)),
            whole((8, LANES)),
            whole((tokens, LANES)),
            whole((rows, LANES)),
            across((rows, HC), early),
            whole((rows, LANES)),
            across((tokens, DK), early),
        ]
        + [by_head((1,) + one.shape[1:], early) for one in saved]
        + [
            pl.BlockSpec((2, 1, DK, DK), lambda s: (0, late(s), 0, 0)),
            by_head((1, DK, DV), late),
            across((tokens, DV), late),
            across((tokens, DV), late),
            across((tokens, DV), late),
        ],
        out_shape=[
            shape((width, total), BF16),
            shape((rows, width), BF16),
            shape((tokens, width), BF16),
            shape((tokens, width), BF16),
            shape((width, width), BF16),
            shape((tokens, width), F32),
            shape((tokens, width), BF16),
            shape((8, width), F32),
            shape((8, tokens), F32),
            shape((8, LANES), F32),
            shape((tokens, LANES), F32),
            shape((rows, LANES), F32),
            shape((rows, H * HC), BF16),
            shape((rows, LANES), F32),
            shape((tokens, H * DK), BF16),
        ]
        + saved
        + [
            shape((2, H, DK, DK), BF16),
            shape((H, DK, DV), F32),
            shape((tokens, H * DV), F32),
            shape((tokens, H * DV), F32),
            shape((tokens, H * DV), BF16),
        ],
        scratch_shapes=[
            pltpu.VMEM((query.shape[0], total), BF16),
            pltpu.VMEM((rows, width), BF16),
            pltpu.VMEM((tokens, width), BF16),
            pltpu.VMEM((tokens, width), BF16),
            pltpu.VMEM((width, width), BF16),
            pltpu.VMEM((tokens, width), F32),
            pltpu.VMEM((tokens, width), BF16),
            pltpu.VMEM((HALO, width), BF16),
            pltpu.VMEM((H, tokens, DV), F32),
            pltpu.VMEM((H, tokens, DK), BF16),
            pltpu.VMEM((H, DK, DV + DK), BF16),
            pltpu.VMEM((H, DK, DV + DK), BF16),
            pltpu.VMEM((H, DK, DV), BF16),
            pltpu.VMEM((H, DK, DV), BF16),
            pltpu.VMEM((tokens, LANES), F32),
            pltpu.VMEM((tokens, LANES), F32),
            pltpu.VMEM((tokens, LANES), F32),
            pltpu.VMEM((rows, HC), F32),
            pltpu.VMEM((tokens, HC), F32),
            pltpu.VMEM((width, HC), BF16),
            pltpu.VMEM((width, LANES), BF16),
            pltpu.VMEM((2, 2, width, DV), BF16),
            pltpu.VMEM(cotangent.shape, BF16),
            pltpu.VMEM(outgate_w.shape, F32),
            pltpu.VMEM(out_w.shape, F32),
            pltpu.VMEM(gate_w.shape, F32),
            pltpu.VMEM(up_w.shape, F32),
            pltpu.VMEM(down_w.shape, F32),
            pltpu.VMEM((8, HC), F32),
            pltpu.VMEM((8, segments.shape[1] + 2 * LANES), F32),
            pltpu.VMEM((8, tokens + LANES), F32),
            sem((6,)),
            sem((len(spans), 16)),
            sem((len(spans), 10)),
            sem((len(spans), SPOTS)),
            sem((2, H)),
            sem((2, H)),
            sem((2,)),
            sem((2, 2)),
            sem((6,)),
            sem((2,)),
        ],
        compiler_params=params(collective_id=0, has_side_effects=True),
        cost_estimate=cost(1e11, 1e8),
        name="mixer_forward",
    )(
        x, query, key, value, gates, *gains, gain, rate, bias, segments, taps, taps, taps,
        cotangent, outgate_w, out_w, gate_w, up_w, down_w,
    )


def backward_kernel(place_ref, slot_ref, *refs):
    exch_ref, grads_ref, refs = refs[9], refs[10], refs[:9] + refs[11:]

    def behind(source, grad):
        slot = slot_ref[source]
        return jnp.where(
            source > place_ref[0],
            grads_ref[slot, 0].astype(F32) + mm(exch_ref[slot, 0], grad, TN),
            grad,
        )

    places = exch_ref.shape[0]
    d_state = lax.fori_loop(
        0, places - 1, lambda lap, grad: behind(places - 1 - lap, grad), jnp.zeros((DK, DV), F32)
    )
    for phase in range(PHASES):
        backward_head(phase, pl.program_id(0), lambda: d_state, *refs)


PHASES = 3


def backward_head(
    phase, head, entering, p_ref, taps_ref, logit_ref, par_ref, cols_ref, back_ref, segr_ref,
    dattn_ref, sin_ref,
    inv_ref, upd_ref, st_ref, stm_ref, amap_ref, rmap_ref,
    dp_ref, dlogit_ref, dtaps_ref, dpar_ref,
    beta_ref, decay_ref, cum_ref, pf_ref, pre_ref, dmix_ref, dstate_ref, dbeta_ref, ddecay_ref,
):
    tokens = cols_ref.shape[0]
    chunks = range(tokens // CHUNK)
    refs = (
        cols_ref, segr_ref, dattn_ref, sin_ref, inv_ref, upd_ref, st_ref, stm_ref, beta_ref, cum_ref, pre_ref,
        dmix_ref, dstate_ref, dbeta_ref, ddecay_ref,
    )
    if phase == 0:

        @pl.when(head == 0)
        def _():
            gate_tables(logit_ref, par_ref, beta_ref, decay_ref, cum_ref)
            dlogit_ref[...] = jnp.zeros_like(dlogit_ref)
            dpar_ref[...] = jnp.zeros_like(dpar_ref)

        pre_ref[...] = mix_taps(p_ref, taps_ref, cols_ref[...], pf_ref)
        d_state = entering()
        for c in reversed(chunks):
            rows = slice(c * CHUNK, (c + 1) * CHUNK)
            dstate_ref[c] = d_state
            if c > 0:
                d_state = mm(amap_ref[0, c], d_state, TN) + mm(rmap_ref[0, c], dattn_ref[rows, :], TN)
        backward_chunks(head, chunks[:1], *refs)
    elif phase == 1:
        backward_chunks(head, chunks[1:3], *refs)
    else:
        backward_chunks(head, chunks[3:], *refs)
        backward_ends(
            head, taps_ref, logit_ref, par_ref, cols_ref, back_ref, dp_ref, dlogit_ref, dtaps_ref, dpar_ref,
            beta_ref, decay_ref, pf_ref, dmix_ref, dbeta_ref, ddecay_ref,
        )


def backward_chunks(
    head, chunks, cols_ref, segr_ref, dattn_ref, sin_ref, inv_ref, upd_ref, st_ref, stm_ref, beta_ref, cum_ref, pre_ref,
    dmix_ref, dstate_ref, dbeta_ref, ddecay_ref,
):
    cols = cols_ref[...]
    beta = lane(beta_ref[...], head + H)
    state_in = sin_ref[0]
    row_ids, col_ids = iota2((CHUNK, CHUNK), 0), iota2((CHUNK, CHUNK), 1)
    for c in chunks:
        rows = slice(c * CHUNK, (c + 1) * CHUNK)
        mixed = pre_ref[rows, :]
        gate = jax.nn.sigmoid(mixed)
        slope = gate * (1.0 + mixed * (1.0 - gate))
        mixed = mixed * gate
        query_raw, key_raw, value = mixed[:, :DK], mixed[:, DK : 2 * DK], mixed[:, 2 * DK :]
        query_size = lax.rsqrt(jnp.sum(query_raw * query_raw, axis=1, keepdims=True) + 1e-06)
        key_size = lax.rsqrt(jnp.sum(key_raw * key_raw, axis=1, keepdims=True) + 1e-06)
        query_unit, key = query_raw * query_size, key_raw * key_size
        query = query_unit * DK**-0.5
        gamma, strict, carry, last = chunk_tables(c, head, cols, segr_ref, cum_ref)
        strength = beta[rows]
        dots = mm(jnp.concatenate([key, query], axis=0), key, NT)
        weights = strict * dots[:CHUNK]
        low = strength * weights
        scores = gamma * dots[CHUNK:]
        if c == 0:
            state = state_in
        else:
            state = st_ref[0, c] + mm(stm_ref[0, c], state_in)
        updates = upd_ref[0, rows, :DV] - mm(upd_ref[0, rows, DV:], state)
        d_attn = dattn_ref[rows, :]
        d_state = dstate_ref[c]
        d_updates = mm(scores, d_attn, TN) + mm(last * key, d_state)
        solved = mm(inv_ref[0, c], d_updates, TN)
        both = jnp.concatenate([d_attn, solved.astype(BF16)], axis=0)
        by_updates = mm(both, updates, NT)
        by_state = mm(both, state, NT)
        d_scores = by_updates[:CHUNK]
        d_low = -by_updates[CHUNK:]
        d_query = carry * by_state[:CHUNK]
        key_state = jnp.sum(key * by_state[CHUNK:], axis=1, keepdims=True)
        d_carry = jnp.sum(query * by_state[:CHUNK], axis=1, keepdims=True) - strength * key_state
        d_beta = (
            jnp.sum(solved * value, axis=1, keepdims=True)
            - carry * key_state
            + jnp.sum(d_low * weights, axis=1, keepdims=True)
        )
        d_dots_q = d_scores * gamma
        d_dots_k = d_low * strength * strict
        by_key = mm(jnp.concatenate([d_dots_q, d_dots_k], axis=0), key)
        d_query += by_key[:CHUNK]
        from_state = mm(updates, d_state, NT)
        d_key = (
            by_key[CHUNK:]
            + mm(
                jnp.concatenate([d_dots_q, d_dots_k], axis=0),
                jnp.concatenate([query, key], axis=0),
                TN,
            )
            - strength * carry * by_state[CHUNK:]
            + last * from_state
        )
        d_last = jnp.sum(key * from_state, axis=1, keepdims=True) * last
        d_spread = d_scores * scores + d_low * low
        final = (iota2((CHUNK, 1), 0) == CHUNK - 1).astype(F32)
        d_carry += final * jnp.sum(d_state * state)
        d_cum = (
            jnp.sum(d_spread, axis=1, keepdims=True)
            - to_column(jnp.sum(d_spread, axis=0, keepdims=True))
            + final * jnp.sum(d_last)
            - d_last
            + d_carry * carry
        )
        d_decay = jnp.sum(
            jnp.where(row_ids <= col_ids, to_row(d_cum), 0.0), axis=1, keepdims=True
        )
        dbeta_ref[rows, :] = jnp.broadcast_to(d_beta, (CHUNK, LANES))
        ddecay_ref[rows, :] = jnp.broadcast_to(d_decay, (CHUNK, LANES))
        d_query = d_query * DK**-0.5
        d_query = query_size * (
            d_query - query_unit * jnp.sum(d_query * query_unit, axis=1, keepdims=True)
        )
        d_key = key_size * (d_key - key * jnp.sum(d_key * key, axis=1, keepdims=True))
        d_value = strength * solved
        dmix_ref[HALO + c * CHUNK : HALO + (c + 1) * CHUNK, :] = slope * jnp.concatenate(
            [d_query, d_key, d_value], axis=1
        )


def backward_ends(
    head, taps_ref, logit_ref, par_ref, cols_ref, back_ref, dp_ref, dlogit_ref, dtaps_ref, dpar_ref,
    beta_ref, decay_ref, pf_ref, dmix_ref, dbeta_ref, ddecay_ref,
):
    cols = cols_ref[...]
    tokens = cols.shape[0]
    lanes = iota2((tokens, LANES), 1)
    slope = jax.nn.sigmoid(logit_ref[HALO:, :] + par_ref[1:2, :]) * -jnp.exp(par_ref[0:1, :])
    here = jnp.where(lanes == head, ddecay_ref[...], 0.0)
    d_first = here * slope
    strengths = beta_ref[...]
    d_second = jnp.where(lanes == head + H, dbeta_ref[...], 0.0) * strengths * (1.0 - strengths)
    dlogit_ref[...] += d_first + d_second
    dpar_ref[0:1, :] += jnp.sum(here * decay_ref[...], axis=0, keepdims=True)
    dpar_ref[1:2, :] += jnp.sum(d_first, axis=0, keepdims=True)

    dmix_ref[:HALO, :] = jnp.zeros((HALO, HC), F32)
    dmix_ref[HALO + tokens :, :] = jnp.zeros((8, HC), F32)
    d_mix = dmix_ref[HALO : HALO + tokens, :]
    dtaps_ref[...] = jnp.zeros_like(dtaps_ref)
    dtaps_ref[0:1, :] = jnp.sum(d_mix * pf_ref[HALO:, :], axis=0, keepdims=True)
    total = dmix_ref[: HALO + tokens, :] * taps_ref[0:1, :]
    for j in range(1, CONV):
        total += dmix_ref[j : j + HALO + tokens, :] * taps_ref[j : j + 1, :] * back_ref[:, j : j + 1]
        dtaps_ref[j : j + 1, :] = jnp.sum(
            d_mix * cols[:, j : j + 1] * pf_ref[HALO - j : HALO - j + tokens, :],
            axis=0,
            keepdims=True,
        )
    dp_ref[...] = total.astype(BF16)


def delta_backward(
    place, slots, proj, taps, logits, par, cols, back, segr, d_attn, state_in, exch, grads, saved
):
    rows = proj.shape[0]
    tokens = rows - HALO
    chunks = tokens // CHUNK
    places = exch.shape[0]
    whole = lambda shape: pl.BlockSpec(shape, lambda h: (0,) * len(shape))
    by_head = lambda shape: pl.BlockSpec(shape, lambda h: (h,) + (0,) * (len(shape) - 1))
    return pl.pallas_call(
        backward_kernel,
        grid=(H,),
        in_specs=[
            pl.BlockSpec(memory_space=pltpu.SMEM),
            pl.BlockSpec(memory_space=pltpu.SMEM),
            pl.BlockSpec((rows, HC), lambda h: (0, h)),
            pl.BlockSpec((8, HC), lambda h: (0, h)),
            whole((rows, LANES)),
            whole((8, LANES)),
            whole((tokens, LANES)),
            whole((rows, LANES)),
            whole(segr.shape),
            pl.BlockSpec((tokens, DV), lambda h: (0, h)),
            by_head((1, DK, DV)),
            pl.BlockSpec((places, 1, DK, DK), lambda h: (0, h, 0, DV // DK)),
            pl.BlockSpec((places, 1, DK, DV), lambda h: (0, h, 0, 0)),
            by_head((1, chunks, CHUNK, CHUNK)),
            by_head((1, tokens, DV + DK)),
            by_head((1, chunks, DK, DV)),
            by_head((1, chunks, DK, DK)),
            by_head((1, chunks, DK, DK)),
            by_head((1, chunks, CHUNK, DK)),
        ],
        out_specs=[
            pl.BlockSpec((rows, HC), lambda h: (0, h)),
            whole((tokens, LANES)),
            pl.BlockSpec((8, HC), lambda h: (0, h)),
            whole((8, LANES)),
        ],
        out_shape=[
            jax.ShapeDtypeStruct((rows, H * HC), BF16),
            jax.ShapeDtypeStruct((tokens, LANES), F32),
            jax.ShapeDtypeStruct((8, H * HC), F32),
            jax.ShapeDtypeStruct((8, LANES), F32),
        ],
        scratch_shapes=[
            pltpu.VMEM((tokens, LANES), F32),
            pltpu.VMEM((tokens, LANES), F32),
            pltpu.VMEM((tokens, LANES), F32),
            pltpu.VMEM((rows, HC), F32),
            pltpu.VMEM((tokens, HC), F32),
            pltpu.VMEM((rows + 8, HC), F32),
            pltpu.VMEM((chunks, DK, DV), F32),
            pltpu.VMEM((tokens, LANES), F32),
            pltpu.VMEM((tokens, LANES), F32),
        ],
        compiler_params=params(),
        cost_estimate=cost(8e9 * H, 5e6 * H),
        name="delta_backward",
    )(place, slots, proj, taps, logits, par, cols, back, segr, d_attn, state_in, exch, grads, *saved)


def mixer_kernel(
    place_ref, slot_ref, part_ref, resp_ref, exch_ref, gpre_ref, gain_ref, w_ref, x_ref, gain2_ref,
    sin_ref, attn_ref, gated_ref, y_ref, h_ref,
):
    head = pl.program_id(0)
    place = place_ref[0]
    places = exch_ref.shape[0]

    def ahead(source, state):
        slot = slot_ref[source]
        return jnp.where(
            source < place,
            exch_ref[slot, 0, :, :DV].astype(F32) + mm(exch_ref[slot, 0, :, DV:], state),
            state,
        )

    state = lax.fori_loop(0, places - 1, ahead, jnp.zeros((DK, DV), F32))
    sin_ref[0] = state
    attn = part_ref[...] + mm(resp_ref[...], state)
    attn_ref[...] = attn
    scale = lax.rsqrt(jnp.mean(attn * attn, axis=-1, keepdims=True) + 1e-05)
    gate = gpre_ref[...]
    gated = (attn * scale * gain_ref[...] * (gate * jax.nn.sigmoid(gate))).astype(BF16)
    gated_ref[...] = gated

    @pl.when(head == 0)
    def _():
        y_ref[...] = x_ref[...].astype(F32)

    y_ref[...] += mm(gated, w_ref[...], NT)

    @pl.when(head == pl.num_programs(0) - 1)
    def _():
        value = y_ref[...]
        size = lax.rsqrt(jnp.mean(value * value, axis=-1, keepdims=True) + 1e-06)
        h_ref[...] = (value * size * gain2_ref[...]).astype(BF16)


def mixer_out(place, slots, part, resp, exch, gpre, gain, weights, x, gain2):
    tokens, width = x.shape
    places = exch.shape[0]
    whole = lambda shape: pl.BlockSpec(shape, lambda h: (0,) * len(shape))
    return pl.pallas_call(
        mixer_kernel,
        grid=(H,),
        in_specs=[
            pl.BlockSpec(memory_space=pltpu.SMEM),
            pl.BlockSpec(memory_space=pltpu.SMEM),
            pl.BlockSpec((tokens, DV), lambda h: (0, h)),
            pl.BlockSpec((tokens, DK), lambda h: (0, h)),
            pl.BlockSpec((places, 1, DK, DV + DK), lambda h: (0, h, 0, 0)),
            pl.BlockSpec((tokens, DV), lambda h: (0, h)),
            whole((1, DV)),
            pl.BlockSpec((width, DV), lambda h: (0, h + AT_OUT // DV)),
            whole((tokens, width)),
            whole((1, width)),
        ],
        out_specs=[
            pl.BlockSpec((1, DK, DV), lambda h: (h, 0, 0)),
            pl.BlockSpec((tokens, DV), lambda h: (0, h)),
            pl.BlockSpec((tokens, DV), lambda h: (0, h)),
            whole((tokens, width)),
            whole((tokens, width)),
        ],
        out_shape=[
            jax.ShapeDtypeStruct((H, DK, DV), F32),
            jax.ShapeDtypeStruct((tokens, H * DV), F32),
            jax.ShapeDtypeStruct((tokens, H * DV), BF16),
            jax.ShapeDtypeStruct((tokens, width), F32),
            jax.ShapeDtypeStruct((tokens, width), BF16),
        ],
        compiler_params=params(),
        cost_estimate=cost(2 * tokens * width * H * DV, 2e7),
        name="mixer_out",
    )(place, slots, part, resp, exch, gpre, gain, weights, x, gain2)


def mixer_back_kernel(
    dmix_ref, w_ref, attn_ref, gpre_ref, gain_ref, resp_ref,
    dattn_ref, dgpre_ref, grad_ref, dgain_ref,
):
    @pl.when(pl.program_id(0) == 0)
    def _():
        dgain_ref[...] = jnp.zeros_like(dgain_ref)

    d_gain, dattn_ref[...], dgpre_ref[...], grad_ref[0] = mixer_back_head(
        dmix_ref, w_ref, attn_ref, gpre_ref, gain_ref, resp_ref
    )
    dgain_ref[0:1, :] += d_gain


def mixer_back_head(dmix_ref, w_ref, attn_ref, gpre_ref, gain_ref, resp_ref):
    d_gated = mm(dmix_ref[...], w_ref[...])
    attn = attn_ref[...]
    size = lax.rsqrt(jnp.mean(attn * attn, axis=-1, keepdims=True) + 1e-05)
    unit = attn * size
    gate = gpre_ref[...]
    slope = jax.nn.sigmoid(gate)
    swish = gate * slope
    gain = gain_ref[...]
    d_gpre = (d_gated * (unit * gain) * (slope * (1.0 + gate * (1.0 - slope)))).astype(BF16)
    d_normed = d_gated * swish
    d_gain = jnp.sum(d_normed * unit, axis=0, keepdims=True)
    d_unit = d_normed * gain
    d_attn = size * (d_unit - unit * jnp.mean(d_unit * unit, axis=-1, keepdims=True))
    d_attn = d_attn.astype(BF16)
    return d_gain, d_attn, d_gpre, mm(resp_ref[...], d_attn, TN).astype(BF16)


def mixer_back(d_mixer, weights, attn, gpre, gain, resp):
    tokens, width = d_mixer.shape
    whole = lambda shape: pl.BlockSpec(shape, lambda h: (0,) * len(shape))
    return pl.pallas_call(
        mixer_back_kernel,
        grid=(H,),
        in_specs=[
            whole((tokens, width)),
            pl.BlockSpec((width, DV), lambda h: (0, h + AT_OUT // DV)),
            pl.BlockSpec((tokens, DV), lambda h: (0, h)),
            pl.BlockSpec((tokens, DV), lambda h: (0, h)),
            whole((1, DV)),
            pl.BlockSpec((tokens, DK), lambda h: (0, h)),
        ],
        out_specs=[
            pl.BlockSpec((tokens, DV), lambda h: (0, h)),
            pl.BlockSpec((tokens, DV), lambda h: (0, h)),
            pl.BlockSpec((1, DK, DV), lambda h: (h, 0, 0)),
            whole((8, DV)),
        ],
        out_shape=[
            jax.ShapeDtypeStruct((tokens, H * DV), BF16),
            jax.ShapeDtypeStruct((tokens, H * DV), BF16),
            jax.ShapeDtypeStruct((H, DK, DV), BF16),
            jax.ShapeDtypeStruct((8, DV), F32),
        ],
        compiler_params=params(),
        cost_estimate=cost(2 * tokens * width * H * DV, 2e7),
        name="mixer_back",
    )(d_mixer, weights, attn, gpre, gain, resp)


def ffn_kernel(
    h_ref, dout_ref, y_ref, gain_ref, turn_ref, weights_ref,
    out_ref, act_ref, dgu_ref, dy_ref, dmix_ref, dgain_ref,
    w_ref, acts_ref, dg_ref, du_ref, res_ref, dh_ref, load_sem, *, inner, block, gain_row,
):
    step = pl.program_id(0)
    blocks = inner // block
    across = dh_ref.shape[1] // (pl.num_programs(0) - blocks)

    def load(which, n):
        cols = pl.multiple_of(n * block, block)
        return pltpu.make_async_copy(
            weights_ref.at[:, pl.ds(AT_FFN + which * inner + cols, block)],
            w_ref.at[which, :, pl.ds(cols, block)],
            load_sem.at[which, n],
        )

    @pl.when(step == 0)
    def _():
        for n in range(blocks):
            for which in range(3):
                load(which, n).start()

    @pl.when(step < blocks)
    def _():
        for which in range(3):
            load(which, step).wait()
        cols = pl.ds(pl.multiple_of(step * block, block), block)
        hidden = h_ref[...]
        gate = mm(hidden, w_ref[0, :, cols])
        up = mm(hidden, w_ref[1, :, cols])
        d_act = mm(dout_ref[...], w_ref[2, :, cols])
        slope = jax.nn.sigmoid(gate)
        swish = gate * slope
        act = (swish * up).astype(BF16)
        act_ref[...] = act
        acts_ref[:, cols] = act
        d_gate = (d_act * up * slope * (1.0 + gate * (1.0 - slope))).astype(BF16)
        d_up = (d_act * swish).astype(BF16)
        dgu_ref[0] = d_gate
        dg_ref[:, cols] = d_gate
        dgu_ref[1] = d_up
        du_ref[:, cols] = d_up

    @pl.when(step >= blocks)
    def _():
        rows = pl.ds(pl.multiple_of((step - blocks) * across, across), across)
        res_ref[:, rows] = y_ref[:, rows] + mm(acts_ref[...], w_ref[2, rows, :], NT)
        dh_ref[:, rows] = mm(dg_ref[...], w_ref[0, rows, :], NT) + mm(du_ref[...], w_ref[1, rows, :], NT)

    @pl.when(step == pl.num_programs(0) - 1)
    def _():
        out_ref[...] = mm(res_ref[...], turn_ref[...], NT).astype(BF16)
        value = y_ref[...]
        size = lax.rsqrt(jnp.mean(value * value, axis=-1, keepdims=True) + 1e-06)
        unit = value * size
        d_hidden = dh_ref[...]
        dgain_ref[...] = jnp.zeros_like(dgain_ref)
        dgain_ref[0:1, :] = jnp.sum(d_hidden * unit, axis=0, keepdims=True)
        d_unit = d_hidden * gain_ref[gain_row : gain_row + 1, :]
        d_y = dout_ref[...].astype(F32) + size * (
            d_unit - unit * jnp.mean(d_unit * unit, axis=-1, keepdims=True)
        )
        dy_ref[...] = d_y
        dmix_ref[...] = d_y.astype(BF16)


def feed_forward(hidden, d_out, y1, gains, gain_row, turn, weights, inner):
    tokens, width = hidden.shape
    block, across = 256, 256
    blocks = inner // block
    once = lambda shape: pl.BlockSpec(shape, lambda j: (0,) * len(shape), pipeline_mode=pl.Buffered(1))
    whole = lambda shape: pl.BlockSpec(shape, lambda j: (0,) * len(shape))
    at = lambda j: jnp.minimum(j, blocks - 1)
    return pl.pallas_call(
        functools.partial(ffn_kernel, inner=inner, block=block, gain_row=gain_row),
        grid=(blocks + width // across,),
        in_specs=[
            once((tokens, width)),
            once((tokens, width)),
            once((tokens, width)),
            once(gains.shape),
            once((width, width)),
            pl.BlockSpec(memory_space=pl.ANY),
        ],
        out_specs=[
            whole((tokens, width)),
            pl.BlockSpec((tokens, block), lambda j: (0, at(j))),
            pl.BlockSpec((2, tokens, block), lambda j: (0, 0, at(j))),
            whole((tokens, width)), whole((tokens, width)), whole((8, width)),
        ],
        out_shape=[
            jax.ShapeDtypeStruct((tokens, width), BF16),
            jax.ShapeDtypeStruct((tokens, inner), BF16),
            jax.ShapeDtypeStruct((2, tokens, inner), BF16),
            jax.ShapeDtypeStruct((tokens, width), F32),
            jax.ShapeDtypeStruct((tokens, width), BF16),
            jax.ShapeDtypeStruct((8, width), F32),
        ],
        scratch_shapes=[
            pltpu.VMEM((3, width, inner), BF16),
            pltpu.VMEM((tokens, inner), BF16),
            pltpu.VMEM((tokens, inner), BF16),
            pltpu.VMEM((tokens, inner), BF16),
            pltpu.VMEM((tokens, width), F32),
            pltpu.VMEM((tokens, width), F32),
            pltpu.SemaphoreType.DMA((3, blocks)),
        ],
        compiler_params=params(),
        cost_estimate=cost(12 * tokens * width * inner, 3e7),
        name="feed_forward",
    )(hidden, d_out, y1, gains, turn, weights)


BLOCK = HC
LEAD, EVERY = 7, 3


def other_index(step):
    return step - jnp.clip((step - LEAD + EVERY - 1) // EVERY, 0, H)


class Blocks:
    def __init__(self, inner):
        self.ups, self.downs = inner // (BLOCK // 2), inner // BLOCK
        self.outs = H * DV // BLOCK
        self.others = self.ups + self.downs + 2 * self.outs
        self.count = self.others + H + 1
        self.starts = [0, self.ups, self.ups + self.downs, self.ups + self.downs + self.outs, self.others]
        self.tail = inner - self.downs * BLOCK
        heads = [LEAD + EVERY * h for h in range(H)]
        rest = [n for n in range(self.count - 1) if n not in heads]
        parts = [rest[low:high] for low, high in zip(self.starts, self.starts[1:])]
        self.up_at, self.down_at, self.out_at, self.gate_at = parts
        self.head_at = heads

    def index(self, kind):
        low, high = self.starts[kind], self.starts[kind + 1]
        return lambda s: jnp.clip(other_index(s) - low, 0, high - low - 1)


def dot_blocks(left, right):
    return lax.dot_general(left, right, (NN, ((), ())), preferred_element_type=F32)


def flip_to(bit):
    here = lax.axis_index("seq")
    along_x = here + 1 - 2 * lax.rem(here, 2)
    along_y = here + 2 - 4 * (here // 2)
    return {"dp": lax.axis_index("dp"), "seq": (2 - bit) * along_x + (bit - 1) * along_y}


def reduce_kernel(
    dout_any, hmid_any, hidden_any, x_any, dy_any, turn_any, dres_ref,
    act_ref, tail_ref, dgu_ref, gated_ref, wout_ref, attn_ref, gpre_ref, gain_ref, resp_ref, win_ref, wl_ref,
    gains_ref, dffn_ref,
    p_ref, taps_q_ref, taps_k_ref, taps_v_ref, logit_ref, par_ref, cols_ref, back_ref, segr_ref, sin_ref, maps_ref,
    inv_ref, upd_ref, st_ref, stm_ref, amap_ref, rmap_ref,
    sum_ref, dx_ref, small_ref,
    taps_ref, dlogit_ref, dtaps_ref, dpar_ref, dgain_ref, dattn_ref, dgpre_ref, lgrad_ref, acc_ref, left_ref,
    total_ref, other_ref,
    beta_ref, decay_ref, cum_ref, pf_ref, pre_ref, dmix_ref, dstate_ref, dbeta_ref, ddecay_ref,
    turn_ref, dps_ref, halo_ref, grads_ref, halves_ref,
    core_keep, core_send, core_recv, near_keep, near_send, near_recv,
    z_keep, pair_send, pair_recv, cross_send, cross_recv, far_send, far_recv, done_ref,
    core_ss, core_rs, near_ss, near_rs, pair_ss, pair_rs, cross_ss, cross_rs, far_ss, far_rs, done_ss, done_rs, own_sem,
    halo_ss, halo_rs, grads_ss, grads_rs, load_sem, small_ss, small_rs, *, blocks,
):
    step = pl.program_id(0)
    steps = pl.num_programs(0)
    place = lax.axis_index("seq")
    count = blocks.count
    half = core_keep.shape[1] * core_keep.shape[2]
    quarter = half // SPOTS
    piece = quarter // PLANES
    mesh = dict(device_id_type=pl.DeviceIdType.MESH)

    def remote(source, target, send, recv, to):
        return pltpu.make_async_remote_copy(
            src_ref=source, dst_ref=target, send_sem=send, recv_sem=recv, device_id=to, **mesh
        )

    def to_core(n):
        mine, slot = lax.rem(n, 3), lax.rem(n, 4)
        return remote(core_send.at[mine], core_recv.at[slot], core_ss.at[mine], core_rs.at[slot], device(core=1))

    def to_near(n):
        slot = lax.rem(n, 4)
        return remote(
            near_send.at[slot], near_recv.at[slot], near_ss.at[slot], near_rs.at[slot], flip_to(1 + lax.rem(n, 2))
        )

    def to_far(n):
        slot = lax.rem(n, 4)
        return remote(
            far_send.at[slot], far_recv.at[slot], far_ss.at[slot], far_rs.at[slot], flip_to(2 - lax.rem(n, 2))
        )

    z = lax.axis_index("dp") // CORES
    inner = (z > 0) & (z < PLANES - 1)
    outer_plane = (z == 0) | (z == PLANES - 1)

    def to_pair(n, pieces):
        slot = lax.rem(n, 4)
        return remote(
            pair_send.at[slot, 0:pieces], pair_recv.at[slot, 0:pieces], pair_ss.at[slot], pair_rs.at[slot],
            device(planes=1 + 2 * lax.rem(z, 2)),
        )

    def to_cross(n, outside):
        planes = 2 if outside else 2 * z - 1
        slot = lax.rem(n, 4)
        return remote(
            cross_send.at[slot, outside], cross_recv.at[n], cross_ss.at[slot, outside], cross_rs.at[n],
            device(planes=planes),
        )

    def bits(n):
        pair = lax.rem(n, 2)
        along_x, along_y = lax.rem(place, 2), place // 2
        return (1 - pair) * along_x + pair * along_y, (1 - pair) * along_y + pair * along_x

    def spread(n):
        slot = lax.rem(n, 4)
        return remote(
            done_ref.at[slot], sum_ref.at[n, bits(n)[0]], done_ss.at[slot], done_rs.at[n], flip_to(1 + lax.rem(n, 2))
        )

    def keep(n):
        slot = lax.rem(n, 4)
        return pltpu.make_async_copy(done_ref.at[slot], sum_ref.at[n, bits(n)[0]], own_sem.at[slot])

    upper = place // 2 == 1
    second = lax.rem(place, 2) == 1

    def give_grads(head):
        return remote(
            lgrad_ref.at[head], grads_ref.at[0, head], grads_ss.at[0, head], grads_rs.at[0, head], device(spot=1)
        )

    def give_half(head):
        return remote(
            halves_ref.at[head], grads_ref.at[1, head], grads_ss.at[1, head], grads_rs.at[1, head], device(spot=2)
        )

    def give_small(stage):
        to = (dict(core=1), dict(spot=1), dict(spot=2), dict(planes=1), dict(planes=2), dict(planes=3))[stage]
        return remote(
            total_ref.at[min(stage, 3)], other_ref.at[stage], small_ss.at[stage], small_rs.at[stage], device(**to)
        )

    def load(at, source, to):
        return pltpu.make_async_copy(source, to, load_sem.at[at])

    def final_loads():
        width = turn_any.shape[0]
        copies = []
        for n in range(2):
            cols = slice(n * (width // 2), (n + 1) * (width // 2))
            copies.append(load(n, turn_any.at[:, cols], turn_ref.at[n]))
            rows = x_any.shape[0]
            copies.append(load(2 + n, x_any.at[:, cols], turn_ref.at[2, n * rows : (n + 1) * rows]))
            for q in range(SPOTS):
                copies.append(
                    load(4 + n * SPOTS + q, dy_any.at[q * quarter : (q + 1) * quarter, cols], core_keep.at[n, q])
                )
        return copies

    def final_stores():
        width = dx_ref.shape[1]
        return [
            load(
                n * SPOTS + q,
                core_keep.at[n, q],
                dx_ref.at[q * quarter : (q + 1) * quarter, n * (width // 2) : (n + 1) * (width // 2)],
            )
            for n in range(2)
            for q in range(SPOTS)
        ]

    def give_halo(head):
        to = {"dp": lax.axis_index("dp"), "seq": lax.rem(place + SPOTS - 1, SPOTS)}
        return remote(dps_ref.at[0:HALO], halo_ref.at[head], halo_ss.at[head], halo_rs.at[head], to)

    @pl.when(step == 0)
    def _():
        greet([dict(planes=d) for d in (1, 2, 3)] + [dict(spot=s) for s in (1, 2, 3)] + [dict(core=1)])
        dgain_ref[...] = jnp.zeros_like(dgain_ref)
        acc_ref[...] = jnp.zeros_like(acc_ref)

    def left(n):
        tokens = dres_ref.shape[0]
        source = (hmid_any, dout_any, hidden_any.at[HALO : HALO + tokens])[n]
        return load(n, source, left_ref.at[n % 2])

    for n, at in enumerate((1, 0, 3, 2)):

        @pl.when(step == n)
        def _(n=n, at=at):
            if n == 0:
                left(0).start()
            if n < 2:
                left(n + 1).start()
            if n < 3:
                left(n).wait()
                turn_ref[at] = jnp.transpose(left_ref[n % 2])
            else:
                turn_ref[at] = jnp.transpose(dres_ref[...])

    def at_stage(lag, sent):
        n = step - lag

        def run(body):
            @pl.when((n >= 0) & (n < count))
            def _():
                @pl.when(n >= sent)
                def _():
                    body(n, True)

                body(n, False)

        return run

    @at_stage(10, 4)
    def _(n, free):
        if free:
            spread(n - 4).wait_send()
            keep(n - 4).wait()
            return
        slot = lax.rem(n, 4)
        to_far(n).wait_recv()
        other = bits(n)[1]
        for which in range(2):
            total = far_send[slot, which].astype(F32) + far_recv[slot, 1 - which].astype(F32)
            done_ref[slot, other + which - 2 * other * which] = total.astype(BF16)
        spread(n).start()
        keep(n).start()

    @at_stage(8, 4)
    def _(n, free):
        if free:
            to_far(n - 4).wait_send()
            return
        slot = lax.rem(n, 4)
        to_cross(n, 0).wait_recv()
        total = (z_keep[slot, 0] + cross_recv[n].astype(F32)).astype(BF16)
        far_send[slot, 0], far_send[slot, 1] = total[:piece], total[piece:]
        to_far(n).start()

    @at_stage(6, 4)
    def _(n, free):
        slot = lax.rem(n, 4)
        if free:

            @pl.when(inner)
            def _():
                to_cross(n - 4, 0).wait_send()
                to_cross(n - 4, 1).wait_send()

            return

        @pl.when(outer_plane)
        def _():
            to_pair(n, 1).wait_recv()

        @pl.when(inner)
        def _():
            to_pair(n, 3).wait_recv()
            for outside, at in enumerate((5 - 2 * z, 2)):
                cross_send[slot, outside] = (
                    z_keep[slot, at] + pair_recv[slot, 1 + outside].astype(F32)
                ).astype(BF16)
                to_cross(n, outside).start()

        z_keep[slot, 0] += pair_recv[slot, 0].astype(F32)

    @at_stage(4, 4)
    def _(n, free):
        slot = lax.rem(n, 4)
        if free:

            @pl.when(outer_plane)
            def _():
                to_pair(n - 4, 3).wait_send()

            @pl.when(inner)
            def _():
                to_pair(n - 4, 1).wait_send()

            return
        to_near(n).wait_recv()
        for which in range(2):
            total = near_keep[slot, which] + near_recv[slot, which].astype(F32)
            for d in range(PLANES):
                z_keep[slot, d, which * piece : (which + 1) * piece] = total[d * piece : (d + 1) * piece]

        @pl.when(outer_plane)
        def _():
            up = 1 - z // 3
            for k in range(3):
                pair_send[slot, k] = z_keep[slot, up * (3 - k) + (1 - up) * (1 + k)].astype(BF16)
            to_pair(n, 3).start()

        @pl.when(inner)
        def _():
            pair_send[slot, 0] = z_keep[slot, 2 * z - 1].astype(BF16)
            to_pair(n, 1).start()

    @at_stage(2, 4)
    def _(n, free):
        if free:
            to_near(n - 4).wait_send()
            return
        slot, mine = lax.rem(n, 4), lax.rem(n, 3)
        first = 1 + lax.rem(n, 2)
        to_core(n).wait_recv()
        whole = lambda quarter: core_keep[mine, quarter] + core_recv[slot, quarter].astype(F32)
        near_keep[slot, 0] = whole(0)
        near_keep[slot, 1] = whole(3 - first)
        near_send[slot, 0] = whole(first).astype(BF16)
        near_send[slot, 1] = whole(3).astype(BF16)
        to_near(n).start()

    since = step - LEAD
    heads_turn = (since >= 0) & (since < EVERY * H) & (lax.rem(jnp.maximum(since, 0), EVERY) == 0)
    other = other_index(step)

    def put(product):
        mine = lax.rem(step, 3)

        @pl.when(step >= 3)
        def _():
            to_core(step - 3).wait_send()

        for q in range(SPOTS):
            core_keep[mine, q] = product[q * quarter : (q + 1) * quarter]
            core_send[mine, q] = product[half + q * quarter : half + (q + 1) * quarter].astype(BF16)
        to_core(step).start()

    def on(kind):
        low, high = blocks.starts[kind], blocks.starts[kind + 1]
        return pl.when((other >= low) & (other < high) & jnp.logical_not(heads_turn))

    @on(0)
    def _():
        put(dot_blocks(turn_ref[1], jnp.concatenate([dgu_ref[0], dgu_ref[1]], axis=1)))

    @on(1)
    def _():
        put(dot_blocks(turn_ref[0], act_ref[...]))

    @on(2)
    def _():
        put(dot_blocks(turn_ref[2], gated_ref[...]))

    @on(3)
    def _():
        gate = other - blocks.starts[3]
        value = jnp.concatenate([dgpre_ref[2 * gate], dgpre_ref[2 * gate + 1]], axis=1)
        acc_ref[...] += mm(value, win_ref[...], NT)
        put(dot_blocks(turn_ref[3], value))

    @pl.when(step == count - 1)
    def _():
        down = dot_blocks(turn_ref[0], tail_ref[...])
        gates = dot_blocks(turn_ref[3], dlogit_ref[...].astype(BF16))
        acc_ref[...] += mm(dlogit_ref[...], wl_ref[...], NT)
        rest = jnp.zeros((down.shape[0], BLOCK - down.shape[1] - LANES), F32)
        put(jnp.concatenate([down, gates, rest], axis=1))

    @pl.when(heads_turn)
    def _():
        head = since // EVERY

        @pl.when(place > 0)
        def _():
            give_halo(head).wait_send()

        @pl.when(place < SPOTS - 1)
        def _():
            give_halo(head).wait_recv()
            tokens = dps_ref.shape[0] - HALO
            dps_ref[tokens:, :] = (
                dps_ref[tokens:, :].astype(F32) + halo_ref[head].astype(F32)
            ).astype(BF16)

        value = dps_ref[HALO:, :]
        acc_ref[...] += mm(value, win_ref[...], NT)
        put(dot_blocks(turn_ref[3], value))

    @pl.when(step < H)
    def _():
        d_gain, dattn_ref[step], dgpre_ref[step], lgrad_ref[step] = mixer_back_head(
            dres_ref, wout_ref, attn_ref, gpre_ref, gain_ref, resp_ref
        )
        dgain_ref[...] += d_gain
        give_grads(step).start()

    @pl.when((step >= 2) & (step < H + 2))
    def _():
        head = step - 2
        give_grads(head).wait()

        @pl.when(upper)
        def _():
            mine, theirs = lgrad_ref[head], grads_ref[0, head]
            earlier = jnp.where(second, theirs, mine)
            later = jnp.where(second, mine, theirs)
            through = jnp.where(second, maps_ref[1, head], maps_ref[0, head])
            halves_ref[head] = (earlier.astype(F32) + mm(through, later, TN)).astype(BF16)
            give_half(head).start()

    ahead = since + EVERY
    for phase in range(PHASES):

        @pl.when((ahead >= 0) & (ahead < EVERY * H) & (lax.rem(jnp.maximum(ahead, 0), EVERY) == phase))
        def _(phase=phase):
            head = ahead // EVERY

            def entering():
                @pl.when(upper)
                def _():
                    grads_ref[1, head] = jnp.zeros((DK, DV), BF16)
                    give_half(head).wait_send()

                @pl.when(jnp.logical_not(upper))
                def _():
                    give_half(head).wait_recv()

                d_state = grads_ref[1, head].astype(F32)
                nearer = grads_ref[0, head].astype(F32) + mm(maps_ref[1, head], d_state, TN)
                return jnp.where(second, d_state, nearer)

            if phase == 0:
                join_taps(taps_ref, taps_q_ref, taps_k_ref, taps_v_ref)
            backward_head(
                phase, head, entering, p_ref, taps_ref, logit_ref, par_ref, cols_ref, back_ref, segr_ref,
                dattn_ref.at[head], sin_ref, inv_ref, upd_ref, st_ref, stm_ref, amap_ref, rmap_ref,
                dps_ref, dlogit_ref, dtaps_ref, dpar_ref, beta_ref, decay_ref, cum_ref, pf_ref, pre_ref, dmix_ref,
                dstate_ref, dbeta_ref, ddecay_ref,
            )
            if phase == PHASES - 1:
                total_ref[0, pl.ds(pl.multiple_of(head * 8, 8), 8), :] = dtaps_ref[...]

                @pl.when(place > 0)
                def _():
                    give_halo(head).start()

    @pl.when(step == count)
    def _():
        for copy in final_loads():
            copy.start()

    @pl.when(step == count + 2)
    def _():
        for copy in final_loads():
            copy.wait()
        tokens, width = acc_ref.shape
        middle = width // 2
        halves_of = lambda ref: jnp.concatenate([ref[0], ref[1]], axis=1)
        value = jnp.concatenate([turn_ref[2, :tokens], turn_ref[2, tokens:]], axis=1).astype(F32)
        size = lax.rsqrt(jnp.mean(value * value, axis=-1, keepdims=True) + 1e-06)
        unit = value * size
        d_hidden = acc_ref[...]
        d_gain = jnp.sum(d_hidden * unit, axis=0, keepdims=True)
        d_unit = d_hidden * gains_ref[0:1, :]
        through = size * (d_unit - unit * jnp.mean(d_unit * unit, axis=-1, keepdims=True))
        d_y = [jnp.concatenate([core_keep[n, q] for q in range(SPOTS)], axis=0) for n in range(2)]
        total = jnp.concatenate(d_y, axis=1) + through

        def natural(part):
            return mm(part[:, :middle], turn_ref[0], NT) + mm(part[:, middle:], turn_ref[1], NT)

        high, low = halves(total)
        total = natural(high) + natural(low)
        for n in range(2):
            for q in range(SPOTS):
                core_keep[n, q] = total[q * quarter : (q + 1) * quarter, n * middle : (n + 1) * middle]
        for copy in final_stores():
            copy.start()
        gains = jnp.concatenate([d_gain, dffn_ref[0:1, :], jnp.zeros((6, width), F32)], axis=0)
        high, mid = halves(gains)
        gains = natural(high) + natural(mid) + natural((gains - high.astype(F32)) - mid.astype(F32))
        base = 8 * H
        total_ref[0, base : base + 8, :] = gains[:, :middle]
        total_ref[0, base + 8 : base + 16, :] = gains[:, middle:]
        total_ref[0, base + 16 : base + 24, : dgain_ref.shape[1]] = dgain_ref[...]
        total_ref[0, base + 16 : base + 24, dgain_ref.shape[1] : dgain_ref.shape[1] + LANES] = dpar_ref[...]
        total_ref[0, base + 16 : base + 24, dgain_ref.shape[1] + LANES :] = jnp.zeros((8, LANES), F32)
        give_small(0).start()

    for stage in range(3):

        @pl.when(step == count + 3 + stage)
        def _(stage=stage):
            give_small(stage).wait_recv()
            total_ref[stage + 1] = total_ref[stage] + other_ref[stage]
            for later in (stage + 1,) if stage < 2 else (3, 4, 5):
                give_small(later).start()

    @pl.when(step == count + 6)
    def _():
        total = total_ref[3]
        for stage in (3, 4, 5):
            give_small(stage).wait_recv()
            total += other_ref[stage]
        small_ref[...] = total
        for stage in range(6):
            give_small(stage).wait_send()
        for copy in final_stores():
            copy.wait()

    @pl.when(step == steps - 1)
    def _():
        for n in range(count - 4, count):
            if n >= count - 3:
                to_core(n).wait_send()
            to_near(n).wait_send()
            to_far(n).wait_send()

            @pl.when(outer_plane)
            def _(n=n):
                to_pair(n, 3).wait_send()

            @pl.when(inner)
            def _(n=n):
                to_pair(n, 1).wait_send()
                to_cross(n, 0).wait_send()
                to_cross(n, 1).wait_send()

            spread(n).wait_send()
            keep(n).wait()

        def arrived(n, carry):
            spread(n).wait_recv()
            return carry

        lax.fori_loop(0, count, arrived, 0)


def reduce_gradients(
    d_out, hidden_mid, hidden, x, d_y, turn, d_mixer, act, d_gu, gated, weights, attn, gpre, gain_out, resp, gains,
    d_ffn, proj, taps, logits, par, cols, back, segr, state_in, maps, saved,
):
    tokens, width = d_mixer.shape
    rows = hidden.shape[0]
    chunks = tokens // CHUNK
    blocks = Blocks(act.shape[1])
    half = width // CORES
    quarter = half // SPOTS
    piece = quarter // PLANES
    small = 8 * H + 24
    anywhere = pl.BlockSpec(memory_space=pl.ANY)
    whole = lambda shape: pl.BlockSpec(shape, lambda s: (0,) * len(shape))
    once = lambda shape: pl.BlockSpec(shape, lambda s: (0,) * len(shape), pipeline_mode=pl.Buffered(1))
    coming = lambda s: jnp.clip((s - (LEAD - EVERY)) // EVERY, 0, H - 1)
    starting = lambda s: jnp.minimum(s, H - 1)
    by_head = lambda shape: pl.BlockSpec(shape, lambda s: (coming(s),) + (0,) * (len(shape) - 1))
    across = lambda shape, at: pl.BlockSpec(shape, lambda s: (0, at(s)))
    sem = pltpu.SemaphoreType.DMA
    up, down, out, gate = (blocks.index(kind) for kind in range(4))
    first_gate = blocks.gate_at[0]

    def win(s):
        no_head = ((s - LEAD) % EVERY != 0) | (s > blocks.head_at[-1])
        is_gate = (s >= first_gate) & (s <= blocks.gate_at[-1]) & no_head
        head = jnp.clip((s - LEAD + EVERY - 1) // EVERY, 0, H - 1)
        return jnp.where(is_gate, AT_GATE // BLOCK + gate(s), H - 1 - head)

    return blocks, pl.pallas_call(
        functools.partial(reduce_kernel, blocks=blocks),
        grid=(blocks.count + 10,),
        in_specs=[anywhere] * 6
        + [
            once((tokens, width)),
            across((tokens, BLOCK), down),
            pl.BlockSpec(
                (tokens, blocks.tail), lambda s: (0, blocks.downs * BLOCK // blocks.tail), pipeline_mode=pl.Buffered(1)
            ),
            pl.BlockSpec((2, tokens, BLOCK // 2), lambda s: (0, 0, up(s))),
            across((tokens, BLOCK), out),
            pl.BlockSpec((width, DV), lambda s: (0, AT_OUT // DV + starting(s))),
            across((tokens, DV), starting),
            across((tokens, DV), starting),
            once((1, DV)),
            across((tokens, DK), starting),
            across((width, BLOCK), win),
            pl.BlockSpec((width, LANES), lambda s: (0, AT_LOGIT // LANES), pipeline_mode=pl.Buffered(1)),
            once((8, width)),
            once((8, width)),
            across((rows, HC), coming),
            *taps_specs(coming),
            once((rows, LANES)),
            once((8, LANES)),
            once((tokens, LANES)),
            once((rows, LANES)),
            once(segr.shape),
            by_head((1, DK, DV)),
            once((2, H, DK, DK)),
            by_head((1, chunks, CHUNK, CHUNK)),
            by_head((1, tokens, DV + DK)),
            by_head((1, chunks, DK, DV)),
            by_head((1, chunks, DK, DK)),
            by_head((1, chunks, DK, DK)),
            by_head((1, chunks, CHUNK, DK)),
        ],
        out_specs=[anywhere, anywhere, whole((small, BLOCK))],
        out_shape=[
            jax.ShapeDtypeStruct((blocks.count, 2, 2, piece, BLOCK), BF16),
            jax.ShapeDtypeStruct((tokens, width), F32),
            jax.ShapeDtypeStruct((small, BLOCK), F32),
        ],
        scratch_shapes=[
            pltpu.VMEM((8, HC), F32),
            pltpu.VMEM((tokens, LANES), F32),
            pltpu.VMEM((8, HC), F32),
            pltpu.VMEM((8, LANES), F32),
            pltpu.VMEM((8, DV), F32),
            pltpu.VMEM((H, tokens, DV), BF16),
            pltpu.VMEM((H, tokens, DV), BF16),
            pltpu.VMEM((H, DK, DV), BF16),
            pltpu.VMEM((tokens, width), F32),
            pltpu.VMEM((2, tokens, width), BF16),
            pltpu.VMEM((4, small, BLOCK), F32),
            pltpu.VMEM((6, small, BLOCK), F32),
            pltpu.VMEM((tokens, LANES), F32),
            pltpu.VMEM((tokens, LANES), F32),
            pltpu.VMEM((tokens, LANES), F32),
            pltpu.VMEM((rows, HC), F32),
            pltpu.VMEM((tokens, HC), F32),
            pltpu.VMEM((rows + 8, HC), F32),
            pltpu.VMEM((chunks, DK, DV), F32),
            pltpu.VMEM((tokens, LANES), F32),
            pltpu.VMEM((tokens, LANES), F32),
            pltpu.VMEM((4, width, tokens), BF16),
            pltpu.VMEM((rows, HC), BF16),
            pltpu.VMEM((H, HALO, HC), BF16),
            pltpu.VMEM((2, H, DK, DV), BF16),
            pltpu.VMEM((H, DK, DV), BF16),
            pltpu.VMEM((3, SPOTS, quarter, BLOCK), F32),
            pltpu.VMEM((3, SPOTS, quarter, BLOCK), BF16),
            pltpu.VMEM((4, SPOTS, quarter, BLOCK), BF16),
            pltpu.VMEM((4, 2, quarter, BLOCK), F32),
            pltpu.VMEM((4, 2, quarter, BLOCK), BF16),
            pltpu.VMEM((4, 2, quarter, BLOCK), BF16),
            pltpu.VMEM((4, PLANES, 2 * piece, BLOCK), F32),
            pltpu.VMEM((4, PLANES - 1, 2 * piece, BLOCK), BF16),
            pltpu.VMEM((4, PLANES - 1, 2 * piece, BLOCK), BF16),
            pltpu.VMEM((4, 2, 2 * piece, BLOCK), BF16),
            pltpu.VMEM((blocks.count, 2 * piece, BLOCK), BF16),
            pltpu.VMEM((4, 2, piece, BLOCK), BF16),
            pltpu.VMEM((4, 2, piece, BLOCK), BF16),
            pltpu.VMEM((4, 2, piece, BLOCK), BF16),
            sem((3,)), sem((4,)), sem((4,)), sem((4,)), sem((4,)), sem((4,)),
            sem((4, 2)), sem((blocks.count,)), sem((4,)), sem((4,)),
            sem((4,)), sem((blocks.count,)), sem((4,)),
            sem((H,)), sem((H,)), sem((2, H)), sem((2, H)),
            sem((4 + 2 * SPOTS,)), sem((6,)), sem((6,)),
        ],
        compiler_params=params(collective_id=1, has_side_effects=True),
        cost_estimate=cost(1e11, 1e8),
        name="reduce_gradients",
    )(
        d_out, hidden_mid, hidden, x, d_y, turn, d_mixer, act, act, d_gu, gated, weights, attn, gpre, gain_out, resp,
        weights, weights, gains, d_ffn, proj, taps, taps, taps, logits, par, cols, back, segr, state_in, maps, *saved,
    )


def unpack_kernel(
    sum_ref, small_ref, dx_ref, query_ref, key_ref, value_ref, gate_ref, logit_ref, out_ref, wg_ref, wu_ref, wd_ref,
    taps_ref, mix_ref, ffn_ref, norm_ref, par_ref, dx_out, *, blocks
):
    dx_out[...] = dx_ref[...]
    for h in range(H):
        part = small_ref[8 * h : 8 * h + CONV, :]
        taps_ref[:, h * DK : (h + 1) * DK] = part[:, :DK]
        taps_ref[:, (H + h) * DK : (H + h + 1) * DK] = part[:, DK : 2 * DK]
        taps_ref[:, 2 * H * DK + h * DV : 2 * H * DK + (h + 1) * DV] = part[:, 2 * DK :]
    for row, ref in enumerate((mix_ref, ffn_ref)):
        for n in range(2):
            at = 8 * H + 8 * n + row
            ref[:, n * small_ref.shape[1] : (n + 1) * small_ref.shape[1]] = small_ref[at : at + 1, :]
    norm_ref[...] = small_ref[8 * H + 16 : 8 * H + 17, :DV]
    par_ref[...] = small_ref[8 * H + 16 : 8 * H + 24, DV : DV + LANES]

    def part(n, low=0, high=BLOCK):
        rows = []
        for spot in range(SPOTS):
            first, other = (spot % 2, spot // 2) if n % 2 == 0 else (spot // 2, spot % 2)
            rows.append(sum_ref[n, first, other, :, low:high])
        return jnp.concatenate(rows, axis=0).astype(F32)

    for h, n in enumerate(blocks.head_at):
        query_ref[:, h * DK : (h + 1) * DK] = part(n, 0, DK)
        key_ref[:, h * DK : (h + 1) * DK] = part(n, DK, 2 * DK)
        value_ref[:, h * DV : (h + 1) * DV] = part(n, 2 * DK, HC)
    for i, n in enumerate(blocks.gate_at):
        gate_ref[:, i * BLOCK : (i + 1) * BLOCK] = part(n)
    for i, n in enumerate(blocks.out_at):
        out_ref[i * BLOCK : (i + 1) * BLOCK, :] = jnp.transpose(part(n))
    middle = BLOCK // 2
    for i, n in enumerate(blocks.up_at):
        wg_ref[:, i * middle : (i + 1) * middle] = part(n, 0, middle)
        wu_ref[:, i * middle : (i + 1) * middle] = part(n, middle, BLOCK)
    for i, n in enumerate(blocks.down_at):
        wd_ref[i * BLOCK : (i + 1) * BLOCK, :] = jnp.transpose(part(n))
    last, tail = blocks.count - 1, blocks.tail
    wd_ref[blocks.downs * BLOCK :, :] = jnp.transpose(part(last, 0, tail))
    logit_ref[...] = jnp.transpose(part(last, tail, tail + LANES))[: 2 * H]


def unpack_gradients(blocks, sums, small, d_inputs):
    rows = SPOTS * sums.shape[3]
    inner = blocks.downs * BLOCK + blocks.tail
    width = d_inputs.shape[1]
    shapes = [
        (rows, H * DK), (rows, H * DK), (rows, H * DV), (rows, H * DV), (2 * H, rows), (H * DV, rows),
        (rows, inner), (rows, inner), (inner, rows), (CONV, H * HC), (1, width), (1, width), (1, DV), (8, LANES),
        d_inputs.shape,
    ]
    return pl.pallas_call(
        functools.partial(unpack_kernel, blocks=blocks),
        out_shape=[jax.ShapeDtypeStruct(shape, F32) for shape in shapes],
        compiler_params=params(),
        cost_estimate=cost(0, 6 * sums.size),
        name="unpack_gradients",
    )(sums, small, d_inputs)


def input_grad_kernel(
    dp_ref, dg_ref, dl_ref, w_ref, wl_ref, x_ref, gain_ref, dy_ref, out_ref, dgain_ref, acc_ref
):
    step = pl.program_id(0)

    @pl.when(step == 0)
    def _():
        acc_ref[...] = mm(dl_ref[...], wl_ref[...], NT)

    @pl.when(step < H)
    def _():
        acc_ref[...] += mm(dp_ref[...], w_ref[...], NT)

    @pl.when(step >= H)
    def _():
        acc_ref[...] += mm(dg_ref[...], w_ref[...], NT)

    @pl.when(step == pl.num_programs(0) - 1)
    def _():
        value = x_ref[...].astype(F32)
        size = lax.rsqrt(jnp.mean(value * value, axis=-1, keepdims=True) + 1e-06)
        unit = value * size
        d_hidden = acc_ref[...]
        dgain_ref[...] = jnp.zeros_like(dgain_ref)
        dgain_ref[0:1, :] = jnp.sum(d_hidden * unit, axis=0, keepdims=True)
        d_unit = d_hidden * gain_ref[...]
        out_ref[...] = dy_ref[...] + size * (
            d_unit - unit * jnp.mean(d_unit * unit, axis=-1, keepdims=True)
        )


def input_grad(d_proj, d_gpre, d_logit, weights, x, gain, d_y):
    tokens, width = x.shape
    block = HC
    second = d_gpre.shape[1] // block
    steps = H + second
    whole = lambda shape: pl.BlockSpec(shape, lambda j: (0,) * len(shape))
    late = lambda j: (0, jnp.maximum(j - H, 0))
    weight = lambda j: (0, jnp.where(j < H, H - 1 - j, j - H + AT_GATE // block))
    in_specs = [
        pl.BlockSpec((tokens, block), lambda j: (0, jnp.minimum(j, H - 1))),
        pl.BlockSpec((tokens, block), late),
        whole((tokens, LANES)),
        pl.BlockSpec((width, block), weight),
        pl.BlockSpec((width, LANES), lambda j: (0, AT_LOGIT // LANES)),
        whole((tokens, width)),
        whole((1, width)),
        whole((tokens, width)),
    ]
    return pl.pallas_call(
        input_grad_kernel,
        grid=(steps,),
        in_specs=in_specs,
        out_specs=[whole((tokens, width)), whole((8, width))],
        out_shape=[
            jax.ShapeDtypeStruct((tokens, width), F32),
            jax.ShapeDtypeStruct((8, width), F32),
        ],
        scratch_shapes=[pltpu.VMEM((tokens, width), F32)],
        compiler_params=params(),
        cost_estimate=cost(2 * tokens * width * steps * block, 3e7),
        name="input_grad",
    )(d_proj, d_gpre, d_logit, weights, weights, x, gain, d_y)


def shifted(block, axis, distance):
    devices = range(lax.axis_size(axis))
    route = [(i - distance, i) for i in devices if i - distance in devices]
    return lax.ppermute(block, axis, route)


def plain_sum(left, right, skip_left=0):
    part = lax.psum_scatter(outer(left, right, skip_left), "dp", scatter_dimension=0, tiled=True)
    return lax.psum(part, "seq").astype(F32)


def by_heads(query, key, value):
    lead = query.shape[:-1]
    parts = [query.reshape(lead + (H, DK)), key.reshape(lead + (H, DK)), value.reshape(lead + (H, DV))]
    return jnp.concatenate(parts, axis=-1).reshape(lead + (H * HC,))


def from_heads(value, heads=H):
    lead = value.shape[:-1]
    parts = value.reshape(lead + (heads, HC))
    return (
        parts[..., :DK].reshape(lead + (heads * DK,)),
        parts[..., DK : 2 * DK].reshape(lead + (heads * DK,)),
        parts[..., 2 * DK :].reshape(lead + (heads * DV,)),
    )


def token_rows(segments, place, tokens):
    ext = jnp.pad(segments, (HALO, LANES), constant_values=-1)
    ext = lax.dynamic_slice_in_dim(ext, place * tokens, tokens + LANES)
    seg = ext[HALO : HALO + tokens]
    blocks = seg.reshape(-1, CHUNK)
    before = ext[HALO - 1 : HALO - 1 + tokens : CHUNK]
    near = [seg] + [ext[HALO - j : HALO - j + tokens] == seg for j in range(1, CONV)]
    near += [(blocks == before[:, None]).reshape(-1), (blocks == blocks[:, -1:]).reshape(-1)]
    near = jnp.stack([row.astype(F32) for row in near])
    later = jnp.stack([(jnp.roll(ext, -j) == ext).astype(F32) for j in range(CONV)])
    return jnp.pad(near, ((0, 8 - near.shape[0]), (0, 0))), jnp.pad(later, ((0, 8 - CONV), (0, 0)))


def wide(value):
    return jnp.pad(value, ((0, 0), (0, LANES - value.shape[1])))


def local(
    inputs, segments, cotangent, norm_gain_mix, w_query, w_key, w_value, w_outgate, w_gates,
    conv_weight, decay_log, dt_bias, out_norm_gain, w_out, norm_gain_ffn, w_ffn_gate, w_ffn_up, w_ffn_down,
):
    tokens, width = inputs.shape[1:]
    place = lax.axis_index("seq")
    planned = (lax.axis_size("dp"), lax.axis_size("seq")) == (PLANES * CORES, SPOTS)
    low = lambda a: a.astype(BF16)
    inner = w_ffn_gate.shape[1]
    gain_out = out_norm_gain[None]

    if planned:
        taps = conv_weight
        shards = (w_query, w_key, w_value, w_outgate, w_gates.T, w_out, w_ffn_gate, w_ffn_up, w_ffn_down)
        outs = mixer_forward(
            inputs[0], cotangent[0], shards, (norm_gain_mix[None], norm_gain_ffn[None]), gain_out,
            decay_log[None], dt_bias[None], segments, conv_weight,
        )
        weights, hidden, x, d_out, turn, y1, hidden_mid, gains, segr, par, cols, back, *outs = outs
        proj, logits, resp, *outs = outs
        saved, (maps, state_in, attn, gpre, gated) = outs[:6], outs[6:]
        gain_row = 1
    else:
        taps = by_heads(conv_weight[:, : H * DK], conv_weight[:, H * DK : 2 * H * DK], conv_weight[:, 2 * H * DK :])
        taps = jnp.pad(taps, ((0, 8 - CONV), (0, 0)))
        par = jnp.pad(jnp.stack([decay_log, dt_bias]), ((0, 6), (0, LANES - H)))
        segr, later = token_rows(segments[0], place, tokens)
        turn = jnp.eye(width, dtype=BF16)
        qkv = by_heads(low(w_query), low(w_key), low(w_value))
        qkv = jnp.concatenate([qkv[:, h * HC : (h + 1) * HC] for h in reversed(range(H))], axis=1)
        gates = jnp.pad(low(w_gates), ((0, 0), (0, AT_GATE - AT_LOGIT - 2 * H)))
        shard = [qkv, gates, low(w_outgate), low(w_out).T, low(w_ffn_gate), low(w_ffn_up), low(w_ffn_down).T]
        weights = lax.all_gather(jnp.concatenate(shard, axis=1), "dp", axis=0, tiled=True)
        gain_mix, gain_ffn = norm_gain_mix[None], norm_gain_ffn[None]
        gains, gain_row = gain_ffn, 0
        cols = jnp.pad(segr.T, ((0, 0), (0, LANES - segr.shape[0])))
        back = jnp.pad(later.T[: tokens + HALO], ((0, 0), (0, LANES - later.shape[0])))
        x, d_out = inputs[0], cotangent[0]
        value = jnp.concatenate([shifted(x[tokens - HALO :], "seq", 1), x], axis=0).astype(F32)
        size = lax.rsqrt(jnp.mean(value * value, axis=-1, keepdims=True) + 1e-06)
        hidden = low(value * size * gain_mix)
        proj, logits, part, resp, exch, *saved = delta_forward(hidden, weights, taps, par, cols, segr)
        exch = lax.all_gather(exch[0], "seq")
        slots = jnp.arange(exch.shape[0], dtype=jnp.int32)
        place_arr = place.reshape((1,)).astype(jnp.int32)
        gpre = outgate(hidden, weights)
        state_in, attn, gated, y1, hidden_mid = mixer_out(
            place_arr, slots, part, resp, exch, gpre, gain_out, weights, x, gain_ffn
        )
    result, act, d_gu, d_y, d_mixer, d_gain_ffn = feed_forward(
        hidden_mid, d_out, y1, gains, gain_row, turn, weights, inner
    )
    if planned:
        blocks, (sums, d_inputs, small) = reduce_gradients(
            d_out, hidden_mid, hidden, x, d_y, turn, d_mixer, act, d_gu, gated, weights, attn, gpre, gain_out, resp,
            gains, d_gain_ffn, proj, taps, logits, par, cols, back, segr, state_in, maps, saved,
        )
        (
            g_query, g_key, g_value, g_og, g_gates, g_out, g_gate, g_up, g_down,
            d_conv, d_gain_mix, d_gain_ffn, d_gain_out, d_par, d_inputs,
        ) = unpack_gradients(blocks, sums, small, d_inputs)
        g_gates = g_gates.T
        d_gain_mix, d_gain_ffn, d_gain_out = d_gain_mix[0], d_gain_ffn[0], d_gain_out[0]
        d_decay_log, d_dt_bias = d_par[0, :H], d_par[1, :H]
    else:
        d_attn, d_gpre, local_grad, d_gain_out = mixer_back(d_mixer, weights, attn, gpre, gain_out, resp)
        grads = lax.all_gather(local_grad, "seq")
        d_proj, d_logits, d_taps, d_par = delta_backward(
            place_arr, slots, proj, taps, logits, par, cols, back, segr, d_attn, state_in, exch, grads, saved
        )
        sent_back = shifted(d_proj[:HALO], "seq", -1)
        d_proj = d_proj.at[tokens:].add(sent_back)[HALO:]
        d_logit = low(d_logits)
        g_down = plain_sum(d_out, act).T
        g_gate = plain_sum(hidden_mid, d_gu[0])
        g_up = plain_sum(hidden_mid, d_gu[1])
        g_out = plain_sum(d_mixer, gated).T
        g_og = plain_sum(hidden, d_gpre, HALO)
        g_query, g_key, g_value = from_heads(plain_sum(hidden, d_proj, HALO))
        g_gates = plain_sum(hidden, d_logit, HALO)
        d_inputs, d_gain_mix = input_grad(d_proj, d_gpre, d_logit, weights, x, gain_mix, d_y)
        d_conv = jnp.concatenate(from_heads(d_taps[:CONV]), axis=1)
        d_gain_mix, d_conv, d_decay_log, d_dt_bias, d_gain_out, d_gain_ffn = lax.psum(
            (d_gain_mix[0], d_conv, d_par[0, :H], d_par[1, :H], d_gain_out[0], d_gain_ffn[0]), ("dp", "seq")
        )
    return (
        result[None], d_inputs[None], d_gain_mix, g_query, g_key, g_value, g_og,
        g_gates[:, : 2 * H], d_conv, d_decay_log, d_dt_bias, d_gain_out, g_out,
        d_gain_ffn, g_gate, g_up, g_down,
    )


def solution(mesh):
    rows, cols, copied = P("dp", None), P(None, "dp"), P()
    tokens = P("dp", "seq", None)
    in_specs = (
        tokens, rows, tokens, copied, rows, rows, rows, rows, rows,
        copied, copied, copied, copied, cols, copied, rows, rows, cols,
    )
    out_specs = (
        tokens, tokens, copied, rows, rows, rows, rows, rows,
        copied, copied, copied, copied, cols, copied, rows, rows, cols,
    )
    return jax.shard_map(local, mesh=mesh, in_specs=in_specs, out_specs=out_specs, check_vma=False)
```

```python
import functools

import jax
import jax.numpy as jnp
from jax import lax
from jax.experimental import pallas as pl
from jax.experimental.pallas import tpu as pltpu
from jax.sharding import PartitionSpec as P

H = 8
DK = 128
DV = 256
CONV = 4
HALO = 16
CHUNK = 128
HC = 2 * DK + DV
LANES = 128
PLANES, CORES, SPOTS = 4, 2, 4

AT_LOGIT = H * HC
AT_GATE = AT_LOGIT + 512
AT_OUT = AT_GATE + H * DV
AT_FFN = AT_OUT + H * DV
VMEM_LIMIT = 62 * 2**20

F32 = jnp.float32
BF16 = jnp.bfloat16
NN = ((1,), (0,))
NT = ((1,), (1,))
TN = ((0,), (0,))


def mm(left, right, dims=NN):
    return lax.dot_general(
        left.astype(BF16), right.astype(BF16), (dims, ((), ())), preferred_element_type=F32
    )


def mm_exact(left, right, dims=NN):
    return lax.dot_general(
        left, right, (dims, ((), ())), precision=lax.Precision.HIGHEST, preferred_element_type=F32
    )


def halves(value):
    high = value.astype(BF16)
    return high, (value - high.astype(F32)).astype(BF16)


def mm_three(left, right):
    left_high, left_low = halves(left)
    right_high, right_low = halves(right)
    return mm(left_high, right_high) + (mm(left_high, right_low) + mm(left_low, right_high))


def params(**more):
    return pltpu.CompilerParams(vmem_limit_bytes=VMEM_LIMIT, **more)


def cost(flops, nbytes):
    return pl.CostEstimate(flops=int(flops), bytes_accessed=int(nbytes), transcendentals=0)


def iota2(shape, axis):
    return lax.broadcasted_iota(jnp.int32, shape, axis)


def lane(value, index):
    picked = jnp.where(iota2(value.shape, 1) == index, value, 0.0)
    return jnp.sum(picked, axis=1, keepdims=True)


def to_row(column):
    size = column.shape[0]
    same = iota2((size, size), 0) == iota2((size, size), 1)
    return jnp.sum(jnp.where(same, column, 0.0), axis=0, keepdims=True)


def to_column(row):
    size = row.shape[1]
    same = iota2((size, size), 0) == iota2((size, size), 1)
    return jnp.sum(jnp.where(same, row, 0.0), axis=1, keepdims=True)


def outgate_kernel(h_ref, w_ref, g_ref):
    g_ref[...] = mm(h_ref[HALO:, :], w_ref[...])


def outgate(hidden, weights):
    rows, width = hidden.shape
    cols = H * DV
    block = 512
    return pl.pallas_call(
        outgate_kernel,
        grid=(cols // block,),
        in_specs=[
            pl.BlockSpec((rows, width), lambda j: (0, 0)),
            pl.BlockSpec((width, block), lambda j: (0, j + AT_GATE // block)),
        ],
        out_specs=pl.BlockSpec((rows - HALO, block), lambda j: (0, j)),
        out_shape=jax.ShapeDtypeStruct((rows - HALO, cols), F32),
        compiler_params=params(),
        cost_estimate=cost(2 * rows * width * cols, 2 * width * cols + 4 * rows * cols),
        name="outgate",
    )(hidden, weights)


def outer_kernel(left_ref, right_ref, out_ref, turn_ref, *, skip):
    @pl.when(pl.program_id(0) == 0)
    def _():
        turn_ref[...] = jnp.transpose(left_ref[skip:, :])

    out_ref[...] = mm(turn_ref[...], right_ref[...]).astype(BF16)


def outer(left, right, skip):
    rows, width = left.shape
    cols = right.shape[1]
    block = next(b for b in (512, 256, 128) if cols % b == 0)
    return pl.pallas_call(
        functools.partial(outer_kernel, skip=skip),
        grid=(cols // block,),
        in_specs=[
            pl.BlockSpec((rows, width), lambda j: (0, 0)),
            pl.BlockSpec((rows - skip, block), lambda j: (0, j)),
        ],
        out_specs=pl.BlockSpec((width, block), lambda j: (0, j)),
        out_shape=jax.ShapeDtypeStruct((width, cols), BF16),
        scratch_shapes=[pltpu.VMEM((width, rows - skip), BF16)],
        compiler_params=params(),
        cost_estimate=cost(2 * rows * width * cols, 2 * width * cols + 2 * rows * cols),
        name="outer",
    )(left, right)


def gate_tables(logit_ref, par_ref, beta_ref, decay_ref, cum_ref):
    logits = logit_ref[HALO:, :]
    beta_ref[...] = jax.nn.sigmoid(logits)
    shifted = logits + par_ref[1:2, :]
    soft = jnp.maximum(shifted, 0.0) + jnp.log1p(jnp.exp(-jnp.abs(shifted)))
    decay_ref[...] = -jnp.exp(par_ref[0:1, :]) * soft
    lower = (iota2((CHUNK, CHUNK), 0) >= iota2((CHUNK, CHUNK), 1)).astype(F32)
    for c in range(logits.shape[0] // CHUNK):
        part = decay_ref[c * CHUNK : (c + 1) * CHUNK, :]
        cum_ref[c * CHUNK : (c + 1) * CHUNK, :] = mm_exact(lower, part)


def join_taps(taps_ref, query_ref, key_ref, value_ref):
    taps_ref[0:CONV, :DK] = query_ref[...]
    taps_ref[0:CONV, DK : 2 * DK] = key_ref[...]
    taps_ref[0:CONV, 2 * DK :] = value_ref[...]


def taps_specs(at):
    return [
        pl.BlockSpec((CONV, DK), lambda s: (0, at(s))),
        pl.BlockSpec((CONV, DK), lambda s: (0, H + at(s))),
        pl.BlockSpec((CONV, DV), lambda s: (0, 2 * H * DK // DV + at(s))),
    ]


def mix_taps(p_ref, taps_ref, cols, pf_ref):
    tokens = cols.shape[0]
    pf_ref[...] = p_ref[...].astype(F32)
    total = pf_ref[HALO:, :] * taps_ref[0:1, :]
    for j in range(1, CONV):
        total += pf_ref[HALO - j : HALO - j + tokens, :] * taps_ref[j : j + 1, :] * cols[:, j : j + 1]
    return total


def chunk_tables(c, head, cols, segr_ref, cum_ref):
    rows = slice(c * CHUNK, (c + 1) * CHUNK)
    cum = lane(cum_ref[rows, :], head)
    cum_row = to_row(cum)
    same = cols[rows, 0:1] == segr_ref[0:1, rows]
    row_ids, col_ids = iota2((CHUNK, CHUNK), 0), iota2((CHUNK, CHUNK), 1)
    gamma = jnp.where((row_ids >= col_ids) & same, jnp.exp(jnp.minimum(cum - cum_row, 0.0)), 0.0)
    strict = jnp.where(row_ids > col_ids, gamma, 0.0)
    carry = jnp.exp(cum) * cols[rows, 4:5]
    last = jnp.exp(cum[CHUNK - 1 :, :] - cum) * cols[rows, 5:6]
    return gamma, strict, carry, last


def unit_lower_inverses(systems):
    size = systems[0].shape[0]
    row_ids, col_ids = iota2((size, size), 0), iota2((size, size), 1)
    eye = (row_ids == col_ids).astype(F32)
    found = [eye - jnp.where(row_ids // 2 == col_ids // 2, low, 0.0) for low in systems]
    width = 2
    while width < size:
        joined = (row_ids // (2 * width) == col_ids // (2 * width)) & (
            row_ids // width != col_ids // width
        )
        first = [mm_three(jnp.where(joined, low, 0.0), inv) for low, inv in zip(systems, found)]
        found = [inv - mm_three(inv, part) for inv, part in zip(found, first)]
        width *= 2
    return found


def flip_spot(value, bits):
    low, high = lax.rem(value, 2), value // 2
    flip = lambda one, other: one + other - 2 * one * other
    return flip(low, bits % 2) + 2 * flip(high, bits // 2)


def device(planes=0, core=0, spot=0):
    place, here = lax.axis_index("dp"), lax.axis_index("seq")
    z = lax.rem(place // CORES + planes, PLANES)
    return {"dp": z * CORES + flip_spot(lax.rem(place, CORES), core), "seq": flip_spot(here, spot)}


def greet(partners):
    barrier = pltpu.get_barrier_semaphore()
    for partner in partners:
        pl.semaphore_signal(barrier, inc=1, device_id=device(**partner), device_id_type=pl.DeviceIdType.MESH)
    pl.semaphore_wait(barrier, len(partners))


def gather_spans(inner):
    spans = [((H - 1) * HC, HC + LANES), ((H - 2) * HC, HC)]
    spans += [(h * HC, 2 * HC) for h in (4, 2, 0)]
    for at, size in ((AT_GATE, H * DV), (AT_OUT, H * DV)) + tuple((AT_FFN + i * inner, inner) for i in range(3)):
        spans += [(at + low, min(1024, size - low)) for low in range(0, size, 1024)]
    return spans


TICKS = (((), (6,)), ((7,), (8,)), ((9,), (10,)), ((11,), (12,)), ((13,), ()), ((14,), ()), ((15,), ()), ((16,), (17,)), (18,), (19,), (20,), (21,), (22,), (23,), (24,), (25,))


class Gathering:
    HALVED = (0, 3, 5, 8, 10, 13, 15)
    STAGES = (0, 1, 2, 3, 5, 7, 8)
    FIRST = ((0, 1, 2, 3, 4, 4, 5), (0, 1, 2, 3, 4, 5, 6), (0, 1, 2, 3, 5, 6, 7))

    def __init__(self, spans, shard_ref, full_ref, sems, pack):
        self.spans, self.shard, self.full, self.pack = spans, shard_ref, full_ref, pack
        self.send_sem, self.recv_sem, self.local_sem = sems
        self.piece = shard_ref.shape[0] // SPOTS
        self.half = full_ref.shape[0] // CORES
        self.z = lax.axis_index("dp") // CORES

    def quarter(self, spot, cols):
        row = flip_spot(lax.axis_index("seq"), spot) * self.piece
        return self.shard.at[pl.ds(pl.multiple_of(row, self.piece), self.piece), cols]

    def own(self, group):
        at, size = self.spans[group]
        cols = pl.ds(at, size)
        block = PLANES * self.piece
        return [
            pltpu.make_async_copy(
                self.quarter(q, cols),
                self.full.at[q * block : q * block + self.piece, cols],
                self.local_sem.at[group, q],
            )
            for q in range(SPOTS)
        ]

    def axis(self, group):
        return 1 + self.HALVED.index(group) % 2 if group in self.HALVED else 0

    def parts(self, group):
        return (0, 3 - self.axis(group)) if self.axis(group) else (0,)

    def copy(self, group, kind, part=0):
        at, size = self.spans[group]
        cols = pl.ds(at, size)
        piece, full = self.piece, self.full
        block = PLANES * piece
        rows = lambda quarter: pl.ds(quarter * block + piece, block - piece)
        axis, sent = self.axis(group), kind
        if kind < 6:
            read, step, written = ((0, 1, 1), (0, -1, 3), (1, 1, 2), (3, -1, 2), (2, 1, 3), (2, -1, 1))[kind]
            quarter = self.parts(group)[part]
            slot = lambda n: full.at[quarter * block + n * piece : quarter * block + (n + 1) * piece, cols]
            source = self.quarter(quarter, cols) if read == 0 else slot(read)
            target = slot(written)
            to, arrival = device(planes=step % PLANES), written - 1 + 7 * part
            sent += 10 * part
        elif kind < 8 and axis:
            source = full.at[rows(self.parts(group)[kind - 6]), cols]
            target = full.at[rows((axis, 3)[kind - 6]), cols]
            to, arrival = device(spot=axis), kind - 3
        elif kind < 8:
            source = full.at[rows(0), cols]
            target = full.at[rows(kind - 5), cols]
            to, arrival = device(spot=kind - 5), kind - 3
        elif kind == 8:
            by = 1 + group % 2
            source = full.at[rows(by), cols]
            target = full.at[rows(3), cols]
            to, arrival = device(spot=3 - by), 5
        else:
            source = full.at[0 : self.half, cols]
            target = full.at[self.half : 2 * self.half, cols]
            to, arrival = device(core=1), 6
        return pltpu.make_async_remote_copy(
            src_ref=source,
            dst_ref=target,
            send_sem=self.send_sem.at[group, sent],
            recv_sem=self.recv_sem.at[group, arrival],
            device_id=to,
            device_id_type=pl.DeviceIdType.MESH,
        )

    def sends(self, kind):
        z = self.z
        return (z < 3, z > 0, (z > 0) & (z < 3), (z > 0) & (z < 3), z == 2, z == 1)[kind]

    def start(self, group, kind):
        @pl.when(self.sends(kind))
        def _():
            for part in range(len(self.parts(group))):
                self.copy(group, kind, part).start()

    def arrive(self, group, kind, condition=None):
        def wait():
            for part in range(len(self.parts(group))):
                self.copy(group, kind, part).wait_recv()

        wait() if condition is None else pl.when(condition)(wait)

    def tick(self, at):
        z = self.z
        due = []
        for group in range(len(self.spans)):
            stages = (self.FIRST + (self.STAGES,) * len(self.spans))[group]
            due += [(stage, group) for stage in range(len(stages)) if group + stages[stage] == at]
        for stage, group in sorted(due, reverse=True):
            by = 1 + group % 2
            if stage == 0:
                self.pack(*self.spans[group])
                self.start(group, 0)
                self.start(group, 1)
                for local in self.own(group):
                    local.start()
            elif stage == 1:
                self.arrive(group, 0, z > 0)
                self.start(group, 2)
                self.arrive(group, 1, z < 3)
                self.start(group, 3)
            elif stage == 2:
                self.arrive(group, 2)
                self.start(group, 4)
                self.start(group, 5)
            elif stage == 3:
                self.arrive(group, 0, z == 0)
                self.arrive(group, 1, z == 3)
                self.copy(group, 5 + by).start()
                self.copy(group, 8 - by).start()
            elif stage == 4:
                if not self.axis(group):
                    self.copy(group, 5 + by).wait_recv()
                    self.copy(group, 8).start()
            elif stage == 5:
                self.copy(group, 8 - by).wait_recv()
                self.copy(group, 5 + by if self.axis(group) else 8).wait_recv()
                for local in self.own(group):
                    local.wait()
                self.copy(group, 9).start()
            else:
                self.copy(group, 9).wait_recv()

    def finish(self):
        for group in range(len(self.spans)):
            for kind in range(6):

                @pl.when(self.sends(kind))
                def _(group=group, kind=kind):
                    for part in range(len(self.parts(group))):
                        self.copy(group, kind, part).wait_send()

            for kind in (6, 7, 9) if self.axis(group) else (6, 7, 8, 9):
                self.copy(group, kind).wait_send()


def forward_kernel(
    h_ref, full_ref, taps_ref, par_ref, cols_ref, segr_ref,
    p_ref, logit_ref, part_ref, resp_ref, exch_ref, inv_ref, upd_ref, st_ref, stm_ref, amap_ref, rmap_ref,
    beta_ref, decay_ref, cum_ref, pf_ref, mix_ref, w_ref, wl_ref, load_sem,
):
    head = pl.program_id(0)
    load_head(head, h_ref, full_ref, par_ref, p_ref, logit_ref, beta_ref, decay_ref, cum_ref, w_ref, wl_ref, load_sem)
    state = forward_head(
        head, p_ref, taps_ref, cols_ref, segr_ref, part_ref, resp_ref, inv_ref, upd_ref, st_ref, stm_ref,
        amap_ref, rmap_ref, beta_ref, cum_ref, pf_ref, mix_ref, lambda: None,
    )
    exch_ref[0, 0] = state.astype(BF16)


def load_head(
    head, h_ref, full_ref, par_ref, p_ref, logit_ref, beta_ref, decay_ref, cum_ref, w_ref, wl_ref, load_sem
):
    def load(slot, at, size, to):
        return pltpu.make_async_copy(full_ref.at[:, pl.ds(at, size)], to, load_sem.at[slot])

    mine = load(0, pl.multiple_of((H - 1 - head) * HC, HC), HC, w_ref)
    mine.start()

    @pl.when(head == 0)
    def _():
        gates = load(1, AT_LOGIT, LANES, wl_ref)
        gates.start()
        gates.wait()
        logit_ref[...] = mm(h_ref[...], wl_ref[...])
        gate_tables(logit_ref, par_ref, beta_ref, decay_ref, cum_ref)

    mine.wait()
    p_ref[...] = mm(h_ref[...], w_ref[...]).astype(BF16)


def forward_head(
    head, p_ref, taps_ref, cols_ref, segr_ref, part_ref, resp_ref, inv_ref, upd_ref, st_ref, stm_ref,
    amap_ref, rmap_ref, beta_ref, cum_ref, pf_ref, mix_ref, between,
):
    cols = cols_ref[...]
    tokens = cols.shape[0]
    total = mix_taps(p_ref, taps_ref, cols, pf_ref)
    mix_ref[...] = total * jax.nn.sigmoid(total)
    between()
    beta = lane(beta_ref[...], head + H)
    chunks = range(tokens // CHUNK)
    tables, lows, keys, queries = [], [], [], []
    for c in chunks:
        rows = slice(c * CHUNK, (c + 1) * CHUNK)
        query = mix_ref[rows, :DK]
        query = query * (lax.rsqrt(jnp.sum(query * query, axis=1, keepdims=True) + 1e-06) * DK**-0.5)
        key = mix_ref[rows, DK : 2 * DK]
        key = key * lax.rsqrt(jnp.sum(key * key, axis=1, keepdims=True) + 1e-06)
        gamma, strict, carry, last = chunk_tables(c, head, cols, segr_ref, cum_ref)
        dots = mm(jnp.concatenate([key, query], axis=0), key, NT)
        lows.append(beta[rows] * strict * dots[:CHUNK])
        tables.append((gamma * dots[CHUNK:], carry, last))
        keys.append(key)
        queries.append(query)
    inverses = unit_lower_inverses(lows)
    state = None
    for c in chunks:
        rows = slice(c * CHUNK, (c + 1) * CHUNK)
        scores, carry, last = tables[c]
        key, query = keys[c], queries[c]
        target = jnp.concatenate([mix_ref[rows, 2 * DK :], carry * key], axis=1) * beta[rows]
        updates = mm(inverses[c], target)
        inv_ref[0, c] = inverses[c].astype(BF16)
        upd_ref[0, rows, :] = updates
        weighted_t = jnp.transpose(last * key)
        both = mm(jnp.concatenate([weighted_t, scores], axis=0), updates)
        eye = (iota2((DK, DK), 0) == iota2((DK, DK), 1)).astype(F32)
        step_map = carry[CHUNK - 1 :, :] * eye - both[:DK, DV:]
        read_map = carry * query - both[DK:, DV:]
        amap_ref[0, c] = step_map.astype(BF16)
        rmap_ref[0, c] = read_map.astype(BF16)
        if c == 0:
            st_ref[0, c] = jnp.zeros((DK, DV), F32)
            stm_ref[0, c] = eye.astype(BF16)
            part_ref[rows, :] = both[DK:, :DV]
            resp_ref[rows, :] = read_map.astype(BF16)
            state = jnp.concatenate([both[:DK, :DV], step_map], axis=1)
        else:
            st_ref[0, c] = state[:, :DV]
            stm_ref[0, c] = state[:, DV:].astype(BF16)
            moved = mm(jnp.concatenate([step_map, read_map], axis=0), state)
            part_ref[rows, :] = both[DK:, :DV] + moved[DK:, :DV]
            resp_ref[rows, :] = moved[DK:, DV:].astype(BF16)
            state = moved[:DK] + jnp.concatenate(
                [both[:DK, :DV], jnp.zeros((DK, DK), F32)], axis=1
            )
    return state


def delta_forward(hidden, weights, taps, par, cols, segr):
    rows, width = hidden.shape
    tokens = rows - HALO
    chunks = tokens // CHUNK
    whole = lambda shape: pl.BlockSpec(shape, lambda h: (0,) * len(shape))
    by_head = lambda shape: pl.BlockSpec(shape, lambda h: (h,) + (0,) * (len(shape) - 1))
    return pl.pallas_call(
        forward_kernel,
        grid=(H,),
        in_specs=[
            whole((rows, width)),
            pl.BlockSpec(memory_space=pl.ANY),
            pl.BlockSpec((8, HC), lambda h: (0, h)),
            whole((8, LANES)),
            whole((tokens, LANES)),
            whole(segr.shape),
        ],
        out_specs=[
            pl.BlockSpec((rows, HC), lambda h: (0, h)),
            whole((rows, LANES)),
            pl.BlockSpec((tokens, DV), lambda h: (0, h)),
            pl.BlockSpec((tokens, DK), lambda h: (0, h)),
            pl.BlockSpec((1, 1, DK, DV + DK), lambda h: (0, h, 0, 0)),
            by_head((1, chunks, CHUNK, CHUNK)),
            by_head((1, tokens, DV + DK)),
            by_head((1, chunks, DK, DV)),
            by_head((1, chunks, DK, DK)),
            by_head((1, chunks, DK, DK)),
            by_head((1, chunks, CHUNK, DK)),
        ],
        out_shape=[
            jax.ShapeDtypeStruct((rows, H * HC), BF16),
            jax.ShapeDtypeStruct((rows, LANES), F32),
            jax.ShapeDtypeStruct((tokens, H * DV), F32),
            jax.ShapeDtypeStruct((tokens, H * DK), BF16),
            jax.ShapeDtypeStruct((1, H, DK, DV + DK), BF16),
        ]
        + saved_shapes(chunks),
        scratch_shapes=[
            pltpu.VMEM((tokens, LANES), F32),
            pltpu.VMEM((tokens, LANES), F32),
            pltpu.VMEM((tokens, LANES), F32),
            pltpu.VMEM((rows, HC), F32),
            pltpu.VMEM((tokens, HC), F32),
            pltpu.VMEM((width, HC), BF16),
            pltpu.VMEM((width, LANES), BF16),
            pltpu.SemaphoreType.DMA((2,)),
        ],
        compiler_params=params(),
        cost_estimate=cost(6e9 * H, 5e6 * H),
        name="delta_forward",
    )(hidden, weights, taps, par, cols, segr)


def saved_shapes(chunks):
    return [
        jax.ShapeDtypeStruct((H, chunks, CHUNK, CHUNK), BF16),
        jax.ShapeDtypeStruct((H, chunks * CHUNK, DV + DK), F32),
        jax.ShapeDtypeStruct((H, chunks, DK, DV), F32),
        jax.ShapeDtypeStruct((H, chunks, DK, DK), BF16),
        jax.ShapeDtypeStruct((H, chunks, DK, DK), BF16),
        jax.ShapeDtypeStruct((H, chunks, CHUNK, DK), BF16),
    ]


def mixer_forward_kernel(
    x_ref, wq_ref, wk_ref, wv_ref, wl_in, gain_mix_ref, gain_ffn_ref, gain_ref, rate_ref, bias_ref, seg_ref,
    taps_q_ref, taps_k_ref, taps_v_ref, cot_any, wo_any, wm_any, wg_any, wu_any, wd_any,
    full_ref, hidden_out, x_out, cot_out, turn_out, y_out, mid_out,
    gains_out, near_ref, par_ref, cols_ref, back_ref, p_ref, logit_ref, resp_out,
    inv_ref, upd_ref, st_ref, stm_ref, amap_ref, rmap_ref, maps_ref, sin_ref, attn_ref, gpre_ref, gated_ref,
    shard_ref, hidden_ref, xs_ref, cots_ref, turn_ref, y_ref, mid_ref, xh_ref, part_ref, resp_ref, exch_ref, stage_ref, half_ref, low_ref,
    beta_ref, decay_ref, cum_ref, pf_ref, mix_ref, w_ref, wl_ref, wb_ref,
    cot_ref, wo_ref, wm_ref, wg_ref, wu_ref, wd_ref, taps_ref, row_ref, later_ref, late_sem,
    send_sem, recv_sem, local_sem, exch_send, exch_recv, load_sem, pair_sem, out_sem, halo_sem, *, spans, inner,
):
    step = pl.program_id(0)
    place = lax.axis_index("seq")
    tokens, width = x_ref.shape

    def late(which):
        source, to = (
            (wo_any, wo_ref), (wm_any, wm_ref), (wg_any, wg_ref), (wu_any, wu_ref), (wd_any, wd_ref), (cot_any, cot_ref),
        )[which]
        return pltpu.make_async_copy(source, to, late_sem.at[which])

    def pack(at, size):
        while size > 0:
            if at < AT_LOGIT:
                head, span = H - 1 - at // HC, HC
                shard_ref[:, at : at + DK] = wq_ref[:, head * DK : (head + 1) * DK].astype(BF16)
                shard_ref[:, at + DK : at + 2 * DK] = wk_ref[:, head * DK : (head + 1) * DK].astype(BF16)
                shard_ref[:, at + 2 * DK : at + HC] = wv_ref[:, head * DV : (head + 1) * DV].astype(BF16)
            elif at < AT_GATE:
                span = LANES
                rest = jnp.zeros((LANES - 2 * H, LANES), F32)
                turned = jnp.transpose(jnp.concatenate([wl_in[...], rest], axis=0))
                shard_ref[:, at : at + LANES] = turned.astype(BF16)
            elif at < AT_OUT:
                span, low = size, at - AT_GATE
                if low == 0:
                    late(0).wait()
                shard_ref[:, at : at + span] = wo_ref[:, low : low + span].astype(BF16)
            elif at < AT_FFN:
                span, low = size, at - AT_OUT
                if low == 0:
                    late(1).wait()
                shard_ref[:, at : at + span] = jnp.transpose(wm_ref[low : low + span, :]).astype(BF16)
            else:
                span, which, low = size, (at - AT_FFN) // inner, (at - AT_FFN) % inner
                if low == 0:
                    late(2 + which).wait()
                if which < 2:
                    shard_ref[:, at : at + span] = (wg_ref, wu_ref)[which][:, low : low + span].astype(BF16)
                else:
                    shard_ref[:, at : at + span] = jnp.transpose(wd_ref[low : low + span, :]).astype(BF16)
            at, size = at + span, size - span

    gathering = Gathering(spans, shard_ref, full_ref, (send_sem, recv_sem, local_sem), pack)
    lead = gathering.FIRST[0][-1] + 1
    final_tick = len(spans) + gathering.STAGES[-1]

    upper = place // 2 == 1
    second = lax.rem(place, 2) == 1

    def give(h):
        return pltpu.make_async_remote_copy(
            src_ref=stage_ref.at[h],
            dst_ref=exch_ref.at[h],
            send_sem=exch_send.at[0, h],
            recv_sem=exch_recv.at[0, h],
            device_id=device(spot=1),
            device_id_type=pl.DeviceIdType.MESH,
        )

    def give_half(h):
        return pltpu.make_async_remote_copy(
            src_ref=half_ref.at[h],
            dst_ref=low_ref.at[h],
            send_sem=exch_send.at[1, h],
            recv_sem=exch_recv.at[1, h],
            device_id=device(spot=2),
            device_id_type=pl.DeviceIdType.MESH,
        )

    def join(h):
        give(h).wait()

        @pl.when(jnp.logical_not(upper))
        def _():
            mine, theirs = stage_ref[h], exch_ref[h]
            later = jnp.where(second, mine, theirs)
            earlier = jnp.where(second, theirs, mine)
            half_ref[h] = (later[:, :DV].astype(F32) + mm(later[:, DV:], earlier[:, :DV])).astype(BF16)
            give_half(h).start()

    def give_halo():
        return pltpu.make_async_remote_copy(
            src_ref=x_ref.at[tokens - HALO : tokens],
            dst_ref=xh_ref,
            send_sem=halo_sem.at[0],
            recv_sem=halo_sem.at[1],
            device_id={"dp": lax.axis_index("dp"), "seq": lax.rem(place + 1, SPOTS)},
            device_id_type=pl.DeviceIdType.MESH,
        )

    def keep(which):
        source, to = (
            (hidden_ref, hidden_out), (xs_ref, x_out), (cots_ref, cot_out), (turn_ref, turn_out),
            (y_ref, y_out), (mid_ref, mid_out),
        )[which]
        return pltpu.make_async_copy(source, to, out_sem.at[which])

    def load_pair(h):
        slot = lax.rem(h, 2)
        return [
            pltpu.make_async_copy(
                full_ref.at[:, pl.ds(pl.multiple_of(at + h * DV, DV), DV)], wb_ref.at[slot, i], pair_sem.at[slot, i]
            )
            for i, at in enumerate((AT_GATE, AT_OUT))
        ]

    @pl.when(step == 0)
    def _():
        greet([dict(planes=d) for d in (1, 2, 3)] + [dict(spot=s) for s in (1, 2, 3)] + [dict(core=1)])

        @pl.when(place < SPOTS - 1)
        def _():
            give_halo().start()

        gathering.tick(0)
        for which in range(6):
            late(which).start()
        at = iota2((1, width), 1)
        piece = width // (PLANES * CORES * SPOTS)
        core, rest = at // (width // 2), at % (width // 2)
        quarter, plane, low = rest // (PLANES * piece), rest // piece % PLANES, rest % piece
        place_dp = lax.axis_index("dp")
        z, c = place_dp // CORES, lax.rem(place_dp, CORES)
        chip = ((z - plane + PLANES) % PLANES) * CORES + (c + core - 2 * c * core)
        order = (chip * SPOTS + flip_spot(quarter, place)) * piece + low
        turn_ref[...] = jnp.where(iota2((width, width), 0) == order, 1.0, 0.0).astype(BF16)
        keep(3).start()
        gathering.tick(1)
        gains = jnp.concatenate([gain_mix_ref[...], gain_ffn_ref[...], jnp.zeros((6, width), F32)], axis=0)
        high, mid = halves(gains)
        rest = (gains - high.astype(F32)) - mid.astype(F32)
        gains_out[...] = mm(high, turn_ref[...]) + mm(mid, turn_ref[...]) + mm(rest, turn_ref[...])
        par_ref[...] = jnp.zeros_like(par_ref)
        par_ref[0:1, :H] = rate_ref[...]
        par_ref[1:2, :H] = bias_ref[...]
        gathering.tick(2)

        row_ref[...] = jnp.full(row_ref.shape, -1.0, F32)
        row_ref[0:1, LANES : LANES + seg_ref.shape[1]] = seg_ref[...].astype(F32)
        row = row_ref[0:1, pl.ds(pl.multiple_of(place * tokens, LANES), tokens + 2 * LANES)]
        seg = row[:, LANES : LANES + tokens]
        near = [seg]
        for j in range(1, CONV):
            moved = pltpu.roll(row, j, 1)[:, LANES : LANES + tokens]
            near.append((moved == seg).astype(F32))
        before, last = [], []
        for n in range(tokens // CHUNK):
            part = seg[:, n * CHUNK : (n + 1) * CHUNK]
            before.append((part == row[:, LANES + n * CHUNK - 1 : LANES + n * CHUNK]).astype(F32))
            last.append((part == part[:, CHUNK - 1 :]).astype(F32))
        near += [jnp.concatenate(before, axis=1), jnp.concatenate(last, axis=1)]
        near.append(jnp.zeros((8 - len(near), tokens), F32))
        near_ref[...] = jnp.concatenate(near, axis=0)
        size = row.shape[1]
        ahead = pltpu.roll(row, size - (LANES - HALO), 1)
        later = [jnp.zeros((1, tokens + LANES), F32)]
        for j in range(1, CONV):
            later.append((pltpu.roll(ahead, size - j, 1) == ahead).astype(F32)[:, : tokens + LANES])
        later.append(jnp.zeros((8 - CONV, tokens + LANES), F32))
        later_ref[...] = jnp.concatenate(later, axis=0)
        blank = jnp.zeros((LANES - 8, LANES), F32)
        for n in range(tokens // LANES):
            span = slice(n * LANES, (n + 1) * LANES)
            cols_ref[span, :] = jnp.transpose(jnp.concatenate([near_ref[:, span], blank], axis=0))
        gathering.tick(3)

        @pl.when(place > 0)
        def _():
            give_halo().wait_recv()

        @pl.when(place == 0)
        def _():
            xh_ref[...] = jnp.zeros_like(xh_ref)

        value = mm(jnp.concatenate([xh_ref[...], x_ref[...]], axis=0), turn_ref[...])
        xs_ref[...] = value[HALO:].astype(BF16)
        keep(1).start()
        size = lax.rsqrt(jnp.mean(value * value, axis=-1, keepdims=True) + 1e-06)
        hidden_ref[...] = (value * size * gains_out[0:1, :]).astype(BF16)
        keep(0).start()
        for at in range(4, lead):
            gathering.tick(at)

    @pl.when((step >= 2) & (step < H + 2))
    def _():
        join(step - 2)

    @pl.when(step < H)
    def _():
        head = step
        for h in range(1, H):

            @pl.when(head == h)
            def _(h=h):
                for at in TICKS[h][0]:
                    gathering.tick(at)

        load_head(
            head, hidden_ref, full_ref, par_ref, p_ref, logit_ref, beta_ref, decay_ref, cum_ref, w_ref, wl_ref, load_sem
        )

        def between():
            for h in range(H):

                @pl.when(head == h)
                def _(h=h):
                    for at in TICKS[h][1]:
                        gathering.tick(at)

        join_taps(taps_ref, taps_q_ref, taps_k_ref, taps_v_ref)
        state = forward_head(
            head, p_ref, taps_ref, cols_ref, near_ref, part_ref.at[head], resp_ref.at[head], inv_ref, upd_ref,
            st_ref, stm_ref, amap_ref, rmap_ref, beta_ref, cum_ref, pf_ref, mix_ref, between,
        )
        resp_out[...] = resp_ref[head]
        stage_ref[head] = state.astype(BF16)
        give(head).start()

        @pl.when(head == H - 1)
        def _():
            for copy in load_pair(0):
                copy.start()

    @pl.when(step >= H)
    def _():
        head = step - H
        for h in range(H):

            @pl.when(head == h)
            def _(h=h):
                for at in TICKS[H + h]:
                    gathering.tick(at)

        @pl.when(head < H - 1)
        def _():
            for copy in load_pair(head + 1):
                copy.start()

        for copy in load_pair(head):
            copy.wait()
        @pl.when(upper)
        def _():
            give_half(head).wait_recv()

        @pl.when(jnp.logical_not(upper))
        def _():
            low_ref[head] = jnp.zeros((DK, DV), BF16)
            give_half(head).wait_send()

        slot = lax.rem(head, 2)
        gate = mm(hidden_ref[HALO:, :], wb_ref[slot, 0])
        gpre_ref[...] = gate
        theirs = exch_ref[head]
        maps_ref[0, 0] = stage_ref[head, :, DV:]
        maps_ref[1, 0] = theirs[:, DV:]
        state = low_ref[head].astype(F32)
        state = jnp.where(second, theirs[:, :DV].astype(F32) + mm(theirs[:, DV:], state), state)
        sin_ref[0] = state
        attn = part_ref[head] + mm(resp_ref[head], state)
        attn_ref[...] = attn
        scale = lax.rsqrt(jnp.mean(attn * attn, axis=-1, keepdims=True) + 1e-05)
        gated = (attn * scale * gain_ref[...] * (gate * jax.nn.sigmoid(gate))).astype(BF16)
        gated_ref[...] = gated

        @pl.when(head == 0)
        def _():
            y_ref[...] = xs_ref[...].astype(F32)
            late(5).wait()
            cots_ref[...] = mm(cot_ref[...], turn_ref[...]).astype(BF16)
            keep(2).start()
            blank = jnp.zeros((LANES - 8, LANES), F32)
            for n in range(tokens // LANES + 1):
                span = slice(n * LANES, (n + 1) * LANES)
                turned = jnp.transpose(jnp.concatenate([later_ref[:, span], blank], axis=0))
                kept = min(LANES, tokens + HALO - n * LANES)
                back_ref[n * LANES : n * LANES + kept, :] = turned[:kept]

        y_ref[...] += mm(gated, wb_ref[slot, 1], NT)

        @pl.when(head == H - 1)
        def _():
            keep(4).start()
            value = y_ref[...]
            size = lax.rsqrt(jnp.mean(value * value, axis=-1, keepdims=True) + 1e-06)
            mid_ref[...] = (value * size * gains_out[1:2, :]).astype(BF16)
            keep(5).start()
            gathering.finish()

            @pl.when(place < SPOTS - 1)
            def _():
                give_halo().wait_send()

            for which in range(6):
                keep(which).wait()


def mixer_forward(x, cotangent, shards, gains, gain, rate, bias, segments, taps):
    tokens, width = x.shape
    rows = tokens + HALO
    chunks = tokens // CHUNK
    query, key, value, outgate_w, gates, out_w, gate_w, up_w, down_w = shards
    inner = down_w.shape[0]
    spans = gather_spans(inner)
    total = AT_FFN + 3 * inner
    once = lambda array: pl.BlockSpec(
        array.shape, lambda s: (0,) * array.ndim, pipeline_mode=pl.Buffered(1)
    )
    whole = lambda shape: pl.BlockSpec(shape, lambda s: (0,) * len(shape))
    early = lambda s: jnp.minimum(s, H - 1)
    late = lambda s: jnp.maximum(s - H, 0)
    by_head = lambda shape, at: pl.BlockSpec(shape, lambda s: (at(s),) + (0,) * (len(shape) - 1))
    across = lambda shape, at: pl.BlockSpec(shape, lambda s: (0, at(s)))
    anywhere = pl.BlockSpec(memory_space=pl.ANY)
    shape = jax.ShapeDtypeStruct
    sem = pltpu.SemaphoreType.DMA
    saved = saved_shapes(chunks)
    return pl.pallas_call(
        functools.partial(mixer_forward_kernel, spans=spans, inner=inner),
        grid=(2 * H,),
        in_specs=[once(a) for a in (x, query, key, value, gates, *gains, gain, rate, bias, segments)]
        + taps_specs(early)
        + [anywhere] * 6,
        out_specs=[anywhere] * 7
        + [
            whole((8, width)),
            whole((8, tokens)),
            whole((8, LANES)),
            whole((tokens, LANES)),
            whole((rows, LANES)),
            across((rows, HC), early),
            whole((rows, LANES)),
            across((tokens, DK), early),
        ]
        + [by_head((1,) + one.shape[1:], early) for one in saved]
        + [
            pl.BlockSpec((2, 1, DK, DK), lambda s: (0, late(s), 0, 0)),
            by_head((1, DK, DV), late),
            across((tokens, DV), late),
            across((tokens, DV), late),
            across((tokens, DV), late),
        ],
        out_shape=[
            shape((width, total), BF16),
            shape((rows, width), BF16),
            shape((tokens, width), BF16),
            shape((tokens, width), BF16),
            shape((width, width), BF16),
            shape((tokens, width), F32),
            shape((tokens, width), BF16),
            shape((8, width), F32),
            shape((8, tokens), F32),
            shape((8, LANES), F32),
            shape((tokens, LANES), F32),
            shape((rows, LANES), F32),
            shape((rows, H * HC), BF16),
            shape((rows, LANES), F32),
            shape((tokens, H * DK), BF16),
        ]
        + saved
        + [
            shape((2, H, DK, DK), BF16),
            shape((H, DK, DV), F32),
            shape((tokens, H * DV), F32),
            shape((tokens, H * DV), F32),
            shape((tokens, H * DV), BF16),
        ],
        scratch_shapes=[
            pltpu.VMEM((query.shape[0], total), BF16),
            pltpu.VMEM((rows, width), BF16),
            pltpu.VMEM((tokens, width), BF16),
            pltpu.VMEM((tokens, width), BF16),
            pltpu.VMEM((width, width), BF16),
            pltpu.VMEM((tokens, width), F32),
            pltpu.VMEM((tokens, width), BF16),
            pltpu.VMEM((HALO, width), BF16),
            pltpu.VMEM((H, tokens, DV), F32),
            pltpu.VMEM((H, tokens, DK), BF16),
            pltpu.VMEM((H, DK, DV + DK), BF16),
            pltpu.VMEM((H, DK, DV + DK), BF16),
            pltpu.VMEM((H, DK, DV), BF16),
            pltpu.VMEM((H, DK, DV), BF16),
            pltpu.VMEM((tokens, LANES), F32),
            pltpu.VMEM((tokens, LANES), F32),
            pltpu.VMEM((tokens, LANES), F32),
            pltpu.VMEM((rows, HC), F32),
            pltpu.VMEM((tokens, HC), F32),
            pltpu.VMEM((width, HC), BF16),
            pltpu.VMEM((width, LANES), BF16),
            pltpu.VMEM((2, 2, width, DV), BF16),
            pltpu.VMEM(cotangent.shape, BF16),
            pltpu.VMEM(outgate_w.shape, F32),
            pltpu.VMEM(out_w.shape, F32),
            pltpu.VMEM(gate_w.shape, F32),
            pltpu.VMEM(up_w.shape, F32),
            pltpu.VMEM(down_w.shape, F32),
            pltpu.VMEM((8, HC), F32),
            pltpu.VMEM((8, segments.shape[1] + 2 * LANES), F32),
            pltpu.VMEM((8, tokens + LANES), F32),
            sem((6,)),
            sem((len(spans), 16)),
            sem((len(spans), 10)),
            sem((len(spans), SPOTS)),
            sem((2, H)),
            sem((2, H)),
            sem((2,)),
            sem((2, 2)),
            sem((6,)),
            sem((2,)),
        ],
        compiler_params=params(collective_id=0, has_side_effects=True),
        cost_estimate=cost(1e11, 1e8),
        name="mixer_forward",
    )(
        x, query, key, value, gates, *gains, gain, rate, bias, segments, taps, taps, taps,
        cotangent, outgate_w, out_w, gate_w, up_w, down_w,
    )


def backward_kernel(place_ref, slot_ref, *refs):
    exch_ref, grads_ref, refs = refs[9], refs[10], refs[:9] + refs[11:]

    def behind(source, grad):
        slot = slot_ref[source]
        return jnp.where(
            source > place_ref[0],
            grads_ref[slot, 0].astype(F32) + mm(exch_ref[slot, 0], grad, TN),
            grad,
        )

    places = exch_ref.shape[0]
    d_state = lax.fori_loop(
        0, places - 1, lambda lap, grad: behind(places - 1 - lap, grad), jnp.zeros((DK, DV), F32)
    )
    for phase in range(PHASES):
        backward_head(phase, pl.program_id(0), lambda: d_state, *refs)


PHASES = 3


def backward_head(
    phase, head, entering, p_ref, taps_ref, logit_ref, par_ref, cols_ref, back_ref, segr_ref,
    dattn_ref, sin_ref,
    inv_ref, upd_ref, st_ref, stm_ref, amap_ref, rmap_ref,
    dp_ref, dlogit_ref, dtaps_ref, dpar_ref,
    beta_ref, decay_ref, cum_ref, pf_ref, pre_ref, dmix_ref, dstate_ref, dbeta_ref, ddecay_ref,
):
    tokens = cols_ref.shape[0]
    chunks = range(tokens // CHUNK)
    refs = (
        cols_ref, segr_ref, dattn_ref, sin_ref, inv_ref, upd_ref, st_ref, stm_ref, beta_ref, cum_ref, pre_ref,
        dmix_ref, dstate_ref, dbeta_ref, ddecay_ref,
    )
    if phase == 0:

        @pl.when(head == 0)
        def _():
            gate_tables(logit_ref, par_ref, beta_ref, decay_ref, cum_ref)
            dlogit_ref[...] = jnp.zeros_like(dlogit_ref)
            dpar_ref[...] = jnp.zeros_like(dpar_ref)

        pre_ref[...] = mix_taps(p_ref, taps_ref, cols_ref[...], pf_ref)
        d_state = entering()
        for c in reversed(chunks):
            rows = slice(c * CHUNK, (c + 1) * CHUNK)
            dstate_ref[c] = d_state
            if c > 0:
                d_state = mm(amap_ref[0, c], d_state, TN) + mm(rmap_ref[0, c], dattn_ref[rows, :], TN)
        backward_chunks(head, chunks[:1], *refs)
    elif phase == 1:
        backward_chunks(head, chunks[1:3], *refs)
    else:
        backward_chunks(head, chunks[3:], *refs)
        backward_ends(
            head, taps_ref, logit_ref, par_ref, cols_ref, back_ref, dp_ref, dlogit_ref, dtaps_ref, dpar_ref,
            beta_ref, decay_ref, pf_ref, dmix_ref, dbeta_ref, ddecay_ref,
        )


def backward_chunks(
    head, chunks, cols_ref, segr_ref, dattn_ref, sin_ref, inv_ref, upd_ref, st_ref, stm_ref, beta_ref, cum_ref, pre_ref,
    dmix_ref, dstate_ref, dbeta_ref, ddecay_ref,
):
    cols = cols_ref[...]
    beta = lane(beta_ref[...], head + H)
    state_in = sin_ref[0]
    row_ids, col_ids = iota2((CHUNK, CHUNK), 0), iota2((CHUNK, CHUNK), 1)
    for c in chunks:
        rows = slice(c * CHUNK, (c + 1) * CHUNK)
        mixed = pre_ref[rows, :]
        gate = jax.nn.sigmoid(mixed)
        slope = gate * (1.0 + mixed * (1.0 - gate))
        mixed = mixed * gate
        query_raw, key_raw, value = mixed[:, :DK], mixed[:, DK : 2 * DK], mixed[:, 2 * DK :]
        query_size = lax.rsqrt(jnp.sum(query_raw * query_raw, axis=1, keepdims=True) + 1e-06)
        key_size = lax.rsqrt(jnp.sum(key_raw * key_raw, axis=1, keepdims=True) + 1e-06)
        query_unit, key = query_raw * query_size, key_raw * key_size
        query = query_unit * DK**-0.5
        gamma, strict, carry, last = chunk_tables(c, head, cols, segr_ref, cum_ref)
        strength = beta[rows]
        dots = mm(jnp.concatenate([key, query], axis=0), key, NT)
        weights = strict * dots[:CHUNK]
        low = strength * weights
        scores = gamma * dots[CHUNK:]
        if c == 0:
            state = state_in
        else:
            state = st_ref[0, c] + mm(stm_ref[0, c], state_in)
        updates = upd_ref[0, rows, :DV] - mm(upd_ref[0, rows, DV:], state)
        d_attn = dattn_ref[rows, :]
        d_state = dstate_ref[c]
        d_updates = mm(scores, d_attn, TN) + mm(last * key, d_state)
        solved = mm(inv_ref[0, c], d_updates, TN)
        both = jnp.concatenate([d_attn, solved.astype(BF16)], axis=0)
        by_updates = mm(both, updates, NT)
        by_state = mm(both, state, NT)
        d_scores = by_updates[:CHUNK]
        d_low = -by_updates[CHUNK:]
        d_query = carry * by_state[:CHUNK]
        key_state = jnp.sum(key * by_state[CHUNK:], axis=1, keepdims=True)
        d_carry = jnp.sum(query * by_state[:CHUNK], axis=1, keepdims=True) - strength * key_state
        d_beta = (
            jnp.sum(solved * value, axis=1, keepdims=True)
            - carry * key_state
            + jnp.sum(d_low * weights, axis=1, keepdims=True)
        )
        d_dots_q = d_scores * gamma
        d_dots_k = d_low * strength * strict
        by_key = mm(jnp.concatenate([d_dots_q, d_dots_k], axis=0), key)
        d_query += by_key[:CHUNK]
        from_state = mm(updates, d_state, NT)
        d_key = (
            by_key[CHUNK:]
            + mm(
                jnp.concatenate([d_dots_q, d_dots_k], axis=0),
                jnp.concatenate([query, key], axis=0),
                TN,
            )
            - strength * carry * by_state[CHUNK:]
            + last * from_state
        )
        d_last = jnp.sum(key * from_state, axis=1, keepdims=True) * last
        d_spread = d_scores * scores + d_low * low
        final = (iota2((CHUNK, 1), 0) == CHUNK - 1).astype(F32)
        d_carry += final * jnp.sum(d_state * state)
        d_cum = (
            jnp.sum(d_spread, axis=1, keepdims=True)
            - to_column(jnp.sum(d_spread, axis=0, keepdims=True))
            + final * jnp.sum(d_last)
            - d_last
            + d_carry * carry
        )
        d_decay = jnp.sum(
            jnp.where(row_ids <= col_ids, to_row(d_cum), 0.0), axis=1, keepdims=True
        )
        dbeta_ref[rows, :] = jnp.broadcast_to(d_beta, (CHUNK, LANES))
        ddecay_ref[rows, :] = jnp.broadcast_to(d_decay, (CHUNK, LANES))
        d_query = d_query * DK**-0.5
        d_query = query_size * (
            d_query - query_unit * jnp.sum(d_query * query_unit, axis=1, keepdims=True)
        )
        d_key = key_size * (d_key - key * jnp.sum(d_key * key, axis=1, keepdims=True))
        d_value = strength * solved
        dmix_ref[HALO + c * CHUNK : HALO + (c + 1) * CHUNK, :] = slope * jnp.concatenate(
            [d_query, d_key, d_value], axis=1
        )


def backward_ends(
    head, taps_ref, logit_ref, par_ref, cols_ref, back_ref, dp_ref, dlogit_ref, dtaps_ref, dpar_ref,
    beta_ref, decay_ref, pf_ref, dmix_ref, dbeta_ref, ddecay_ref,
):
    cols = cols_ref[...]
    tokens = cols.shape[0]
    lanes = iota2((tokens, LANES), 1)
    slope = jax.nn.sigmoid(logit_ref[HALO:, :] + par_ref[1:2, :]) * -jnp.exp(par_ref[0:1, :])
    here = jnp.where(lanes == head, ddecay_ref[...], 0.0)
    d_first = here * slope
    strengths = beta_ref[...]
    d_second = jnp.where(lanes == head + H, dbeta_ref[...], 0.0) * strengths * (1.0 - strengths)
    dlogit_ref[...] += d_first + d_second
    dpar_ref[0:1, :] += jnp.sum(here * decay_ref[...], axis=0, keepdims=True)
    dpar_ref[1:2, :] += jnp.sum(d_first, axis=0, keepdims=True)

    dmix_ref[:HALO, :] = jnp.zeros((HALO, HC), F32)
    dmix_ref[HALO + tokens :, :] = jnp.zeros((8, HC), F32)
    d_mix = dmix_ref[HALO : HALO + tokens, :]
    dtaps_ref[...] = jnp.zeros_like(dtaps_ref)
    dtaps_ref[0:1, :] = jnp.sum(d_mix * pf_ref[HALO:, :], axis=0, keepdims=True)
    total = dmix_ref[: HALO + tokens, :] * taps_ref[0:1, :]
    for j in range(1, CONV):
        total += dmix_ref[j : j + HALO + tokens, :] * taps_ref[j : j + 1, :] * back_ref[:, j : j + 1]
        dtaps_ref[j : j + 1, :] = jnp.sum(
            d_mix * cols[:, j : j + 1] * pf_ref[HALO - j : HALO - j + tokens, :],
            axis=0,
            keepdims=True,
        )
    dp_ref[...] = total.astype(BF16)


def delta_backward(
    place, slots, proj, taps, logits, par, cols, back, segr, d_attn, state_in, exch, grads, saved
):
    rows = proj.shape[0]
    tokens = rows - HALO
    chunks = tokens // CHUNK
    places = exch.shape[0]
    whole = lambda shape: pl.BlockSpec(shape, lambda h: (0,) * len(shape))
    by_head = lambda shape: pl.BlockSpec(shape, lambda h: (h,) + (0,) * (len(shape) - 1))
    return pl.pallas_call(
        backward_kernel,
        grid=(H,),
        in_specs=[
            pl.BlockSpec(memory_space=pltpu.SMEM),
            pl.BlockSpec(memory_space=pltpu.SMEM),
            pl.BlockSpec((rows, HC), lambda h: (0, h)),
            pl.BlockSpec((8, HC), lambda h: (0, h)),
            whole((rows, LANES)),
            whole((8, LANES)),
            whole((tokens, LANES)),
            whole((rows, LANES)),
            whole(segr.shape),
            pl.BlockSpec((tokens, DV), lambda h: (0, h)),
            by_head((1, DK, DV)),
            pl.BlockSpec((places, 1, DK, DK), lambda h: (0, h, 0, DV // DK)),
            pl.BlockSpec((places, 1, DK, DV), lambda h: (0, h, 0, 0)),
            by_head((1, chunks, CHUNK, CHUNK)),
            by_head((1, tokens, DV + DK)),
            by_head((1, chunks, DK, DV)),
            by_head((1, chunks, DK, DK)),
            by_head((1, chunks, DK, DK)),
            by_head((1, chunks, CHUNK, DK)),
        ],
        out_specs=[
            pl.BlockSpec((rows, HC), lambda h: (0, h)),
            whole((tokens, LANES)),
            pl.BlockSpec((8, HC), lambda h: (0, h)),
            whole((8, LANES)),
        ],
        out_shape=[
            jax.ShapeDtypeStruct((rows, H * HC), BF16),
            jax.ShapeDtypeStruct((tokens, LANES), F32),
            jax.ShapeDtypeStruct((8, H * HC), F32),
            jax.ShapeDtypeStruct((8, LANES), F32),
        ],
        scratch_shapes=[
            pltpu.VMEM((tokens, LANES), F32),
            pltpu.VMEM((tokens, LANES), F32),
            pltpu.VMEM((tokens, LANES), F32),
            pltpu.VMEM((rows, HC), F32),
            pltpu.VMEM((tokens, HC), F32),
            pltpu.VMEM((rows + 8, HC), F32),
            pltpu.VMEM((chunks, DK, DV), F32),
            pltpu.VMEM((tokens, LANES), F32),
            pltpu.VMEM((tokens, LANES), F32),
        ],
        compiler_params=params(),
        cost_estimate=cost(8e9 * H, 5e6 * H),
        name="delta_backward",
    )(place, slots, proj, taps, logits, par, cols, back, segr, d_attn, state_in, exch, grads, *saved)


def mixer_kernel(
    place_ref, slot_ref, part_ref, resp_ref, exch_ref, gpre_ref, gain_ref, w_ref, x_ref, gain2_ref,
    sin_ref, attn_ref, gated_ref, y_ref, h_ref,
):
    head = pl.program_id(0)
    place = place_ref[0]
    places = exch_ref.shape[0]

    def ahead(source, state):
        slot = slot_ref[source]
        return jnp.where(
            source < place,
            exch_ref[slot, 0, :, :DV].astype(F32) + mm(exch_ref[slot, 0, :, DV:], state),
            state,
        )

    state = lax.fori_loop(0, places - 1, ahead, jnp.zeros((DK, DV), F32))
    sin_ref[0] = state
    attn = part_ref[...] + mm(resp_ref[...], state)
    attn_ref[...] = attn
    scale = lax.rsqrt(jnp.mean(attn * attn, axis=-1, keepdims=True) + 1e-05)
    gate = gpre_ref[...]
    gated = (attn * scale * gain_ref[...] * (gate * jax.nn.sigmoid(gate))).astype(BF16)
    gated_ref[...] = gated

    @pl.when(head == 0)
    def _():
        y_ref[...] = x_ref[...].astype(F32)

    y_ref[...] += mm(gated, w_ref[...], NT)

    @pl.when(head == pl.num_programs(0) - 1)
    def _():
        value = y_ref[...]
        size = lax.rsqrt(jnp.mean(value * value, axis=-1, keepdims=True) + 1e-06)
        h_ref[...] = (value * size * gain2_ref[...]).astype(BF16)


def mixer_out(place, slots, part, resp, exch, gpre, gain, weights, x, gain2):
    tokens, width = x.shape
    places = exch.shape[0]
    whole = lambda shape: pl.BlockSpec(shape, lambda h: (0,) * len(shape))
    return pl.pallas_call(
        mixer_kernel,
        grid=(H,),
        in_specs=[
            pl.BlockSpec(memory_space=pltpu.SMEM),
            pl.BlockSpec(memory_space=pltpu.SMEM),
            pl.BlockSpec((tokens, DV), lambda h: (0, h)),
            pl.BlockSpec((tokens, DK), lambda h: (0, h)),
            pl.BlockSpec((places, 1, DK, DV + DK), lambda h: (0, h, 0, 0)),
            pl.BlockSpec((tokens, DV), lambda h: (0, h)),
            whole((1, DV)),
            pl.BlockSpec((width, DV), lambda h: (0, h + AT_OUT // DV)),
            whole((tokens, width)),
            whole((1, width)),
        ],
        out_specs=[
            pl.BlockSpec((1, DK, DV), lambda h: (h, 0, 0)),
            pl.BlockSpec((tokens, DV), lambda h: (0, h)),
            pl.BlockSpec((tokens, DV), lambda h: (0, h)),
            whole((tokens, width)),
            whole((tokens, width)),
        ],
        out_shape=[
            jax.ShapeDtypeStruct((H, DK, DV), F32),
            jax.ShapeDtypeStruct((tokens, H * DV), F32),
            jax.ShapeDtypeStruct((tokens, H * DV), BF16),
            jax.ShapeDtypeStruct((tokens, width), F32),
            jax.ShapeDtypeStruct((tokens, width), BF16),
        ],
        compiler_params=params(),
        cost_estimate=cost(2 * tokens * width * H * DV, 2e7),
        name="mixer_out",
    )(place, slots, part, resp, exch, gpre, gain, weights, x, gain2)


def mixer_back_kernel(
    dmix_ref, w_ref, attn_ref, gpre_ref, gain_ref, resp_ref,
    dattn_ref, dgpre_ref, grad_ref, dgain_ref,
):
    @pl.when(pl.program_id(0) == 0)
    def _():
        dgain_ref[...] = jnp.zeros_like(dgain_ref)

    d_gain, dattn_ref[...], dgpre_ref[...], grad_ref[0] = mixer_back_head(
        dmix_ref, w_ref, attn_ref, gpre_ref, gain_ref, resp_ref
    )
    dgain_ref[0:1, :] += d_gain


def mixer_back_head(dmix_ref, w_ref, attn_ref, gpre_ref, gain_ref, resp_ref):
    d_gated = mm(dmix_ref[...], w_ref[...])
    attn = attn_ref[...]
    size = lax.rsqrt(jnp.mean(attn * attn, axis=-1, keepdims=True) + 1e-05)
    unit = attn * size
    gate = gpre_ref[...]
    slope = jax.nn.sigmoid(gate)
    swish = gate * slope
    gain = gain_ref[...]
    d_gpre = (d_gated * (unit * gain) * (slope * (1.0 + gate * (1.0 - slope)))).astype(BF16)
    d_normed = d_gated * swish
    d_gain = jnp.sum(d_normed * unit, axis=0, keepdims=True)
    d_unit = d_normed * gain
    d_attn = size * (d_unit - unit * jnp.mean(d_unit * unit, axis=-1, keepdims=True))
    d_attn = d_attn.astype(BF16)
    return d_gain, d_attn, d_gpre, mm(resp_ref[...], d_attn, TN).astype(BF16)


def mixer_back(d_mixer, weights, attn, gpre, gain, resp):
    tokens, width = d_mixer.shape
    whole = lambda shape: pl.BlockSpec(shape, lambda h: (0,) * len(shape))
    return pl.pallas_call(
        mixer_back_kernel,
        grid=(H,),
        in_specs=[
            whole((tokens, width)),
            pl.BlockSpec((width, DV), lambda h: (0, h + AT_OUT // DV)),
            pl.BlockSpec((tokens, DV), lambda h: (0, h)),
            pl.BlockSpec((tokens, DV), lambda h: (0, h)),
            whole((1, DV)),
            pl.BlockSpec((tokens, DK), lambda h: (0, h)),
        ],
        out_specs=[
            pl.BlockSpec((tokens, DV), lambda h: (0, h)),
            pl.BlockSpec((tokens, DV), lambda h: (0, h)),
            pl.BlockSpec((1, DK, DV), lambda h: (h, 0, 0)),
            whole((8, DV)),
        ],
        out_shape=[
            jax.ShapeDtypeStruct((tokens, H * DV), BF16),
            jax.ShapeDtypeStruct((tokens, H * DV), BF16),
            jax.ShapeDtypeStruct((H, DK, DV), BF16),
            jax.ShapeDtypeStruct((8, DV), F32),
        ],
        compiler_params=params(),
        cost_estimate=cost(2 * tokens * width * H * DV, 2e7),
        name="mixer_back",
    )(d_mixer, weights, attn, gpre, gain, resp)


def ffn_kernel(
    h_ref, dout_ref, gain_ref, y_any, turn_any, weights_ref,
    out_ref, act_ref, dgu_ref, dy_ref, dmix_ref, dgain_ref,
    w_ref, acts_ref, dg_ref, du_ref, res_ref, dh_ref, y_ref, turn_ref, load_sem, late_sem,
    *, inner, block, across, gain_row,
):
    step = pl.program_id(0)
    blocks = inner // block
    ends = blocks + dh_ref.shape[1] // across
    late = [
        pltpu.make_async_copy(source, to, late_sem.at[n])
        for n, (source, to) in enumerate(((y_any, y_ref), (turn_any, turn_ref)))
    ]

    def load(which, n):
        cols = pl.multiple_of(n * block, block)
        return pltpu.make_async_copy(
            weights_ref.at[:, pl.ds(AT_FFN + which * inner + cols, block)],
            w_ref.at[which, :, pl.ds(cols, block)],
            load_sem.at[which, n],
        )

    @pl.when(step == 0)
    def _():
        for n in range(blocks):
            for which in range(3):
                load(which, n).start()
        for copy in late:
            copy.start()

    @pl.when(step == blocks)
    def _():
        for copy in late:
            copy.wait()

    @pl.when(step < blocks)
    def _():
        for which in range(3):
            load(which, step).wait()
        cols = pl.ds(pl.multiple_of(step * block, block), block)
        hidden = h_ref[...]
        gate = mm(hidden, w_ref[0, :, cols])
        up = mm(hidden, w_ref[1, :, cols])
        d_act = mm(dout_ref[...], w_ref[2, :, cols])
        slope = jax.nn.sigmoid(gate)
        swish = gate * slope
        act = (swish * up).astype(BF16)
        act_ref[...] = act
        acts_ref[:, cols] = act
        d_gate = (d_act * up * slope * (1.0 + gate * (1.0 - slope))).astype(BF16)
        d_up = (d_act * swish).astype(BF16)
        dgu_ref[0] = d_gate
        dg_ref[:, cols] = d_gate
        dgu_ref[1] = d_up
        du_ref[:, cols] = d_up

    @pl.when((step >= blocks) & (step < ends))
    def _():
        rows = pl.ds(pl.multiple_of((step - blocks) * across, across), across)
        res_ref[:, rows] = y_ref[:, rows] + mm(acts_ref[...], w_ref[2, rows, :], NT)
        dh_ref[:, rows] = mm(dg_ref[...], w_ref[0, rows, :], NT) + mm(du_ref[...], w_ref[1, rows, :], NT)

    @pl.when(step == ends)
    def _():
        dgain_ref[...] = jnp.zeros_like(dgain_ref)

    @pl.when(step >= ends)
    def _():
        size = out_ref.shape[0]
        rows = pl.ds(pl.multiple_of((step - ends) * size, size), size)
        out_ref[...] = mm(res_ref[rows, :], turn_ref[...], NT).astype(BF16)
        value = y_ref[rows, :]
        size = lax.rsqrt(jnp.mean(value * value, axis=-1, keepdims=True) + 1e-06)
        unit = value * size
        d_hidden = dh_ref[rows, :]
        dgain_ref[0:1, :] += jnp.sum(d_hidden * unit, axis=0, keepdims=True)
        d_unit = d_hidden * gain_ref[gain_row : gain_row + 1, :]
        d_y = dout_ref[rows, :].astype(F32) + size * (
            d_unit - unit * jnp.mean(d_unit * unit, axis=-1, keepdims=True)
        )
        dy_ref[...] = d_y
        dmix_ref[...] = d_y.astype(BF16)


def feed_forward(hidden, d_out, y1, gains, gain_row, turn, weights, inner):
    tokens, width = hidden.shape
    block, across, part = 256, 512, 128
    blocks = inner // block
    ends = blocks + width // across
    once = lambda shape: pl.BlockSpec(shape, lambda j: (0,) * len(shape), pipeline_mode=pl.Buffered(1))
    whole = lambda shape: pl.BlockSpec(shape, lambda j: (0,) * len(shape))
    at = lambda j: jnp.minimum(j, blocks - 1)
    rows = pl.BlockSpec((part, width), lambda j: (jnp.maximum(j - ends, 0), 0))
    return pl.pallas_call(
        functools.partial(ffn_kernel, inner=inner, block=block, across=across, gain_row=gain_row),
        grid=(ends + tokens // part,),
        in_specs=[
            once((tokens, width)),
            once((tokens, width)),
            once(gains.shape),
        ]
        + [pl.BlockSpec(memory_space=pl.ANY)] * 3,
        out_specs=[
            rows,
            pl.BlockSpec((tokens, block), lambda j: (0, at(j))),
            pl.BlockSpec((2, tokens, block), lambda j: (0, 0, at(j))),
            rows, rows, whole((8, width)),
        ],
        out_shape=[
            jax.ShapeDtypeStruct((tokens, width), BF16),
            jax.ShapeDtypeStruct((tokens, inner), BF16),
            jax.ShapeDtypeStruct((2, tokens, inner), BF16),
            jax.ShapeDtypeStruct((tokens, width), F32),
            jax.ShapeDtypeStruct((tokens, width), BF16),
            jax.ShapeDtypeStruct((8, width), F32),
        ],
        scratch_shapes=[
            pltpu.VMEM((3, width, inner), BF16),
            pltpu.VMEM((tokens, inner), BF16),
            pltpu.VMEM((tokens, inner), BF16),
            pltpu.VMEM((tokens, inner), BF16),
            pltpu.VMEM((tokens, width), F32),
            pltpu.VMEM((tokens, width), F32),
            pltpu.VMEM((tokens, width), F32),
            pltpu.VMEM((width, width), BF16),
            pltpu.SemaphoreType.DMA((3, blocks)),
            pltpu.SemaphoreType.DMA((2,)),
        ],
        compiler_params=params(),
        cost_estimate=cost(12 * tokens * width * inner, 3e7),
        name="feed_forward",
    )(hidden, d_out, gains, y1, turn, weights)


BLOCK = HC
LEAD, EVERY = 8, 3


def other_index(step):
    return step - jnp.clip((step - LEAD + EVERY - 1) // EVERY, 0, H)


class Blocks:
    def __init__(self, inner):
        self.ups, self.downs = inner // (BLOCK // 2), inner // BLOCK
        self.outs = H * DV // BLOCK
        self.others = self.ups + self.downs + 2 * self.outs
        self.count = self.others + H + 1
        self.starts = [0, self.ups, self.ups + self.downs, self.ups + self.downs + self.outs, self.others]
        self.tail = inner - self.downs * BLOCK
        heads = [LEAD + EVERY * h for h in range(H)]
        rest = [n for n in range(self.count - 1) if n not in heads]
        parts = [rest[low:high] for low, high in zip(self.starts, self.starts[1:])]
        self.up_at, self.down_at, self.out_at, self.gate_at = parts
        self.head_at = heads

    def index(self, kind):
        low, high = self.starts[kind], self.starts[kind + 1]
        return lambda s: jnp.clip(other_index(s) - low, 0, high - low - 1)


def dot_blocks(left, right):
    return lax.dot_general(left, right, (NN, ((), ())), preferred_element_type=F32)


def flip_to(bit):
    here = lax.axis_index("seq")
    along_x = here + 1 - 2 * lax.rem(here, 2)
    along_y = here + 2 - 4 * (here // 2)
    return {"dp": lax.axis_index("dp"), "seq": (2 - bit) * along_x + (bit - 1) * along_y}


def reduce_kernel(
    dout_any, hmid_any, hidden_any, x_any, dy_any, turn_any, dres_ref,
    act_ref, tail_ref, dgu_ref, gated_ref, wout_ref, attn_ref, gpre_ref, gain_ref, resp_ref, win_ref, wl_ref,
    gains_ref, dffn_ref,
    p_ref, taps_q_ref, taps_k_ref, taps_v_ref, logit_ref, par_ref, cols_ref, back_ref, segr_ref, sin_ref, maps_ref,
    inv_ref, upd_ref, st_ref, stm_ref, amap_ref, rmap_ref,
    sum_ref, dx_ref, small_ref,
    taps_ref, dlogit_ref, dtaps_ref, dpar_ref, dgain_ref, dattn_ref, dgpre_ref, lgrad_ref, acc_ref, left_ref,
    total_ref, other_ref,
    beta_ref, decay_ref, cum_ref, pf_ref, pre_ref, dmix_ref, dstate_ref, dbeta_ref, ddecay_ref,
    turn_ref, dps_ref, halo_ref, grads_ref, halves_ref,
    core_keep, core_send, core_recv, near_keep, near_send, near_recv,
    z_keep, pair_send, pair_recv, cross_send, cross_recv, far_send, far_recv, done_ref,
    core_ss, core_rs, near_ss, near_rs, pair_ss, pair_rs, cross_ss, cross_rs, far_ss, far_rs, done_ss, done_rs, own_sem,
    halo_ss, halo_rs, grads_ss, grads_rs, load_sem, small_ss, small_rs, *, blocks,
):
    step = pl.program_id(0)
    steps = pl.num_programs(0)
    place = lax.axis_index("seq")
    count = blocks.count
    half = core_keep.shape[1] * core_keep.shape[2]
    quarter = half // SPOTS
    piece = quarter // PLANES
    mesh = dict(device_id_type=pl.DeviceIdType.MESH)

    def remote(source, target, send, recv, to):
        return pltpu.make_async_remote_copy(
            src_ref=source, dst_ref=target, send_sem=send, recv_sem=recv, device_id=to, **mesh
        )

    def to_core(n):
        mine, slot = lax.rem(n, 3), lax.rem(n, 4)
        return remote(core_send.at[mine], core_recv.at[slot], core_ss.at[mine], core_rs.at[slot], device(core=1))

    def to_near(n):
        slot = lax.rem(n, 4)
        return remote(
            near_send.at[slot], near_recv.at[slot], near_ss.at[slot], near_rs.at[slot], flip_to(1 + lax.rem(n, 2))
        )

    def to_far(n):
        slot = lax.rem(n, 4)
        return remote(
            far_send.at[slot], far_recv.at[slot], far_ss.at[slot], far_rs.at[slot], flip_to(2 - lax.rem(n, 2))
        )

    z = lax.axis_index("dp") // CORES
    inner = (z > 0) & (z < PLANES - 1)
    outer_plane = (z == 0) | (z == PLANES - 1)

    def to_pair(n, pieces):
        slot = lax.rem(n, 4)
        return remote(
            pair_send.at[slot, 0:pieces], pair_recv.at[slot, 0:pieces], pair_ss.at[slot], pair_rs.at[slot],
            device(planes=1 + 2 * lax.rem(z, 2)),
        )

    def to_cross(n, outside):
        planes = 2 if outside else 2 * z - 1
        slot = lax.rem(n, 4)
        return remote(
            cross_send.at[slot, outside], cross_recv.at[n], cross_ss.at[slot, outside], cross_rs.at[n],
            device(planes=planes),
        )

    def bits(n):
        pair = lax.rem(n, 2)
        along_x, along_y = lax.rem(place, 2), place // 2
        return (1 - pair) * along_x + pair * along_y, (1 - pair) * along_y + pair * along_x

    def spread(n):
        slot = lax.rem(n, 4)
        return remote(
            done_ref.at[slot], sum_ref.at[n, bits(n)[0]], done_ss.at[slot], done_rs.at[n], flip_to(1 + lax.rem(n, 2))
        )

    def keep(n):
        slot = lax.rem(n, 4)
        return pltpu.make_async_copy(done_ref.at[slot], sum_ref.at[n, bits(n)[0]], own_sem.at[slot])

    upper = place // 2 == 1
    second = lax.rem(place, 2) == 1

    def give_grads(head):
        return remote(
            lgrad_ref.at[head], grads_ref.at[0, head], grads_ss.at[0, head], grads_rs.at[0, head], device(spot=1)
        )

    def give_half(head):
        return remote(
            halves_ref.at[head], grads_ref.at[1, head], grads_ss.at[1, head], grads_rs.at[1, head], device(spot=2)
        )

    def give_small(stage):
        to = (dict(core=1), dict(spot=1), dict(spot=2), dict(planes=1), dict(planes=2), dict(planes=3))[stage]
        return remote(
            total_ref.at[min(stage, 3)], other_ref.at[stage], small_ss.at[stage], small_rs.at[stage], device(**to)
        )

    def load(at, source, to):
        return pltpu.make_async_copy(source, to, load_sem.at[at])

    def final_loads():
        width = turn_any.shape[0]
        copies = []
        for n in range(2):
            cols = slice(n * (width // 2), (n + 1) * (width // 2))
            copies.append(load(n, turn_any.at[:, cols], turn_ref.at[n]))
            rows = x_any.shape[0]
            copies.append(load(2 + n, x_any.at[:, cols], turn_ref.at[2, n * rows : (n + 1) * rows]))
            for q in range(SPOTS):
                copies.append(
                    load(4 + n * SPOTS + q, dy_any.at[q * quarter : (q + 1) * quarter, cols], core_keep.at[n, q])
                )
        return copies

    def final_stores():
        width = dx_ref.shape[1]
        return [
            load(
                n * SPOTS + q,
                core_keep.at[n, q],
                dx_ref.at[q * quarter : (q + 1) * quarter, n * (width // 2) : (n + 1) * (width // 2)],
            )
            for n in range(2)
            for q in range(SPOTS)
        ]

    def give_halo(head):
        to = {"dp": lax.axis_index("dp"), "seq": lax.rem(place + SPOTS - 1, SPOTS)}
        return remote(dps_ref.at[0:HALO], halo_ref.at[head], halo_ss.at[head], halo_rs.at[head], to)

    @pl.when(step == 0)
    def _():
        greet([dict(planes=d) for d in (1, 2, 3)] + [dict(spot=s) for s in (1, 2, 3)] + [dict(core=1)])
        dgain_ref[...] = jnp.zeros_like(dgain_ref)
        acc_ref[...] = jnp.zeros_like(acc_ref)

    def left(n):
        tokens = dres_ref.shape[0]
        source = (hmid_any, dout_any, hidden_any.at[HALO : HALO + tokens])[n]
        return load(n, source, left_ref.at[n % 2])

    for n, at in enumerate((1, 0, 3, 2)):

        @pl.when(step == n)
        def _(n=n, at=at):
            if n == 0:
                left(0).start()
            if n < 2:
                left(n + 1).start()
            if n < 3:
                left(n).wait()
                turn_ref[at] = jnp.transpose(left_ref[n % 2])
            else:
                turn_ref[at] = jnp.transpose(dres_ref[...])

    def at_stage(lag, sent):
        n = step - lag

        def run(body):
            @pl.when((n >= 0) & (n < count))
            def _():
                @pl.when(n >= sent)
                def _():
                    body(n, True)

                body(n, False)

        return run

    @at_stage(10, 4)
    def _(n, free):
        if free:
            spread(n - 4).wait_send()
            keep(n - 4).wait()
            return
        slot = lax.rem(n, 4)
        to_far(n).wait_recv()
        other = bits(n)[1]
        for which in range(2):
            total = far_send[slot, which].astype(F32) + far_recv[slot, 1 - which].astype(F32)
            done_ref[slot, other + which - 2 * other * which] = total.astype(BF16)
        spread(n).start()
        keep(n).start()

    @at_stage(8, 4)
    def _(n, free):
        if free:
            to_far(n - 4).wait_send()
            return
        slot = lax.rem(n, 4)
        to_cross(n, 0).wait_recv()
        total = (z_keep[slot, 0] + cross_recv[n].astype(F32)).astype(BF16)
        far_send[slot, 0], far_send[slot, 1] = total[:piece], total[piece:]
        to_far(n).start()

    @at_stage(6, 4)
    def _(n, free):
        slot = lax.rem(n, 4)
        if free:

            @pl.when(inner)
            def _():
                to_cross(n - 4, 0).wait_send()
                to_cross(n - 4, 1).wait_send()

            return

        @pl.when(outer_plane)
        def _():
            to_pair(n, 1).wait_recv()

        @pl.when(inner)
        def _():
            to_pair(n, 3).wait_recv()
            for outside, at in enumerate((5 - 2 * z, 2)):
                cross_send[slot, outside] = (
                    z_keep[slot, at] + pair_recv[slot, 1 + outside].astype(F32)
                ).astype(BF16)
                to_cross(n, outside).start()

        z_keep[slot, 0] += pair_recv[slot, 0].astype(F32)

    @at_stage(4, 4)
    def _(n, free):
        slot = lax.rem(n, 4)
        if free:

            @pl.when(outer_plane)
            def _():
                to_pair(n - 4, 3).wait_send()

            @pl.when(inner)
            def _():
                to_pair(n - 4, 1).wait_send()

            return
        to_near(n).wait_recv()
        for which in range(2):
            total = near_keep[slot, which] + near_recv[slot, which].astype(F32)
            for d in range(PLANES):
                z_keep[slot, d, which * piece : (which + 1) * piece] = total[d * piece : (d + 1) * piece]

        @pl.when(outer_plane)
        def _():
            up = 1 - z // 3
            for k in range(3):
                pair_send[slot, k] = z_keep[slot, up * (3 - k) + (1 - up) * (1 + k)].astype(BF16)
            to_pair(n, 3).start()

        @pl.when(inner)
        def _():
            pair_send[slot, 0] = z_keep[slot, 2 * z - 1].astype(BF16)
            to_pair(n, 1).start()

    @at_stage(2, 4)
    def _(n, free):
        if free:
            to_near(n - 4).wait_send()
            return
        slot, mine = lax.rem(n, 4), lax.rem(n, 3)
        first = 1 + lax.rem(n, 2)
        to_core(n).wait_recv()
        whole = lambda quarter: core_keep[mine, quarter] + core_recv[slot, quarter].astype(F32)
        near_keep[slot, 0] = whole(0)
        near_keep[slot, 1] = whole(3 - first)
        near_send[slot, 0] = whole(first).astype(BF16)
        near_send[slot, 1] = whole(3).astype(BF16)
        to_near(n).start()

    since = step - LEAD
    heads_turn = (since >= 0) & (since < EVERY * H) & (lax.rem(jnp.maximum(since, 0), EVERY) == 0)
    other = other_index(step)

    def put(product):
        mine = lax.rem(step, 3)

        @pl.when(step >= 3)
        def _():
            to_core(step - 3).wait_send()

        for q in range(SPOTS):
            core_keep[mine, q] = product[q * quarter : (q + 1) * quarter]
            core_send[mine, q] = product[half + q * quarter : half + (q + 1) * quarter].astype(BF16)
        to_core(step).start()

    def on(kind):
        low, high = blocks.starts[kind], blocks.starts[kind + 1]
        return pl.when((other >= low) & (other < high) & jnp.logical_not(heads_turn))

    @on(0)
    def _():
        put(dot_blocks(turn_ref[1], jnp.concatenate([dgu_ref[0], dgu_ref[1]], axis=1)))

    @on(1)
    def _():
        put(dot_blocks(turn_ref[0], act_ref[...]))

    @on(2)
    def _():
        put(dot_blocks(turn_ref[2], gated_ref[...]))

    @on(3)
    def _():
        gate = other - blocks.starts[3]
        value = jnp.concatenate([dgpre_ref[2 * gate], dgpre_ref[2 * gate + 1]], axis=1)
        acc_ref[...] += mm(value, win_ref[...], NT)
        put(dot_blocks(turn_ref[3], value))

    @pl.when(step == count - 1)
    def _():
        down = dot_blocks(turn_ref[0], tail_ref[...])
        gates = dot_blocks(turn_ref[3], dlogit_ref[...].astype(BF16))
        acc_ref[...] += mm(dlogit_ref[...], wl_ref[...], NT)
        rest = jnp.zeros((down.shape[0], BLOCK - down.shape[1] - LANES), F32)
        put(jnp.concatenate([down, gates, rest], axis=1))

    @pl.when(heads_turn)
    def _():
        head = since // EVERY

        @pl.when(place > 0)
        def _():
            give_halo(head).wait_send()

        @pl.when(place < SPOTS - 1)
        def _():
            give_halo(head).wait_recv()
            tokens = dps_ref.shape[0] - HALO
            dps_ref[tokens:, :] = (
                dps_ref[tokens:, :].astype(F32) + halo_ref[head].astype(F32)
            ).astype(BF16)

        value = dps_ref[HALO:, :]
        acc_ref[...] += mm(value, win_ref[...], NT)
        put(dot_blocks(turn_ref[3], value))

    @pl.when(step < H)
    def _():
        d_gain, dattn_ref[step], dgpre_ref[step], lgrad_ref[step] = mixer_back_head(
            dres_ref, wout_ref, attn_ref, gpre_ref, gain_ref, resp_ref
        )
        dgain_ref[...] += d_gain
        give_grads(step).start()

    @pl.when((step >= 2) & (step < H + 2))
    def _():
        head = step - 2
        give_grads(head).wait()

        @pl.when(upper)
        def _():
            mine, theirs = lgrad_ref[head], grads_ref[0, head]
            earlier = jnp.where(second, theirs, mine)
            later = jnp.where(second, mine, theirs)
            through = jnp.where(second, maps_ref[1, head], maps_ref[0, head])
            halves_ref[head] = (earlier.astype(F32) + mm(through, later, TN)).astype(BF16)
            give_half(head).start()

    ahead = since + EVERY
    for phase in range(PHASES):

        @pl.when((ahead >= 0) & (ahead < EVERY * H) & (lax.rem(jnp.maximum(ahead, 0), EVERY) == phase))
        def _(phase=phase):
            head = ahead // EVERY

            def entering():
                @pl.when(upper)
                def _():
                    grads_ref[1, head] = jnp.zeros((DK, DV), BF16)
                    give_half(head).wait_send()

                @pl.when(jnp.logical_not(upper))
                def _():
                    give_half(head).wait_recv()

                d_state = grads_ref[1, head].astype(F32)
                nearer = grads_ref[0, head].astype(F32) + mm(maps_ref[1, head], d_state, TN)
                return jnp.where(second, d_state, nearer)

            if phase == 0:
                join_taps(taps_ref, taps_q_ref, taps_k_ref, taps_v_ref)
            backward_head(
                phase, head, entering, p_ref, taps_ref, logit_ref, par_ref, cols_ref, back_ref, segr_ref,
                dattn_ref.at[head], sin_ref, inv_ref, upd_ref, st_ref, stm_ref, amap_ref, rmap_ref,
                dps_ref, dlogit_ref, dtaps_ref, dpar_ref, beta_ref, decay_ref, cum_ref, pf_ref, pre_ref, dmix_ref,
                dstate_ref, dbeta_ref, ddecay_ref,
            )
            if phase == PHASES - 1:
                total_ref[0, pl.ds(pl.multiple_of(head * 8, 8), 8), :] = dtaps_ref[...]

                @pl.when(place > 0)
                def _():
                    give_halo(head).start()

    @pl.when(step == count)
    def _():
        for copy in final_loads():
            copy.start()

    @pl.when(step == count + 2)
    def _():
        for copy in final_loads():
            copy.wait()
        tokens, width = acc_ref.shape
        middle = width // 2
        halves_of = lambda ref: jnp.concatenate([ref[0], ref[1]], axis=1)
        value = jnp.concatenate([turn_ref[2, :tokens], turn_ref[2, tokens:]], axis=1).astype(F32)
        size = lax.rsqrt(jnp.mean(value * value, axis=-1, keepdims=True) + 1e-06)
        unit = value * size
        d_hidden = acc_ref[...]
        d_gain = jnp.sum(d_hidden * unit, axis=0, keepdims=True)
        d_unit = d_hidden * gains_ref[0:1, :]
        through = size * (d_unit - unit * jnp.mean(d_unit * unit, axis=-1, keepdims=True))
        d_y = [jnp.concatenate([core_keep[n, q] for q in range(SPOTS)], axis=0) for n in range(2)]
        total = jnp.concatenate(d_y, axis=1) + through

        def natural(part):
            return mm(part[:, :middle], turn_ref[0], NT) + mm(part[:, middle:], turn_ref[1], NT)

        high, low = halves(total)
        total = natural(high) + natural(low)
        for n in range(2):
            for q in range(SPOTS):
                core_keep[n, q] = total[q * quarter : (q + 1) * quarter, n * middle : (n + 1) * middle]
        for copy in final_stores():
            copy.start()
        gains = jnp.concatenate([d_gain, dffn_ref[0:1, :], jnp.zeros((6, width), F32)], axis=0)
        high, mid = halves(gains)
        gains = natural(high) + natural(mid) + natural((gains - high.astype(F32)) - mid.astype(F32))
        base = 8 * H
        total_ref[0, base : base + 8, :] = gains[:, :middle]
        total_ref[0, base + 8 : base + 16, :] = gains[:, middle:]
        total_ref[0, base + 16 : base + 24, : dgain_ref.shape[1]] = dgain_ref[...]
        total_ref[0, base + 16 : base + 24, dgain_ref.shape[1] : dgain_ref.shape[1] + LANES] = dpar_ref[...]
        total_ref[0, base + 16 : base + 24, dgain_ref.shape[1] + LANES :] = jnp.zeros((8, LANES), F32)
        give_small(0).start()

    for stage in range(3):

        @pl.when(step == count + 3 + stage)
        def _(stage=stage):
            give_small(stage).wait_recv()
            total_ref[stage + 1] = total_ref[stage] + other_ref[stage]
            for later in (stage + 1,) if stage < 2 else (3, 4, 5):
                give_small(later).start()

    @pl.when(step == count + 6)
    def _():
        total = total_ref[3]
        for stage in (3, 4, 5):
            give_small(stage).wait_recv()
            total += other_ref[stage]
        small_ref[...] = total
        for stage in range(6):
            give_small(stage).wait_send()
        for copy in final_stores():
            copy.wait()

    @pl.when(step == steps - 1)
    def _():
        for n in range(count - 4, count):
            if n >= count - 3:
                to_core(n).wait_send()
            to_near(n).wait_send()
            to_far(n).wait_send()

            @pl.when(outer_plane)
            def _(n=n):
                to_pair(n, 3).wait_send()

            @pl.when(inner)
            def _(n=n):
                to_pair(n, 1).wait_send()
                to_cross(n, 0).wait_send()
                to_cross(n, 1).wait_send()

            spread(n).wait_send()
            keep(n).wait()

        def arrived(n, carry):
            spread(n).wait_recv()
            return carry

        lax.fori_loop(0, count, arrived, 0)


def reduce_gradients(
    d_out, hidden_mid, hidden, x, d_y, turn, d_mixer, act, d_gu, gated, weights, attn, gpre, gain_out, resp, gains,
    d_ffn, proj, taps, logits, par, cols, back, segr, state_in, maps, saved,
):
    tokens, width = d_mixer.shape
    rows = hidden.shape[0]
    chunks = tokens // CHUNK
    blocks = Blocks(act.shape[1])
    half = width // CORES
    quarter = half // SPOTS
    piece = quarter // PLANES
    small = 8 * H + 24
    anywhere = pl.BlockSpec(memory_space=pl.ANY)
    whole = lambda shape: pl.BlockSpec(shape, lambda s: (0,) * len(shape))
    once = lambda shape: pl.BlockSpec(shape, lambda s: (0,) * len(shape), pipeline_mode=pl.Buffered(1))
    coming = lambda s: jnp.clip((s - (LEAD - EVERY)) // EVERY, 0, H - 1)
    starting = lambda s: jnp.minimum(s, H - 1)
    by_head = lambda shape: pl.BlockSpec(shape, lambda s: (coming(s),) + (0,) * (len(shape) - 1))
    across = lambda shape, at: pl.BlockSpec(shape, lambda s: (0, at(s)))
    sem = pltpu.SemaphoreType.DMA
    up, down, out, gate = (blocks.index(kind) for kind in range(4))
    first_gate = blocks.gate_at[0]

    def win(s):
        no_head = ((s - LEAD) % EVERY != 0) | (s > blocks.head_at[-1])
        is_gate = (s >= first_gate) & (s <= blocks.gate_at[-1]) & no_head
        head = jnp.clip((s - LEAD + EVERY - 1) // EVERY, 0, H - 1)
        return jnp.where(is_gate, AT_GATE // BLOCK + gate(s), H - 1 - head)

    return blocks, pl.pallas_call(
        functools.partial(reduce_kernel, blocks=blocks),
        grid=(blocks.count + 10,),
        in_specs=[anywhere] * 6
        + [
            once((tokens, width)),
            across((tokens, BLOCK), down),
            pl.BlockSpec(
                (tokens, blocks.tail), lambda s: (0, blocks.downs * BLOCK // blocks.tail), pipeline_mode=pl.Buffered(1)
            ),
            pl.BlockSpec((2, tokens, BLOCK // 2), lambda s: (0, 0, up(s))),
            across((tokens, BLOCK), out),
            pl.BlockSpec((width, DV), lambda s: (0, AT_OUT // DV + starting(s))),
            across((tokens, DV), starting),
            across((tokens, DV), starting),
            once((1, DV)),
            across((tokens, DK), starting),
            across((width, BLOCK), win),
            pl.BlockSpec((width, LANES), lambda s: (0, AT_LOGIT // LANES), pipeline_mode=pl.Buffered(1)),
            once((8, width)),
            once((8, width)),
            across((rows, HC), coming),
            *taps_specs(coming),
            once((rows, LANES)),
            once((8, LANES)),
            once((tokens, LANES)),
            once((rows, LANES)),
            once(segr.shape),
            by_head((1, DK, DV)),
            once((2, H, DK, DK)),
            by_head((1, chunks, CHUNK, CHUNK)),
            by_head((1, tokens, DV + DK)),
            by_head((1, chunks, DK, DV)),
            by_head((1, chunks, DK, DK)),
            by_head((1, chunks, DK, DK)),
            by_head((1, chunks, CHUNK, DK)),
        ],
        out_specs=[anywhere, anywhere, whole((small, BLOCK))],
        out_shape=[
            jax.ShapeDtypeStruct((blocks.count, 2, 2, piece, BLOCK), BF16),
            jax.ShapeDtypeStruct((tokens, width), F32),
            jax.ShapeDtypeStruct((small, BLOCK), F32),
        ],
        scratch_shapes=[
            pltpu.VMEM((8, HC), F32),
            pltpu.VMEM((tokens, LANES), F32),
            pltpu.VMEM((8, HC), F32),
            pltpu.VMEM((8, LANES), F32),
            pltpu.VMEM((8, DV), F32),
            pltpu.VMEM((H, tokens, DV), BF16),
            pltpu.VMEM((H, tokens, DV), BF16),
            pltpu.VMEM((H, DK, DV), BF16),
            pltpu.VMEM((tokens, width), F32),
            pltpu.VMEM((2, tokens, width), BF16),
            pltpu.VMEM((4, small, BLOCK), F32),
            pltpu.VMEM((6, small, BLOCK), F32),
            pltpu.VMEM((tokens, LANES), F32),
            pltpu.VMEM((tokens, LANES), F32),
            pltpu.VMEM((tokens, LANES), F32),
            pltpu.VMEM((rows, HC), F32),
            pltpu.VMEM((tokens, HC), F32),
            pltpu.VMEM((rows + 8, HC), F32),
            pltpu.VMEM((chunks, DK, DV), F32),
            pltpu.VMEM((tokens, LANES), F32),
            pltpu.VMEM((tokens, LANES), F32),
            pltpu.VMEM((4, width, tokens), BF16),
            pltpu.VMEM((rows, HC), BF16),
            pltpu.VMEM((H, HALO, HC), BF16),
            pltpu.VMEM((2, H, DK, DV), BF16),
            pltpu.VMEM((H, DK, DV), BF16),
            pltpu.VMEM((3, SPOTS, quarter, BLOCK), F32),
            pltpu.VMEM((3, SPOTS, quarter, BLOCK), BF16),
            pltpu.VMEM((4, SPOTS, quarter, BLOCK), BF16),
            pltpu.VMEM((4, 2, quarter, BLOCK), F32),
            pltpu.VMEM((4, 2, quarter, BLOCK), BF16),
            pltpu.VMEM((4, 2, quarter, BLOCK), BF16),
            pltpu.VMEM((4, PLANES, 2 * piece, BLOCK), F32),
            pltpu.VMEM((4, PLANES - 1, 2 * piece, BLOCK), BF16),
            pltpu.VMEM((4, PLANES - 1, 2 * piece, BLOCK), BF16),
            pltpu.VMEM((4, 2, 2 * piece, BLOCK), BF16),
            pltpu.VMEM((blocks.count, 2 * piece, BLOCK), BF16),
            pltpu.VMEM((4, 2, piece, BLOCK), BF16),
            pltpu.VMEM((4, 2, piece, BLOCK), BF16),
            pltpu.VMEM((4, 2, piece, BLOCK), BF16),
            sem((3,)), sem((4,)), sem((4,)), sem((4,)), sem((4,)), sem((4,)),
            sem((4, 2)), sem((blocks.count,)), sem((4,)), sem((4,)),
            sem((4,)), sem((blocks.count,)), sem((4,)),
            sem((H,)), sem((H,)), sem((2, H)), sem((2, H)),
            sem((4 + 2 * SPOTS,)), sem((6,)), sem((6,)),
        ],
        compiler_params=params(collective_id=1, has_side_effects=True),
        cost_estimate=cost(1e11, 1e8),
        name="reduce_gradients",
    )(
        d_out, hidden_mid, hidden, x, d_y, turn, d_mixer, act, act, d_gu, gated, weights, attn, gpre, gain_out, resp,
        weights, weights, gains, d_ffn, proj, taps, taps, taps, logits, par, cols, back, segr, state_in, maps, *saved,
    )


def unpack_kernel(
    sum_ref, small_ref, dx_ref, query_ref, key_ref, value_ref, gate_ref, logit_ref, out_ref, wg_ref, wu_ref, wd_ref,
    taps_ref, mix_ref, ffn_ref, norm_ref, par_ref, dx_out, *, blocks
):
    dx_out[...] = dx_ref[...]
    for h in range(H):
        part = small_ref[8 * h : 8 * h + CONV, :]
        taps_ref[:, h * DK : (h + 1) * DK] = part[:, :DK]
        taps_ref[:, (H + h) * DK : (H + h + 1) * DK] = part[:, DK : 2 * DK]
        taps_ref[:, 2 * H * DK + h * DV : 2 * H * DK + (h + 1) * DV] = part[:, 2 * DK :]
    for row, ref in enumerate((mix_ref, ffn_ref)):
        for n in range(2):
            at = 8 * H + 8 * n + row
            ref[:, n * small_ref.shape[1] : (n + 1) * small_ref.shape[1]] = small_ref[at : at + 1, :]
    norm_ref[...] = small_ref[8 * H + 16 : 8 * H + 17, :DV]
    par_ref[...] = small_ref[8 * H + 16 : 8 * H + 24, DV : DV + LANES]

    def part(n, low=0, high=BLOCK):
        rows = []
        for spot in range(SPOTS):
            first, other = (spot % 2, spot // 2) if n % 2 == 0 else (spot // 2, spot % 2)
            rows.append(sum_ref[n, first, other, :, low:high])
        return jnp.concatenate(rows, axis=0).astype(F32)

    for h, n in enumerate(blocks.head_at):
        query_ref[:, h * DK : (h + 1) * DK] = part(n, 0, DK)
        key_ref[:, h * DK : (h + 1) * DK] = part(n, DK, 2 * DK)
        value_ref[:, h * DV : (h + 1) * DV] = part(n, 2 * DK, HC)
    for i, n in enumerate(blocks.gate_at):
        gate_ref[:, i * BLOCK : (i + 1) * BLOCK] = part(n)
    for i, n in enumerate(blocks.out_at):
        out_ref[i * BLOCK : (i + 1) * BLOCK, :] = jnp.transpose(part(n))
    middle = BLOCK // 2
    for i, n in enumerate(blocks.up_at):
        wg_ref[:, i * middle : (i + 1) * middle] = part(n, 0, middle)
        wu_ref[:, i * middle : (i + 1) * middle] = part(n, middle, BLOCK)
    for i, n in enumerate(blocks.down_at):
        wd_ref[i * BLOCK : (i + 1) * BLOCK, :] = jnp.transpose(part(n))
    last, tail = blocks.count - 1, blocks.tail
    wd_ref[blocks.downs * BLOCK :, :] = jnp.transpose(part(last, 0, tail))
    logit_ref[...] = jnp.transpose(part(last, tail, tail + LANES))[: 2 * H]


def unpack_gradients(blocks, sums, small, d_inputs):
    rows = SPOTS * sums.shape[3]
    inner = blocks.downs * BLOCK + blocks.tail
    width = d_inputs.shape[1]
    shapes = [
        (rows, H * DK), (rows, H * DK), (rows, H * DV), (rows, H * DV), (2 * H, rows), (H * DV, rows),
        (rows, inner), (rows, inner), (inner, rows), (CONV, H * HC), (1, width), (1, width), (1, DV), (8, LANES),
        d_inputs.shape,
    ]
    return pl.pallas_call(
        functools.partial(unpack_kernel, blocks=blocks),
        out_shape=[jax.ShapeDtypeStruct(shape, F32) for shape in shapes],
        compiler_params=params(),
        cost_estimate=cost(0, 6 * sums.size),
        name="unpack_gradients",
    )(sums, small, d_inputs)


def input_grad_kernel(
    dp_ref, dg_ref, dl_ref, w_ref, wl_ref, x_ref, gain_ref, dy_ref, out_ref, dgain_ref, acc_ref
):
    step = pl.program_id(0)

    @pl.when(step == 0)
    def _():
        acc_ref[...] = mm(dl_ref[...], wl_ref[...], NT)

    @pl.when(step < H)
    def _():
        acc_ref[...] += mm(dp_ref[...], w_ref[...], NT)

    @pl.when(step >= H)
    def _():
        acc_ref[...] += mm(dg_ref[...], w_ref[...], NT)

    @pl.when(step == pl.num_programs(0) - 1)
    def _():
        value = x_ref[...].astype(F32)
        size = lax.rsqrt(jnp.mean(value * value, axis=-1, keepdims=True) + 1e-06)
        unit = value * size
        d_hidden = acc_ref[...]
        dgain_ref[...] = jnp.zeros_like(dgain_ref)
        dgain_ref[0:1, :] = jnp.sum(d_hidden * unit, axis=0, keepdims=True)
        d_unit = d_hidden * gain_ref[...]
        out_ref[...] = dy_ref[...] + size * (
            d_unit - unit * jnp.mean(d_unit * unit, axis=-1, keepdims=True)
        )


def input_grad(d_proj, d_gpre, d_logit, weights, x, gain, d_y):
    tokens, width = x.shape
    block = HC
    second = d_gpre.shape[1] // block
    steps = H + second
    whole = lambda shape: pl.BlockSpec(shape, lambda j: (0,) * len(shape))
    late = lambda j: (0, jnp.maximum(j - H, 0))
    weight = lambda j: (0, jnp.where(j < H, H - 1 - j, j - H + AT_GATE // block))
    in_specs = [
        pl.BlockSpec((tokens, block), lambda j: (0, jnp.minimum(j, H - 1))),
        pl.BlockSpec((tokens, block), late),
        whole((tokens, LANES)),
        pl.BlockSpec((width, block), weight),
        pl.BlockSpec((width, LANES), lambda j: (0, AT_LOGIT // LANES)),
        whole((tokens, width)),
        whole((1, width)),
        whole((tokens, width)),
    ]
    return pl.pallas_call(
        input_grad_kernel,
        grid=(steps,),
        in_specs=in_specs,
        out_specs=[whole((tokens, width)), whole((8, width))],
        out_shape=[
            jax.ShapeDtypeStruct((tokens, width), F32),
            jax.ShapeDtypeStruct((8, width), F32),
        ],
        scratch_shapes=[pltpu.VMEM((tokens, width), F32)],
        compiler_params=params(),
        cost_estimate=cost(2 * tokens * width * steps * block, 3e7),
        name="input_grad",
    )(d_proj, d_gpre, d_logit, weights, weights, x, gain, d_y)


def shifted(block, axis, distance):
    devices = range(lax.axis_size(axis))
    route = [(i - distance, i) for i in devices if i - distance in devices]
    return lax.ppermute(block, axis, route)


def plain_sum(left, right, skip_left=0):
    part = lax.psum_scatter(outer(left, right, skip_left), "dp", scatter_dimension=0, tiled=True)
    return lax.psum(part, "seq").astype(F32)


def by_heads(query, key, value):
    lead = query.shape[:-1]
    parts = [query.reshape(lead + (H, DK)), key.reshape(lead + (H, DK)), value.reshape(lead + (H, DV))]
    return jnp.concatenate(parts, axis=-1).reshape(lead + (H * HC,))


def from_heads(value, heads=H):
    lead = value.shape[:-1]
    parts = value.reshape(lead + (heads, HC))
    return (
        parts[..., :DK].reshape(lead + (heads * DK,)),
        parts[..., DK : 2 * DK].reshape(lead + (heads * DK,)),
        parts[..., 2 * DK :].reshape(lead + (heads * DV,)),
    )


def token_rows(segments, place, tokens):
    ext = jnp.pad(segments, (HALO, LANES), constant_values=-1)
    ext = lax.dynamic_slice_in_dim(ext, place * tokens, tokens + LANES)
    seg = ext[HALO : HALO + tokens]
    blocks = seg.reshape(-1, CHUNK)
    before = ext[HALO - 1 : HALO - 1 + tokens : CHUNK]
    near = [seg] + [ext[HALO - j : HALO - j + tokens] == seg for j in range(1, CONV)]
    near += [(blocks == before[:, None]).reshape(-1), (blocks == blocks[:, -1:]).reshape(-1)]
    near = jnp.stack([row.astype(F32) for row in near])
    later = jnp.stack([(jnp.roll(ext, -j) == ext).astype(F32) for j in range(CONV)])
    return jnp.pad(near, ((0, 8 - near.shape[0]), (0, 0))), jnp.pad(later, ((0, 8 - CONV), (0, 0)))


def wide(value):
    return jnp.pad(value, ((0, 0), (0, LANES - value.shape[1])))


def local(
    inputs, segments, cotangent, norm_gain_mix, w_query, w_key, w_value, w_outgate, w_gates,
    conv_weight, decay_log, dt_bias, out_norm_gain, w_out, norm_gain_ffn, w_ffn_gate, w_ffn_up, w_ffn_down,
):
    tokens, width = inputs.shape[1:]
    place = lax.axis_index("seq")
    planned = (lax.axis_size("dp"), lax.axis_size("seq")) == (PLANES * CORES, SPOTS)
    low = lambda a: a.astype(BF16)
    inner = w_ffn_gate.shape[1]
    gain_out = out_norm_gain[None]

    if planned:
        taps = conv_weight
        shards = (w_query, w_key, w_value, w_outgate, w_gates.T, w_out, w_ffn_gate, w_ffn_up, w_ffn_down)
        outs = mixer_forward(
            inputs[0], cotangent[0], shards, (norm_gain_mix[None], norm_gain_ffn[None]), gain_out,
            decay_log[None], dt_bias[None], segments, conv_weight,
        )
        weights, hidden, x, d_out, turn, y1, hidden_mid, gains, segr, par, cols, back, *outs = outs
        proj, logits, resp, *outs = outs
        saved, (maps, state_in, attn, gpre, gated) = outs[:6], outs[6:]
        gain_row = 1
    else:
        taps = by_heads(conv_weight[:, : H * DK], conv_weight[:, H * DK : 2 * H * DK], conv_weight[:, 2 * H * DK :])
        taps = jnp.pad(taps, ((0, 8 - CONV), (0, 0)))
        par = jnp.pad(jnp.stack([decay_log, dt_bias]), ((0, 6), (0, LANES - H)))
        segr, later = token_rows(segments[0], place, tokens)
        turn = jnp.eye(width, dtype=BF16)
        qkv = by_heads(low(w_query), low(w_key), low(w_value))
        qkv = jnp.concatenate([qkv[:, h * HC : (h + 1) * HC] for h in reversed(range(H))], axis=1)
        gates = jnp.pad(low(w_gates), ((0, 0), (0, AT_GATE - AT_LOGIT - 2 * H)))
        shard = [qkv, gates, low(w_outgate), low(w_out).T, low(w_ffn_gate), low(w_ffn_up), low(w_ffn_down).T]
        weights = lax.all_gather(jnp.concatenate(shard, axis=1), "dp", axis=0, tiled=True)
        gain_mix, gain_ffn = norm_gain_mix[None], norm_gain_ffn[None]
        gains, gain_row = gain_ffn, 0
        cols = jnp.pad(segr.T, ((0, 0), (0, LANES - segr.shape[0])))
        back = jnp.pad(later.T[: tokens + HALO], ((0, 0), (0, LANES - later.shape[0])))
        x, d_out = inputs[0], cotangent[0]
        value = jnp.concatenate([shifted(x[tokens - HALO :], "seq", 1), x], axis=0).astype(F32)
        size = lax.rsqrt(jnp.mean(value * value, axis=-1, keepdims=True) + 1e-06)
        hidden = low(value * size * gain_mix)
        proj, logits, part, resp, exch, *saved = delta_forward(hidden, weights, taps, par, cols, segr)
        exch = lax.all_gather(exch[0], "seq")
        slots = jnp.arange(exch.shape[0], dtype=jnp.int32)
        place_arr = place.reshape((1,)).astype(jnp.int32)
        gpre = outgate(hidden, weights)
        state_in, attn, gated, y1, hidden_mid = mixer_out(
            place_arr, slots, part, resp, exch, gpre, gain_out, weights, x, gain_ffn
        )
    result, act, d_gu, d_y, d_mixer, d_gain_ffn = feed_forward(
        hidden_mid, d_out, y1, gains, gain_row, turn, weights, inner
    )
    if planned:
        blocks, (sums, d_inputs, small) = reduce_gradients(
            d_out, hidden_mid, hidden, x, d_y, turn, d_mixer, act, d_gu, gated, weights, attn, gpre, gain_out, resp,
            gains, d_gain_ffn, proj, taps, logits, par, cols, back, segr, state_in, maps, saved,
        )
        (
            g_query, g_key, g_value, g_og, g_gates, g_out, g_gate, g_up, g_down,
            d_conv, d_gain_mix, d_gain_ffn, d_gain_out, d_par, d_inputs,
        ) = unpack_gradients(blocks, sums, small, d_inputs)
        g_gates = g_gates.T
        d_gain_mix, d_gain_ffn, d_gain_out = d_gain_mix[0], d_gain_ffn[0], d_gain_out[0]
        d_decay_log, d_dt_bias = d_par[0, :H], d_par[1, :H]
    else:
        d_attn, d_gpre, local_grad, d_gain_out = mixer_back(d_mixer, weights, attn, gpre, gain_out, resp)
        grads = lax.all_gather(local_grad, "seq")
        d_proj, d_logits, d_taps, d_par = delta_backward(
            place_arr, slots, proj, taps, logits, par, cols, back, segr, d_attn, state_in, exch, grads, saved
        )
        sent_back = shifted(d_proj[:HALO], "seq", -1)
        d_proj = d_proj.at[tokens:].add(sent_back)[HALO:]
        d_logit = low(d_logits)
        g_down = plain_sum(d_out, act).T
        g_gate = plain_sum(hidden_mid, d_gu[0])
        g_up = plain_sum(hidden_mid, d_gu[1])
        g_out = plain_sum(d_mixer, gated).T
        g_og = plain_sum(hidden, d_gpre, HALO)
        g_query, g_key, g_value = from_heads(plain_sum(hidden, d_proj, HALO))
        g_gates = plain_sum(hidden, d_logit, HALO)
        d_inputs, d_gain_mix = input_grad(d_proj, d_gpre, d_logit, weights, x, gain_mix, d_y)
        d_conv = jnp.concatenate(from_heads(d_taps[:CONV]), axis=1)
        d_gain_mix, d_conv, d_decay_log, d_dt_bias, d_gain_out, d_gain_ffn = lax.psum(
            (d_gain_mix[0], d_conv, d_par[0, :H], d_par[1, :H], d_gain_out[0], d_gain_ffn[0]), ("dp", "seq")
        )
    return (
        result[None], d_inputs[None], d_gain_mix, g_query, g_key, g_value, g_og,
        g_gates[:, : 2 * H], d_conv, d_decay_log, d_dt_bias, d_gain_out, g_out,
        d_gain_ffn, g_gate, g_up, g_down,
    )


def solution(mesh):
    rows, cols, copied = P("dp", None), P(None, "dp"), P()
    tokens = P("dp", "seq", None)
    in_specs = (
        tokens, rows, tokens, copied, rows, rows, rows, rows, rows,
        copied, copied, copied, copied, cols, copied, rows, rows, cols,
    )
    out_specs = (
        tokens, tokens, copied, rows, rows, rows, rows, rows,
        copied, copied, copied, copied, cols, copied, rows, rows, cols,
    )
    return jax.shard_map(local, mesh=mesh, in_specs=in_specs, out_specs=out_specs, check_vma=False)
```
